32 devices in a mesh: seg: 8 (over z, x), rep: 4 (over y, core).
Axes of the slice: x: 2, y: 2, z: 4, core: 2. Of those that a mesh axis runs over, the one named last changes fastest.
Arguments:
- layer_input: bfloat16 [4, 1536, 1024], P('rep', 'seg'), may hold values from -6 to 6
- live: int32 [4, 1536], P('rep', 'seg'), may hold values from 0 to 1, as said below
- knn_index: int32 [4, 1536, 128], P('rep', 'seg'), may hold values from -1 to 2879, as said below
- mem_keys: bfloat16 [4, 1536, 1024], P('rep', 'seg'), may hold values from -6 to 6
- mem_values: bfloat16 [4, 1536, 1024], P('rep', 'seg'), may hold values from -6 to 6
- gain_attn: bfloat16 [1024], P(('seg', 'rep')), may hold values from 0.099609375 to 1.8984375
- w_query: bfloat16 [1024, 1024], P(('seg', 'rep')), may hold values from -0.1875 to 0.1875
- w_key: bfloat16 [1024, 1024], P(('seg', 'rep')), may hold values from -0.1875 to 0.1875
- w_value: bfloat16 [1024, 1024], P(('seg', 'rep')), may hold values from -0.1875 to 0.1875
- w_out: bfloat16 [1024, 1024], P(('seg', 'rep')), may hold values from -2 to 2
- gain_ffn: bfloat16 [1024], P(('seg', 'rep')), may hold values from 0.099609375 to 1.8984375
- w_gate: bfloat16 [1024, 2816], P(('seg', 'rep')), may hold values from -0.1875 to 0.1875
- w_up: bfloat16 [1024, 2816], P(('seg', 'rep')), may hold values from -0.1875 to 0.1875
- w_down: bfloat16 [2816, 1024], P(('seg', 'rep')), may hold values from -0.109375 to 0.109375
- cotangent: bfloat16 [4, 1536, 1024], P('rep', 'seg'), may hold values from -6 to 6
Outputs:
- layer_output: bfloat16 [4, 1536, 1024], P('rep', 'seg')
- grad_x: bfloat16 [4, 1536, 1024], P('rep', 'seg')
- grad_gain_attn: float32 [1024], P(('seg', 'rep'))
- grad_w_query: float32 [1024, 1024], P(('seg', 'rep'))
- grad_w_key: float32 [1024, 1024], P(('seg', 'rep'))
- grad_w_value: float32 [1024, 1024], P(('seg', 'rep'))
- grad_w_out: float32 [1024, 1024], P(('seg', 'rep'))
- grad_gain_ffn: float32 [1024], P(('seg', 'rep'))
- grad_w_gate: float32 [1024, 2816], P(('seg', 'rep'))
- grad_w_up: float32 [1024, 2816], P(('seg', 'rep'))
- grad_w_down: float32 [2816, 1024], P(('seg', 'rep'))
The draws below stay inside these ranges and needn't reach their ends.
Inputs may be any that keep to these rules, and one draw needn't show every extreme that they name: `knn_index`: each pick is a live slot of the query's row (m) or of the paired row (1536 + m) that lies in an earlier segment than the query's own; -1 marks an empty pick; a slot may repeat and counts once; queries of a row's first segment retrieve nothing. Padded slots fill the tail of a document's last segment; the first token of every segment is live; in every draw some pair of rows each hold one document over all their segments.
All inputs are finite; a program needn't handle non-finite values.
Results may differ from the reference program's by a relative error of at most 0.023.
Values may be sent and summed in bfloat16 or wider, within the bound.
No kernel may reach another device: no remote copies, remote signals or barrier semaphores. Data moves between devices by JAX's collectives and lax.ppermute only.
A program may use at most 320 MiB of HBM per device.

```python
import jax
import jax.numpy as jnp
from jax import lax

D = 1024
FF = 2816
H = 8
HD = 128
SEG = 192
TOPK = 128
TOKENS = 1536
BATCH = 4


def live_table(key):
    segments = TOKENS // SEG
    key_row, key_coin, key_count = jax.random.split(key, 3)
    full_row = jax.random.randint(key_row, (), 0, BATCH)
    coin = jax.random.randint(key_coin, (BATCH, segments), 0, 4) == 0
    last_seg = jnp.arange(segments) == segments - 1
    row_ids = jnp.arange(BATCH)[:, None]
    whole = (row_ids == full_row) | (jnp.bitwise_xor(row_ids, 1) == full_row)
    ends = jnp.where(whole, last_seg[None, :], coin | last_seg[None, :])
    counts = jax.random.randint(key_count, (BATCH, segments), max(SEG // 8, 1), SEG + 1)
    counts = jnp.where(ends, counts, SEG)
    position = jnp.arange(SEG)
    table = position[None, None, :] < counts[:, :, None]
    return (table.astype(jnp.int32).reshape(BATCH, TOKENS), full_row)


def draw_live(key, part):
    table, full_row = live_table(key)
    return table


def draw_knn_index(key, part):
    table, full_row = live_table(key)
    key = jax.random.fold_in(key, 7)
    key_pick, key_side = jax.random.split(key)
    seg_ids = jnp.arange(TOKENS) // SEG
    upper = jnp.maximum(seg_ids * SEG, 1)
    picks = jax.random.randint(key_pick, (BATCH, TOKENS, TOPK), 0, upper[None, :, None])
    side = jax.random.randint(key_side, (BATCH, TOKENS, TOPK), 0, 2)
    rows = jnp.arange(BATCH)[:, None, None]
    source = jnp.where(side == 1, jnp.bitwise_xor(rows, 1), rows)
    looked = table[source, picks]
    usable = (seg_ids[None, :, None] > 0) & (looked == 1)
    result = jnp.where(usable, picks + side * TOKENS, -1).astype(jnp.int32)
    places = jnp.arange(TOKENS)[None, :, None]
    slots = jnp.arange(TOPK)[None, None, :]
    at_query = (rows == full_row) & (places == TOKENS - SEG)
    result = jnp.where(at_query & (slots == 0), TOKENS - SEG - 1, result)
    result = jnp.where(at_query & (slots == 1), 2 * TOKENS - SEG - 1, result)
    return result.astype(jnp.int32)


def block_levels(own_key, extent, cuts, low, top_value):
    level = 1.0
    for dim, shards_of in cuts:
        steps = jax.random.uniform(jax.random.fold_in(jax.random.fold_in(own_key, 6), dim), (shards_of,), jnp.float32, low / len(cuts), top_value / len(cuts))
        level = level * jnp.repeat(jnp.exp(steps), extent[dim] // shards_of).reshape((-1,) + (1,) * (len(extent) - 1 - dim))
    return level


def bell_draw(stream_key, shape, scale, reach, shards=(), kind=jnp.bfloat16):
    level = block_levels(stream_key, shape, shards, -0.22, 0.18) if shards else 1.0
    values = jax.random.normal(stream_key, shape, jnp.float32) * scale * level
    return jnp.minimum(jnp.maximum(values, -reach), reach).astype(kind)


def setup_inputs(seed: int = 0) -> dict:
    key_list = jax.random.split(jax.random.key(seed), 16)
    layer_input = bell_draw(key_list[0], (BATCH, TOKENS, D), 1.0, 6.0, ((0, 4), (1, 8)))
    live = draw_live(jax.random.fold_in(key_list[15], 71), 0)
    knn_index = draw_knn_index(jax.random.fold_in(key_list[15], 71), 0)
    mem_keys = bell_draw(key_list[3], (BATCH, TOKENS, D), 1.0, 6.0, ((0, 4), (1, 8)))
    mem_values = bell_draw(key_list[4], (BATCH, TOKENS, D), 1.0, 6.0, ((0, 4), (1, 8)))
    gain_attn = jnp.clip(1.0 + 0.18 * jax.random.normal(key_list[5], (D,), jnp.float32), 0.099609375, 1.8984375).astype(jnp.bfloat16)
    w_query = bell_draw(key_list[6], (D, D), D ** -0.5, 0.1875, ((0, 32),))
    w_key = bell_draw(key_list[7], (D, D), D ** -0.5, 0.1875, ((0, 32),))
    w_value = bell_draw(key_list[8], (D, D), D ** -0.5, 0.1875, ((0, 32),))
    w_out = bell_draw(key_list[9], (D, D), (D // 128) ** -0.5, 2.0, ((0, 32),))
    gain_ffn = jnp.clip(1.0 + 0.18 * jax.random.normal(key_list[10], (D,), jnp.float32), 0.099609375, 1.8984375).astype(jnp.bfloat16)
    w_gate = bell_draw(key_list[11], (D, FF), D ** -0.5, 0.1875, ((0, 32),))
    w_up = bell_draw(key_list[12], (D, FF), D ** -0.5, 0.1875, ((0, 32),))
    w_down = bell_draw(key_list[13], (FF, D), FF ** -0.5, 0.109375, ((0, 32),))
    cotangent = bell_draw(key_list[14], (BATCH, TOKENS, D), 1.0, 6.0, ((0, 4), (1, 8)))
    return {"layer_input": layer_input, "live": live, "knn_index": knn_index, "mem_keys": mem_keys, "mem_values": mem_values, "gain_attn": gain_attn, "w_query": w_query, "w_key": w_key, "w_value": w_value, "w_out": w_out, "gain_ffn": gain_ffn, "w_gate": w_gate, "w_up": w_up, "w_down": w_down, "cotangent": cotangent}


@jax.custom_vjp
def low(v):
    return lax.optimization_barrier(v.astype(jnp.bfloat16)).astype(jnp.float32)

@jax.custom_vjp
def low_back(v):
    return v

def low_keep(v):
    return (low(v), None)

def low_pass(kept, grad):
    return (grad,)

def back_keep(v):
    return (v, None)

def back_low(kept, grad):
    return (low(grad),)
low.defvjp(low_keep, low_pass)
low_back.defvjp(back_keep, back_low)
EPSILON = 1e-05
NEG_BIG = -1e+30
ROPE_BASE = 10000.0

def rms_norm(values, gain):
    return values * lax.rsqrt(lax.optimization_barrier(jnp.mean(values * values, axis=-1, keepdims=True)) + EPSILON) * gain

def rope_table():
    position = jnp.arange(SEG).astype(jnp.float32)
    freqs = ROPE_BASE ** (-(2.0 * jnp.arange(HD // 2).astype(jnp.float32)) / HD)
    angle = position[:, None] * freqs[None, :]
    return (jnp.cos(angle), jnp.sin(angle))

def rotate(values, cosine, sine):
    half = HD // 2
    first = values[..., :half]
    second = values[..., half:]
    cos_b = cosine[:, None, :]
    sin_b = sine[:, None, :]
    return jnp.concatenate([first * cos_b - second * sin_b, first * sin_b + second * cos_b], -1)

def project(left, right):
    return jnp.dot(left, right, precision=lax.Precision.HIGHEST)

def segment_layer(x_float, weights, mem_k, mem_v, allow_local, allow_mem):
    g_attn, wq, wk, wv, wo, g_ffn, wg, wu, wd = weights
    cosine, sine = rope_table()
    h_one = low(rms_norm(x_float, g_attn))
    queries = low(rotate(low_back(project(h_one, wq)).reshape(SEG, H, HD), cosine, sine))
    keys_local = low(rotate(low_back(project(h_one, wk)).reshape(SEG, H, HD), cosine, sine))
    values_local = low_back(low(project(h_one, wv))).reshape(SEG, H, HD)
    scale = HD ** (-0.5)
    s_local = jnp.einsum('qhd,khd->hqk', queries, keys_local, precision=lax.Precision.HIGHEST) * scale
    s_memory = jnp.einsum('qhd,khd->hqk', queries, mem_k, precision=lax.Precision.HIGHEST) * scale
    scores = low_back(jnp.concatenate([s_local, s_memory], -1))
    allowed = jnp.concatenate([allow_local, allow_mem], -1)
    scores = jnp.where(allowed[None], scores, NEG_BIG)
    chances = low(jax.nn.softmax(scores, axis=-1))
    all_values = jnp.concatenate([values_local, mem_v], 0)
    attended = jnp.einsum('hqk,khd->qhd', chances, all_values, precision=lax.Precision.HIGHEST).reshape(SEG, D)
    attended = low_back(low(attended))
    x_one = x_float + low_back(project(attended, wo))
    h_two = low(rms_norm(x_one, g_ffn))
    gate = low_back(project(h_two, wg))
    upward = low_back(project(h_two, wu))
    hidden = low(jax.nn.silu(gate) * upward)
    return x_one + project(hidden, wd)

def reference(layer_input, live, knn_index, mem_keys, mem_values, gain_attn, w_query, w_key, w_value, w_out, gain_ffn, w_gate, w_up, w_down, cotangent):
    weights = tuple((w.astype(jnp.float32) for w in (gain_attn, w_query, w_key, w_value, w_out, gain_ffn, w_gate, w_up, w_down)))
    segments = TOKENS // SEG
    number = BATCH * segments
    x_all = layer_input.astype(jnp.float32).reshape(number, SEG, D)
    cot_all = cotangent.astype(jnp.float32).reshape(number, SEG, D)
    live_all = live.reshape(number, SEG)
    picks_all = knn_index.reshape(number, SEG, TOPK)
    row_ids = (jnp.arange(number, dtype=jnp.int32) // segments).astype(jnp.int32)
    mem_k = mem_keys.astype(jnp.float32).reshape(BATCH, TOKENS, H, HD)
    mem_v = mem_values.astype(jnp.float32).reshape(BATCH, TOKENS, H, HD)
    position = jnp.arange(SEG, dtype=jnp.int32)
    causal = position[None, :] <= position[:, None]
    diagonal = position[None, :] == position[:, None]

    def one_segment(totals, item):
        x_float, cot_float, live_seg, picks, row_id = item
        paired = jnp.bitwise_xor(row_id, 1).astype(jnp.int32)
        allow_local = causal & ((live_seg[None, :] == 1) | diagonal)
        columns = jnp.where(picks >= 0, picks, 2 * TOKENS).astype(jnp.int32)
        allow_mem = jnp.zeros((SEG, 2 * TOKENS), jnp.float32).at[position[:, None], columns].set(1.0, mode='drop') > 0.5
        keys_row = jnp.concatenate([mem_k[row_id], mem_k[paired]], 0)
        values_row = jnp.concatenate([mem_v[row_id], mem_v[paired]], 0)

        def apply(x_in, *params):
            return segment_layer(x_in, params, keys_row, values_row, allow_local, allow_mem)
        result, pull = jax.vjp(apply, x_float, *weights)
        grads = pull(cot_float)
        new_totals = tuple((t + g for t, g in zip(totals, grads[1:])))
        return (new_totals, (result, grads[0]))
    start_totals = tuple((jnp.zeros_like(w) for w in weights))
    totals, (results, grad_inputs) = lax.scan(one_segment, start_totals, (x_all, cot_all, live_all, picks_all, row_ids))
    layer_output = results.reshape(BATCH, TOKENS, D).astype(jnp.bfloat16)
    grad_x = grad_inputs.reshape(BATCH, TOKENS, D).astype(jnp.bfloat16)
    return (layer_output, grad_x, totals[0], totals[1], totals[2], totals[3], totals[4], totals[5], totals[6], totals[7], totals[8])
```

```python
import jax
import jax.numpy as jnp
from jax import lax
from jax.experimental import pallas as pl
from jax.experimental.pallas import tpu as pltpu
from jax.sharding import PartitionSpec as P

H = 8
HD = 128
EPSILON = 1e-05
NEG_BIG = -1e30
POS_BIG = 1e30
ROPE_BASE = 10000.0
LANES = 128
KERNEL_SEGMENTS = 16

BF = jnp.bfloat16
F32 = jnp.float32


def cdiv(a, b):
    return -(-a // b)


def flip(value, axis, bit):
    count = lax.axis_size(axis)
    return lax.ppermute(value, axis, [(i, i ^ bit) for i in range(count)])


def core_swap(value):
    return flip(value, "rep", 1)


def ordered(mine, other, bit, axis):
    first = jnp.where(bit == 0, mine, other)
    second = jnp.where(bit == 0, other, mine)
    return jnp.concatenate([first, second], axis)


def pick(value, index, axis):
    return lax.dynamic_index_in_dim(value, index, axis, keepdims=False)


def seg_bits():
    bit = 2
    out = []
    while bit < lax.axis_size("seg"):
        out.append(bit)
        bit *= 2
    return out


def gather_chips(shard):
    rows, cols = shard.shape
    seg = lax.axis_index("seg")
    cur = shard[None, None]
    for bit in seg_bits():
        side = (seg // bit) % 2
        cur = ordered(cur, flip(cur, "seg", bit), side, 0)
    cur = cur.reshape(-1, 1, 1, rows, cols)
    cur = ordered(cur, flip(cur, "seg", 1), seg % 2, 1)
    cur = ordered(cur, flip(cur, "rep", 2), lax.axis_index("rep") // 2, 2)
    return cur.reshape(-1, cols)


def halve(value, axis_name, bit, side, axis):
    recv = flip(pick(value, 1 - side, axis), axis_name, bit)
    kept = pick(value, side, axis)
    return (kept.astype(F32) + recv.astype(F32)).astype(BF)


def reduce_chips(full, x_first):
    total, cols = full.shape
    n_seg = lax.axis_size("seg")
    seg = lax.axis_index("seg")
    side_y = lax.axis_index("rep") // 2
    cur = full.reshape(n_seg // 2, 2, 2, total // (2 * n_seg), cols)
    if x_first:
        cur = halve(cur, "seg", 1, seg % 2, 1)
        cur = halve(cur, "rep", 2, side_y, 1)
    else:
        cur = halve(cur, "rep", 2, side_y, 2)
        cur = halve(cur, "seg", 1, seg % 2, 1)
    for bit in reversed(seg_bits()):
        cur = cur.reshape((2, cur.shape[0] // 2) + cur.shape[1:])
        cur = halve(cur, "seg", bit, (seg // bit) % 2, 0)
    return cur.reshape(cur.shape[-2:])


def matmul(left, right):
    return jnp.dot(left, right, preferred_element_type=F32)


def matmul_rows(left, right):
    return lax.dot_general(left, right, (((0,), (0,)), ((), ())), preferred_element_type=F32)


def matmul_cols(left, right):
    return lax.dot_general(left, right, (((1,), (1,)), ((), ())), preferred_element_type=F32)


def norm_forward(values, gain):
    inverse = lax.rsqrt(jnp.mean(values * values, axis=-1, keepdims=True) + EPSILON)
    return (values * inverse * gain, inverse)


def norm_backward(values, inverse, gain, grad_out):
    normed = values * inverse
    scaled = grad_out * gain
    grad_values = inverse * (scaled - normed * jnp.mean(scaled * normed, axis=-1, keepdims=True))
    return (grad_values, normed)


def rope_tables(seg_len):
    position = jnp.arange(seg_len).astype(F32)
    freqs = ROPE_BASE ** (-(2.0 * jnp.arange(HD // 2).astype(F32)) / HD)
    angle = position[:, None] * freqs[None, :]
    cosine, sine = jnp.cos(angle), jnp.sin(angle)
    return (jnp.concatenate([cosine, cosine], -1), jnp.concatenate([-sine, sine], -1))


def rope_heads(values, cosine, sine):
    half = HD // 2
    swapped = jnp.concatenate([values[..., half:], values[..., :half]], -1)
    return values * cosine[:, None, :] + swapped * sine[:, None, :]


def mask_kernel(n_cols, cols_ref, out_ref, scratch):
    queries = cols_ref.shape[1]
    picks = cols_ref[0]
    pad = scratch.shape[0]
    high = lax.shift_right_arithmetic(picks, 7)
    low = jnp.bitwise_and(picks, LANES - 1)
    iota_high = lax.broadcasted_iota(jnp.int32, (pad, picks.shape[1]), 0)
    iota_low = lax.broadcasted_iota(jnp.int32, (LANES, picks.shape[1]), 0)
    for i in range(queries):
        hot_high = jnp.where(iota_high == high[i : i + 1, :], 1.0, 0.0).astype(BF)
        hot_low = jnp.where(iota_low == low[i : i + 1, :], 1.0, 0.0).astype(BF)
        scratch[:, i, :] = matmul_cols(hot_high, hot_low)
    out_ref[0] = jnp.where(scratch[0:n_cols] > 0.5, POS_BIG, NEG_BIG).astype(BF)


def build_mask(columns, n_cols):
    rows, queries, picks = columns.shape
    block = 16
    return pl.pallas_call(
        lambda *refs: mask_kernel(n_cols, *refs),
        grid=(rows, queries // block),
        in_specs=[pl.BlockSpec((1, block, picks), lambda r, g: (r, g, 0))],
        out_specs=pl.BlockSpec((1, n_cols, block, LANES), lambda r, g: (r, 0, g, 0)),
        out_shape=jax.ShapeDtypeStruct((rows, n_cols, queries, LANES), BF),
        scratch_shapes=[pltpu.VMEM((cdiv(n_cols, 8) * 8, block, LANES), F32)],
        compiler_params=pltpu.CompilerParams(vmem_limit_bytes=16 * 1024 * 1024),
        name="mask_build",
    )(columns)


def lane_blocks(value):
    return [value[:, i : i + LANES] for i in range(0, value.shape[1], LANES)]


def forward_kernel(n_pieces, q_ref, k_ref, v_ref, live_ref, mask_ref, *refs):
    pieces = refs[:n_pieces]
    o_ref, of_ref, p_ref, pl_ref, inv_ref, s_ref = refs[n_pieces:]
    scale = HD ** (-0.5)
    queries = q_ref[0]
    seg_len = queries.shape[0]
    row = lax.broadcasted_iota(jnp.int32, (seg_len, seg_len), 0)
    col = lax.broadcasted_iota(jnp.int32, (seg_len, seg_len), 1)
    allow = (col == row) | ((col < row) & (live_ref[0] == 1))
    s_local = jnp.where(allow, matmul_cols(queries, k_ref[0]) * scale, NEG_BIG)
    top = None
    per = pieces[0].shape[1] // LANES
    for t in range(n_pieces):
        scores = matmul_cols(queries, pieces[t][0]) * scale
        parts = lane_blocks(scores)
        for i in range(per):
            part = jnp.minimum(parts[i], mask_ref[0, t * per + i].astype(F32))
            s_ref[t, :, i * LANES : (i + 1) * LANES] = part
            top = part if top is None else jnp.maximum(top, part)
    row_max = jnp.max(s_local, axis=-1, keepdims=True)
    if top is not None:
        row_max = jnp.maximum(row_max, jnp.max(top, axis=-1, keepdims=True))
    e_local = jnp.exp(s_local - row_max)
    low = e_local.astype(BF)
    pl_ref[0, 0] = low
    acc = matmul(low, v_ref[0])
    total = None
    for t in range(n_pieces):
        expo = jnp.exp(s_ref[t] - row_max)
        for part in lane_blocks(expo):
            total = part if total is None else total + part
        low = expo.astype(BF)
        p_ref[0, 0, t] = low
        acc = acc + matmul(low, pieces[t][1])
    row_total = jnp.sum(e_local, axis=-1, keepdims=True)
    if total is not None:
        row_total = row_total + jnp.sum(total, axis=-1, keepdims=True)
    inverse = 1.0 / row_total
    out = acc * inverse
    of_ref[0] = out
    o_ref[0] = out.astype(BF)
    inv_ref[0, 0] = inverse


def backward_kernel(n_pieces, do_ref, of_ref, q_ref, k_ref, v_ref, inv_ref, pl_ref, p_ref, cos_ref, sin_ref, *refs):
    pieces = refs[:n_pieces]
    (d_ref,) = refs[n_pieces:]
    scale = HD ** (-0.5)
    d_out = do_ref[0]
    inverse = inv_ref[0, 0]
    delta = jnp.sum(d_out.astype(F32) * of_ref[0], axis=-1, keepdims=True)
    chances = pl_ref[0, 0].astype(F32) * inverse
    ds = (chances * (matmul_cols(d_out, v_ref[0]) - delta)).astype(BF)
    dq = matmul(ds, k_ref[0])
    dk = matmul_rows(ds, q_ref[0])
    dv = matmul_rows(chances.astype(BF), d_out)
    for t in range(n_pieces):
        dp = matmul_cols(d_out, pieces[t][1])
        ds = (p_ref[0, 0, t].astype(F32) * ((dp - delta) * inverse)).astype(BF)
        dq = dq + matmul(ds, pieces[t][0])
    cosine = cos_ref[...]
    sine = sin_ref[...]

    def back(value):
        return (value * cosine - pltpu.roll(value, HD // 2, 1) * sine) * scale

    d_ref[0, 0] = back(dq).astype(BF)
    d_ref[1, 0] = back(dk).astype(BF)
    d_ref[2, 0] = dv.astype(BF)


def attention_specs(n_pieces, piece_rows, seg_len):
    head = pl.BlockSpec((1, seg_len, HD), lambda h, r: (r, 0, h))
    piece = pl.BlockSpec((2, piece_rows, HD), lambda h, r: (0, 0, h))
    p_spec = pl.BlockSpec((1, 1, n_pieces, seg_len, piece_rows), lambda h, r: (r, h, 0, 0, 0))
    pl_spec = pl.BlockSpec((1, 1, seg_len, seg_len), lambda h, r: (r, h, 0, 0))
    inv_spec = pl.BlockSpec((1, 1, seg_len, 1), lambda h, r: (r, h, 0, 0))
    return head, piece, p_spec, pl_spec, inv_spec


def attention_forward(queries, keys, values, live, mask, pieces):
    rows, seg_len, width = queries.shape
    heads = width // HD
    n_pieces = len(pieces)
    piece_rows = pieces[0].shape[1]
    head, piece, p_spec, pl_spec, inv_spec = attention_specs(n_pieces, piece_rows, seg_len)
    flops = 4 * rows * heads * seg_len * HD * (n_pieces * piece_rows + seg_len)
    return pl.pallas_call(
        lambda *refs: forward_kernel(n_pieces, *refs),
        grid=(heads, rows),
        in_specs=[
            head,
            head,
            head,
            pl.BlockSpec((1, 1, seg_len), lambda h, r: (r, 0, 0)),
            pl.BlockSpec((1,) + mask.shape[1:], lambda h, r: (r, 0, 0, 0)),
        ]
        + [piece] * n_pieces,
        out_specs=[head, head, p_spec, pl_spec, inv_spec],
        out_shape=[
            jax.ShapeDtypeStruct(queries.shape, BF),
            jax.ShapeDtypeStruct(queries.shape, F32),
            jax.ShapeDtypeStruct((rows, heads, n_pieces, seg_len, piece_rows), BF),
            jax.ShapeDtypeStruct((rows, heads, seg_len, seg_len), BF),
            jax.ShapeDtypeStruct((rows, heads, seg_len, 1), F32),
        ],
        scratch_shapes=[pltpu.VMEM((n_pieces, seg_len, piece_rows), F32)],
        compiler_params=pltpu.CompilerParams(vmem_limit_bytes=40 * 1024 * 1024),
        cost_estimate=pl.CostEstimate(flops=8 * flops, bytes_accessed=20000000, transcendentals=flops // 512),
        name="attention_forward",
    )(queries, keys, values, live, mask, *pieces)


def attention_backward(d_out, out_f32, queries, keys, values, inverse, p_local, p_memory, cosine, sine, pieces):
    rows, seg_len, width = queries.shape
    heads = width // HD
    n_pieces = len(pieces)
    piece_rows = pieces[0].shape[1]
    head, piece, p_spec, pl_spec, inv_spec = attention_specs(n_pieces, piece_rows, seg_len)
    table = pl.BlockSpec((seg_len, HD), lambda h, r: (0, 0))
    flops = 4 * rows * heads * seg_len * HD * (n_pieces * piece_rows + seg_len)
    return pl.pallas_call(
        lambda *refs: backward_kernel(n_pieces, *refs),
        grid=(heads, rows),
        in_specs=[head, head, head, head, head, inv_spec, pl_spec, p_spec, table, table] + [piece] * n_pieces,
        out_specs=pl.BlockSpec((3, 1, seg_len, HD), lambda h, r: (0, r, 0, h)),
        out_shape=jax.ShapeDtypeStruct((3, rows, seg_len, width), BF),
        compiler_params=pltpu.CompilerParams(vmem_limit_bytes=40 * 1024 * 1024),
        cost_estimate=pl.CostEstimate(flops=8 * flops, bytes_accessed=20000000, transcendentals=0),
        name="attention_backward",
    )(d_out, out_f32, queries, keys, values, inverse, p_local, p_memory, cosine, sine, *pieces)


def allow_local_of(live):
    seg_len = live.shape[-1]
    position = jnp.arange(seg_len, dtype=jnp.int32)
    same = position[None, :] == position[:, None]
    return same[None] | ((position[None, :] < position[:, None])[None] & (live == 1))


def split_heads(value):
    rows, seg_len, width = value.shape
    return value.reshape(rows, seg_len, width // HD, HD)


def stream_forward(queries, keys, values, live, allow, memory):
    scale = HD ** (-0.5)
    q4, k4, v4 = split_heads(queries), split_heads(keys), split_heads(values)
    scores = jnp.einsum("rqhd,rkhd->rhqk", q4, k4, preferred_element_type=F32) * scale
    scores = jnp.where(allow_local_of(live)[:, None], scores, NEG_BIG)
    row_max = jnp.max(scores, axis=-1)
    expo = jnp.exp(scores - row_max[..., None])
    state = (
        row_max,
        jnp.sum(expo, axis=-1),
        jnp.einsum("rhqk,rkhd->rhqd", expo.astype(BF), v4, preferred_element_type=F32),
    )

    def step(running, item):
        row_max, row_total, acc = running
        block, allowed = item
        k3 = block[0].reshape(block.shape[1], -1, HD)
        v3 = block[1].reshape(block.shape[1], -1, HD)
        scores = jnp.einsum("rqhd,khd->rhqk", q4, k3, preferred_element_type=F32) * scale
        scores = jnp.where(allowed[:, None] > 0, scores, NEG_BIG)
        new_max = jnp.maximum(row_max, jnp.max(scores, axis=-1))
        shrink = jnp.exp(row_max - new_max)
        expo = jnp.exp(scores - new_max[..., None])
        acc = acc * shrink[..., None] + jnp.einsum(
            "rhqk,khd->rhqd", expo.astype(BF), v3, preferred_element_type=F32
        )
        return (new_max, row_total * shrink + jnp.sum(expo, axis=-1), acc), None

    (row_max, row_total, acc), unused = lax.scan(step, state, (memory, allow))
    out = (acc / row_total[..., None]).transpose(0, 2, 1, 3).reshape(queries.shape)
    return out.astype(BF), out, row_max + jnp.log(row_total)


def stream_backward(d_out, out_f32, queries, keys, values, live, log_total, allow, memory, cosine, sine):
    scale = HD ** (-0.5)
    q4, k4, v4, d4 = split_heads(queries), split_heads(keys), split_heads(values), split_heads(d_out)
    delta = jnp.sum(d4.astype(F32) * split_heads(out_f32), axis=-1).transpose(0, 2, 1)
    scores = jnp.einsum("rqhd,rkhd->rhqk", q4, k4, preferred_element_type=F32) * scale
    scores = jnp.where(allow_local_of(live)[:, None], scores, NEG_BIG)
    chances = jnp.exp(scores - log_total[..., None])
    dp = jnp.einsum("rqhd,rkhd->rhqk", d4, v4, preferred_element_type=F32)
    ds = (chances * (dp - delta[..., None])).astype(BF)
    dq = jnp.einsum("rhqk,rkhd->rqhd", ds, k4, preferred_element_type=F32)
    dk = jnp.einsum("rhqk,rqhd->rkhd", ds, q4, preferred_element_type=F32)
    dv = jnp.einsum("rhqk,rqhd->rkhd", chances.astype(BF), d4, preferred_element_type=F32)

    def step(running, item):
        block, allowed = item
        k3 = block[0].reshape(block.shape[1], -1, HD)
        v3 = block[1].reshape(block.shape[1], -1, HD)
        scores = jnp.einsum("rqhd,khd->rhqk", q4, k3, preferred_element_type=F32) * scale
        scores = jnp.where(allowed[:, None] > 0, scores, NEG_BIG)
        chances = jnp.exp(scores - log_total[..., None])
        dp = jnp.einsum("rqhd,khd->rhqk", d4, v3, preferred_element_type=F32)
        ds = (chances * (dp - delta[..., None])).astype(BF)
        return running + jnp.einsum("rhqk,khd->rqhd", ds, k3, preferred_element_type=F32), None

    dq, unused = lax.scan(step, dq, (memory, allow))

    def back(value):
        turned = rope_heads(value.reshape((-1,) + value.shape[2:]), jnp.tile(cosine, (value.shape[0], 1)), -jnp.tile(sine, (value.shape[0], 1)))
        return (turned * scale).reshape(queries.shape).astype(BF)

    return jnp.stack([back(dq), back(dk), dv.reshape(queries.shape).astype(BF)])


def local(
    layer_input,
    live,
    knn_index,
    mem_keys,
    mem_values,
    gain_attn,
    w_query,
    w_key,
    w_value,
    w_out,
    gain_ffn,
    w_gate,
    w_up,
    w_down,
    cotangent,
):
    seg_len, width = layer_input.shape[1:]
    half = width // 2
    ff = w_gate.shape[1]
    ff_half = ff // 2
    n_seg = lax.axis_size("seg")
    tokens = seg_len * n_seg
    seg = lax.axis_index("seg")
    core = lax.axis_index("rep") % 2
    n_z = n_seg // 2
    use_kernel = n_seg <= KERNEL_SEGMENTS

    def cut(value, index, size):
        return lax.dynamic_slice_in_dim(value, index * size, size, value.ndim - 1)

    def trade_columns(value):
        size = value.shape[-1] // 2
        return ordered(cut(value, core, size), core_swap(cut(value, 1 - core, size)), core, 0)

    def both_rows(value):
        return jnp.concatenate([value[None], core_swap(value)[None]], 0)

    def gain_columns(a, b):
        return jnp.concatenate([a[:, None], b[:, None], jnp.zeros((a.shape[0], LANES - 2), BF)], 1)

    def thirds(value, index):
        return cut(value, index, half)

    gains = gain_columns(gain_attn, gain_ffn)
    mine = jnp.concatenate([thirds(w_query, core), thirds(w_key, core), thirds(w_value, core), gains], 1)
    theirs = jnp.concatenate(
        [thirds(w_query, 1 - core), thirds(w_key, 1 - core), thirds(w_value, 1 - core), gains], 1
    )
    w_qkv_all = gather_chips(ordered(mine, core_swap(theirs), core, 0))
    w_qkv = w_qkv_all[:, : 3 * half]
    g_attn = w_qkv_all[:, 3 * half].astype(F32)
    g_ffn = w_qkv_all[:, 3 * half + 1].astype(F32)

    memory = jnp.stack([mem_keys[0], mem_values[0]])
    kv = jnp.concatenate([cut(memory, core, half), core_swap(cut(memory, 1 - core, half))], 1)

    coded = both_rows(knn_index[0] * 2 + live[0][:, None])
    live_both = jnp.bitwise_and(coded[:, :, 0], 1)[:, None, :]
    picks = lax.shift_right_arithmetic(coded, 1)
    pair = picks >= tokens
    slot = jnp.where(pair, picks - tokens, picks)
    slot_seg = slot // seg_len
    swapped = jnp.arange(2, dtype=jnp.int32)[:, None, None]
    kv_row = jnp.bitwise_xor(pair.astype(jnp.int32), swapped)
    within = kv_row * seg_len + (slot - slot_seg * seg_len)
    kv_rows = 2 * seg_len

    if use_kernel:
        distance = seg // 2 - slot_seg // 2
        piece_no = jnp.where(slot_seg % 2 == seg % 2, distance - 1, n_z - 1 + distance)
        columns = jnp.where(picks >= 0, piece_no * kv_rows + within, -1)
        mask = build_mask(columns, (2 * n_z - 1) * kv_rows // LANES)
        hops = [kv]
        for unused in range(n_z - 1):
            hops.append(lax.ppermute(hops[-1], "seg", [(i, i + 2) for i in range(n_seg - 2)]))
        across = [lax.ppermute(kv, "seg", [(i, i + 1) for i in range(0, n_seg, 2)])]
        across += [flip(piece, "seg", 1) for piece in hops[1:]]
        pieces = hops[1:] + across
    else:
        columns = jnp.where(picks >= 0, slot_seg * kv_rows + within, n_seg * kv_rows)
        rows_at = jnp.arange(2)[:, None, None]
        queries_at = jnp.arange(seg_len)[None, :, None]
        allow = jnp.zeros((2, seg_len, n_seg * kv_rows), BF).at[rows_at, queries_at, columns].set(1.0, mode="drop")
        allow = allow.reshape(2, seg_len, n_seg, kv_rows).transpose(2, 0, 1, 3)
        gathered = lax.all_gather(kv, "seg", axis=0)

    gate_up = jnp.concatenate([trade_columns(w_gate), trade_columns(w_up)], 1)
    w_o_all = gather_chips(trade_columns(w_out))
    gate_up_all = gather_chips(gate_up)
    w_d_all = gather_chips(trade_columns(w_down))
    wg = gate_up_all[:, :ff_half]
    wu = gate_up_all[:, ff_half:]

    def own_rows(value):
        size = value.shape[0] // 2
        pairs = value.reshape(2, size, value.shape[1])
        return ordered(pick(pairs, core, 0), core_swap(pick(pairs, 1 - core, 0)), core, 1)

    wo = own_rows(w_o_all)
    wd = own_rows(w_d_all)

    x_both = both_rows(layer_input[0])
    g_both = both_rows(cotangent[0])
    x_float = x_both.reshape(2 * seg_len, width).astype(F32)
    grad_out = g_both.reshape(2 * seg_len, width)
    cosine, sine = rope_tables(seg_len)
    cos_two = jnp.tile(cosine, (2, 1))
    sin_two = jnp.tile(sine, (2, 1))
    h_float, inv_one = norm_forward(x_float, g_attn)
    h_one = h_float.astype(BF)
    qkv = matmul(h_one, w_qkv)
    heads_here = half // HD
    turned = rope_heads(qkv[:, : 2 * half].reshape(2 * seg_len, 2 * heads_here, HD), cos_two, sin_two)
    turned = turned.reshape(2 * seg_len, 2 * half).astype(BF)
    queries = turned[:, :half].reshape(2, seg_len, half)
    keys = turned[:, half:].reshape(2, seg_len, half)
    values = qkv[:, 2 * half :].astype(BF).reshape(2, seg_len, half)
    if use_kernel:
        out_low, out_f32, p_memory, p_local, inverse = attention_forward(
            queries, keys, values, live_both, mask, pieces
        )
    else:
        out_low, out_f32, log_total = stream_forward(queries, keys, values, live_both, allow, gathered)
    attended = out_low.reshape(2 * seg_len, half)

    def both_sums(part):
        low = part.astype(BF)
        other = core_swap(jnp.concatenate([low[seg_len:], low[:seg_len]], 0))
        return low.astype(F32) + other.astype(F32)

    x_one = x_float + both_sums(matmul(attended, wo))
    h_two_f, inv_two = norm_forward(x_one, g_ffn)
    h_two = h_two_f.astype(BF)
    gate = matmul(h_two, wg)
    upward = matmul(h_two, wu)
    sigma = jax.nn.sigmoid(gate)
    swish = gate * sigma
    hidden = (swish * upward).astype(BF)
    down = matmul(hidden, wd)
    layer_output = (x_one[:seg_len] + down[:seg_len] + core_swap(down[seg_len:].astype(BF)).astype(F32)).astype(BF)

    hidden_all = ordered(hidden, core_swap_rows(hidden, seg_len), core, 1)
    grad_wd = matmul_rows(hidden_all, cut(grad_out, core, half)).astype(BF)
    d_hidden = matmul_cols(grad_out, wd)
    d_gate = (d_hidden * upward * sigma * (1.0 + gate * (1.0 - sigma))).astype(BF)
    d_up = (d_hidden * swish).astype(BF)
    grad_wg = matmul_rows(h_two, d_gate).astype(BF)
    grad_wu = matmul_rows(h_two, d_up).astype(BF)
    d_h_two = both_sums(matmul_cols(d_gate, wg) + matmul_cols(d_up, wu))
    d_x_norm, normed_two = norm_backward(x_one, inv_two, g_ffn, d_h_two)
    grad_g_ffn = jnp.sum(d_h_two[:seg_len] * normed_two[:seg_len], axis=0)
    d_x_one = grad_out.astype(F32) + d_x_norm
    d_branch = d_x_one.astype(BF)
    attended_all = ordered(attended, core_swap_rows(attended, seg_len), core, 1)
    grad_wo = matmul_rows(attended_all, cut(d_branch, core, half)).astype(BF)
    d_att = matmul_cols(d_branch, wo).astype(BF).reshape(2, seg_len, half)

    if use_kernel:
        d_qkv = attention_backward(
            d_att, out_f32, queries, keys, values, inverse, p_local, p_memory, cosine, sine, pieces
        )
    else:
        d_qkv = stream_backward(
            d_att, out_f32, queries, keys, values, live_both, log_total, allow, gathered, cosine, sine
        )
    d_qkv = d_qkv.reshape(3, 2 * seg_len, half).transpose(1, 0, 2).reshape(2 * seg_len, 3 * half)
    grad_qkv = matmul_rows(h_one, d_qkv).astype(BF)
    part = matmul_cols(d_qkv, w_qkv)
    d_h_one = part[:seg_len] + core_swap(part[seg_len:].astype(BF)).astype(F32)
    x_own = x_float[:seg_len]
    d_x_first, normed_one = norm_backward(x_own, inv_one[:seg_len], g_attn, d_h_one)
    grad_g_attn = jnp.sum(d_h_one * normed_one, axis=0)
    grad_x = (d_x_one[:seg_len] + d_x_first).astype(BF)

    def finish(value):
        size = value.shape[0] // 2
        pairs = value.reshape(2, size, value.shape[1])
        return pick(pairs, core, 0), core_swap(pick(pairs, 1 - core, 0))

    def whole(value):
        mine, other = finish(value)
        return ordered(mine, other, core, 1).astype(F32)

    sum_wd = whole(reduce_chips(grad_wd, True))
    sum_wg = whole(reduce_chips(grad_wg, True))
    sum_wu = whole(reduce_chips(grad_wu, False))
    sum_wo = whole(reduce_chips(grad_wo, False))
    grad_qkv = jnp.concatenate([grad_qkv, gain_columns(grad_g_attn.astype(BF), grad_g_ffn.astype(BF))], 1)
    mine, other = finish(reduce_chips(grad_qkv, False))

    def third(i):
        return ordered(mine[:, i * half : (i + 1) * half], other[:, i * half : (i + 1) * half], core, 1).astype(F32)

    sum_gains = mine[:, 3 * half : 3 * half + 2].astype(F32) + other[:, 3 * half : 3 * half + 2].astype(F32)
    return (
        layer_output[None],
        grad_x[None],
        sum_gains[:, 0],
        third(0),
        third(1),
        third(2),
        sum_wo,
        sum_gains[:, 1],
        sum_wg,
        sum_wu,
        sum_wd,
    )


def core_swap_rows(value, seg_len):
    return core_swap(jnp.concatenate([value[seg_len:], value[:seg_len]], 0))


def solution(mesh):
    tokens = P("rep", "seg", None)
    vector = P(("seg", "rep"))
    matrix = P(("seg", "rep"), None)
    return jax.shard_map(
        local,
        mesh=mesh,
        in_specs=(
            tokens,
            P("rep", "seg"),
            tokens,
            tokens,
            tokens,
            vector,
            matrix,
            matrix,
            matrix,
            matrix,
            vector,
            matrix,
            matrix,
            matrix,
            tokens,
        ),
        out_specs=(tokens, tokens, vector, matrix, matrix, matrix, matrix, vector, matrix, matrix, matrix),
        check_vma=False,
    )
```

```python
import jax
import jax.numpy as jnp
from jax import lax
from jax.experimental import pallas as pl
from jax.experimental.pallas import tpu as pltpu
from jax.sharding import PartitionSpec as P

H = 8
HD = 128
EPSILON = 1e-05
NEG_BIG = -1e30
POS_BIG = 1e30
ROPE_BASE = 10000.0
LANES = 128
KERNEL_HIGH = 2

BF = jnp.bfloat16
F32 = jnp.float32


def cdiv(a, b):
    return -(-a // b)


def flip(value, axis, bit):
    count = lax.axis_size(axis)
    return lax.ppermute(value, axis, [(i, i ^ bit) for i in range(count)])


def flip_core(value):
    return flip(value, "rep", 1)


def flip_y(value):
    return flip(value, "rep", 2)


def flip_x(value):
    return flip(value, "seg", 1)


def flip_z(value):
    return flip(value, "seg", 2)


def ordered(mine, other, bit, axis):
    first = jnp.where(bit == 0, mine, other)
    second = jnp.where(bit == 0, other, mine)
    return jnp.concatenate([first, second], axis)


def pick(value, index, axis):
    return lax.dynamic_index_in_dim(value, index, axis, keepdims=False)


def cut(value, start, size, axis=-1):
    return lax.dynamic_slice_in_dim(value, start, size, axis % value.ndim)


def fence(*values):
    return lax.optimization_barrier(values)


def place():
    seg = lax.axis_index("seg")
    rep = lax.axis_index("rep")
    return seg % 2, (seg // 2) % 2, seg // 4, rep // 2, rep % 2


def high_bits():
    bit = 4
    out = []
    while bit < lax.axis_size("seg"):
        out.append(bit)
        bit *= 2
    return out


def gather_high(cur):
    seg = lax.axis_index("seg")
    for bit in high_bits():
        cur = ordered(cur, flip(cur, "seg", bit), (seg // bit) % 2, 0)
    return cur


def gather_x(cur):
    return ordered(cur, flip_x(cur), place()[0], 2)


def gather_y(cur):
    return ordered(cur, flip_y(cur), place()[3], 3)


def flat(cur):
    return cur.reshape(-1, cur.shape[-1])


def halve(value, axis_name, bit, side, axis):
    recv = flip(pick(value, 1 - side, axis), axis_name, bit)
    kept = pick(value, side, axis)
    return (kept.astype(F32) + recv.astype(F32)).astype(BF)


def reduce_plane(full, low, x_first):
    x, unused, unused, y, unused = place()
    high = lax.axis_size("seg") // 4
    total, cols = full.shape
    cur = full.reshape(high, low, 2, 2, total // (high * low * 4), cols)
    if x_first:
        cur = halve(cur, "seg", 1, x, 2)
        return halve(cur, "rep", 2, y, 2)
    cur = halve(cur, "rep", 2, y, 3)
    return halve(cur, "seg", 1, x, 2)


def reduce_high(cur):
    seg = lax.axis_index("seg")
    for bit in reversed(high_bits()):
        cur = cur.reshape((2, cur.shape[0] // 2) + cur.shape[1:])
        cur = halve(cur, "seg", bit, (seg // bit) % 2, 0)
    return cur[0]


def trade_core(quarters):
    core = place()[4]
    low, unused, rows, cols = 2, 2, quarters.shape[1], quarters.shape[2]
    four = quarters.reshape(2, 2, rows, cols)
    return ordered(pick(four, core, 1), flip_core(pick(four, 1 - core, 1)), core, 1)


def trade_z(halves):
    low = place()[1]
    return ordered(pick(halves, low, 0)[None], flip_z(pick(halves, 1 - low, 0))[None], low, 0)


def gather_z_four(halves):
    seg = lax.axis_index("seg")
    low = (seg // 2) % 2
    keep, give = pick(halves, low, 0)[None, None], pick(halves, 1 - low, 0)[None, None]
    near = ordered(keep, flip(give, "seg", 2), low, 1)
    far = ordered(flip(keep, "seg", 4), flip(give, "seg", 6), low, 1)
    return ordered(near, far, (seg // 4) % 2, 0)[:, :, None, None]


def start_gather(traded):
    return traded[None, :, None, None]


def untrade(sums):
    unused, low, unused, unused, core = place()
    twice, cols = sums.shape[1:]
    mine = ordered(pick(sums, low, 0)[None], flip_z(pick(sums, 1 - low, 0))[None], low, 0)
    four = mine.reshape(2, 2, twice // 2, cols)
    kept = pick(four, core, 1)[:, None]
    return ordered(kept, flip_core(pick(four, 1 - core, 1))[:, None], core, 1)


def swap_pairs(value):
    blocks = value.reshape((value.shape[0], 2, 2, value.shape[1] // 4) + value.shape[2:])
    return jnp.stack([blocks[:, :, 1], blocks[:, :, 0]], 2).reshape(value.shape)


def all_quarters(mine, far, of_tokens):
    unused, low, unused, unused, core = place()
    other = flip_core(jnp.stack([mine, far]))
    if of_tokens:
        other = swap_pairs(other)
    near_half = ordered(mine, other[0], core, 1)
    far_half = ordered(far, other[1], core, 1)
    return ordered(near_half, far_half, low, 1)


def all_blocks(near_pair, far):
    low = place()[1]
    far_pair = jnp.stack([far, flip_core(far)])
    return ordered(near_pair, far_pair, low, 0)


def core_sums(part):
    blocks = part.reshape((2, 2, part.shape[0] // 4) + part.shape[1:])
    return (blocks[:, 0] + flip_core(blocks[:, 1].astype(BF)).astype(F32)).astype(BF)


def own_sums(sums):
    low = place()[1]
    return pick(sums, low, 0).astype(F32) + flip_z(pick(sums, 1 - low, 0)).astype(F32)


def all_sums(sums):
    both = (sums.astype(F32) + flip_z(sums).astype(F32)).astype(BF)
    return jnp.concatenate([both[:, None], flip_core(both)[:, None]], 1).astype(F32)


def unit_blocks(n_blocks):
    order = []
    for block in range(n_blocks):
        high, low, rest, core = block // 16, (block // 8) % 2, (block // 2) % 4, block % 2
        order.append((low * 2 + core, high * 4 + rest))
    return order


def split_units(matrix, n_blocks):
    rows, total = matrix.shape
    size = total // n_blocks

    def body(in_ref, out_ref):
        for block, (quarter, at) in enumerate(unit_blocks(n_blocks)):
            out_ref[quarter, :, at * size : (at + 1) * size] = in_ref[:, block * size : (block + 1) * size]

    return pl.pallas_call(
        body,
        out_shape=jax.ShapeDtypeStruct((4, rows, total // 4), matrix.dtype),
        name="split_units",
    )(matrix)


def join_units(quarters, n_blocks):
    unused, rows, quarter_size = quarters.shape
    size = 4 * quarter_size // n_blocks

    def body(in_ref, out_ref):
        for block, (quarter, at) in enumerate(unit_blocks(n_blocks)):
            out_ref[:, block * size : (block + 1) * size] = in_ref[
                quarter, :, at * size : (at + 1) * size
            ].astype(F32)

    return pl.pallas_call(
        body,
        out_shape=jax.ShapeDtypeStruct((rows, 4 * quarter_size), F32),
        name="join_units",
    )(quarters)


def matmul(left, right):
    return jnp.dot(left, right, preferred_element_type=F32)


def matmul_rows(left, right):
    return lax.dot_general(left, right, (((0,), (0,)), ((), ())), preferred_element_type=F32)


def matmul_cols(left, right):
    return lax.dot_general(left, right, (((1,), (1,)), ((), ())), preferred_element_type=F32)


def norm_forward(values, gain):
    inverse = lax.rsqrt(jnp.mean(values * values, axis=-1, keepdims=True) + EPSILON)
    return (values * inverse * gain, inverse)


def norm_backward(values, inverse, gain, grad_out):
    normed = values * inverse
    scaled = grad_out * gain
    grad_values = inverse * (scaled - normed * jnp.mean(scaled * normed, axis=-1, keepdims=True))
    return (grad_values, normed)


def rope_tables(seg_len):
    position = jnp.arange(seg_len).astype(F32)
    freqs = ROPE_BASE ** (-(2.0 * jnp.arange(HD // 2).astype(F32)) / HD)
    angle = position[:, None] * freqs[None, :]
    cosine, sine = jnp.cos(angle), jnp.sin(angle)
    return (jnp.concatenate([cosine, cosine], -1), jnp.concatenate([-sine, sine], -1))


def rope_heads(values, cosine, sine):
    half = HD // 2
    swapped = jnp.concatenate([values[..., half:], values[..., :half]], -1)
    return values * cosine[:, None, :] + swapped * sine[:, None, :]


def mask_kernel(n_cols, cols_ref, out_ref, scratch):
    queries = cols_ref.shape[1]
    picks = cols_ref[0]
    pad = scratch.shape[0]
    high = lax.shift_right_arithmetic(picks, 7)
    low = jnp.bitwise_and(picks, LANES - 1).astype(F32)
    rows = 16
    iota_high = lax.broadcasted_iota(jnp.int32, (pad, picks.shape[1]), 0)
    iota_low = lax.broadcasted_iota(jnp.int32, (rows, picks.shape[1]), 0).astype(F32).astype(BF)
    one, zero = jnp.ones_like(iota_low), jnp.zeros_like(iota_low)
    for i in range(queries):
        hot_high = jnp.where(iota_high == high[i : i + 1, :], 1.0, 0.0).astype(BF)
        wanted = jnp.broadcast_to(low[i : i + 1, :], iota_low.shape).astype(BF)
        hot_low = jnp.concatenate(
            [jnp.where(iota_low == wanted - float(first), one, zero) for first in range(0, LANES, rows)], 0
        )
        scratch[:, i, :] = matmul_cols(hot_high, hot_low)
    out_ref[0] = jnp.where(scratch[0:n_cols] > 0.5, POS_BIG, NEG_BIG).astype(BF)


def build_mask(columns, n_cols):
    rows, queries, picks = columns.shape
    block = 16
    pad = cdiv(n_cols, 8) * 8
    return pl.pallas_call(
        lambda *refs: mask_kernel(n_cols, *refs),
        grid=(rows, queries // block),
        in_specs=[pl.BlockSpec((1, block, picks), lambda r, g: (r, g, 0))],
        out_specs=pl.BlockSpec((1, n_cols, block, LANES), lambda r, g: (r, 0, g, 0)),
        out_shape=jax.ShapeDtypeStruct((rows, n_cols, queries, LANES), BF),
        scratch_shapes=[pltpu.VMEM((pad, block, LANES), F32)],
        compiler_params=pltpu.CompilerParams(vmem_limit_bytes=16 * 1024 * 1024),
        cost_estimate=pl.CostEstimate(
            flops=20 * rows * queries * pad * picks * LANES, bytes_accessed=5000000, transcendentals=0
        ),
        name="mask_build",
    )(columns)


def lane_blocks(value):
    return [value[:, i : i + LANES] for i in range(0, value.shape[1], LANES)]


PIECES = ((0, 0), (0, 1), (1, 0), (1, 1), (2, 0), (3, 0), (2, 1))
N_COMMON = 5
N_GROUPS = 4


def forward_kernel(q_ref, k_ref, v_ref, live_ref, mask_ref, *refs):
    key_refs, value_refs = refs[:N_GROUPS], refs[N_GROUPS : 2 * N_GROUPS]
    o_ref, of_ref, p_ref, pl_ref, inv_ref, s_ref, top_ref, total_ref, acc_ref = refs[2 * N_GROUPS :]
    scale = HD ** (-0.5)
    upper = pl.program_id(1) >= 2
    queries = q_ref[0]
    seg_len = queries.shape[0]
    row = lax.broadcasted_iota(jnp.int32, (seg_len, seg_len), 0)
    col = lax.broadcasted_iota(jnp.int32, (seg_len, seg_len), 1)
    allow = (col == row) | ((col < row) & (live_ref[0] == 1))
    s_local = jnp.where(allow, matmul_cols(queries, k_ref[0]) * scale, NEG_BIG)
    per = key_refs[0].shape[1] // LANES

    def score(t, top):
        group, low = PIECES[t]
        parts = lane_blocks(matmul_cols(queries, key_refs[group][low]) * scale)
        for i in range(per):
            part = jnp.minimum(parts[i], mask_ref[0, t * per + i].astype(F32))
            s_ref[t, :, i * LANES : (i + 1) * LANES] = part
            top = part if top is None else jnp.maximum(top, part)
        return top

    top = None
    for t in range(N_COMMON):
        top = score(t, top)
    top_ref[...] = top

    @pl.when(upper)
    def more_scores():
        more = top_ref[...]
        for t in range(N_COMMON, len(PIECES)):
            more = score(t, more)
        top_ref[...] = more

    row_max = jnp.maximum(
        jnp.max(s_local, axis=-1, keepdims=True), jnp.max(top_ref[...], axis=-1, keepdims=True)
    )
    e_local = jnp.exp(s_local - row_max)
    low_local = e_local.astype(BF)
    pl_ref[0, 0] = low_local

    def weigh(t, total, acc):
        group, low = PIECES[t]
        expo = jnp.exp(s_ref[t] - row_max)
        for part in lane_blocks(expo):
            total = part if total is None else total + part
        chances = expo.astype(BF)
        p_ref[0, 0, t] = chances
        return total, acc + matmul(chances, value_refs[group][low])

    total, acc = None, matmul(low_local, v_ref[0])
    for t in range(N_COMMON):
        total, acc = weigh(t, total, acc)
    total_ref[...] = total
    acc_ref[...] = acc

    @pl.when(upper)
    def more_values():
        total, acc = total_ref[...], acc_ref[...]
        for t in range(N_COMMON, len(PIECES)):
            total, acc = weigh(t, total, acc)
        total_ref[...] = total
        acc_ref[...] = acc

    row_total = jnp.sum(e_local, axis=-1, keepdims=True) + jnp.sum(total_ref[...], axis=-1, keepdims=True)
    inverse = 1.0 / row_total
    out = acc_ref[...] * inverse
    of_ref[0] = out
    o_ref[0] = out.astype(BF)
    inv_ref[0, 0] = inverse


def backward_local_kernel(do_ref, of_ref, q_ref, k_ref, v_ref, inv_ref, pl_ref, cos_ref, sin_ref, dkv_ref, dq_ref):
    scale = HD ** (-0.5)
    d_out = do_ref[0]
    delta = jnp.sum(d_out.astype(F32) * of_ref[0], axis=-1, keepdims=True)
    chances = pl_ref[0, 0].astype(F32) * inv_ref[0, 0]
    ds = (chances * (matmul_cols(d_out, v_ref[0]) - delta)).astype(BF)
    dq_ref[0] = matmul(ds, k_ref[0])
    dk = matmul_rows(ds, q_ref[0])
    dkv_ref[0, 0] = ((dk * cos_ref[...] - pltpu.roll(dk, HD // 2, 1) * sin_ref[...]) * scale).astype(BF)
    dkv_ref[1, 0] = matmul_rows(chances.astype(BF), d_out).astype(BF)


def backward_kernel(do_ref, of_ref, local_ref, inv_ref, p_ref, cos_ref, sin_ref, *refs):
    key_refs, value_refs = refs[:N_GROUPS], refs[N_GROUPS : 2 * N_GROUPS]
    out_ref, dq_ref = refs[2 * N_GROUPS :]
    scale = HD ** (-0.5)
    upper = pl.program_id(1) >= 2
    d_out = do_ref[0]
    inverse = inv_ref[0, 0]
    delta = jnp.sum(d_out.astype(F32) * of_ref[0], axis=-1, keepdims=True)

    def piece(t, dq):
        group, low = PIECES[t]
        dp = matmul_cols(d_out, value_refs[group][low])
        ds = (p_ref[0, 0, t].astype(F32) * ((dp - delta) * inverse)).astype(BF)
        return dq + matmul(ds, key_refs[group][low])

    dq = local_ref[0]
    for t in range(N_COMMON):
        dq = piece(t, dq)
    dq_ref[...] = dq

    @pl.when(upper)
    def more():
        dq = dq_ref[...]
        for t in range(N_COMMON, len(PIECES)):
            dq = piece(t, dq)
        dq_ref[...] = dq

    dq = dq_ref[...]
    out_ref[0] = ((dq * cos_ref[...] - pltpu.roll(dq, HD // 2, 1) * sin_ref[...]) * scale).astype(BF)


def attention_specs(piece_rows, seg_len):
    head = pl.BlockSpec((1, seg_len, HD), lambda h, r: (r, 0, h))
    piece = pl.BlockSpec((2, piece_rows, HD), lambda h, r: (0, 0, h))
    p_spec = pl.BlockSpec((1, 1, len(PIECES), seg_len, piece_rows), lambda h, r: (r, h, 0, 0, 0))
    pl_spec = pl.BlockSpec((1, 1, seg_len, seg_len), lambda h, r: (r, h, 0, 0))
    inv_spec = pl.BlockSpec((1, 1, seg_len, 1), lambda h, r: (r, h, 0, 0))
    return head, piece, p_spec, pl_spec, inv_spec


def attention_forward(queries, keys, values, live, mask, key_pieces, value_pieces):
    blocks, seg_len, width = queries.shape
    heads = width // HD
    piece_rows = key_pieces[0].shape[1]
    head, piece, p_spec, pl_spec, inv_spec = attention_specs(piece_rows, seg_len)
    flops = 4 * blocks * heads * seg_len * HD * (len(PIECES) * piece_rows + seg_len)
    return pl.pallas_call(
        forward_kernel,
        grid=(heads, blocks),
        in_specs=[
            head,
            head,
            head,
            pl.BlockSpec((1, 1, seg_len), lambda h, r: (r, 0, 0)),
            pl.BlockSpec((1,) + mask.shape[1:], lambda h, r: (r, 0, 0, 0)),
        ]
        + [piece] * (2 * N_GROUPS),
        out_specs=[head, head, p_spec, pl_spec, inv_spec],
        out_shape=[
            jax.ShapeDtypeStruct(queries.shape, BF),
            jax.ShapeDtypeStruct(queries.shape, F32),
            jax.ShapeDtypeStruct((blocks, heads, len(PIECES), seg_len, piece_rows), BF),
            jax.ShapeDtypeStruct((blocks, heads, seg_len, seg_len), BF),
            jax.ShapeDtypeStruct((blocks, heads, seg_len, 1), F32),
        ],
        scratch_shapes=[
            pltpu.VMEM((len(PIECES), seg_len, piece_rows), F32),
            pltpu.VMEM((seg_len, LANES), F32),
            pltpu.VMEM((seg_len, LANES), F32),
            pltpu.VMEM((seg_len, HD), F32),
        ],
        compiler_params=pltpu.CompilerParams(vmem_limit_bytes=40 * 1024 * 1024),
        cost_estimate=pl.CostEstimate(flops=8 * flops, bytes_accessed=20000000, transcendentals=flops // 512),
        name="attention_forward",
    )(queries, keys, values, live, mask, *key_pieces, *value_pieces)


def attention_backward_local(d_out, out_f32, queries, keys, values, inverse, p_local, cosine, sine):
    blocks, seg_len, width = queries.shape
    head, unused, unused, pl_spec, inv_spec = attention_specs(seg_len, seg_len)
    table = pl.BlockSpec((seg_len, HD), lambda h, r: (0, 0))
    return pl.pallas_call(
        backward_local_kernel,
        grid=(width // HD, blocks),
        in_specs=[head, head, head, head, head, inv_spec, pl_spec, table, table],
        out_specs=[pl.BlockSpec((2, 1, seg_len, HD), lambda h, r: (0, r, 0, h)), head],
        out_shape=[
            jax.ShapeDtypeStruct((2, blocks, seg_len, width), BF),
            jax.ShapeDtypeStruct(queries.shape, F32),
        ],
        compiler_params=pltpu.CompilerParams(vmem_limit_bytes=16 * 1024 * 1024),
        cost_estimate=pl.CostEstimate(flops=3000000000, bytes_accessed=5000000, transcendentals=0),
        name="attention_backward_local",
    )(d_out, out_f32, queries, keys, values, inverse, p_local, cosine, sine)


def attention_backward(d_out, out_f32, dq_local, inverse, p_memory, cosine, sine, key_pieces, value_pieces):
    blocks, seg_len, width = d_out.shape
    heads = width // HD
    piece_rows = key_pieces[0].shape[1]
    head, piece, p_spec, unused, inv_spec = attention_specs(piece_rows, seg_len)
    table = pl.BlockSpec((seg_len, HD), lambda h, r: (0, 0))
    flops = 4 * blocks * heads * seg_len * HD * len(PIECES) * piece_rows
    return pl.pallas_call(
        backward_kernel,
        grid=(heads, blocks),
        in_specs=[head, head, head, inv_spec, p_spec, table, table] + [piece] * (2 * N_GROUPS),
        out_specs=head,
        out_shape=jax.ShapeDtypeStruct((blocks, seg_len, width), BF),
        scratch_shapes=[pltpu.VMEM((seg_len, HD), F32)],
        compiler_params=pltpu.CompilerParams(vmem_limit_bytes=40 * 1024 * 1024),
        cost_estimate=pl.CostEstimate(flops=8 * flops, bytes_accessed=20000000, transcendentals=0),
        name="attention_backward",
    )(d_out, out_f32, dq_local, inverse, p_memory, cosine, sine, *key_pieces, *value_pieces)


def allow_local_of(live):
    seg_len = live.shape[-1]
    position = jnp.arange(seg_len, dtype=jnp.int32)
    same = position[None, :] == position[:, None]
    return same[None] | ((position[None, :] < position[:, None])[None] & (live == 1))


def split_heads(value):
    rows, seg_len, width = value.shape
    return value.reshape(rows, seg_len, width // HD, HD)


def stream_forward(queries, keys, values, live, allow, memory):
    scale = HD ** (-0.5)
    q4, k4, v4 = split_heads(queries), split_heads(keys), split_heads(values)
    scores = jnp.einsum("rqhd,rkhd->rhqk", q4, k4, preferred_element_type=F32) * scale
    scores = jnp.where(allow_local_of(live)[:, None], scores, NEG_BIG)
    row_max = jnp.max(scores, axis=-1)
    expo = jnp.exp(scores - row_max[..., None])
    state = (
        row_max,
        jnp.sum(expo, axis=-1),
        jnp.einsum("rhqk,rkhd->rhqd", expo.astype(BF), v4, preferred_element_type=F32),
    )

    def step(running, item):
        row_max, row_total, acc = running
        block, allowed = item
        k3 = block[0].reshape(block.shape[1], -1, HD)
        v3 = block[1].reshape(block.shape[1], -1, HD)
        scores = jnp.einsum("rqhd,khd->rhqk", q4, k3, preferred_element_type=F32) * scale
        scores = jnp.where(allowed[:, None] > 0, scores, NEG_BIG)
        new_max = jnp.maximum(row_max, jnp.max(scores, axis=-1))
        shrink = jnp.exp(row_max - new_max)
        expo = jnp.exp(scores - new_max[..., None])
        acc = acc * shrink[..., None] + jnp.einsum(
            "rhqk,khd->rhqd", expo.astype(BF), v3, preferred_element_type=F32
        )
        return (new_max, row_total * shrink + jnp.sum(expo, axis=-1), acc), None

    (row_max, row_total, acc), unused = lax.scan(step, state, (memory, allow))
    out = (acc / row_total[..., None]).transpose(0, 2, 1, 3).reshape(queries.shape)
    return out.astype(BF), out, row_max + jnp.log(row_total)


def stream_backward(d_out, out_f32, queries, keys, values, live, log_total, allow, memory, cosine, sine):
    scale = HD ** (-0.5)
    q4, k4, v4, d4 = split_heads(queries), split_heads(keys), split_heads(values), split_heads(d_out)
    delta = jnp.sum(d4.astype(F32) * split_heads(out_f32), axis=-1).transpose(0, 2, 1)
    scores = jnp.einsum("rqhd,rkhd->rhqk", q4, k4, preferred_element_type=F32) * scale
    scores = jnp.where(allow_local_of(live)[:, None], scores, NEG_BIG)
    chances = jnp.exp(scores - log_total[..., None])
    dp = jnp.einsum("rqhd,rkhd->rhqk", d4, v4, preferred_element_type=F32)
    ds = (chances * (dp - delta[..., None])).astype(BF)
    dq = jnp.einsum("rhqk,rkhd->rqhd", ds, k4, preferred_element_type=F32)
    dk = jnp.einsum("rhqk,rqhd->rkhd", ds, q4, preferred_element_type=F32)
    dv = jnp.einsum("rhqk,rqhd->rkhd", chances.astype(BF), d4, preferred_element_type=F32)

    def step(running, item):
        block, allowed = item
        k3 = block[0].reshape(block.shape[1], -1, HD)
        v3 = block[1].reshape(block.shape[1], -1, HD)
        scores = jnp.einsum("rqhd,khd->rhqk", q4, k3, preferred_element_type=F32) * scale
        scores = jnp.where(allowed[:, None] > 0, scores, NEG_BIG)
        chances = jnp.exp(scores - log_total[..., None])
        dp = jnp.einsum("rqhd,khd->rhqk", d4, v3, preferred_element_type=F32)
        ds = (chances * (dp - delta[..., None])).astype(BF)
        return running + jnp.einsum("rhqk,khd->rqhd", ds, k3, preferred_element_type=F32), None

    dq, unused = lax.scan(step, dq, (memory, allow))

    def back(value):
        turned = rope_heads(value.reshape((-1,) + value.shape[2:]), jnp.tile(cosine, (value.shape[0], 1)), -jnp.tile(sine, (value.shape[0], 1)))
        return (turned * scale).reshape(queries.shape).astype(BF)

    return jnp.stack([back(dq), back(dk), dv.reshape(queries.shape).astype(BF)])


def local(
    layer_input,
    live,
    knn_index,
    mem_keys,
    mem_values,
    gain_attn,
    w_query,
    w_key,
    w_value,
    w_out,
    gain_ffn,
    w_gate,
    w_up,
    w_down,
    cotangent,
):
    seg_len, width = layer_input.shape[1:]
    quarter = width // 4
    n_seg = lax.axis_size("seg")
    n_devices = n_seg * lax.axis_size("rep")
    tokens = seg_len * n_seg
    n_high = n_seg // 4
    x, low, high, y, core = place()
    use_kernel = n_high <= KERNEL_HIGH
    kv_rows = 2 * seg_len
    group_tokens = 4 * seg_len

    def by_quarter(value):
        return [value[:, i * quarter : (i + 1) * quarter] for i in range(4)]

    gains = jnp.concatenate(
        [gain_attn[:, None], gain_ffn[:, None], jnp.zeros((gain_attn.shape[0], LANES - 2), BF)], 1
    )
    stacked = [by_quarter(w) for w in (w_query, w_key, w_value, w_out)]
    qo = jnp.stack([jnp.concatenate([s[i] for s in stacked] + [gains], 1) for i in range(4)])

    def core_quarters(value, side):
        return jnp.stack([cut(value, side * quarter, quarter), cut(value, (2 + side) * quarter, quarter)])

    def core_memory(side):
        return jnp.stack([core_quarters(mem_keys[0], side), core_quarters(mem_values[0], side)])

    coded = knn_index[0] * 2 + live[0][:, None]
    kv = jnp.concatenate([core_memory(core), flip_core(core_memory(1 - core))], 2)
    qo = trade_core(qo)
    coded_pair = jnp.stack([coded, flip_core(coded)])
    qo, kv, coded, coded_pair = fence(qo, kv, coded, coded_pair)
    x_own, w_gate, w_up = layer_input[0], w_gate, w_up
    x_own, w_gate, w_up, qo = fence(x_own, w_gate, w_up, qo)

    kv_near, kv_far = pick(kv, low, 1), flip_z(pick(kv, 1 - low, 1))
    pieces = ordered(kv_near[:, None], kv_far[:, None], low, 1)
    own_k, own_v = pieces[0], pieces[1]
    coded_far = flip_z(coded)
    if use_kernel:
        qo = gather_z_four(qo)
    else:
        qo = gather_high(start_gather(trade_z(qo).reshape(2, -1, qo.shape[-1])))
    x_pair = jnp.stack([x_own, flip_core(x_own)])
    gate = split_units(w_gate, n_devices)
    upw = split_units(w_up, n_devices)
    qo, own_k, own_v, coded_far, x_pair, gate, upw = fence(qo, own_k, own_v, coded_far, x_pair, gate, upw)

    coded = all_blocks(coded_pair, coded_far)
    live_all = jnp.bitwise_and(coded[:, :, 0], 1)[:, None, :]
    picks = lax.shift_right_arithmetic(coded, 1)
    pair = picks >= tokens
    slot = jnp.where(pair, picks - tokens, picks)
    slot_seg = slot // seg_len
    swapped = (jnp.arange(4, dtype=jnp.int32) % 2)[:, None, None]
    kv_row = jnp.bitwise_xor(pair.astype(jnp.int32), swapped)
    within = kv_row * seg_len + (slot - slot_seg * seg_len)

    split = 2 * quarter
    x_far = flip_z(x_pair[0])
    gate = trade_core(gate)
    upw = trade_core(upw)

    def trade_rows(value):
        return start_gather(trade_z(value).reshape(2, -1, value.shape[-1]))

    down_w = w_down[None, None, None, None]
    if use_kernel:
        slot_x, slot_low = slot_seg % 2, (slot_seg // 2) % 2
        same_x = slot_x == x
        in_group = jnp.where(same_x, 5, 4 + 2 * slot_low)
        before = jnp.where(same_x, 0, 2) + slot_low
        piece_no = jnp.where(slot_seg // 4 == high, in_group, before)
        columns = jnp.where(picks >= 0, piece_no * kv_rows + within, -1)
        mask = build_mask(columns, len(PIECES) * kv_rows // LANES)
        up_high = [(i, i + 4) for i in range(n_seg - 4)]

        def cross(value):
            return lax.ppermute(value, "seg", up_high)

        cross_k = cross(own_k)
        side_k = flip_x(own_k)
        qo_a, qo_b = gather_x(qo[..., :split]), gather_y(qo[..., split:])
        qo_a, qo_b, cross_k, side_k, own_v, x_far, gate, upw, down_w = fence(
            qo_a, qo_b, cross_k, side_k, own_v, x_far, gate, upw, down_w
        )
        cross_v = cross(own_v)
        cross_side_k = flip_x(cross_k)
        qo_a, qo_b = gather_y(qo_a), gather_x(qo_b)
        gate, upw = trade_rows(gate), trade_rows(upw)
        down_w = gather_high(down_w)
        x_all = all_blocks(x_pair, x_far)
        qo_a, qo_b, cross_v, cross_side_k, own_v, gate, upw, down_w, x_all = fence(
            qo_a, qo_b, cross_v, cross_side_k, own_v, gate, upw, down_w, x_all
        )
        cross_side_v = flip_x(cross_v)
        side_v = flip_x(own_v)
        key_pieces = (cross_k, cross_side_k, side_k, own_k)
    else:
        qo_a, qo_b = gather_y(gather_x(qo[..., :split])), gather_x(gather_y(qo[..., split:]))
        x_all = all_blocks(x_pair, x_far)
        gate, upw = trade_rows(gate), trade_rows(upw)
        down_w = gather_high(down_w)
        columns = jnp.where(picks >= 0, slot_seg * kv_rows + within, n_seg * kv_rows)
        blocks_at = jnp.arange(4)[:, None, None]
        queries_at = jnp.arange(seg_len)[None, :, None]
        allow = jnp.zeros((4, seg_len, n_seg * kv_rows), BF).at[blocks_at, queries_at, columns].set(1.0, mode="drop")
        allow = allow.reshape(4, seg_len, n_seg, kv_rows).transpose(2, 0, 1, 3)
        memory = jnp.stack([own_k, own_v], 1)[None, :, None]
        memory = gather_x(gather_high(memory)).reshape(n_seg, 2, kv_rows, quarter)

    w_a, w_b = flat(qo_a), flat(qo_b)
    wo_near = w_b[:, quarter : 2 * quarter]
    g_attn = w_b[:, 2 * quarter].astype(F32)
    g_ffn = w_b[:, 2 * quarter + 1].astype(F32)
    gate = gather_high(gate)
    upw = gather_high(upw)

    x_float = x_all.reshape(group_tokens, width).astype(F32)
    cosine, sine = rope_tables(seg_len)
    cos_all = jnp.tile(cosine, (4, 1))
    sin_all = jnp.tile(sine, (4, 1))
    h_float, inv_one = norm_forward(x_float, g_attn)
    h_one = h_float.astype(BF)
    turned = rope_heads(matmul(h_one, w_a).reshape(group_tokens, -1, HD), cos_all, sin_all)
    turned = turned.reshape(group_tokens, 2 * quarter).astype(BF)
    w_v = w_b[:, :quarter]
    queries = turned[:, :quarter].reshape(4, seg_len, quarter)
    keys = turned[:, quarter:].reshape(4, seg_len, quarter)
    values = matmul(h_one, w_v).astype(BF).reshape(4, seg_len, quarter)
    if use_kernel:
        queries, keys, values, cross_side_v, side_v, gate, upw, down_w, wo_near = fence(
            queries, keys, values, cross_side_v, side_v, gate, upw, down_w, wo_near
        )
        value_pieces = (cross_v, cross_side_v, side_v, own_v)
        out_low, out_f32, p_memory, p_local, inverse = attention_forward(
            queries, keys, values, live_all, mask, key_pieces, value_pieces
        )
    else:
        out_low, out_f32, log_total = stream_forward(queries, keys, values, live_all, allow, memory)
    wo_far = flip_z(wo_near)
    gate, upw = gather_x(gate), gather_y(upw)
    down_w = gather_x(down_w)
    g_own = cotangent[0]
    out_low, wo_far, gate, upw, down_w, g_own = fence(out_low, wo_far, gate, upw, down_w, g_own)

    att_near = out_low.reshape(group_tokens, quarter)
    att_far = flip_z(att_near)
    gate, upw = gather_y(gate), gather_x(upw)
    wo = all_quarters(wo_near, wo_far, False)
    g_pair = jnp.stack([g_own, flip_core(g_own)])
    att_near, att_far, gate, upw, down_w, wo, g_own = fence(att_near, att_far, gate, upw, down_w, wo, g_own)

    wg, wu = flat(gate), flat(upw)
    wd = flat(gather_y(down_w))
    g_far = flip_z(g_own)
    attended = all_quarters(att_near, att_far, True)
    x_one = x_float + matmul(attended, wo)
    h_two_f, inv_two = norm_forward(x_one, g_ffn)
    h_two = h_two_f.astype(BF)
    gate_out = matmul(h_two, wg)
    up_out = matmul(h_two, wu)
    sigma = jax.nn.sigmoid(gate_out)
    swish = gate_out * sigma
    hidden = (swish * up_out).astype(BF)
    grad_out = all_blocks(g_pair, g_far).reshape(group_tokens, width)

    d_hidden = matmul_cols(grad_out, wd)
    d_gate = (d_hidden * up_out * sigma * (1.0 + gate_out * (1.0 - sigma))).astype(BF)
    d_up = (d_hidden * swish).astype(BF)
    sums = core_sums(matmul_cols(d_gate, wg) + matmul_cols(d_up, wu))
    sums, hidden, h_two, d_gate, d_up, wd = fence(sums, hidden, h_two, d_gate, d_up, wd)

    d_h_two = all_sums(sums).reshape(group_tokens, width)
    plane_wg = reduce_plane(matmul_rows(h_two, d_gate).astype(BF), 2, True)
    plane_wu = reduce_plane(matmul_rows(h_two, d_up).astype(BF), 2, False)
    grad_wd = matmul_rows(hidden, grad_out).astype(BF)
    down_sums = core_sums(matmul(hidden, wd))
    d_h_two, plane_wg, plane_wu, down_sums, grad_wd = fence(d_h_two, plane_wg, plane_wu, down_sums, grad_wd)

    own = 2 * low * seg_len
    d_x_norm, normed_two = norm_backward(x_one, inv_two, g_ffn, d_h_two)
    d_x_one = grad_out.astype(F32) + d_x_norm
    d_branch = d_x_one.astype(BF)
    grad_g_ffn = jnp.sum(cut(d_h_two, own, seg_len, 0) * cut(normed_two, own, seg_len, 0), axis=0)
    at_quarter = (2 * low + core) * quarter
    d_att = matmul_cols(d_branch, cut(wo, at_quarter, quarter, 0)).astype(BF).reshape(4, seg_len, quarter)
    plane_wd = reduce_plane(grad_wd, 1, True)
    high_wg = reduce_high(plane_wg)
    high_wu = reduce_high(plane_wu)
    layer_output = (cut(x_one, own, seg_len, 0) + own_sums(down_sums)).astype(BF)

    if use_kernel:
        d_kv, dq_local = attention_backward_local(
            d_att, out_f32, queries, keys, values, inverse, p_local, cosine, sine
        )
        d_kv, dq_local, d_att, d_branch, plane_wd, high_wg, high_wu, layer_output = fence(
            d_kv, dq_local, d_att, d_branch, plane_wd, high_wg, high_wu, layer_output
        )
    else:
        d_qkv = stream_backward(
            d_att, out_f32, queries, keys, values, live_all, log_total, allow, memory, cosine, sine
        )
        d_kv, d_q = d_qkv[1:], d_qkv[0]
    d_kv = d_kv.reshape(2, group_tokens, quarter)
    grad_kv = jnp.concatenate([matmul_rows(h_one, d_kv[i]).astype(BF) for i in range(2)], 1)
    grad_wo = matmul_rows(attended, cut(d_branch, at_quarter, quarter)).astype(BF)
    if use_kernel:
        d_att, grad_kv, grad_wo, dq_local = fence(d_att, grad_kv, grad_wo, dq_local)
        d_q = attention_backward(
            d_att, out_f32, dq_local, inverse, p_memory, cosine, sine, key_pieces, value_pieces
        )
    plane_kv = reduce_plane(grad_kv, 2, True)
    plane_wo = reduce_plane(grad_wo, 2, False)
    high_wd = reduce_high(plane_wd)
    four_wg = untrade(high_wg)
    four_wu = untrade(high_wu)
    d_q, plane_kv, plane_wo, high_wd, four_wg, four_wu = fence(d_q, plane_kv, plane_wo, high_wd, four_wg, four_wu)

    d_q = d_q.reshape(group_tokens, quarter)
    d_h_part = (
        matmul_cols(d_q, w_a[:, :quarter]) + matmul_cols(d_kv[0], w_a[:, quarter:]) + matmul_cols(d_kv[1], w_v)
    )
    grad_g_attn = jnp.sum(d_h_part * (x_float * inv_one), axis=0)
    d_h_sums = core_sums(d_h_part)
    grad_q = matmul_rows(h_one, d_q).astype(BF)
    grad_gains = jnp.concatenate(
        [
            grad_g_attn.astype(BF)[:, None],
            grad_g_ffn.astype(BF)[:, None],
            jnp.zeros((width, LANES - 2), BF),
        ],
        1,
    )
    plane_q = reduce_plane(jnp.concatenate([grad_q, grad_gains], 1), 2, False)
    high_kvo = reduce_high(jnp.concatenate([plane_kv, plane_wo], -1))
    d_h_one = own_sums(d_h_sums)
    x_own = cut(x_float, own, seg_len, 0)
    d_x_first, unused = norm_backward(x_own, cut(inv_one, own, seg_len, 0), g_attn, d_h_one)
    grad_x = (cut(d_x_one, own, seg_len, 0) + d_x_first).astype(BF)

    sum_wd = high_wd[0].astype(F32)
    sum_wg = join_units(four_wg.reshape(4, -1, high_wg.shape[-1]), n_devices)
    sum_wu = join_units(four_wu.reshape(4, -1, high_wu.shape[-1]), n_devices)
    sums = untrade(jnp.concatenate([reduce_high(plane_q), high_kvo], -1))
    sums = sums.reshape(4, -1, sums.shape[-1]).astype(F32)
    after = quarter + LANES

    def columns_of(at):
        return jnp.concatenate([sums[i][:, at : at + quarter] for i in range(4)], 1)

    sum_gains = jnp.sum(sums[:, :, quarter : quarter + 2], axis=0)
    return (
        layer_output[None],
        grad_x[None],
        sum_gains[:, 0],
        columns_of(0),
        columns_of(after),
        columns_of(after + quarter),
        columns_of(after + 2 * quarter),
        sum_gains[:, 1],
        sum_wg,
        sum_wu,
        sum_wd,
    )


def solution(mesh):
    tokens = P("rep", "seg", None)
    vector = P(("seg", "rep"))
    matrix = P(("seg", "rep"), None)
    return jax.shard_map(
        local,
        mesh=mesh,
        in_specs=(
            tokens,
            P("rep", "seg"),
            tokens,
            tokens,
            tokens,
            vector,
            matrix,
            matrix,
            matrix,
            matrix,
            vector,
            matrix,
            matrix,
            matrix,
            tokens,
        ),
        out_specs=(tokens, tokens, vector, matrix, matrix, matrix, matrix, vector, matrix, matrix, matrix),
        check_vma=False,
    )
```

```python
import jax
import jax.numpy as jnp
from jax import lax
from jax.experimental import pallas as pl
from jax.experimental.pallas import tpu as pltpu
from jax.sharding import PartitionSpec as P

H = 8
HD = 128
EPSILON = 1e-05
NEG_BIG = -1e30
POS_BIG = 1e30
ROPE_BASE = 10000.0
LANES = 128
KERNEL_HIGH = 2

SHORT = pl.CostEstimate(flops=1000, bytes_accessed=1000, transcendentals=0)

BF = jnp.bfloat16
F32 = jnp.float32


def cdiv(a, b):
    return -(-a // b)


def flip(value, axis, bit):
    count = lax.axis_size(axis)
    return lax.ppermute(value, axis, [(i, i ^ bit) for i in range(count)])


def flip_core(value):
    return flip(value, "rep", 1)


def flip_y(value):
    return flip(value, "rep", 2)


def flip_x(value):
    return flip(value, "seg", 1)


def flip_z(value):
    return flip(value, "seg", 2)


def ordered(mine, other, bit, axis):
    first = jnp.where(bit == 0, mine, other)
    second = jnp.where(bit == 0, other, mine)
    return jnp.concatenate([first, second], axis)


def pick(value, index, axis):
    return lax.dynamic_index_in_dim(value, index, axis, keepdims=False)


def cut(value, start, size, axis=-1):
    return lax.dynamic_slice_in_dim(value, start, size, axis % value.ndim)


def fence(*values):
    return lax.optimization_barrier(values)


def place():
    seg = lax.axis_index("seg")
    rep = lax.axis_index("rep")
    return seg % 2, (seg // 2) % 2, seg // 4, rep // 2, rep % 2


def high_bits():
    bit = 4
    out = []
    while bit < lax.axis_size("seg"):
        out.append(bit)
        bit *= 2
    return out


def gather_high(cur):
    seg = lax.axis_index("seg")
    for bit in high_bits():
        cur = ordered(cur, flip(cur, "seg", bit), (seg // bit) % 2, 0)
    return cur


def gather_x(cur):
    return ordered(cur, flip_x(cur), place()[0], 2)


def gather_y(cur):
    return ordered(cur, flip_y(cur), place()[3], 3)


def gather_high_pair(cur):
    seg = lax.axis_index("seg")
    cur = cur[:, None]
    bits = high_bits()
    for bit in bits[:-1]:
        cur = ordered(cur, flip(cur, "seg", bit), (seg // bit) % 2, 1)
    recv = flip(cur, "seg", bits[-1])
    side = (seg // bits[-1]) % 2
    return [ordered(cur[i], recv[i], side, 0)[:, :, None, None] for i in range(2)]


def flat(cur):
    return cur.reshape(-1, cur.shape[-1])


def halve(value, axis_name, bit, side, axis):
    recv = flip(pick(value, 1 - side, axis), axis_name, bit)
    kept = pick(value, side, axis)
    return (kept.astype(F32) + recv.astype(F32)).astype(BF)


def plane_shape(value, low):
    high = lax.axis_size("seg") // 4
    return value.reshape(high, low, 2, -1, value.shape[-1])


def halves(cur, axis, side):
    return pick(cur, side, axis), pick(cur, 1 - side, axis)


def plane_flips(parts):
    n_rep = lax.axis_size("rep")
    count = lax.axis_size("seg") * n_rep
    far = [(i, i ^ n_rep ^ 2) for i in range(count)]
    return flip_x(parts[0]), flip_y(parts[1]), lax.ppermute(parts[2], ("seg", "rep"), far)


def add_all(first, *others):
    total = first.astype(F32)
    for other in others:
        total = total + other.astype(F32)
    return total.astype(BF)


def z_parts(cur):
    unused, low, high, unused, unused = place()
    here, there = pick(cur, high, 0), pick(cur, 1 - high, 0)
    return pick(here, low, 0), pick(there, low, 0), pick(there, 1 - low, 0), pick(here, 1 - low, 0)


def z_flips(parts):
    return flip(parts[1], "seg", 4), flip(parts[2], "seg", 6), flip_z(parts[3])


def z_total(kept, flips):
    return ordered(add_all(kept, flips[0])[None], add_all(flips[1], flips[2])[None], place()[1], 0)


def z_plain(cur):
    low = place()[1]
    sums = reduce_high(cur)
    return ordered(pick(sums, low, 0)[None], flip_z(pick(sums, 1 - low, 0))[None], low, 0)


def reduce_high(cur):
    seg = lax.axis_index("seg")
    for bit in reversed(high_bits()):
        cur = cur.reshape((2, cur.shape[0] // 2) + cur.shape[1:])
        cur = halve(cur, "seg", bit, (seg // bit) % 2, 0)
    return cur[0]


def trade_core(quarters):
    core = place()[4]
    low, unused, rows, cols = 2, 2, quarters.shape[1], quarters.shape[2]
    four = quarters.reshape(2, 2, rows, cols)
    return ordered(pick(four, core, 1), flip_core(pick(four, 1 - core, 1)), core, 1)


def trade_z(halves):
    low = place()[1]
    return ordered(pick(halves, low, 0)[None], flip_z(pick(halves, 1 - low, 0))[None], low, 0)


def gather_z_four(halves):
    seg = lax.axis_index("seg")
    low = (seg // 2) % 2
    keep, give = pick(halves, low, 0)[None, None], pick(halves, 1 - low, 0)[None, None]
    near = ordered(keep, flip(give, "seg", 2), low, 1)
    far = ordered(flip(keep, "seg", 4), flip(give, "seg", 6), low, 1)
    return ordered(near, far, (seg // 4) % 2, 0)[:, :, None, None]


def start_gather(traded):
    return traded[None, :, None, None]


def reduce_core(mine):
    core = place()[4]
    four = mine.reshape(2, 2, mine.shape[1] // 2, mine.shape[2])
    kept = pick(four, core, 1)[:, None]
    four = ordered(kept, flip_core(pick(four, 1 - core, 1))[:, None], core, 1)
    return four.reshape((4,) + four.shape[2:])


def swap_pairs(value):
    blocks = value.reshape((value.shape[0], 2, 2, value.shape[1] // 4) + value.shape[2:])
    return jnp.stack([blocks[:, :, 1], blocks[:, :, 0]], 2).reshape(value.shape)


def all_quarters(mine, far, of_tokens):
    unused, low, unused, unused, core = place()
    other = flip_core(jnp.stack([mine, far]))
    if of_tokens:
        other = swap_pairs(other)
    near_half = ordered(mine, other[0], core, 1)
    far_half = ordered(far, other[1], core, 1)
    return ordered(near_half, far_half, low, 1)


def all_blocks(by_low):
    both = jnp.stack([by_low, flip_core(by_low)], 1)
    return both.reshape((-1,) + by_low.shape[1:])


def two_rows(value):
    return ordered(value[None], flip_z(value)[None], place()[1], 0)


def core_parts(part):
    blocks = part.reshape((2, 2, part.shape[0] // 4) + part.shape[1:])
    return blocks[:, 0].astype(BF), blocks[:, 1].astype(BF)


def core_sums(part):
    blocks = part.reshape((2, 2, part.shape[0] // 4) + part.shape[1:])
    return (blocks[:, 0] + flip_core(blocks[:, 1].astype(BF)).astype(F32)).astype(BF)


def own_sums(sums):
    low = place()[1]
    return pick(sums, low, 0).astype(F32) + flip_z(pick(sums, 1 - low, 0)).astype(F32)


def z_sums(sums):
    return (sums.astype(F32) + flip_z(sums).astype(F32)).astype(BF)


def both_cores(sums):
    return jnp.stack([sums, flip_core(sums)], 1).astype(F32)


def unit_blocks(n_blocks):
    order = []
    for block in range(n_blocks):
        high, low, rest, core = block // 16, (block // 8) % 2, (block // 2) % 4, block % 2
        order.append((low * 2 + core, high * 4 + rest))
    return order


def split_units(one, two, n_blocks):
    rows, total = one.shape
    size = total // n_blocks

    def body(one_ref, two_ref, out_ref):
        for half, in_ref in enumerate((one_ref, two_ref)):
            for block, (quarter, at) in enumerate(unit_blocks(n_blocks)):
                out_ref[quarter, half * rows : (half + 1) * rows, at * size : (at + 1) * size] = in_ref[
                    :, block * size : (block + 1) * size
                ]

    return pl.pallas_call(
        body,
        out_shape=jax.ShapeDtypeStruct((4, 2 * rows, total // 4), one.dtype),
        cost_estimate=SHORT,
        name="split_units",
    )(one, two)


def join_units(quarters, n_blocks):
    unused, rows, quarter_size = quarters.shape
    size = 4 * quarter_size // n_blocks

    def body(in_ref, out_ref):
        for block, (quarter, at) in enumerate(unit_blocks(n_blocks)):
            out_ref[:, block * size : (block + 1) * size] = in_ref[
                quarter, :, at * size : (at + 1) * size
            ].astype(F32)

    return pl.pallas_call(
        body,
        out_shape=jax.ShapeDtypeStruct((rows, 4 * quarter_size), F32),
        cost_estimate=SHORT,
        name="join_units",
    )(quarters)


def matmul(left, right):
    return jnp.dot(left, right, preferred_element_type=F32)


def matmul_rows(left, right):
    return lax.dot_general(left, right, (((0,), (0,)), ((), ())), preferred_element_type=F32)


def matmul_cols(left, right):
    return lax.dot_general(left, right, (((1,), (1,)), ((), ())), preferred_element_type=F32)


def norm_forward(values, gain):
    inverse = lax.rsqrt(jnp.mean(values * values, axis=-1, keepdims=True) + EPSILON)
    return (values * inverse * gain, inverse)


def norm_backward(values, inverse, gain, grad_out):
    normed = values * inverse
    scaled = grad_out * gain
    grad_values = inverse * (scaled - normed * jnp.mean(scaled * normed, axis=-1, keepdims=True))
    return (grad_values, normed)


def rope_tables(seg_len):
    position = jnp.arange(seg_len).astype(F32)
    freqs = ROPE_BASE ** (-(2.0 * jnp.arange(HD // 2).astype(F32)) / HD)
    angle = position[:, None] * freqs[None, :]
    cosine, sine = jnp.cos(angle), jnp.sin(angle)
    return (jnp.concatenate([cosine, cosine], -1), jnp.concatenate([-sine, sine], -1))


def rope_heads(values, cosine, sine):
    half = HD // 2
    swapped = jnp.concatenate([values[..., half:], values[..., :half]], -1)
    return values * cosine[:, None, :] + swapped * sine[:, None, :]


def mask_kernel(n_cols, cols_ref, live_ref, out_ref, scratch):
    queries = cols_ref.shape[1]
    picks = cols_ref[0]
    pad = scratch.shape[0]
    high = lax.shift_right_arithmetic(picks, 7)
    low = jnp.bitwise_and(picks, LANES - 1)
    iota_high = lax.broadcasted_iota(jnp.int32, (pad, picks.shape[1]), 0)
    iota_low = lax.broadcasted_iota(jnp.int32, (LANES, picks.shape[1]), 0)
    for i in range(queries):
        hot_high = jnp.where(iota_high == high[i : i + 1, :], 1.0, 0.0).astype(BF)
        hot_low = jnp.where(iota_low == low[i : i + 1, :], 1.0, 0.0).astype(BF)
        scratch[:, i, :] = matmul_cols(hot_high, hot_low)
    out_ref[0, 0:n_cols] = jnp.where(scratch[0:n_cols] > 0.5, POS_BIG, NEG_BIG).astype(BF)
    row = lax.broadcasted_iota(jnp.int32, (queries, LANES), 0) + pl.program_id(1) * queries
    for part in range(out_ref.shape[1] - n_cols):
        col = lax.broadcasted_iota(jnp.int32, (queries, LANES), 1) + part * LANES
        live = live_ref[0, :, part * LANES : (part + 1) * LANES]
        allow = (col == row) | ((col < row) & (live == 1))
        out_ref[0, n_cols + part] = jnp.where(allow, POS_BIG, NEG_BIG).astype(BF)


def build_mask(columns, live, n_cols):
    rows, queries, picks = columns.shape
    block = 16
    pad = cdiv(n_cols, 8) * 8
    n_local = live.shape[2] // LANES
    return pl.pallas_call(
        lambda *refs: mask_kernel(n_cols, *refs),
        grid=(rows, queries // block),
        in_specs=[
            pl.BlockSpec((1, block, picks), lambda r, g: (r, g, 0)),
            pl.BlockSpec((1, 1, live.shape[2]), lambda r, g: (r, 0, 0)),
        ],
        out_specs=pl.BlockSpec((1, n_cols + n_local, block, LANES), lambda r, g: (r, 0, g, 0)),
        out_shape=jax.ShapeDtypeStruct((rows, n_cols + n_local, queries, LANES), BF),
        scratch_shapes=[pltpu.VMEM((pad, block, LANES), F32)],
        compiler_params=pltpu.CompilerParams(vmem_limit_bytes=16 * 1024 * 1024),
        cost_estimate=SHORT,
        name="mask_build",
    )(columns, live)


def project_kernel(x_ref, wa_ref, wb_ref, cos_ref, sin_ref, q_ref, k_ref, v_ref, h_ref, inv_ref, gain_ref):
    quarter = q_ref.shape[2]

    @pl.when(pl.program_id(0) == 0)
    def gains():
        gain_ref[...] = jnp.transpose(wb_ref[:, quarter:].astype(F32), (1, 0))[0:8]

    x = x_ref[0].astype(F32)
    inverse = lax.rsqrt(jnp.mean(x * x, axis=-1, keepdims=True) + EPSILON)
    h = (x * inverse * gain_ref[0:1, :]).astype(BF)
    h_ref[0] = h
    inv_ref[0] = inverse
    turned = matmul(h, wa_ref[:, : 2 * quarter])
    for head in range(2 * quarter // HD):
        value = turned[:, head * HD : (head + 1) * HD]
        value = (value * cos_ref[...] + pltpu.roll(value, HD // 2, 1) * sin_ref[...]).astype(BF)
        if head < quarter // HD:
            q_ref[0, :, head * HD : (head + 1) * HD] = value
        else:
            at = head * HD - quarter
            k_ref[0, :, at : at + HD] = value
    v_ref[0] = matmul(h, wa_ref[:, 2 * quarter :]).astype(BF)


def project(x_all, w_a, w_b, cosine, sine):
    blocks, seg_len, width = x_all.shape
    quarter = w_a.shape[1] // 3
    whole = lambda array: pl.BlockSpec(array.shape, lambda r: (0, 0))
    head = pl.BlockSpec((1, seg_len, quarter), lambda r: (r, 0, 0))
    full = pl.BlockSpec((1, seg_len, width), lambda r: (r, 0, 0))
    out = jax.ShapeDtypeStruct((blocks, seg_len, quarter), BF)
    return pl.pallas_call(
        project_kernel,
        grid=(blocks,),
        in_specs=[full, whole(w_a), whole(w_b), whole(cosine), whole(sine)],
        out_specs=[head, head, head, full, pl.BlockSpec((1, seg_len, 1), lambda r: (r, 0, 0))],
        out_shape=[out, out, out, jax.ShapeDtypeStruct(x_all.shape, BF), jax.ShapeDtypeStruct((blocks, seg_len, 1), F32)],
        scratch_shapes=[pltpu.VMEM((8, width), F32)],
        compiler_params=pltpu.CompilerParams(vmem_limit_bytes=24 * 1024 * 1024),
        cost_estimate=SHORT,
        name="project",
    )(x_all, w_a, w_b, cosine, sine)


def plane_place():
    x, low, unused, y, core = place()
    return jnp.stack([x, y, 2 * low + core]).astype(jnp.int32)


def by_x(at, block, product, keep_ref, send_ref):
    rows = product.shape[0] // 2

    def write(ref):
        for part in range(2):
            ref[block // 2 * 2 + part] = product[part * rows : (part + 1) * rows]

    @pl.when(block % 2 == at[0])
    def mine():
        write(keep_ref)

    @pl.when(block % 2 != at[0])
    def theirs():
        write(send_ref)


def by_y(at, block, product, keep_ref, send_ref):
    rows = product.shape[0] // 2
    upper, lower = product[:rows], product[rows:]
    keep_ref[block] = jnp.where(at[1] == 0, upper, lower)
    send_ref[block] = jnp.where(at[1] == 0, lower, upper)


def by_both(at, block, product, keep_ref, x_ref, y_ref, xy_ref):
    rows = product.shape[0] // 2
    upper, lower = product[:rows], product[rows:]
    near = jnp.where(at[1] == 0, upper, lower)
    far = jnp.where(at[1] == 0, lower, upper)

    @pl.when(block % 2 == at[0])
    def mine():
        keep_ref[block // 2] = near
        y_ref[block // 2] = far

    @pl.when(block % 2 != at[0])
    def theirs():
        x_ref[block // 2] = near
        xy_ref[block // 2] = far


def gradient(left, rights, how, column_block=None):
    tokens, width = left.shape
    n_blocks = lax.axis_size("seg")
    rows = width // n_blocks
    sizes = [column_block or right.shape[1] for right in rights]
    cols = sum(sizes)
    if rows % LANES:
        x, unused, unused, y, unused = place()
        if column_block:
            rights = [cut(rights[0], plane_place()[2] * column_block, column_block)]
        full = matmul_rows(left, jnp.concatenate(rights, 1)).astype(BF).reshape(-1, 2, 2, rows // 2, cols)
        near, side = halves(full, 1, x)
        if how is by_x:
            return [near.reshape(-1, rows // 2, cols), side.reshape(-1, rows // 2, cols)]
        if how is by_y:
            return [part.reshape(-1, rows // 2, cols) for part in halves(full, 2, y)]
        return [halves(near, 1, y)[0], halves(side, 1, y)[0], halves(near, 1, y)[1], halves(side, 1, y)[1]]
    shape = {
        by_x: (2, (n_blocks, rows // 2, cols)),
        by_y: (2, (n_blocks, rows // 2, cols)),
        by_both: (4, (n_blocks // 2, rows // 2, cols)),
    }[how]

    def body(at_ref, left_ref, *refs):
        at = [at_ref[0], at_ref[1]]
        parts = [matmul_rows(left_ref[...], right_ref[...]).astype(F32) for right_ref in refs[: len(rights)]]
        product = parts[0] if len(parts) == 1 else jnp.concatenate(parts, 1)
        how(at, pl.program_id(0), product.astype(BF), *refs[len(rights) :])

    column = lambda i, at: (0, at[2]) if column_block else (0, 0)
    return pl.pallas_call(
        body,
        grid_spec=pltpu.PrefetchScalarGridSpec(
            num_scalar_prefetch=1,
            grid=(n_blocks,),
            in_specs=[pl.BlockSpec((tokens, rows), lambda i, at: (0, i))]
            + [pl.BlockSpec((tokens, size), column) for size in sizes],
            out_specs=[pl.BlockSpec(shape[1], lambda i, at: (0, 0, 0))] * shape[0],
        ),
        out_shape=[jax.ShapeDtypeStruct(shape[1], BF)] * shape[0],
        compiler_params=pltpu.CompilerParams(vmem_limit_bytes=16 * 1024 * 1024),
        cost_estimate=SHORT,
        name="gradient_" + how.__name__,
    )(plane_place(), left, *rights)


def gradient_units(left, right):
    tokens, width = left.shape
    n_high = lax.axis_size("seg") // 4
    rows = width // (4 * n_high)
    cols = right.shape[1]
    step = 256
    if rows % 8:
        full = matmul_rows(left, right).astype(BF).reshape(-1, 2, 2, rows, cols)
        return [part.reshape(-1, rows, cols) for part in halves(full, 1, place()[0])]

    def body(at_ref, left_ref, right_ref, keep_ref, send_ref):
        product = matmul_rows(left_ref[...], right_ref[...])
        for high in range(n_high):
            for y in range(2):
                first = (high * 4 + y) * rows
                second = first + 2 * rows
                zero, one = product[first : first + rows], product[second : second + rows]
                keep_ref[high * 2 + y] = jnp.where(at_ref[0] == 0, zero, one).astype(BF)
                send_ref[high * 2 + y] = jnp.where(at_ref[0] == 0, one, zero).astype(BF)

    shape = (n_high * 2, rows, cols)
    return pl.pallas_call(
        body,
        grid_spec=pltpu.PrefetchScalarGridSpec(
            num_scalar_prefetch=1,
            grid=(cols // step,),
            in_specs=[
                pl.BlockSpec((tokens, width), lambda i, at: (0, 0)),
                pl.BlockSpec((tokens, step), lambda i, at: (0, i)),
            ],
            out_specs=[pl.BlockSpec((n_high * 2, rows, step), lambda i, at: (0, 0, i))] * 2,
        ),
        out_shape=[jax.ShapeDtypeStruct(shape, BF)] * 2,
        compiler_params=pltpu.CompilerParams(vmem_limit_bytes=16 * 1024 * 1024),
        cost_estimate=SHORT,
        name="gradient_units",
    )(plane_place(), left, right)


def add_low(one, two):
    return (one.astype(F32) + two.astype(F32)).astype(BF)


def lane_blocks(value):
    return [value[:, i : i + LANES] for i in range(0, value.shape[1], LANES)]


PIECES = ((0, 0), (0, 1), (1, 0), (1, 1), (2, 0), (3, 0), (2, 1))
N_COMMON = 5
N_GROUPS = 4


def forward_kernel(q_ref, k_ref, v_ref, mine_ref, other_ref, *refs):
    key_refs, value_refs = refs[:N_GROUPS], refs[N_GROUPS : 2 * N_GROUPS]
    o_ref, of_ref, p_ref, pl_ref, inv_ref, s_ref, top_ref, total_ref, acc_ref = refs[2 * N_GROUPS :]
    scale = HD ** (-0.5)
    upper = pl.program_id(1) >= 2
    queries = q_ref[0]
    seg_len = queries.shape[0]
    per = key_refs[0].shape[1] // LANES
    first = pl.program_id(1) % 2 == 0

    def bias(at):
        return jnp.where(first, mine_ref[0, at], other_ref[0, at]).astype(F32)

    local_bias = jnp.concatenate([bias(len(PIECES) * per + i) for i in range(cdiv(seg_len, LANES))], 1)
    s_local = jnp.minimum(matmul_cols(queries, k_ref[0]) * scale, local_bias[:, :seg_len])

    def score(t, top):
        group, low = PIECES[t]
        parts = lane_blocks(matmul_cols(queries, key_refs[group][low]) * scale)
        for i in range(per):
            part = jnp.minimum(parts[i], bias(t * per + i))
            s_ref[t, :, i * LANES : (i + 1) * LANES] = part
            top = part if top is None else jnp.maximum(top, part)
        return top

    top = None
    for t in range(N_COMMON):
        top = score(t, top)
    top_ref[...] = top

    @pl.when(upper)
    def more_scores():
        more = top_ref[...]
        for t in range(N_COMMON, len(PIECES)):
            more = score(t, more)
        top_ref[...] = more

    row_max = jnp.maximum(
        jnp.max(s_local, axis=-1, keepdims=True), jnp.max(top_ref[...], axis=-1, keepdims=True)
    )
    e_local = jnp.exp(s_local - row_max)
    low_local = e_local.astype(BF)
    pl_ref[0, 0] = low_local

    def weigh(t, total, acc):
        group, low = PIECES[t]
        expo = jnp.exp(s_ref[t] - row_max)
        for part in lane_blocks(expo):
            total = part if total is None else total + part
        chances = expo.astype(BF)
        p_ref[0, 0, t] = chances
        return total, acc + matmul(chances, value_refs[group][low])

    total, acc = None, matmul(low_local, v_ref[0])
    for t in range(N_COMMON):
        total, acc = weigh(t, total, acc)
    total_ref[...] = total
    acc_ref[...] = acc

    @pl.when(upper)
    def more_values():
        total, acc = total_ref[...], acc_ref[...]
        for t in range(N_COMMON, len(PIECES)):
            total, acc = weigh(t, total, acc)
        total_ref[...] = total
        acc_ref[...] = acc

    row_total = jnp.sum(e_local, axis=-1, keepdims=True) + jnp.sum(total_ref[...], axis=-1, keepdims=True)
    inverse = 1.0 / row_total
    out = acc_ref[...] * inverse
    of_ref[0] = out
    o_ref[0] = out.astype(BF)
    inv_ref[0, 0] = inverse


def backward_local_kernel(do_ref, of_ref, q_ref, k_ref, v_ref, inv_ref, pl_ref, cos_ref, sin_ref, dkv_ref, dq_ref):
    scale = HD ** (-0.5)
    d_out = do_ref[0]
    delta = jnp.sum(d_out.astype(F32) * of_ref[0], axis=-1, keepdims=True)
    chances = pl_ref[0, 0].astype(F32) * inv_ref[0, 0]
    ds = (chances * (matmul_cols(d_out, v_ref[0]) - delta)).astype(BF)
    dq_ref[0] = matmul(ds, k_ref[0])
    dk = matmul_rows(ds, q_ref[0])
    dkv_ref[0, 0] = ((dk * cos_ref[...] - pltpu.roll(dk, HD // 2, 1) * sin_ref[...]) * scale).astype(BF)
    dkv_ref[1, 0] = matmul_rows(chances.astype(BF), d_out).astype(BF)


def backward_kernel(do_ref, of_ref, local_ref, inv_ref, p_ref, cos_ref, sin_ref, *refs):
    key_refs, value_refs = refs[:N_GROUPS], refs[N_GROUPS : 2 * N_GROUPS]
    out_ref, dq_ref = refs[2 * N_GROUPS :]
    scale = HD ** (-0.5)
    upper = pl.program_id(1) >= 2
    d_out = do_ref[0]
    inverse = inv_ref[0, 0]
    delta = jnp.sum(d_out.astype(F32) * of_ref[0], axis=-1, keepdims=True)

    def piece(t, dq):
        group, low = PIECES[t]
        dp = matmul_cols(d_out, value_refs[group][low])
        ds = (p_ref[0, 0, t].astype(F32) * ((dp - delta) * inverse)).astype(BF)
        return dq + matmul(ds, key_refs[group][low])

    dq = local_ref[0]
    for t in range(N_COMMON):
        dq = piece(t, dq)
    dq_ref[...] = dq

    @pl.when(upper)
    def more():
        dq = dq_ref[...]
        for t in range(N_COMMON, len(PIECES)):
            dq = piece(t, dq)
        dq_ref[...] = dq

    dq = dq_ref[...]
    out_ref[0] = ((dq * cos_ref[...] - pltpu.roll(dq, HD // 2, 1) * sin_ref[...]) * scale).astype(BF)


def attention_specs(piece_rows, seg_len):
    head = pl.BlockSpec((1, seg_len, HD), lambda h, r: (r, 0, h))
    piece = pl.BlockSpec((2, piece_rows, HD), lambda h, r: (0, 0, h))
    p_spec = pl.BlockSpec((1, 1, len(PIECES), seg_len, piece_rows), lambda h, r: (r, h, 0, 0, 0))
    pl_spec = pl.BlockSpec((1, 1, seg_len, seg_len), lambda h, r: (r, h, 0, 0))
    inv_spec = pl.BlockSpec((1, 1, seg_len, 1), lambda h, r: (r, h, 0, 0))
    return head, piece, p_spec, pl_spec, inv_spec


def attention_forward(queries, keys, values, mask, other_mask, key_pieces, value_pieces):
    blocks, seg_len, width = queries.shape
    heads = width // HD
    piece_rows = key_pieces[0].shape[1]
    head, piece, p_spec, pl_spec, inv_spec = attention_specs(piece_rows, seg_len)
    return pl.pallas_call(
        forward_kernel,
        grid=(heads, blocks),
        in_specs=[
            head,
            head,
            head,
            pl.BlockSpec((1,) + mask.shape[1:], lambda h, r: (r // 2, 0, 0, 0)),
            pl.BlockSpec((1,) + mask.shape[1:], lambda h, r: (r // 2, 0, 0, 0)),
        ]
        + [piece] * (2 * N_GROUPS),
        out_specs=[head, head, p_spec, pl_spec, inv_spec],
        out_shape=[
            jax.ShapeDtypeStruct(queries.shape, BF),
            jax.ShapeDtypeStruct(queries.shape, F32),
            jax.ShapeDtypeStruct((blocks, heads, len(PIECES), seg_len, piece_rows), BF),
            jax.ShapeDtypeStruct((blocks, heads, seg_len, seg_len), BF),
            jax.ShapeDtypeStruct((blocks, heads, seg_len, 1), F32),
        ],
        scratch_shapes=[
            pltpu.VMEM((len(PIECES), seg_len, piece_rows), F32),
            pltpu.VMEM((seg_len, LANES), F32),
            pltpu.VMEM((seg_len, LANES), F32),
            pltpu.VMEM((seg_len, HD), F32),
        ],
        compiler_params=pltpu.CompilerParams(vmem_limit_bytes=40 * 1024 * 1024),
        cost_estimate=SHORT,
        name="attention_forward",
    )(queries, keys, values, mask, other_mask, *key_pieces, *value_pieces)


def attention_backward_local(d_out, out_f32, queries, keys, values, inverse, p_local, cosine, sine):
    blocks, seg_len, width = queries.shape
    head, unused, unused, pl_spec, inv_spec = attention_specs(seg_len, seg_len)
    table = pl.BlockSpec((seg_len, HD), lambda h, r: (0, 0))
    return pl.pallas_call(
        backward_local_kernel,
        grid=(width // HD, blocks),
        in_specs=[head, head, head, head, head, inv_spec, pl_spec, table, table],
        out_specs=[pl.BlockSpec((2, 1, seg_len, HD), lambda h, r: (0, r, 0, h)), head],
        out_shape=[
            jax.ShapeDtypeStruct((2, blocks, seg_len, width), BF),
            jax.ShapeDtypeStruct(queries.shape, F32),
        ],
        compiler_params=pltpu.CompilerParams(vmem_limit_bytes=16 * 1024 * 1024),
        cost_estimate=SHORT,
        name="attention_backward_local",
    )(d_out, out_f32, queries, keys, values, inverse, p_local, cosine, sine)


def attention_backward(d_out, out_f32, dq_local, inverse, p_memory, cosine, sine, key_pieces, value_pieces):
    blocks, seg_len, width = d_out.shape
    heads = width // HD
    piece_rows = key_pieces[0].shape[1]
    head, piece, p_spec, unused, inv_spec = attention_specs(piece_rows, seg_len)
    table = pl.BlockSpec((seg_len, HD), lambda h, r: (0, 0))
    return pl.pallas_call(
        backward_kernel,
        grid=(heads, blocks),
        in_specs=[head, head, head, inv_spec, p_spec, table, table] + [piece] * (2 * N_GROUPS),
        out_specs=head,
        out_shape=jax.ShapeDtypeStruct((blocks, seg_len, width), BF),
        scratch_shapes=[pltpu.VMEM((seg_len, HD), F32)],
        compiler_params=pltpu.CompilerParams(vmem_limit_bytes=40 * 1024 * 1024),
        cost_estimate=SHORT,
        name="attention_backward",
    )(d_out, out_f32, dq_local, inverse, p_memory, cosine, sine, *key_pieces, *value_pieces)


def allow_local_of(live):
    seg_len = live.shape[-1]
    position = jnp.arange(seg_len, dtype=jnp.int32)
    same = position[None, :] == position[:, None]
    return same[None] | ((position[None, :] < position[:, None])[None] & (live == 1))


def split_heads(value):
    rows, seg_len, width = value.shape
    return value.reshape(rows, seg_len, width // HD, HD)


def stream_forward(queries, keys, values, live, allow, memory):
    scale = HD ** (-0.5)
    q4, k4, v4 = split_heads(queries), split_heads(keys), split_heads(values)
    scores = jnp.einsum("rqhd,rkhd->rhqk", q4, k4, preferred_element_type=F32) * scale
    scores = jnp.where(allow_local_of(live)[:, None], scores, NEG_BIG)
    row_max = jnp.max(scores, axis=-1)
    expo = jnp.exp(scores - row_max[..., None])
    state = (
        row_max,
        jnp.sum(expo, axis=-1),
        jnp.einsum("rhqk,rkhd->rhqd", expo.astype(BF), v4, preferred_element_type=F32),
    )

    def step(running, item):
        row_max, row_total, acc = running
        block, allowed = item
        k3 = block[0].reshape(block.shape[1], -1, HD)
        v3 = block[1].reshape(block.shape[1], -1, HD)
        scores = jnp.einsum("rqhd,khd->rhqk", q4, k3, preferred_element_type=F32) * scale
        scores = jnp.where(allowed[:, None] > 0, scores, NEG_BIG)
        new_max = jnp.maximum(row_max, jnp.max(scores, axis=-1))
        shrink = jnp.exp(row_max - new_max)
        expo = jnp.exp(scores - new_max[..., None])
        acc = acc * shrink[..., None] + jnp.einsum(
            "rhqk,khd->rhqd", expo.astype(BF), v3, preferred_element_type=F32
        )
        return (new_max, row_total * shrink + jnp.sum(expo, axis=-1), acc), None

    (row_max, row_total, acc), unused = lax.scan(step, state, (memory, allow))
    out = (acc / row_total[..., None]).transpose(0, 2, 1, 3).reshape(queries.shape)
    return out.astype(BF), out, row_max + jnp.log(row_total)


def stream_backward(d_out, out_f32, queries, keys, values, live, log_total, allow, memory, cosine, sine):
    scale = HD ** (-0.5)
    q4, k4, v4, d4 = split_heads(queries), split_heads(keys), split_heads(values), split_heads(d_out)
    delta = jnp.sum(d4.astype(F32) * split_heads(out_f32), axis=-1).transpose(0, 2, 1)
    scores = jnp.einsum("rqhd,rkhd->rhqk", q4, k4, preferred_element_type=F32) * scale
    scores = jnp.where(allow_local_of(live)[:, None], scores, NEG_BIG)
    chances = jnp.exp(scores - log_total[..., None])
    dp = jnp.einsum("rqhd,rkhd->rhqk", d4, v4, preferred_element_type=F32)
    ds = (chances * (dp - delta[..., None])).astype(BF)
    dq = jnp.einsum("rhqk,rkhd->rqhd", ds, k4, preferred_element_type=F32)
    dk = jnp.einsum("rhqk,rqhd->rkhd", ds, q4, preferred_element_type=F32)
    dv = jnp.einsum("rhqk,rqhd->rkhd", chances.astype(BF), d4, preferred_element_type=F32)

    def step(running, item):
        block, allowed = item
        k3 = block[0].reshape(block.shape[1], -1, HD)
        v3 = block[1].reshape(block.shape[1], -1, HD)
        scores = jnp.einsum("rqhd,khd->rhqk", q4, k3, preferred_element_type=F32) * scale
        scores = jnp.where(allowed[:, None] > 0, scores, NEG_BIG)
        chances = jnp.exp(scores - log_total[..., None])
        dp = jnp.einsum("rqhd,khd->rhqk", d4, v3, preferred_element_type=F32)
        ds = (chances * (dp - delta[..., None])).astype(BF)
        return running + jnp.einsum("rhqk,khd->rqhd", ds, k3, preferred_element_type=F32), None

    dq, unused = lax.scan(step, dq, (memory, allow))

    def back(value):
        turned = rope_heads(value.reshape((-1,) + value.shape[2:]), jnp.tile(cosine, (value.shape[0], 1)), -jnp.tile(sine, (value.shape[0], 1)))
        return (turned * scale).reshape(queries.shape).astype(BF)

    return jnp.stack([back(dq), back(dk), dv.reshape(queries.shape).astype(BF)])


def local(
    layer_input,
    live,
    knn_index,
    mem_keys,
    mem_values,
    gain_attn,
    w_query,
    w_key,
    w_value,
    w_out,
    gain_ffn,
    w_gate,
    w_up,
    w_down,
    cotangent,
):
    seg_len, width = layer_input.shape[1:]
    quarter = width // 4
    n_seg = lax.axis_size("seg")
    n_devices = n_seg * lax.axis_size("rep")
    tokens = seg_len * n_seg
    n_high = n_seg // 4
    x, low, high, y, core = place()
    use_kernel = n_high <= KERNEL_HIGH
    kv_rows = 2 * seg_len
    group_tokens = 4 * seg_len

    def by_quarter(value):
        return [value[:, i * quarter : (i + 1) * quarter] for i in range(4)]

    gains = jnp.concatenate(
        [gain_attn[:, None], gain_ffn[:, None], jnp.zeros((gain_attn.shape[0], LANES - 2), BF)], 1
    )
    stacked = [by_quarter(w) for w in (w_query, w_key, w_value, w_out)]
    qo = jnp.stack([jnp.concatenate([s[i] for s in stacked] + [gains], 1) for i in range(4)])

    def core_quarters(value, side):
        return jnp.stack([cut(value, side * quarter, quarter), cut(value, (2 + side) * quarter, quarter)])

    def core_memory(side):
        return jnp.stack([core_quarters(mem_keys[0], side), core_quarters(mem_values[0], side)])

    coded = two_rows(knn_index[0] * 2 + live[0][:, None])
    kv = ordered(core_memory(core), flip_core(core_memory(1 - core)), core, 2)
    qo = trade_core(qo)
    down_w = w_down[None, None, None, None]
    qo, kv, coded, w_gate_, w_up_ = fence(qo, kv, coded, w_gate, w_up)

    kv_near, kv_far = pick(kv, low, 1), flip_z(pick(kv, 1 - low, 1))
    pieces = ordered(kv_near[:, None], kv_far[:, None], low, 1)
    own_k, own_v = pieces[0], pieces[1]
    if use_kernel:
        qo = gather_z_four(qo)
    else:
        qo = gather_high(start_gather(trade_z(qo).reshape(2, -1, qo.shape[-1])))
    x_two = two_rows(layer_input[0])
    gate_up = split_units(w_gate_, w_up_, n_devices)

    def places_of(codes, row_core):
        picks = lax.shift_right_arithmetic(codes, 1)
        pair = picks >= tokens
        slot = jnp.where(pair, picks - tokens, picks)
        slot_seg = slot // seg_len
        kv_row = jnp.bitwise_xor(pair.astype(jnp.int32), row_core)
        return picks, slot_seg, kv_row * seg_len + (slot - slot_seg * seg_len)

    if use_kernel:
        picks, slot_seg, within = places_of(coded, core)
        slot_x, slot_low = slot_seg % 2, (slot_seg // 2) % 2
        same_x = slot_x == x
        in_group = jnp.where(same_x, 5, 4 + 2 * slot_low)
        before = jnp.where(same_x, 0, 2) + slot_low
        piece_no = jnp.where(slot_seg // 4 == high, in_group, before)
        columns = jnp.where(picks >= 0, piece_no * kv_rows + within, -1)
        live_two = jnp.bitwise_and(coded[:, :, 0], 1)[:, None, :]
        live_two = jnp.pad(live_two, ((0, 0), (0, 0), (0, cdiv(seg_len, LANES) * LANES - seg_len)))
        qo, own_k, own_v, x_two, gate_up, columns, down_w = fence(
            qo, own_k, own_v, x_two, gate_up, columns, down_w
        )
    else:
        qo, own_k, own_v, gate_up = fence(qo, own_k, own_v, gate_up)

    split = 3 * quarter
    x_all = all_blocks(x_two)
    down_w = gather_high(down_w)
    gate_up = gate_up.reshape(2, 2, 2, -1, gate_up.shape[-1])
    gate_up = ordered(pick(gate_up, core, 1), flip_core(pick(gate_up, 1 - core, 1)), core, 2)

    def trade_rows(value):
        near, far = pick(value, low, 0), flip_z(pick(value, 1 - low, 0))
        return ordered(near[:, None], far[:, None], low, 1)

    if use_kernel:
        mask = build_mask(columns, live_two, len(PIECES) * kv_rows // LANES)
        up_high = [(i, i + 4) for i in range(n_seg - 4)]

        def cross(value):
            return lax.ppermute(value, "seg", up_high)

        cross_k = cross(own_k)
        side_k = flip_x(own_k)
        qo_a, qo_b = gather_x(qo[..., :split]), gather_y(qo[..., split:])
        qo_a, qo_b, cross_k, side_k, own_v, x_all, gate_up, mask, down_w = fence(
            qo_a, qo_b, cross_k, side_k, own_v, x_all, gate_up, mask, down_w
        )
        cross_v = cross(own_v)
        cross_side_k = flip_x(cross_k)
        qo_a, qo_b = gather_y(qo_a), gather_x(qo_b)
        gate_up = trade_rows(gate_up)
        other_mask = flip_core(mask)
        qo_a, qo_b, cross_v, cross_side_k, own_v, gate_up, other_mask = fence(
            qo_a, qo_b, cross_v, cross_side_k, own_v, gate_up, other_mask
        )
        cross_side_v = flip_x(cross_v)
        side_v = flip_x(own_v)
        key_pieces = (cross_k, cross_side_k, side_k, own_k)
    else:
        qo_a, qo_b = gather_y(gather_x(qo[..., :split])), gather_x(gather_y(qo[..., split:]))
        gate_up = trade_rows(gate_up)
        coded = all_blocks(coded)
        row_core = jnp.bitwise_xor(core, jnp.arange(4, dtype=jnp.int32) % 2)[:, None, None]
        picks, slot_seg, within = places_of(coded, row_core)
        live_all = jnp.bitwise_and(coded[:, :, 0], 1)[:, None, :]
        columns = jnp.where(picks >= 0, slot_seg * kv_rows + within, n_seg * kv_rows)
        blocks_at = jnp.arange(4)[:, None, None]
        queries_at = jnp.arange(seg_len)[None, :, None]
        allow = jnp.zeros((4, seg_len, n_seg * kv_rows), BF).at[blocks_at, queries_at, columns].set(1.0, mode="drop")
        allow = allow.reshape(4, seg_len, n_seg, kv_rows).transpose(2, 0, 1, 3)
        memory = jnp.stack([own_k, own_v], 1)[None, :, None]
        memory = gather_x(gather_high(memory)).reshape(n_seg, 2, kv_rows, quarter)

    w_a, w_b = flat(qo_a), flat(qo_b)
    wo_near = w_b[:, :quarter]
    g_attn = w_b[:, quarter].astype(F32)
    g_ffn = w_b[:, quarter + 1].astype(F32)
    gate, upw = gather_high_pair(gate_up)

    cosine, sine = rope_tables(seg_len)
    queries, keys, values, h_one, inv_one = project(x_all, w_a, w_b, cosine, sine)
    h_one = h_one.reshape(group_tokens, width)
    inv_one = inv_one.reshape(group_tokens, 1)
    x_float = x_all.reshape(group_tokens, width).astype(F32)
    if use_kernel:
        queries, keys, values, cross_side_v, side_v, gate, upw, down_w, wo_near = fence(
            queries, keys, values, cross_side_v, side_v, gate, upw, down_w, wo_near
        )
        value_pieces = (cross_v, cross_side_v, side_v, own_v)
        out_low, out_f32, p_memory, p_local, inverse = attention_forward(
            queries, keys, values, mask, other_mask, key_pieces, value_pieces
        )
    else:
        out_low, out_f32, log_total = stream_forward(queries, keys, values, live_all, allow, memory)
    wo_far = flip_z(wo_near)
    gate, upw = gather_x(gate), gather_y(upw)
    down_w = gather_x(down_w)
    g_own = cotangent[0]
    out_low, wo_far, gate, upw, down_w, g_own = fence(out_low, wo_far, gate, upw, down_w, g_own)

    att_near = out_low.reshape(group_tokens, quarter)
    att_far = flip_z(att_near)
    gate, upw = gather_y(gate), gather_x(upw)
    wo = all_quarters(wo_near, wo_far, False)
    g_two = two_rows(g_own)
    att_near, att_far, gate, upw, down_w, wo, g_two = fence(att_near, att_far, gate, upw, down_w, wo, g_two)

    wg, wu = flat(gate), flat(upw)
    down_recv = flip_y(down_w)
    attended = all_quarters(att_near, att_far, True)
    x_one = x_float + matmul(attended, wo)
    h_two_f, inv_two = norm_forward(x_one, g_ffn)
    h_two = h_two_f.astype(BF)
    gate_out = matmul(h_two, wg)
    up_out = matmul(h_two, wu)
    sigma = jax.nn.sigmoid(gate_out)
    swish = gate_out * sigma
    hidden = (swish * up_out).astype(BF)
    grad_out = all_blocks(g_two).reshape(group_tokens, width)

    down_w, hidden = fence(down_w, hidden)
    wd = flat(ordered(down_w, down_recv, y, 3))
    d_hidden = matmul_cols(grad_out, wd)
    d_gate = (d_hidden * up_out * sigma * (1.0 + gate_out * (1.0 - sigma))).astype(BF)
    d_up = (d_hidden * swish).astype(BF)
    sums = core_sums(matmul_cols(d_gate, wg) + matmul_cols(d_up, wu))
    sums, hidden, h_two, d_gate, d_up, wd = fence(sums, hidden, h_two, d_gate, d_up, wd)

    far_sums = flip_z(sums)
    keep_wg, give_wg = gradient(h_two, [d_gate], by_x)
    keep_wu, give_wu = gradient(h_two, [d_up], by_y)
    down_keep, down_give = core_parts(matmul(hidden, wd))
    sums, keep_wg, give_wg, keep_wu, give_wu, down_keep, down_give = fence(
        sums, keep_wg, give_wg, keep_wu, give_wu, down_keep, down_give
    )
    summed = add_low(sums, far_sums)
    recv_wg, recv_wu = flip_x(give_wg), flip_y(give_wu)
    down_recv = flip_core(down_give)

    own = 2 * low * seg_len
    d_h_two = both_cores(summed).reshape(group_tokens, width)
    d_x_norm, unused = norm_backward(x_one, inv_two, g_ffn, d_h_two)
    d_x_one = grad_out.astype(F32) + d_x_norm
    d_branch = d_x_one.astype(BF)
    at_quarter = (2 * low + core) * quarter
    d_att = matmul_cols(d_branch, cut(wo, at_quarter, quarter, 0)).astype(BF).reshape(4, seg_len, quarter)

    keep_wg, keep_wu, down_keep, d_att, d_branch = fence(keep_wg, keep_wu, down_keep, d_att, d_branch)
    keep_wg, give_wg = halves(plane_shape(add_low(keep_wg, recv_wg), 2), 2, y)
    keep_wu, give_wu = halves(plane_shape(add_low(keep_wu, recv_wu), 2), 2, x)
    down_keep = add_low(down_keep, down_recv)
    down_give = pick(down_keep, 1 - low, 0)
    down_keep = pick(down_keep, low, 0)

    d_att, give_wg, give_wu, down_give = fence(d_att, give_wg, give_wu, down_give)
    recv_wg, recv_wu = flip_y(give_wg), flip_x(give_wu)
    down_recv = flip_z(down_give)
    if use_kernel:
        d_kv, dq_local = attention_backward_local(
            d_att, out_f32, queries, keys, values, inverse, p_local, cosine, sine
        )
        dq_local, d_kv, hidden, attended = fence(dq_local, d_kv, hidden, attended)
    else:
        d_qkv = stream_backward(
            d_att, out_f32, queries, keys, values, live_all, log_total, allow, memory, cosine, sine
        )
        d_kv, d_q = d_qkv[1:], d_qkv[0]
    d_kv = d_kv.reshape(2, group_tokens, quarter)
    keep_wd, give_wd = gradient_units(hidden, grad_out)
    keep_kv, give_kv = gradient(h_one, [d_kv[0], d_kv[1]], by_y)
    keep_wo, give_wo = gradient(attended, [d_branch], by_x, quarter)
    keep_wg, keep_wu, give_wd, give_kv, give_wo = fence(keep_wg, keep_wu, give_wd, give_kv, give_wo)
    recv_wd, recv_kv, recv_wo = flip_x(give_wd), flip_y(give_kv), flip_x(give_wo)
    plane_gu = jnp.concatenate([add_low(keep_wg, recv_wg), add_low(keep_wu, recv_wu)], -2)
    if use_kernel:
        gu_parts = z_parts(plane_gu)
        gu_parts, d_att = fence(gu_parts, d_att)
        gu_flips = z_flips(gu_parts)
        d_q = attention_backward(
            d_att, out_f32, dq_local, inverse, p_memory, cosine, sine, key_pieces, value_pieces
        )
        gu_kept, d_q, keep_kv, keep_wo, keep_wd, down_keep = fence(
            gu_parts[0], d_q, keep_kv, keep_wo, keep_wd, down_keep
        )

    d_q = d_q.reshape(group_tokens, quarter)
    parts_q = gradient(h_one, [d_q], by_both)
    keep_q, give_q = parts_q[0], tuple(parts_q[1:])
    give_q, d_q, keep_kv, keep_wo, keep_wd = fence(give_q, d_q, keep_kv, keep_wo, keep_wd)
    recv_q = plane_flips(give_q)
    keep_kv, give_kv = halves(plane_shape(add_low(keep_kv, recv_kv), 2), 2, x)
    keep_wo, give_wo = halves(plane_shape(add_low(keep_wo, recv_wo), 2), 2, y)
    keep_wd, give_wd = halves(plane_shape(add_low(keep_wd, recv_wd), 1), 2, y)
    d_h_part = (
        matmul_cols(d_q, w_a[:, :quarter])
        + matmul_cols(d_kv[0], w_a[:, quarter : 2 * quarter])
        + matmul_cols(d_kv[1], w_a[:, 2 * quarter :])
    )
    d_h_keep, d_h_give = core_parts(d_h_part)
    keep_q, keep_kv, keep_wo, give_kv, give_wo, give_wd, d_h_give = fence(
        keep_q, keep_kv, keep_wo, give_kv, give_wo, give_wd, d_h_give
    )
    recv_kv, recv_wo, recv_wd = flip_x(give_kv), flip_y(give_wo), flip_y(give_wd)
    d_h_recv = flip_core(d_h_give)
    plane_q = add_all(keep_q, *recv_q).reshape(n_high, 2, -1, quarter)
    z_gu = z_total(gu_kept, gu_flips) if use_kernel else z_plain(plane_gu)
    gu_rows = z_gu.shape[1] // 2
    four_wg = reduce_core(z_gu[:, :gu_rows])
    four_wu = reduce_core(z_gu[:, gu_rows:])
    plane_qkvo = jnp.concatenate([plane_q, add_low(keep_kv, recv_kv), add_low(keep_wo, recv_wo)], -1)
    if use_kernel:
        all_parts = z_parts(plane_qkvo)
        all_parts, keep_wd, d_h_keep, four_wg, four_wu, down_keep = fence(
            all_parts, keep_wd, d_h_keep, four_wg, four_wu, down_keep
        )
        all_flips = z_flips(all_parts)
    d_h_one = own_sums(add_low(d_h_keep, d_h_recv))
    sum_wd = reduce_high(add_low(keep_wd, recv_wd))[0].astype(F32)
    sum_wg = join_units(four_wg, n_devices)
    sum_wu = join_units(four_wu, n_devices)
    down = down_keep.astype(F32) + down_recv.astype(F32)
    layer_output = (cut(x_one, own, seg_len, 0) + down).astype(BF)
    if use_kernel:
        kept, sum_wg, sum_wu, layer_output = fence(all_parts[0], sum_wg, sum_wu, layer_output)
        z_qkvo = z_total(kept, all_flips)
    else:
        z_qkvo = z_plain(plane_qkvo)
    sums = reduce_core(z_qkvo).astype(F32)
    x_own = cut(x_float, own, seg_len, 0)
    d_x_first, unused = norm_backward(x_own, cut(inv_one, own, seg_len, 0), g_attn, d_h_one)
    grad_x = (cut(d_x_one, own, seg_len, 0) + d_x_first).astype(BF)
    sum_q, sum_k, sum_v, sum_o = [
        jnp.concatenate([sums[i][:, at * quarter : (at + 1) * quarter] for i in range(4)], 1) for at in range(4)
    ]

    def gain_gradient(gain, *pairs):
        return sum(jnp.sum(w.astype(F32) * g, axis=1) for w, g in pairs) / gain.astype(F32)

    grad_g_attn = gain_gradient(gain_attn, (w_query, sum_q), (w_key, sum_k), (w_value, sum_v))
    grad_g_ffn = gain_gradient(gain_ffn, (w_gate, sum_wg), (w_up, sum_wu))
    return (
        layer_output[None],
        grad_x[None],
        grad_g_attn,
        sum_q,
        sum_k,
        sum_v,
        sum_o,
        grad_g_ffn,
        sum_wg,
        sum_wu,
        sum_wd,
    )


def solution(mesh):
    tokens = P("rep", "seg", None)
    vector = P(("seg", "rep"))
    matrix = P(("seg", "rep"), None)
    return jax.shard_map(
        local,
        mesh=mesh,
        in_specs=(
            tokens,
            P("rep", "seg"),
            tokens,
            tokens,
            tokens,
            vector,
            matrix,
            matrix,
            matrix,
            matrix,
            vector,
            matrix,
            matrix,
            matrix,
            tokens,
        ),
        out_specs=(tokens, tokens, vector, matrix, matrix, matrix, matrix, vector, matrix, matrix, matrix),
        check_vma=False,
    )
```

```python
import jax
import jax.numpy as jnp
from jax import lax
from jax.experimental import pallas as pl
from jax.experimental.pallas import tpu as pltpu
from jax.sharding import PartitionSpec as P

H = 8
HD = 128
EPSILON = 1e-05
NEG_BIG = -1e30
POS_BIG = 1e30
ROPE_BASE = 10000.0
LANES = 128
KERNEL_HIGH = 2
VMEM_BYTES = 44 * 1024 * 1024

SHORT = pl.CostEstimate(flops=1000, bytes_accessed=1000, transcendentals=0)

BF = jnp.bfloat16
F32 = jnp.float32


def cdiv(a, b):
    return -(-a // b)


def flip(value, axis, bit):
    count = lax.axis_size(axis)
    return lax.ppermute(value, axis, [(i, i ^ bit) for i in range(count)])


def flip_core(value):
    return flip(value, "rep", 1)


def flip_y(value):
    return flip(value, "rep", 2)


def flip_x(value):
    return flip(value, "seg", 1)


def flip_z(value):
    return flip(value, "seg", 2)


def ordered(mine, other, bit, axis):
    first = jnp.where(bit == 0, mine, other)
    second = jnp.where(bit == 0, other, mine)
    return jnp.concatenate([first, second], axis)


def pick(value, index, axis):
    return lax.dynamic_index_in_dim(value, index, axis, keepdims=False)


def cut(value, start, size, axis=-1):
    return lax.dynamic_slice_in_dim(value, start, size, axis % value.ndim)


def fence(*values):
    return lax.optimization_barrier(values)


def place():
    seg = lax.axis_index("seg")
    rep = lax.axis_index("rep")
    return seg % 2, (seg // 2) % 2, seg // 4, rep // 2, rep % 2


def high_bits():
    bit = 4
    out = []
    while bit < lax.axis_size("seg"):
        out.append(bit)
        bit *= 2
    return out


def gather_high(cur):
    seg = lax.axis_index("seg")
    for bit in high_bits():
        cur = ordered(cur, flip(cur, "seg", bit), (seg // bit) % 2, 0)
    return cur


def gather_x(cur):
    return ordered(cur, flip_x(cur), place()[0], 2)


def gather_y(cur):
    return ordered(cur, flip_y(cur), place()[3], 3)


def gather_high_pair(cur):
    seg = lax.axis_index("seg")
    cur = cur[:, None]
    bits = high_bits()
    for bit in bits[:-1]:
        cur = ordered(cur, flip(cur, "seg", bit), (seg // bit) % 2, 1)
    recv = flip(cur, "seg", bits[-1])
    side = (seg // bits[-1]) % 2
    return [ordered(cur[i], recv[i], side, 0)[:, :, None, None] for i in range(2)]


def flat(cur):
    return cur.reshape(-1, cur.shape[-1])


def halve(value, axis_name, bit, side, axis):
    recv = flip(pick(value, 1 - side, axis), axis_name, bit)
    kept = pick(value, side, axis)
    return (kept.astype(F32) + recv.astype(F32)).astype(BF)


def plane_shape(value, low):
    high = lax.axis_size("seg") // 4
    return value.reshape(high, low, 2, -1, value.shape[-1])


def halves(cur, axis, side):
    return pick(cur, side, axis), pick(cur, 1 - side, axis)


def plane_flips(parts):
    n_rep = lax.axis_size("rep")
    count = lax.axis_size("seg") * n_rep
    far = [(i, i ^ n_rep ^ 2) for i in range(count)]
    return flip_x(parts[0]), flip_y(parts[1]), lax.ppermute(parts[2], ("seg", "rep"), far)


def add_all(first, *others):
    total = first.astype(F32)
    for other in others:
        total = total + other.astype(F32)
    return total.astype(BF)


def z_flips(parts):
    return flip_z(parts[1]), flip(parts[2], "seg", 4), flip(parts[3], "seg", 6)


def z_plain(cur):
    low = place()[1]
    sums = reduce_high(cur)
    return ordered(pick(sums, low, 0)[None], flip_z(pick(sums, 1 - low, 0))[None], low, 0)


def reduce_high(cur):
    seg = lax.axis_index("seg")
    for bit in reversed(high_bits()):
        cur = cur.reshape((2, cur.shape[0] // 2) + cur.shape[1:])
        cur = halve(cur, "seg", bit, (seg // bit) % 2, 0)
    return cur[0]


def trade_core(quarters):
    core = place()[4]
    low, unused, rows, cols = 2, 2, quarters.shape[1], quarters.shape[2]
    four = quarters.reshape(2, 2, rows, cols)
    return ordered(pick(four, core, 1), flip_core(pick(four, 1 - core, 1)), core, 1)


def trade_z(halves):
    low = place()[1]
    return ordered(pick(halves, low, 0)[None], flip_z(pick(halves, 1 - low, 0))[None], low, 0)


def gather_z_four(halves):
    seg = lax.axis_index("seg")
    low = (seg // 2) % 2
    keep, give = pick(halves, low, 0)[None, None], pick(halves, 1 - low, 0)[None, None]
    near = ordered(keep, flip(give, "seg", 2), low, 1)
    far = ordered(flip(keep, "seg", 4), flip(give, "seg", 6), low, 1)
    return ordered(near, far, (seg // 4) % 2, 0)[:, :, None, None]


def start_gather(traded):
    return traded[None, :, None, None]


def core_halves(mine):
    core = place()[4]
    four = mine.reshape(2, 2, mine.shape[1] // 2, mine.shape[2])
    return halves(four, 1, core)


def swap_pairs(value):
    blocks = value.reshape((value.shape[0], 2, 2, value.shape[1] // 4) + value.shape[2:])
    return jnp.stack([blocks[:, :, 1], blocks[:, :, 0]], 2).reshape(value.shape)


def all_quarters(mine, other):
    unused, low, unused, unused, core = place()
    near_half = ordered(mine[0], other[0], core, 1)
    far_half = ordered(mine[1], other[1], core, 1)
    return ordered(near_half, far_half, low, 1)


def all_blocks(by_low):
    both = jnp.stack([by_low, flip_core(by_low)], 1)
    return both.reshape((-1,) + by_low.shape[1:])


def two_rows(value):
    return ordered(value[None], flip_z(value)[None], place()[1], 0)


def core_parts(part):
    blocks = part.reshape((2, 2, part.shape[0] // 4) + part.shape[1:])
    return blocks[:, 0].astype(BF), blocks[:, 1].astype(BF)


def core_sums(part):
    blocks = part.reshape((2, 2, part.shape[0] // 4) + part.shape[1:])
    return (blocks[:, 0] + flip_core(blocks[:, 1].astype(BF)).astype(F32)).astype(BF)


def own_sums(sums):
    low = place()[1]
    return pick(sums, low, 0).astype(F32) + flip_z(pick(sums, 1 - low, 0)).astype(F32)


def z_sums(sums):
    return (sums.astype(F32) + flip_z(sums).astype(F32)).astype(BF)


def both_cores(sums):
    return jnp.stack([sums, flip_core(sums)], 1).astype(F32)


def unit_blocks(n_blocks):
    order = []
    for block in range(n_blocks):
        high, low, rest, core = block // 16, (block // 8) % 2, (block // 2) % 4, block % 2
        order.append((low * 2 + core, high * 4 + rest))
    return order


def split_units(one, two, n_blocks):
    rows, total = one.shape
    size = total // n_blocks

    def body(one_ref, two_ref, out_ref):
        for half, in_ref in enumerate((one_ref, two_ref)):
            for block, (quarter, at) in enumerate(unit_blocks(n_blocks)):
                out_ref[quarter, half * rows : (half + 1) * rows, at * size : (at + 1) * size] = in_ref[
                    :, block * size : (block + 1) * size
                ]

    return pl.pallas_call(
        body,
        out_shape=jax.ShapeDtypeStruct((4, 2 * rows, total // 4), one.dtype),
        cost_estimate=SHORT,
        name="split_units",
    )(one, two)


def matmul(left, right):
    return jnp.dot(left, right, preferred_element_type=F32)


def matmul_rows(left, right):
    return lax.dot_general(left, right, (((0,), (0,)), ((), ())), preferred_element_type=F32)


def matmul_cols(left, right):
    return lax.dot_general(left, right, (((1,), (1,)), ((), ())), preferred_element_type=F32)


def norm_forward(values, gain):
    inverse = lax.rsqrt(jnp.mean(values * values, axis=-1, keepdims=True) + EPSILON)
    return (values * inverse * gain, inverse)


def norm_backward(values, inverse, gain, grad_out):
    normed = values * inverse
    scaled = grad_out * gain
    grad_values = inverse * (scaled - normed * jnp.mean(scaled * normed, axis=-1, keepdims=True))
    return (grad_values, normed)


def rope_tables(seg_len):
    position = jnp.arange(seg_len).astype(F32)
    freqs = ROPE_BASE ** (-(2.0 * jnp.arange(HD // 2).astype(F32)) / HD)
    angle = position[:, None] * freqs[None, :]
    cosine, sine = jnp.cos(angle), jnp.sin(angle)
    return (jnp.concatenate([cosine, cosine], -1), jnp.concatenate([-sine, sine], -1))


def rope_heads(values, cosine, sine):
    half = HD // 2
    swapped = jnp.concatenate([values[..., half:], values[..., :half]], -1)
    return values * cosine[:, None, :] + swapped * sine[:, None, :]


def mask_kernel(n_cols, cols_ref, live_ref, out_ref, scratch):
    queries = cols_ref.shape[1]
    picks = cols_ref[0]
    pad = scratch.shape[0]
    high = lax.shift_right_arithmetic(picks, 7)
    low = jnp.bitwise_and(picks, LANES - 1)
    iota_high = lax.broadcasted_iota(jnp.int32, (pad, picks.shape[1]), 0)
    iota_low = lax.broadcasted_iota(jnp.int32, (LANES, picks.shape[1]), 0)
    for i in range(queries):
        hot_high = jnp.where(iota_high == high[i : i + 1, :], 1.0, 0.0).astype(BF)
        hot_low = jnp.where(iota_low == low[i : i + 1, :], 1.0, 0.0).astype(BF)
        scratch[:, i, :] = matmul_cols(hot_high, hot_low)
    out_ref[0, 0:n_cols] = jnp.where(scratch[0:n_cols] > 0.5, POS_BIG, NEG_BIG).astype(BF)
    row = lax.broadcasted_iota(jnp.int32, (queries, LANES), 0) + pl.program_id(1) * queries
    for part in range(out_ref.shape[1] - n_cols):
        col = lax.broadcasted_iota(jnp.int32, (queries, LANES), 1) + part * LANES
        live = live_ref[0, :, part * LANES : (part + 1) * LANES]
        allow = (col == row) | ((col < row) & (live == 1))
        out_ref[0, n_cols + part] = jnp.where(allow, POS_BIG, NEG_BIG).astype(BF)


def build_mask(columns, live, n_cols):
    rows, queries, picks = columns.shape
    block = 16
    pad = cdiv(n_cols, 8) * 8
    n_local = live.shape[2] // LANES
    return pl.pallas_call(
        lambda *refs: mask_kernel(n_cols, *refs),
        grid=(rows, queries // block),
        in_specs=[
            pl.BlockSpec((1, block, picks), lambda r, g: (r, g, 0)),
            pl.BlockSpec((1, 1, live.shape[2]), lambda r, g: (r, 0, 0)),
        ],
        out_specs=pl.BlockSpec((1, n_cols + n_local, block, LANES), lambda r, g: (r, 0, g, 0)),
        out_shape=jax.ShapeDtypeStruct((rows, n_cols + n_local, queries, LANES), BF),
        scratch_shapes=[pltpu.VMEM((pad, block, LANES), F32)],
        compiler_params=pltpu.CompilerParams(vmem_limit_bytes=VMEM_BYTES),
        cost_estimate=pl.CostEstimate(flops=12000000000, bytes_accessed=3000000, transcendentals=0),
        name="mask_build",
    )(columns, live)


def project_kernel(x_ref, wa_ref, wb_ref, cos_ref, sin_ref, q_ref, k_ref, v_ref, h_ref, inv_ref, gain_ref):
    quarter = q_ref.shape[2]

    @pl.when(pl.program_id(0) == 0)
    def gains():
        gain_ref[...] = jnp.transpose(wb_ref[:, quarter:].astype(F32), (1, 0))[0:8]

    x = x_ref[0].astype(F32)
    inverse = lax.rsqrt(jnp.mean(x * x, axis=-1, keepdims=True) + EPSILON)
    h = (x * inverse * gain_ref[0:1, :]).astype(BF)
    h_ref[0] = h
    inv_ref[0] = inverse
    turned = matmul(h, wa_ref[:, : 2 * quarter])
    for head in range(2 * quarter // HD):
        value = turned[:, head * HD : (head + 1) * HD]
        value = (value * cos_ref[...] + pltpu.roll(value, HD // 2, 1) * sin_ref[...]).astype(BF)
        if head < quarter // HD:
            q_ref[0, :, head * HD : (head + 1) * HD] = value
        else:
            at = head * HD - quarter
            k_ref[0, :, at : at + HD] = value
    v_ref[0] = matmul(h, wa_ref[:, 2 * quarter :]).astype(BF)


def project(x_all, w_a, w_b, cosine, sine):
    blocks, seg_len, width = x_all.shape
    quarter = w_a.shape[1] // 3
    whole = lambda array: pl.BlockSpec(array.shape, lambda r: (0, 0))
    head = pl.BlockSpec((1, seg_len, quarter), lambda r: (r, 0, 0))
    full = pl.BlockSpec((1, seg_len, width), lambda r: (r, 0, 0))
    out = jax.ShapeDtypeStruct((blocks, seg_len, quarter), BF)
    return pl.pallas_call(
        project_kernel,
        grid=(blocks,),
        in_specs=[full, whole(w_a), whole(w_b), whole(cosine), whole(sine)],
        out_specs=[head, head, head, full, pl.BlockSpec((1, seg_len, 1), lambda r: (r, 0, 0))],
        out_shape=[out, out, out, jax.ShapeDtypeStruct(x_all.shape, BF), jax.ShapeDtypeStruct((blocks, seg_len, 1), F32)],
        scratch_shapes=[pltpu.VMEM((8, width), F32)],
        compiler_params=pltpu.CompilerParams(vmem_limit_bytes=VMEM_BYTES),
        cost_estimate=SHORT,
        name="project",
    )(x_all, w_a, w_b, cosine, sine)


def plane_place():
    x, low, unused, y, core = place()
    return jnp.stack([x, y, 2 * low + core]).astype(jnp.int32)


def gradient(*entries):
    tokens, width = entries[0][0].shape
    n_blocks = lax.axis_size("seg")
    rows = width // n_blocks
    half = rows // 2
    sizes = [[entry[3] or right.shape[1] for right in entry[1]] for entry in entries]
    if rows % LANES:
        x, unused, unused, y, unused = place()
        outs = []
        for left, rights, way, columns in entries:
            if columns:
                rights = [cut(right, plane_place()[2] * columns, columns) for right in rights]
            full = jnp.concatenate([matmul_rows(left, right).astype(BF) for right in rights], 1)
            full = full.reshape(-1, 2, 2, half, full.shape[1])
            if way == "xy":
                near, side = halves(full, 1, x)
                near, side = halves(near, 1, y), halves(side, 1, y)
                parts = [near[0], side[0], near[1], side[1]]
            else:
                parts = halves(full, 1, x) if way == "x" else halves(full, 2, y)
            outs.append([part.reshape(-1, half, part.shape[-1]) for part in parts])
        return outs
    lefts = []
    for entry in entries:
        if not any(entry[0] is left for left in lefts):
            lefts.append(entry[0])
    which = [[entry[0] is left for left in lefts].index(True) for entry in entries]
    counts = [4 if entry[2] == "xy" else 2 for entry in entries]
    shapes = []
    for entry, size, count in zip(entries, sizes, counts):
        blocks = n_blocks // 2 if entry[2] == "xy" else n_blocks
        shapes += [(blocks, half, sum(size))] * count
    n_rights = sum(len(size) for size in sizes)

    def body(at_ref, *refs):
        left_refs, right_refs = refs[: len(lefts)], list(refs[len(lefts) : len(lefts) + n_rights])
        out_refs = list(refs[len(lefts) + n_rights :])
        block = pl.program_id(0)
        same_x = block % 2 == at_ref[0]
        for entry, i, size, count in zip(entries, which, sizes, counts):
            outs, out_refs = out_refs[:count], out_refs[count:]
            start = 0
            for width_here in size:
                product = matmul_rows(left_refs[i][...], right_refs.pop(0)[...]).astype(BF)
                upper, lower = product[:half], product[half:]
                near = jnp.where(at_ref[1] == 0, upper, lower)
                far = jnp.where(at_ref[1] == 0, lower, upper)
                span = slice(start, start + width_here)
                start += width_here
                if entry[2] == "y":
                    outs[0][block, :, span] = near
                    outs[1][block, :, span] = far
                    continue
                for mine in (True, False):

                    @pl.when(same_x if mine else jnp.logical_not(same_x))
                    def write(mine=mine, upper=upper, lower=lower, near=near, far=far, span=span, outs=outs):
                        if entry[2] == "x":
                            ref = outs[0] if mine else outs[1]
                            ref[block // 2 * 2, :, span] = upper
                            ref[block // 2 * 2 + 1, :, span] = lower
                        else:
                            (outs[0] if mine else outs[1])[block // 2, :, span] = near
                            (outs[2] if mine else outs[3])[block // 2, :, span] = far

    in_specs = [pl.BlockSpec((tokens, rows), lambda i, at: (0, i))] * len(lefts)
    for entry, size in zip(entries, sizes):
        column = (lambda i, at: (0, at[2])) if entry[3] else (lambda i, at: (0, 0))
        in_specs += [pl.BlockSpec((tokens, width_here), column) for width_here in size]
    outs = pl.pallas_call(
        body,
        grid_spec=pltpu.PrefetchScalarGridSpec(
            num_scalar_prefetch=1,
            grid=(n_blocks,),
            in_specs=in_specs,
            out_specs=[pl.BlockSpec(shape, lambda i, at: (0, 0, 0)) for shape in shapes],
        ),
        out_shape=[jax.ShapeDtypeStruct(shape, BF) for shape in shapes],
        compiler_params=pltpu.CompilerParams(vmem_limit_bytes=VMEM_BYTES),
        cost_estimate=SHORT,
        name="gradient",
    )(plane_place(), *lefts, *[right for entry in entries for right in entry[1]])
    groups = []
    for count in counts:
        groups.append(outs[:count])
        outs = outs[count:]
    return groups


def split_sums(keep, recv, way):
    n_blocks, rows, cols = keep.shape

    def body(at_ref, keep_ref, recv_ref, mine_ref, give_ref):
        side = at_ref[1] if way == "y" else at_ref[0]
        for block in range(n_blocks // 2):
            for at, out_ref in ((2 * block + side, mine_ref), (2 * block + 1 - side, give_ref)):
                out_ref[block] = (keep_ref[at].astype(F32) + recv_ref[at].astype(F32)).astype(BF)

    vmem = pl.BlockSpec(memory_space=pltpu.VMEM)
    return pl.pallas_call(
        body,
        in_specs=[pl.BlockSpec(memory_space=pltpu.SMEM)] + [vmem] * 2,
        out_specs=[vmem] * 2,
        out_shape=[jax.ShapeDtypeStruct((n_blocks // 2, rows, cols), BF)] * 2,
        compiler_params=pltpu.CompilerParams(vmem_limit_bytes=VMEM_BYTES),
        cost_estimate=SHORT,
        name="split_sums",
    )(plane_place(), keep, recv)


def gradient_units(left, right):
    tokens, width = left.shape
    n_high = lax.axis_size("seg") // 4
    rows = width // (4 * n_high)
    cols = right.shape[1]
    step = 256
    if rows % 8:
        full = matmul_rows(left, right).astype(BF).reshape(-1, 2, 2, rows, cols)
        return halves(full, 1, place()[0])

    def body(at_ref, left_ref, right_ref, keep_ref, give_ref):
        product = matmul_rows(left_ref[...], right_ref[...])
        for high in range(n_high):
            for y in range(2):
                zero, one = [
                    product[(high * 4 + x * 2 + y) * rows : (high * 4 + x * 2 + y + 1) * rows] for x in range(2)
                ]
                keep_ref[high, y] = jnp.where(at_ref[0] == 0, zero, one).astype(BF)
                give_ref[high, y] = jnp.where(at_ref[0] == 0, one, zero).astype(BF)

    shape = (n_high, 2, rows, cols)
    return pl.pallas_call(
        body,
        grid_spec=pltpu.PrefetchScalarGridSpec(
            num_scalar_prefetch=1,
            grid=(cols // step,),
            in_specs=[
                pl.BlockSpec((tokens, width), lambda i, at: (0, 0)),
                pl.BlockSpec((tokens, step), lambda i, at: (0, i)),
            ],
            out_specs=[pl.BlockSpec((n_high, 2, rows, step), lambda i, at: (0, 0, 0, i))] * 2,
        ),
        out_shape=[jax.ShapeDtypeStruct(shape, BF)] * 2,
        compiler_params=pltpu.CompilerParams(vmem_limit_bytes=VMEM_BYTES),
        cost_estimate=SHORT,
        name="gradient_units",
    )(plane_place(), left, right)


def group_place():
    unused, low, high, unused, core = place()
    return jnp.stack([2 * high + low, low, core]).astype(jnp.int32)


def plane_sort(*groups):
    sizes = [group[0].shape[-1] for group in groups]
    shape = (groups[0][0].shape[1], sum(sizes))

    def body(at_ref, *refs):
        out_refs = refs[-4:]
        for way in range(4):
            start = 0
            left = list(refs[:-4])
            for size, group in zip(sizes, groups):
                total = None
                for unused in group:
                    part = left.pop(0)[at_ref[0] ^ way].astype(F32)
                    total = part if total is None else total + part
                out_refs[way][:, start : start + size] = total.astype(BF)
                start += size

    vmem = pl.BlockSpec(memory_space=pltpu.VMEM)
    return pl.pallas_call(
        body,
        in_specs=[pl.BlockSpec(memory_space=pltpu.SMEM)] + [vmem] * sum(len(group) for group in groups),
        out_specs=[vmem] * 4,
        out_shape=[jax.ShapeDtypeStruct(shape, BF)] * 4,
        compiler_params=pltpu.CompilerParams(vmem_limit_bytes=VMEM_BYTES),
        cost_estimate=SHORT,
        name="plane_sort",
    )(group_place(), *[array for group in groups for array in group])


def z_merge(kept, from_1, from_2, from_3):
    rows, cols = kept.shape
    half = rows // 2

    def body(at_ref, kept_ref, one_ref, two_ref, three_ref, keep_ref, give_ref):
        same = kept_ref[...].astype(F32) + two_ref[...].astype(F32)
        other = one_ref[...].astype(F32) + three_ref[...].astype(F32)
        for quarter, value in ((at_ref[1], same), (1 - at_ref[1], other)):
            upper, lower = value[:half], value[half:]
            keep_ref[quarter] = jnp.where(at_ref[2] == 0, upper, lower).astype(BF)
            give_ref[quarter] = jnp.where(at_ref[2] == 0, lower, upper).astype(BF)

    vmem = pl.BlockSpec(memory_space=pltpu.VMEM)
    return pl.pallas_call(
        body,
        in_specs=[pl.BlockSpec(memory_space=pltpu.SMEM)] + [vmem] * 4,
        out_specs=[vmem] * 2,
        out_shape=[jax.ShapeDtypeStruct((2, half, cols), BF)] * 2,
        compiler_params=pltpu.CompilerParams(vmem_limit_bytes=VMEM_BYTES),
        cost_estimate=SHORT,
        name="z_merge",
    )(group_place(), kept, from_1, from_2, from_3)


def join_quarters(mine, recv, core_ref, start, size, z_low, core):
    return jnp.where(
        core_ref[2] == core, mine[z_low, :, start : start + size], recv[z_low, :, start : start + size]
    ).astype(F32)


def join_columns(mine, recv, weights, gain, n_matrices):
    rows, cols = mine.shape[1:]
    size = cols // n_matrices

    def body(at_ref, mine_ref, recv_ref, gain_ref, *refs):
        weight_refs, out_refs = refs[: len(weights)], refs[len(weights) :]
        total = jnp.zeros((rows, 1), F32)
        for i in range(n_matrices):
            for z_low in range(2):
                for core in range(2):
                    at = (2 * z_low + core) * size
                    value = join_quarters(mine_ref, recv_ref, at_ref, i * size, size, z_low, core)
                    out_refs[i][:, at : at + size] = value
                    if i < len(weights):
                        product = value * weight_refs[i][:, at : at + size].astype(F32)
                        total = total + jnp.sum(product, axis=1, keepdims=True)
        out_refs[-1][...] = total / gain_ref[...]

    vmem = pl.BlockSpec(memory_space=pltpu.VMEM)
    outs = pl.pallas_call(
        body,
        in_specs=[pl.BlockSpec(memory_space=pltpu.SMEM)] + [vmem] * (3 + len(weights)),
        out_specs=[vmem] * (n_matrices + 1),
        out_shape=[jax.ShapeDtypeStruct((rows, 4 * size), F32)] * n_matrices + [jax.ShapeDtypeStruct((rows, 1), F32)],
        cost_estimate=SHORT,
        name="join_columns",
    )(group_place(), mine, recv, gain.astype(F32)[:, None], *weights)
    return outs[:-1] + [outs[-1][:, 0]] if isinstance(outs, list) else list(outs[:-1]) + [outs[-1][:, 0]]


def join_units(mine, recv, weights, gain, n_blocks):
    rows, both = mine.shape[1:]
    quarter_size = both // 2
    size = 4 * quarter_size // n_blocks

    def body(at_ref, mine_ref, recv_ref, gain_ref, one_weight, two_weight, one_ref, two_ref, total_ref):
        total = jnp.zeros((rows, 1), F32)
        for half, (out_ref, weight_ref) in enumerate(((one_ref, one_weight), (two_ref, two_weight))):
            for block, (quarter, at) in enumerate(unit_blocks(n_blocks)):
                start = half * quarter_size + at * size
                out_ref[:, block * size : (block + 1) * size] = join_quarters(
                    mine_ref, recv_ref, at_ref, start, size, quarter // 2, quarter % 2
                )
            total = total + jnp.sum(out_ref[...] * weight_ref[...].astype(F32), axis=1, keepdims=True)
        total_ref[...] = total / gain_ref[...]

    vmem = pl.BlockSpec(memory_space=pltpu.VMEM)
    one, two, total = pl.pallas_call(
        body,
        in_specs=[pl.BlockSpec(memory_space=pltpu.SMEM)] + [vmem] * 5,
        out_specs=[vmem] * 3,
        out_shape=[jax.ShapeDtypeStruct((rows, 4 * quarter_size), F32)] * 2 + [jax.ShapeDtypeStruct((rows, 1), F32)],
        cost_estimate=SHORT,
        name="join_units",
    )(group_place(), mine, recv, gain.astype(F32)[:, None], *weights)
    return one, two, total[:, 0]


def pair_add(one, two):
    def body(at_ref, one_ref, two_ref, own_ref, give_ref):
        for way, out_ref in enumerate((own_ref, give_ref)):
            at = at_ref[1] ^ way
            out_ref[...] = (one_ref[at].astype(F32) + two_ref[at].astype(F32)).astype(BF)

    vmem = pl.BlockSpec(memory_space=pltpu.VMEM)
    return pl.pallas_call(
        body,
        in_specs=[pl.BlockSpec(memory_space=pltpu.SMEM)] + [vmem] * 2,
        out_specs=[vmem] * 2,
        out_shape=[jax.ShapeDtypeStruct(one.shape[1:], BF)] * 2,
        compiler_params=pltpu.CompilerParams(vmem_limit_bytes=VMEM_BYTES),
        cost_estimate=SHORT,
        name="pair_add",
    )(group_place(), one, two)


def back_project(lefts, weights, transposed=True):
    block = lefts[0].shape[0] // 4
    out = weights[0].shape[0] if transposed else weights[0].shape[1]

    def body(*refs):
        left_refs, weight_refs = refs[: len(lefts)], refs[len(lefts) : 2 * len(lefts)]
        keep_ref, give_ref = refs[2 * len(lefts) :]
        total = None
        for left_ref, weight_ref in zip(left_refs, weight_refs):
            part = (matmul_cols if transposed else matmul)(left_ref[...], weight_ref[...])
            total = part if total is None else total + part
        total = total.astype(BF)
        for i in range(4):
            (keep_ref, give_ref)[i % 2][i // 2] = total[i * block : (i + 1) * block]

    return pl.pallas_call(
        body,
        in_specs=[pl.BlockSpec(memory_space=pltpu.VMEM)] * (2 * len(lefts)),
        out_specs=[pl.BlockSpec(memory_space=pltpu.VMEM)] * 2,
        out_shape=[jax.ShapeDtypeStruct((2, block, out), BF)] * 2,
        compiler_params=pltpu.CompilerParams(vmem_limit_bytes=VMEM_BYTES),
        cost_estimate=SHORT,
        name="back_project",
    )(*lefts, *weights)


def branch_back(mine, recv, x_one, inverse, gain, grad_out, w_out):
    blocks, seg_len, width = x_one.shape
    quarter = width // 4

    def body(at_ref, mine_ref, recv_ref, x_ref, inv_ref, gain_ref, g_ref, w_ref, branch_ref, att_ref, own_ref):
        block = pl.program_id(0)
        grad = jnp.where(block % 2 == 0, mine_ref[0], recv_ref[0]).astype(F32)
        inverse = inv_ref[0]
        normed = x_ref[0] * inverse
        scaled = grad * gain_ref[...]
        mean = jnp.mean(scaled * normed, axis=-1, keepdims=True)
        total = g_ref[0].astype(F32) + inverse * (scaled - normed * mean)
        low = total.astype(BF)
        branch_ref[0] = low
        att_ref[0] = matmul_cols(low, w_ref[...]).astype(BF)

        @pl.when(block == 2 * at_ref[1])
        def own():
            own_ref[...] = total

    pair = pl.BlockSpec((1, seg_len, width), lambda i, at: (i // 2, 0, 0))
    full = pl.BlockSpec((1, seg_len, width), lambda i, at: (i, 0, 0))
    return pl.pallas_call(
        body,
        grid_spec=pltpu.PrefetchScalarGridSpec(
            num_scalar_prefetch=1,
            grid=(blocks,),
            in_specs=[
                pair,
                pair,
                full,
                pl.BlockSpec((1, seg_len, 1), lambda i, at: (i, 0, 0)),
                pl.BlockSpec((1, width), lambda i, at: (0, 0)),
                full,
                pl.BlockSpec((quarter, width), lambda i, at: (2 * at[1] + at[2], 0)),
            ],
            out_specs=[
                full,
                pl.BlockSpec((1, seg_len, quarter), lambda i, at: (i, 0, 0)),
                pl.BlockSpec((seg_len, width), lambda i, at: (0, 0)),
            ],
        ),
        out_shape=[
            jax.ShapeDtypeStruct((blocks, seg_len, width), BF),
            jax.ShapeDtypeStruct((blocks, seg_len, quarter), BF),
            jax.ShapeDtypeStruct((seg_len, width), F32),
        ],
        compiler_params=pltpu.CompilerParams(vmem_limit_bytes=VMEM_BYTES),
        cost_estimate=SHORT,
        name="branch_back",
    )(group_place(), mine, recv, x_one, inverse, gain, grad_out, w_out)


def add_kernel(one, two):
    def body(one_ref, two_ref, out_ref):
        out_ref[...] = (one_ref[...].astype(F32) + two_ref[...].astype(F32)).astype(BF)

    return pl.pallas_call(
        body,
        in_specs=[pl.BlockSpec(memory_space=pltpu.VMEM)] * 2,
        out_specs=pl.BlockSpec(memory_space=pltpu.VMEM),
        out_shape=jax.ShapeDtypeStruct(one.shape, BF),
        compiler_params=pltpu.CompilerParams(vmem_limit_bytes=VMEM_BYTES),
        cost_estimate=SHORT,
        name="add_kernel",
    )(one, two)


def add_low(one, two):
    return (one.astype(F32) + two.astype(F32)).astype(BF)


def lane_blocks(value):
    return [value[:, i : i + LANES] for i in range(0, value.shape[1], LANES)]


PIECES = ((0, 0), (0, 1), (1, 0), (1, 1), (2, 0), (3, 0), (2, 1))
N_COMMON = 5
N_GROUPS = 4


def forward_kernel(q_ref, k_ref, v_ref, mine_ref, other_ref, *refs):
    key_refs, value_refs = refs[:N_GROUPS], refs[N_GROUPS : 2 * N_GROUPS]
    o_ref, of_ref, p_ref, pl_ref, inv_ref, s_ref, top_ref, total_ref, acc_ref = refs[2 * N_GROUPS :]
    scale = HD ** (-0.5)
    upper = pl.program_id(1) >= 2
    queries = q_ref[0]
    seg_len = queries.shape[0]
    per = key_refs[0].shape[1] // LANES
    first = pl.program_id(1) % 2 == 0

    def bias(at):
        return jnp.where(first, mine_ref[0, at], other_ref[0, at]).astype(F32)

    local_bias = jnp.concatenate([bias(len(PIECES) * per + i) for i in range(cdiv(seg_len, LANES))], 1)
    s_local = jnp.minimum(matmul_cols(queries, k_ref[0]) * scale, local_bias[:, :seg_len])

    def score(t, top):
        group, low = PIECES[t]
        parts = lane_blocks(matmul_cols(queries, key_refs[group][low]) * scale)
        for i in range(per):
            part = jnp.minimum(parts[i], bias(t * per + i))
            s_ref[t, :, i * LANES : (i + 1) * LANES] = part
            top = part if top is None else jnp.maximum(top, part)
        return top

    top = None
    for t in range(N_COMMON):
        top = score(t, top)
    top_ref[...] = top

    @pl.when(upper)
    def more_scores():
        more = top_ref[...]
        for t in range(N_COMMON, len(PIECES)):
            more = score(t, more)
        top_ref[...] = more

    row_max = jnp.maximum(
        jnp.max(s_local, axis=-1, keepdims=True), jnp.max(top_ref[...], axis=-1, keepdims=True)
    )
    e_local = jnp.exp(s_local - row_max)
    low_local = e_local.astype(BF)
    pl_ref[0, 0] = low_local

    def weigh(t, total, acc):
        group, low = PIECES[t]
        expo = jnp.exp(s_ref[t] - row_max)
        for part in lane_blocks(expo):
            total = part if total is None else total + part
        chances = expo.astype(BF)
        p_ref[0, 0, t] = chances
        return total, acc + matmul(chances, value_refs[group][low])

    total, acc = None, matmul(low_local, v_ref[0])
    for t in range(N_COMMON):
        total, acc = weigh(t, total, acc)
    total_ref[...] = total
    acc_ref[...] = acc

    @pl.when(upper)
    def more_values():
        total, acc = total_ref[...], acc_ref[...]
        for t in range(N_COMMON, len(PIECES)):
            total, acc = weigh(t, total, acc)
        total_ref[...] = total
        acc_ref[...] = acc

    row_total = jnp.sum(e_local, axis=-1, keepdims=True) + jnp.sum(total_ref[...], axis=-1, keepdims=True)
    inverse = 1.0 / row_total
    out = acc_ref[...] * inverse
    of_ref[0] = out
    o_ref[0] = out.astype(BF)
    inv_ref[0, 0] = inverse


def backward_local_kernel(do_ref, of_ref, q_ref, k_ref, v_ref, inv_ref, pl_ref, cos_ref, sin_ref, dkv_ref, dq_ref):
    scale = HD ** (-0.5)
    d_out = do_ref[0]
    delta = jnp.sum(d_out.astype(F32) * of_ref[0], axis=-1, keepdims=True)
    chances = pl_ref[0, 0].astype(F32) * inv_ref[0, 0]
    ds = (chances * (matmul_cols(d_out, v_ref[0]) - delta)).astype(BF)
    dq_ref[0] = matmul(ds, k_ref[0])
    dk = matmul_rows(ds, q_ref[0])
    dkv_ref[0, 0] = ((dk * cos_ref[...] - pltpu.roll(dk, HD // 2, 1) * sin_ref[...]) * scale).astype(BF)
    dkv_ref[1, 0] = matmul_rows(chances.astype(BF), d_out).astype(BF)


def backward_kernel(do_ref, of_ref, local_ref, inv_ref, p_ref, cos_ref, sin_ref, *refs):
    key_refs, value_refs = refs[:N_GROUPS], refs[N_GROUPS : 2 * N_GROUPS]
    out_ref, dq_ref = refs[2 * N_GROUPS :]
    scale = HD ** (-0.5)
    upper = pl.program_id(1) >= 2
    d_out = do_ref[0]
    inverse = inv_ref[0, 0]
    delta = jnp.sum(d_out.astype(F32) * of_ref[0], axis=-1, keepdims=True)

    def piece(t, dq):
        group, low = PIECES[t]
        dp = matmul_cols(d_out, value_refs[group][low])
        ds = (p_ref[0, 0, t].astype(F32) * ((dp - delta) * inverse)).astype(BF)
        return dq + matmul(ds, key_refs[group][low])

    dq = local_ref[0]
    for t in range(N_COMMON):
        dq = piece(t, dq)
    dq_ref[...] = dq

    @pl.when(upper)
    def more():
        dq = dq_ref[...]
        for t in range(N_COMMON, len(PIECES)):
            dq = piece(t, dq)
        dq_ref[...] = dq

    dq = dq_ref[...]
    out_ref[0] = ((dq * cos_ref[...] - pltpu.roll(dq, HD // 2, 1) * sin_ref[...]) * scale).astype(BF)


def attention_specs(piece_rows, seg_len):
    head = pl.BlockSpec((1, seg_len, HD), lambda h, r: (r, 0, h))
    piece = pl.BlockSpec((2, piece_rows, HD), lambda h, r: (0, 0, h))
    p_spec = pl.BlockSpec((1, 1, len(PIECES), seg_len, piece_rows), lambda h, r: (r, h, 0, 0, 0))
    pl_spec = pl.BlockSpec((1, 1, seg_len, seg_len), lambda h, r: (r, h, 0, 0))
    inv_spec = pl.BlockSpec((1, 1, seg_len, 1), lambda h, r: (r, h, 0, 0))
    return head, piece, p_spec, pl_spec, inv_spec


def attention_forward(queries, keys, values, mask, other_mask, key_pieces, value_pieces):
    blocks, seg_len, width = queries.shape
    heads = width // HD
    piece_rows = key_pieces[0].shape[1]
    head, piece, p_spec, pl_spec, inv_spec = attention_specs(piece_rows, seg_len)
    return pl.pallas_call(
        forward_kernel,
        grid=(heads, blocks),
        in_specs=[
            head,
            head,
            head,
            pl.BlockSpec((1,) + mask.shape[1:], lambda h, r: (r // 2, 0, 0, 0)),
            pl.BlockSpec((1,) + mask.shape[1:], lambda h, r: (r // 2, 0, 0, 0)),
        ]
        + [piece] * (2 * N_GROUPS),
        out_specs=[head, head, p_spec, pl_spec, inv_spec],
        out_shape=[
            jax.ShapeDtypeStruct(queries.shape, BF),
            jax.ShapeDtypeStruct(queries.shape, F32),
            jax.ShapeDtypeStruct((blocks, heads, len(PIECES), seg_len, piece_rows), BF),
            jax.ShapeDtypeStruct((blocks, heads, seg_len, seg_len), BF),
            jax.ShapeDtypeStruct((blocks, heads, seg_len, 1), F32),
        ],
        scratch_shapes=[
            pltpu.VMEM((len(PIECES), seg_len, piece_rows), F32),
            pltpu.VMEM((seg_len, LANES), F32),
            pltpu.VMEM((seg_len, LANES), F32),
            pltpu.VMEM((seg_len, HD), F32),
        ],
        compiler_params=pltpu.CompilerParams(vmem_limit_bytes=VMEM_BYTES),
        cost_estimate=SHORT,
        name="attention_forward",
    )(queries, keys, values, mask, other_mask, *key_pieces, *value_pieces)


def attention_backward_local(d_out, out_f32, queries, keys, values, inverse, p_local, cosine, sine):
    blocks, seg_len, width = queries.shape
    head, unused, unused, pl_spec, inv_spec = attention_specs(seg_len, seg_len)
    table = pl.BlockSpec((seg_len, HD), lambda h, r: (0, 0))
    return pl.pallas_call(
        backward_local_kernel,
        grid=(width // HD, blocks),
        in_specs=[head, head, head, head, head, inv_spec, pl_spec, table, table],
        out_specs=[pl.BlockSpec((2, 1, seg_len, HD), lambda h, r: (0, r, 0, h)), head],
        out_shape=[
            jax.ShapeDtypeStruct((2, blocks, seg_len, width), BF),
            jax.ShapeDtypeStruct(queries.shape, F32),
        ],
        compiler_params=pltpu.CompilerParams(vmem_limit_bytes=VMEM_BYTES),
        cost_estimate=SHORT,
        name="attention_backward_local",
    )(d_out, out_f32, queries, keys, values, inverse, p_local, cosine, sine)


def attention_backward(d_out, out_f32, dq_local, inverse, p_memory, cosine, sine, key_pieces, value_pieces):
    blocks, seg_len, width = d_out.shape
    heads = width // HD
    piece_rows = key_pieces[0].shape[1]
    head, piece, p_spec, unused, inv_spec = attention_specs(piece_rows, seg_len)
    table = pl.BlockSpec((seg_len, HD), lambda h, r: (0, 0))
    return pl.pallas_call(
        backward_kernel,
        grid=(heads, blocks),
        in_specs=[head, head, head, inv_spec, p_spec, table, table] + [piece] * (2 * N_GROUPS),
        out_specs=head,
        out_shape=jax.ShapeDtypeStruct((blocks, seg_len, width), BF),
        scratch_shapes=[pltpu.VMEM((seg_len, HD), F32)],
        compiler_params=pltpu.CompilerParams(vmem_limit_bytes=VMEM_BYTES),
        cost_estimate=SHORT,
        name="attention_backward",
    )(d_out, out_f32, dq_local, inverse, p_memory, cosine, sine, *key_pieces, *value_pieces)


def allow_local_of(live):
    seg_len = live.shape[-1]
    position = jnp.arange(seg_len, dtype=jnp.int32)
    same = position[None, :] == position[:, None]
    return same[None] | ((position[None, :] < position[:, None])[None] & (live == 1))


def split_heads(value):
    rows, seg_len, width = value.shape
    return value.reshape(rows, seg_len, width // HD, HD)


def stream_forward(queries, keys, values, live, allow, memory):
    scale = HD ** (-0.5)
    q4, k4, v4 = split_heads(queries), split_heads(keys), split_heads(values)
    scores = jnp.einsum("rqhd,rkhd->rhqk", q4, k4, preferred_element_type=F32) * scale
    scores = jnp.where(allow_local_of(live)[:, None], scores, NEG_BIG)
    row_max = jnp.max(scores, axis=-1)
    expo = jnp.exp(scores - row_max[..., None])
    state = (
        row_max,
        jnp.sum(expo, axis=-1),
        jnp.einsum("rhqk,rkhd->rhqd", expo.astype(BF), v4, preferred_element_type=F32),
    )

    def step(running, item):
        row_max, row_total, acc = running
        block, allowed = item
        k3 = block[0].reshape(block.shape[1], -1, HD)
        v3 = block[1].reshape(block.shape[1], -1, HD)
        scores = jnp.einsum("rqhd,khd->rhqk", q4, k3, preferred_element_type=F32) * scale
        scores = jnp.where(allowed[:, None] > 0, scores, NEG_BIG)
        new_max = jnp.maximum(row_max, jnp.max(scores, axis=-1))
        shrink = jnp.exp(row_max - new_max)
        expo = jnp.exp(scores - new_max[..., None])
        acc = acc * shrink[..., None] + jnp.einsum(
            "rhqk,khd->rhqd", expo.astype(BF), v3, preferred_element_type=F32
        )
        return (new_max, row_total * shrink + jnp.sum(expo, axis=-1), acc), None

    (row_max, row_total, acc), unused = lax.scan(step, state, (memory, allow))
    out = (acc / row_total[..., None]).transpose(0, 2, 1, 3).reshape(queries.shape)
    return out.astype(BF), out, row_max + jnp.log(row_total)


def stream_backward(d_out, out_f32, queries, keys, values, live, log_total, allow, memory, cosine, sine):
    scale = HD ** (-0.5)
    q4, k4, v4, d4 = split_heads(queries), split_heads(keys), split_heads(values), split_heads(d_out)
    delta = jnp.sum(d4.astype(F32) * split_heads(out_f32), axis=-1).transpose(0, 2, 1)
    scores = jnp.einsum("rqhd,rkhd->rhqk", q4, k4, preferred_element_type=F32) * scale
    scores = jnp.where(allow_local_of(live)[:, None], scores, NEG_BIG)
    chances = jnp.exp(scores - log_total[..., None])
    dp = jnp.einsum("rqhd,rkhd->rhqk", d4, v4, preferred_element_type=F32)
    ds = (chances * (dp - delta[..., None])).astype(BF)
    dq = jnp.einsum("rhqk,rkhd->rqhd", ds, k4, preferred_element_type=F32)
    dk = jnp.einsum("rhqk,rqhd->rkhd", ds, q4, preferred_element_type=F32)
    dv = jnp.einsum("rhqk,rqhd->rkhd", chances.astype(BF), d4, preferred_element_type=F32)

    def step(running, item):
        block, allowed = item
        k3 = block[0].reshape(block.shape[1], -1, HD)
        v3 = block[1].reshape(block.shape[1], -1, HD)
        scores = jnp.einsum("rqhd,khd->rhqk", q4, k3, preferred_element_type=F32) * scale
        scores = jnp.where(allowed[:, None] > 0, scores, NEG_BIG)
        chances = jnp.exp(scores - log_total[..., None])
        dp = jnp.einsum("rqhd,khd->rhqk", d4, v3, preferred_element_type=F32)
        ds = (chances * (dp - delta[..., None])).astype(BF)
        return running + jnp.einsum("rhqk,khd->rqhd", ds, k3, preferred_element_type=F32), None

    dq, unused = lax.scan(step, dq, (memory, allow))

    def back(value):
        turned = rope_heads(value.reshape((-1,) + value.shape[2:]), jnp.tile(cosine, (value.shape[0], 1)), -jnp.tile(sine, (value.shape[0], 1)))
        return (turned * scale).reshape(queries.shape).astype(BF)

    return jnp.stack([back(dq), back(dk), dv.reshape(queries.shape).astype(BF)])


def local(
    layer_input,
    live,
    knn_index,
    mem_keys,
    mem_values,
    gain_attn,
    w_query,
    w_key,
    w_value,
    w_out,
    gain_ffn,
    w_gate,
    w_up,
    w_down,
    cotangent,
):
    seg_len, width = layer_input.shape[1:]
    quarter = width // 4
    n_seg = lax.axis_size("seg")
    n_devices = n_seg * lax.axis_size("rep")
    tokens = seg_len * n_seg
    n_high = n_seg // 4
    x, low, high, y, core = place()
    use_kernel = n_high <= KERNEL_HIGH
    kv_rows = 2 * seg_len
    group_tokens = 4 * seg_len

    def by_quarter(value):
        return [value[:, i * quarter : (i + 1) * quarter] for i in range(4)]

    gains = jnp.concatenate(
        [gain_attn[:, None], gain_ffn[:, None], jnp.zeros((gain_attn.shape[0], LANES - 2), BF)], 1
    )
    stacked = [by_quarter(w) for w in (w_query, w_key, w_value, w_out)]
    qo = jnp.stack([jnp.concatenate([s[i] for s in stacked] + [gains], 1) for i in range(4)])

    def core_quarters(value, side):
        return jnp.stack([cut(value, side * quarter, quarter), cut(value, (2 + side) * quarter, quarter)])

    def core_memory(side):
        return jnp.stack([core_quarters(mem_keys[0], side), core_quarters(mem_values[0], side)])

    coded = knn_index[0] * 2 + live[0][:, None]
    qo = qo.reshape(2, 2, -1, qo.shape[-1])
    qo_keep, qo_give = halves(qo, 1, core)
    kv_keep, kv_give = core_memory(core), core_memory(1 - core)
    qo_recv, kv_recv, coded_recv = flip_core(qo_give), flip_core(kv_give), flip_z(coded)
    qo_keep, kv_keep, coded, qo_recv, kv_recv, coded_recv, w_gate_, w_up_ = fence(
        qo_keep, kv_keep, coded, qo_recv, kv_recv, coded_recv, w_gate, w_up
    )

    qo_keep, qo_give = halves(ordered(qo_keep, qo_recv, core, 1), 0, low)
    kv_keep, kv_give = halves(ordered(kv_keep, kv_recv, core, 2), 1, low)
    coded = ordered(coded[None], coded_recv[None], low, 0)
    kv_recv = flip_z(kv_give)
    qo_near = flip_z(qo_give)
    down_w = w_down[None, None, None, None]
    x_own = layer_input[0]
    gate_up = split_units(w_gate_, w_up_, n_devices).reshape(2, 2, 2, -1, w_gate.shape[1] // 4)

    def places_of(codes, row_core):
        picks = lax.shift_right_arithmetic(codes, 1)
        pair = picks >= tokens
        slot = jnp.where(pair, picks - tokens, picks)
        slot_seg = slot // seg_len
        kv_row = jnp.bitwise_xor(pair.astype(jnp.int32), row_core)
        return picks, slot_seg, kv_row * seg_len + (slot - slot_seg * seg_len)

    split = 3 * quarter
    g_own = cotangent[0]
    cosine, sine = rope_tables(seg_len)
    if use_kernel:
        qo_far, qo_side = flip(qo_keep, "seg", 4), flip(qo_give, "seg", 6)
        picks, slot_seg, within = places_of(coded, core)
        slot_x, slot_low = slot_seg % 2, (slot_seg // 2) % 2
        same_x = slot_x == x
        in_group = jnp.where(same_x, 5, 4 + 2 * slot_low)
        before = jnp.where(same_x, 0, 2) + slot_low
        piece_no = jnp.where(slot_seg // 4 == high, in_group, before)
        columns = jnp.where(picks >= 0, piece_no * kv_rows + within, -1)
        live_two = jnp.bitwise_and(coded[:, :, 0], 1)[:, None, :]
        live_two = jnp.pad(live_two, ((0, 0), (0, 0), (0, cdiv(seg_len, LANES) * LANES - seg_len)))
        down_recv = flip(down_w, "seg", 4)
        (
            qo_keep, qo_near, qo_far, qo_side, kv_keep, kv_recv, x_own, gate_up, columns, live_two, down_w, down_recv
        ) = fence(
            qo_keep, qo_near, qo_far, qo_side, kv_keep, kv_recv, x_own, gate_up, columns, live_two, down_w, down_recv
        )

        pieces = ordered(kv_keep[:, None], kv_recv[:, None], low, 1)
        own_k, own_v = pieces[0], pieces[1]
        near = ordered(qo_keep[None, None], qo_near[None, None], low, 1)
        far = ordered(qo_far[None, None], qo_side[None, None], low, 1)
        qo = ordered(near, far, high, 0)[:, :, None, None]
        qo_a, qo_b = qo[..., :split], qo[..., split:]
        up_high = [(i, i + 4) for i in range(n_seg - 4)]

        def cross(value):
            return lax.ppermute(value, "seg", up_high)

        cross_k, side_k = cross(own_k), flip_x(own_k)
        a_recv, b_recv = flip_x(qo_a), flip_y(qo_b)
        x_recv = flip_z(x_own)
        gu_keep, gu_give = halves(gate_up, 1, core)
        gu_recv = flip_core(gu_give)
        mask = build_mask(columns, live_two, len(PIECES) * kv_rows // LANES)
        qo_a, qo_b, a_recv, b_recv, cross_k, side_k, own_v, x_own, x_recv, gu_keep, gu_recv, mask, down_w, down_recv = fence(
            qo_a, qo_b, a_recv, b_recv, cross_k, side_k, own_v, x_own, x_recv, gu_keep, gu_recv, mask, down_w, down_recv
        )

        cross_v, cross_side_k = cross(own_v), flip_x(cross_k)
        qo_a, qo_b = ordered(qo_a, a_recv, x, 2), ordered(qo_b, b_recv, y, 3)
        a_recv, b_recv = flip_y(qo_a), flip_x(qo_b)
        gu_keep, gu_give = halves(ordered(gu_keep, gu_recv, core, 2), 0, low)
        gu_recv = flip_z(gu_give)
        x_two = ordered(x_own[None], x_recv[None], low, 0)
        x_recv = flip_core(x_two)
        qo_a, qo_b, a_recv, b_recv, cross_v, cross_side_k, own_v, gu_keep, gu_recv, x_two, x_recv, mask, down_w, down_recv = fence(
            qo_a, qo_b, a_recv, b_recv, cross_v, cross_side_k, own_v, gu_keep, gu_recv, x_two, x_recv, mask, down_w, down_recv
        )

        cross_side_v, side_v = flip_x(cross_v), flip_x(own_v)
        other_mask = flip_core(mask)
        w_a, w_b = flat(ordered(qo_a, a_recv, y, 3)), flat(ordered(qo_b, b_recv, x, 2))
        gate_up = ordered(gu_keep[:, None], gu_recv[:, None], low, 1)[:, None]
        gu_recv = flip(gate_up, "seg", 4)
        down_w = ordered(down_w, down_recv, high, 0)
        down_recv = flip_y(down_w)
        x_all = jnp.stack([x_two, x_recv], 1).reshape(4, seg_len, width)
        queries, keys, values, h_one, inv_one = project(x_all, w_a, w_b, cosine, sine)
        wo_near = w_b[:, :quarter]
        queries, keys, values, cross_side_v, side_v, gate_up, gu_recv, down_w, down_recv, wo_near, g_own, other_mask = fence(
            queries, keys, values, cross_side_v, side_v, gate_up, gu_recv, down_w, down_recv, wo_near, g_own, other_mask
        )

        key_pieces = (cross_k, cross_side_k, side_k, own_k)
        value_pieces = (cross_v, cross_side_v, side_v, own_v)
        gate, upw = [ordered(gate_up[i], gu_recv[i], high, 0)[:, :, None, None] for i in range(2)]
        down_w = ordered(down_w, down_recv, y, 3)
        down_a, down_b = down_w[..., : width // 2], down_w[..., width // 2 :]
        g_recv, u_recv, a_recv, wo_far = flip_x(gate), flip_y(upw), flip_x(down_a), flip_z(wo_near)
        out_low, out_f32, p_memory, p_local, inverse = attention_forward(
            queries, keys, values, mask, other_mask, key_pieces, value_pieces
        )
        out_low, gate, upw, g_recv, u_recv, down_a, a_recv, down_b, wo_near, wo_far, g_own = fence(
            out_low, gate, upw, g_recv, u_recv, down_a, a_recv, down_b, wo_near, wo_far, g_own
        )
    else:
        qo = gather_high(ordered(qo_keep[None], qo_near[None], low, 0)[None, :, None, None])
        kv = ordered(kv_keep[:, None], kv_recv[:, None], low, 1)
        w_a, w_b = flat(gather_y(gather_x(qo[..., :split]))), flat(gather_x(gather_y(qo[..., split:])))
        x_all = all_blocks(two_rows(x_own))
        gu_keep, gu_give = halves(gate_up, 1, core)
        gu_keep, gu_give = halves(ordered(gu_keep, flip_core(gu_give), core, 2), 0, low)
        gate, upw = gather_high_pair(ordered(gu_keep[:, None], flip_z(gu_give)[:, None], low, 1))
        down_w = gather_y(gather_high(down_w))
        down_a, down_b = down_w[..., : width // 2], down_w[..., width // 2 :]
        coded = all_blocks(coded)
        row_core = jnp.bitwise_xor(core, jnp.arange(4, dtype=jnp.int32) % 2)[:, None, None]
        picks, slot_seg, within = places_of(coded, row_core)
        live_all = jnp.bitwise_and(coded[:, :, 0], 1)[:, None, :]
        columns = jnp.where(picks >= 0, slot_seg * kv_rows + within, n_seg * kv_rows)
        blocks_at = jnp.arange(4)[:, None, None]
        queries_at = jnp.arange(seg_len)[None, :, None]
        allow = jnp.zeros((4, seg_len, n_seg * kv_rows), BF).at[blocks_at, queries_at, columns].set(1.0, mode="drop")
        allow = allow.reshape(4, seg_len, n_seg, kv_rows).transpose(2, 0, 1, 3)
        memory = jnp.swapaxes(kv, 0, 1)[None, :, None]
        memory = gather_x(gather_high(memory)).reshape(n_seg, 2, kv_rows, quarter)
        queries, keys, values, h_one, inv_one = project(x_all, w_a, w_b, cosine, sine)
        wo_near = w_b[:, :quarter]
        out_low, out_f32, log_total = stream_forward(queries, keys, values, live_all, allow, memory)
        g_recv, u_recv, a_recv, wo_far = flip_x(gate), flip_y(upw), flip_x(down_a), flip_z(wo_near)

    h_one = h_one.reshape(group_tokens, width)
    inv_one = inv_one.reshape(group_tokens, 1)
    x_float = x_all.reshape(group_tokens, width).astype(F32)
    g_attn = w_b[:, quarter].astype(F32)
    g_ffn = w_b[:, quarter + 1].astype(F32)
    att_near = out_low.reshape(group_tokens, quarter)
    att_far = flip_z(att_near)
    gate, upw = ordered(gate, g_recv, x, 2), ordered(upw, u_recv, y, 3)
    g_recv, u_recv = flip_y(gate), flip_x(upw)
    wo_both = jnp.stack([wo_near, wo_far])
    wo_recv = flip_core(wo_both)
    g_far = flip_z(g_own)
    att_near, att_far, gate, upw, g_recv, u_recv, down_b, wo_both, wo_recv, g_own, g_far = fence(
        att_near, att_far, gate, upw, g_recv, u_recv, down_b, wo_both, wo_recv, g_own, g_far
    )

    att_both = jnp.stack([att_near, att_far])
    att_recv = flip_core(att_both)
    down_recv = flip_x(down_b)
    g_two = ordered(g_own[None], g_far[None], low, 0)
    g_recv_core = flip_core(g_two)
    wg, wu = flat(ordered(gate, g_recv, y, 3)), flat(ordered(upw, u_recv, x, 2))
    wo = all_quarters(wo_both, wo_recv)
    attended = all_quarters(att_both, swap_pairs(att_recv))
    x_one = x_float + matmul(attended, wo)
    h_two_f, inv_two = norm_forward(x_one, g_ffn)
    h_two = h_two_f.astype(BF)
    gate_out = matmul(h_two, wg)
    up_out = matmul(h_two, wu)
    sigma = jax.nn.sigmoid(gate_out)
    swish = gate_out * sigma
    hidden = (swish * up_out).astype(BF)
    grad_out = jnp.stack([g_two, g_recv_core], 1).reshape(group_tokens, width)

    down_b, hidden = fence(down_b, hidden)
    wd = jnp.concatenate([flat(ordered(down_a, a_recv, x, 2)), flat(ordered(down_b, down_recv, x, 2))], 1)
    d_hidden = matmul_cols(grad_out, wd)
    d_gate = (d_hidden * up_out * sigma * (1.0 + gate_out * (1.0 - sigma))).astype(BF)
    d_up = (d_hidden * swish).astype(BF)
    sums_keep, sums_give = back_project([d_gate, d_up], [wg, wu])
    sums = add_low(sums_keep, flip_core(sums_give))
    sums, hidden, h_two, d_gate, d_up, wd = fence(sums, hidden, h_two, d_gate, d_up, wd)

    far_sums = flip_z(sums)
    (keep_g, give_g), (keep_u, give_u) = gradient((h_two, [d_gate], "x", None), (h_two, [d_up], "y", None))
    keep_g, give_g, keep_u, give_u, hidden, wd = fence(keep_g, give_g, keep_u, give_u, hidden, wd)
    recv_g, recv_u = flip_x(give_g), flip_y(give_u)
    down_keep, down_give = back_project([hidden], [wd], False)
    down_recv = flip_core(down_give)
    keep_wd, give_wd = gradient_units(hidden, grad_out)
    sums, far_sums, keep_g, keep_u, down_keep, down_recv, keep_wd, give_wd = fence(
        sums, far_sums, keep_g, keep_u, down_keep, down_recv, keep_wd, give_wd
    )

    own = 2 * low * seg_len
    summed = add_kernel(sums, far_sums)
    summed_recv = flip_core(summed)
    recv_wd = flip_x(give_wd)
    d_branch, d_att, d_x_own = branch_back(
        summed,
        summed_recv,
        x_one.reshape(4, seg_len, width),
        inv_two.reshape(4, seg_len, 1),
        g_ffn[None],
        grad_out.reshape(4, seg_len, width),
        wo,
    )
    d_branch = d_branch.reshape(group_tokens, width)
    keep_g, keep_u, recv_g, recv_u, d_att, d_branch, down_keep, down_recv = fence(
        keep_g, keep_u, recv_g, recv_u, d_att, d_branch, down_keep, down_recv
    )

    keep_g, give_g = split_sums(keep_g, recv_g, "y")
    keep_u, give_u = split_sums(keep_u, recv_u, "x")
    down_own, down_give = pair_add(down_keep, down_recv)
    w_thirds = [w_a[:, i * quarter : (i + 1) * quarter] for i in range(3)]
    if use_kernel:
        recv_g, recv_u = flip_y(give_g), flip_x(give_u)
        down_recv = flip_z(down_give)
        d_kv, dq_local = attention_backward_local(
            d_att, out_f32, queries, keys, values, inverse, p_local, cosine, sine
        )
        d_kv = d_kv.reshape(2, group_tokens, quarter)
        (keep_kv, give_kv), (keep_wo, give_wo) = gradient(
            (h_one, [d_kv[0], d_kv[1]], "y", None), (attended, [d_branch], "y", quarter)
        )
        give_kvo = jnp.concatenate([give_kv, give_wo], -1)
        keep_kvo = jnp.concatenate([keep_kv, keep_wo], -1)
        keep_kvo, give_kvo, keep_g, recv_g, keep_u, recv_u, dq_local, keep_wd, recv_wd = fence(
            keep_kvo, give_kvo, keep_g, recv_g, keep_u, recv_u, dq_local, keep_wd, recv_wd
        )
        gu_parts = plane_sort((keep_g, recv_g), (keep_u, recv_u))
        recv_kvo = flip_y(give_kvo)
        gu_flips = z_flips(gu_parts)
        keep_wd, give_wd = split_sums(
            keep_wd.reshape((-1,) + keep_wd.shape[2:]), recv_wd.reshape((-1,) + keep_wd.shape[2:]), "y"
        )
        recv_wd = flip_y(give_wd)
        d_q = attention_backward(
            d_att, out_f32, dq_local, inverse, p_memory, cosine, sine, key_pieces, value_pieces
        )
        d_q, keep_kvo = fence(d_q, keep_kvo)

        d_q = d_q.reshape(group_tokens, quarter)
        ((keep_q, *give_q),) = gradient((h_one, [d_q], "xy", None))
        keep_q, give_q, d_q, keep_kvo, recv_kvo, gu_kept, gu_flips = fence(
            keep_q, give_q, d_q, keep_kvo, recv_kvo, gu_parts[0], gu_flips
        )
        keep_kvo, give_kvo = split_sums(keep_kvo, recv_kvo, "x")
        recv_q = plane_flips(give_q)
        recv_kvo = flip_x(give_kvo)
        d_h_keep, d_h_give = back_project([d_q, d_kv[0], d_kv[1]], w_thirds)
        d_h_recv = flip_core(d_h_give)
        gu_keep, gu_give = z_merge(gu_kept, *gu_flips)
        keep_q, recv_q, keep_kvo, recv_kvo, keep_wd, recv_wd, d_h_keep, d_h_recv, gu_keep, gu_give = fence(
            keep_q, recv_q, keep_kvo, recv_kvo, keep_wd, recv_wd, d_h_keep, d_h_recv, gu_keep, gu_give
        )
        parts = plane_sort((keep_q,) + tuple(recv_q), (keep_kvo, recv_kvo))
        flips = z_flips(parts)
        d_h_own, d_h_give = pair_add(d_h_keep, d_h_recv)
        d_h_recv = flip_z(d_h_give)
        gu_recv = flip_core(gu_give)
        sum_wg, sum_wu, grad_g_ffn = join_units(gu_keep, gu_recv, (w_gate, w_up), gain_ffn, n_devices)
        wd_own = add_kernel(keep_wd, recv_wd)
        wd_own, wd_give = pick(wd_own, high, 0), pick(wd_own, 1 - high, 0)
        wd_recv = flip(wd_give, "seg", 4)
        kept, flips, d_h_own, d_h_recv, wd_own, wd_recv, sum_wg, sum_wu = fence(
            parts[0], flips, d_h_own, d_h_recv, wd_own, wd_recv, sum_wg, sum_wu
        )
        qkvo_keep, qkvo_give = z_merge(kept, *flips)
        qkvo_recv = flip_core(qkvo_give)
        sum_wd = wd_own.astype(F32) + wd_recv.astype(F32)
    else:
        down_recv = flip_z(down_give)
        d_q, *d_kv = stream_backward(
            d_att, out_f32, queries, keys, values, live_all, log_total, allow, memory, cosine, sine
        ).reshape(3, group_tokens, quarter)

        def by_chip(value):
            return value.reshape(n_high, 2, -1, value.shape[-1])

        (keep_qkv, *give_qkv), (keep_wo, *give_wo) = gradient(
            (h_one, [d_q, d_kv[0], d_kv[1]], "xy", None), (attended, [d_branch], "xy", quarter)
        )
        plane_gu = [add_low(keep_g, flip_y(give_g)), add_low(keep_u, flip_x(give_u))]
        z_gu = z_plain(by_chip(jnp.concatenate(plane_gu, -1)))
        plane_qkvo = [add_all(keep_qkv, *plane_flips(give_qkv)), add_all(keep_wo, *plane_flips(give_wo))]
        z_qkvo = z_plain(by_chip(jnp.concatenate(plane_qkvo, -1)))
        (gu_keep, gu_give), (qkvo_keep, qkvo_give) = core_halves(z_gu), core_halves(z_qkvo)
        qkvo_recv, gu_recv = flip_core(qkvo_give), flip_core(gu_give)
        keep_wd, give_wd = halves(add_low(keep_wd, recv_wd), 1, y)
        recv_wd = flip_y(give_wd)
        d_h_keep, d_h_give = back_project([d_q, d_kv[0], d_kv[1]], w_thirds)
        d_h_own, d_h_give = pair_add(d_h_keep, flip_core(d_h_give))
        d_h_recv = flip_z(d_h_give)
        sum_wd = reduce_high(add_low(keep_wd, recv_wd)[:, None])[0].astype(F32)
        sum_wg, sum_wu, grad_g_ffn = join_units(gu_keep, gu_recv, (w_gate, w_up), gain_ffn, n_devices)
    layer_output = (cut(x_one, own, seg_len, 0) + down_own.astype(F32) + down_recv.astype(F32)).astype(BF)
    sum_q, sum_k, sum_v, sum_o, grad_g_attn = join_columns(
        qkvo_keep, qkvo_recv, (w_query, w_key, w_value), gain_attn, 4
    )
    d_h_one = d_h_own.astype(F32) + d_h_recv.astype(F32)
    x_own = cut(x_float, own, seg_len, 0)
    d_x_first, unused = norm_backward(x_own, cut(inv_one, own, seg_len, 0), g_attn, d_h_one)
    grad_x = (d_x_own + d_x_first).astype(BF)
    return (
        layer_output[None],
        grad_x[None],
        grad_g_attn,
        sum_q,
        sum_k,
        sum_v,
        sum_o,
        grad_g_ffn,
        sum_wg,
        sum_wu,
        sum_wd,
    )


def solution(mesh):
    tokens = P("rep", "seg", None)
    vector = P(("seg", "rep"))
    matrix = P(("seg", "rep"), None)
    return jax.shard_map(
        local,
        mesh=mesh,
        in_specs=(
            tokens,
            P("rep", "seg"),
            tokens,
            tokens,
            tokens,
            vector,
            matrix,
            matrix,
            matrix,
            matrix,
            vector,
            matrix,
            matrix,
            matrix,
            tokens,
        ),
        out_specs=(tokens, tokens, vector, matrix, matrix, matrix, matrix, vector, matrix, matrix, matrix),
        check_vma=False,
    )
```

```python
import jax
import jax.numpy as jnp
from jax import lax
from jax.experimental import pallas as pl
from jax.experimental.pallas import tpu as pltpu
from jax.sharding import PartitionSpec as P

H = 8
HD = 128
EPSILON = 1e-05
NEG_BIG = -1e30
POS_BIG = 1e30
ROPE_BASE = 10000.0
LANES = 128
KERNEL_HIGH = 2
VMEM_BYTES = 44 * 1024 * 1024

SHORT = pl.CostEstimate(flops=1000, bytes_accessed=1000, transcendentals=0)

BF = jnp.bfloat16
F32 = jnp.float32


def cdiv(a, b):
    return -(-a // b)


def flip(value, axis, bit):
    count = lax.axis_size(axis)
    return lax.ppermute(value, axis, [(i, i ^ bit) for i in range(count)])


def flip_core(value):
    return flip(value, "rep", 1)


def flip_y(value):
    return flip(value, "rep", 2)


def flip_x(value):
    return flip(value, "seg", 1)


def flip_z(value):
    return flip(value, "seg", 2)


def ordered(mine, other, bit, axis):
    first = jnp.where(bit == 0, mine, other)
    second = jnp.where(bit == 0, other, mine)
    return jnp.concatenate([first, second], axis)


def pick(value, index, axis):
    return lax.dynamic_index_in_dim(value, index, axis, keepdims=False)


def cut(value, start, size, axis=-1):
    return lax.dynamic_slice_in_dim(value, start, size, axis % value.ndim)


def fence(*values):
    return lax.optimization_barrier(values)


def place():
    seg = lax.axis_index("seg")
    rep = lax.axis_index("rep")
    return seg % 2, (seg // 2) % 2, seg // 4, rep // 2, rep % 2


def high_bits():
    bit = 4
    out = []
    while bit < lax.axis_size("seg"):
        out.append(bit)
        bit *= 2
    return out


def gather_high(cur):
    seg = lax.axis_index("seg")
    for bit in high_bits():
        cur = ordered(cur, flip(cur, "seg", bit), (seg // bit) % 2, 0)
    return cur


def gather_x(cur):
    return ordered(cur, flip_x(cur), place()[0], 2)


def gather_y(cur):
    return ordered(cur, flip_y(cur), place()[3], 3)


def gather_high_pair(cur):
    seg = lax.axis_index("seg")
    cur = cur[:, None]
    bits = high_bits()
    for bit in bits[:-1]:
        cur = ordered(cur, flip(cur, "seg", bit), (seg // bit) % 2, 1)
    recv = flip(cur, "seg", bits[-1])
    side = (seg // bits[-1]) % 2
    return [ordered(cur[i], recv[i], side, 0)[:, :, None, None] for i in range(2)]


def flat(cur):
    return cur.reshape(-1, cur.shape[-1])


def halve(value, axis_name, bit, side, axis):
    recv = flip(pick(value, 1 - side, axis), axis_name, bit)
    kept = pick(value, side, axis)
    return (kept.astype(F32) + recv.astype(F32)).astype(BF)


def plane_shape(value, low):
    high = lax.axis_size("seg") // 4
    return value.reshape(high, low, 2, -1, value.shape[-1])


def halves(cur, axis, side):
    return pick(cur, side, axis), pick(cur, 1 - side, axis)


def plane_flips(parts):
    n_rep = lax.axis_size("rep")
    count = lax.axis_size("seg") * n_rep
    far = [(i, i ^ n_rep ^ 2) for i in range(count)]
    return flip_x(parts[0]), flip_y(parts[1]), lax.ppermute(parts[2], ("seg", "rep"), far)


def add_all(first, *others):
    total = first.astype(F32)
    for other in others:
        total = total + other.astype(F32)
    return total.astype(BF)


def z_flips(parts):
    return flip_z(parts[1]), flip(parts[2], "seg", 4), flip(parts[3], "seg", 6)


def z_plain(cur):
    low = place()[1]
    sums = reduce_high(cur)
    return ordered(pick(sums, low, 0)[None], flip_z(pick(sums, 1 - low, 0))[None], low, 0)


def reduce_high(cur):
    seg = lax.axis_index("seg")
    for bit in reversed(high_bits()):
        cur = cur.reshape((2, cur.shape[0] // 2) + cur.shape[1:])
        cur = halve(cur, "seg", bit, (seg // bit) % 2, 0)
    return cur[0]


def trade_core(quarters):
    core = place()[4]
    low, unused, rows, cols = 2, 2, quarters.shape[1], quarters.shape[2]
    four = quarters.reshape(2, 2, rows, cols)
    return ordered(pick(four, core, 1), flip_core(pick(four, 1 - core, 1)), core, 1)


def trade_z(halves):
    low = place()[1]
    return ordered(pick(halves, low, 0)[None], flip_z(pick(halves, 1 - low, 0))[None], low, 0)


def gather_z_four(halves):
    seg = lax.axis_index("seg")
    low = (seg // 2) % 2
    keep, give = pick(halves, low, 0)[None, None], pick(halves, 1 - low, 0)[None, None]
    near = ordered(keep, flip(give, "seg", 2), low, 1)
    far = ordered(flip(keep, "seg", 4), flip(give, "seg", 6), low, 1)
    return ordered(near, far, (seg // 4) % 2, 0)[:, :, None, None]


def start_gather(traded):
    return traded[None, :, None, None]


def core_halves(mine):
    core = place()[4]
    four = mine.reshape(2, 2, mine.shape[1] // 2, mine.shape[2])
    return halves(four, 1, core)


def all_blocks(by_low):
    both = jnp.stack([by_low, flip_core(by_low)], 1)
    return both.reshape((-1,) + by_low.shape[1:])


def two_rows(value):
    return ordered(value[None], flip_z(value)[None], place()[1], 0)


def core_parts(part):
    blocks = part.reshape((2, 2, part.shape[0] // 4) + part.shape[1:])
    return blocks[:, 0].astype(BF), blocks[:, 1].astype(BF)


def core_sums(part):
    blocks = part.reshape((2, 2, part.shape[0] // 4) + part.shape[1:])
    return (blocks[:, 0] + flip_core(blocks[:, 1].astype(BF)).astype(F32)).astype(BF)


def own_sums(sums):
    low = place()[1]
    return pick(sums, low, 0).astype(F32) + flip_z(pick(sums, 1 - low, 0)).astype(F32)


def z_sums(sums):
    return (sums.astype(F32) + flip_z(sums).astype(F32)).astype(BF)


def both_cores(sums):
    return jnp.stack([sums, flip_core(sums)], 1).astype(F32)


def unit_blocks(n_blocks):
    order = []
    for block in range(n_blocks):
        high, low, rest, core = block // 16, (block // 8) % 2, (block // 2) % 4, block % 2
        order.append((low * 2 + core, high * 4 + rest))
    return order


def split_units(one, two, n_blocks):
    rows, total = one.shape
    size = total // n_blocks

    def body(one_ref, two_ref, out_ref):
        for half, in_ref in enumerate((one_ref, two_ref)):
            for block, (quarter, at) in enumerate(unit_blocks(n_blocks)):
                out_ref[quarter, half * rows : (half + 1) * rows, at * size : (at + 1) * size] = in_ref[
                    :, block * size : (block + 1) * size
                ]

    return pl.pallas_call(
        body,
        out_shape=jax.ShapeDtypeStruct((4, 2 * rows, total // 4), one.dtype),
        cost_estimate=SHORT,
        name="split_units",
    )(one, two)


def matmul(left, right):
    return jnp.dot(left, right, preferred_element_type=F32)


def matmul_rows(left, right):
    return lax.dot_general(left, right, (((0,), (0,)), ((), ())), preferred_element_type=F32)


def matmul_cols(left, right):
    return lax.dot_general(left, right, (((1,), (1,)), ((), ())), preferred_element_type=F32)


def norm_forward(values, gain):
    inverse = lax.rsqrt(jnp.mean(values * values, axis=-1, keepdims=True) + EPSILON)
    return (values * inverse * gain, inverse)


def norm_backward(values, inverse, gain, grad_out):
    normed = values * inverse
    scaled = grad_out * gain
    grad_values = inverse * (scaled - normed * jnp.mean(scaled * normed, axis=-1, keepdims=True))
    return (grad_values, normed)


def rope_tables(seg_len):
    position = jnp.arange(seg_len).astype(F32)
    freqs = ROPE_BASE ** (-(2.0 * jnp.arange(HD // 2).astype(F32)) / HD)
    angle = position[:, None] * freqs[None, :]
    cosine, sine = jnp.cos(angle), jnp.sin(angle)
    return (jnp.concatenate([cosine, cosine], -1), jnp.concatenate([-sine, sine], -1))


def rope_heads(values, cosine, sine):
    half = HD // 2
    swapped = jnp.concatenate([values[..., half:], values[..., :half]], -1)
    return values * cosine[:, None, :] + swapped * sine[:, None, :]


def mask_kernel(n_cols, cols_ref, live_ref, out_ref, scratch):
    queries = cols_ref.shape[1]
    picks = cols_ref[0]
    pad = scratch.shape[0]
    high = lax.shift_right_arithmetic(picks, 7)
    low = jnp.bitwise_and(picks, LANES - 1)
    iota_high = lax.broadcasted_iota(jnp.int32, (pad, picks.shape[1]), 0)
    iota_low = lax.broadcasted_iota(jnp.int32, (LANES, picks.shape[1]), 0)
    for i in range(queries):
        hot_high = jnp.where(iota_high == high[i : i + 1, :], 1.0, 0.0).astype(BF)
        hot_low = jnp.where(iota_low == low[i : i + 1, :], 1.0, 0.0).astype(BF)
        scratch[:, i, :] = matmul_cols(hot_high, hot_low)
    out_ref[0, 0:n_cols] = jnp.where(scratch[0:n_cols] > 0.5, POS_BIG, NEG_BIG).astype(BF)
    row = lax.broadcasted_iota(jnp.int32, (queries, LANES), 0) + pl.program_id(1) * queries
    for part in range(out_ref.shape[1] - n_cols):
        col = lax.broadcasted_iota(jnp.int32, (queries, LANES), 1) + part * LANES
        live = live_ref[0, :, part * LANES : (part + 1) * LANES]
        allow = (col == row) | ((col < row) & (live == 1))
        out_ref[0, n_cols + part] = jnp.where(allow, POS_BIG, NEG_BIG).astype(BF)


def build_mask(columns, live, n_cols):
    rows, queries, picks = columns.shape
    block = 16
    pad = cdiv(n_cols, 8) * 8
    n_local = live.shape[2] // LANES
    return pl.pallas_call(
        lambda *refs: mask_kernel(n_cols, *refs),
        grid=(rows, queries // block),
        in_specs=[
            pl.BlockSpec((1, block, picks), lambda r, g: (r, g, 0)),
            pl.BlockSpec((1, 1, live.shape[2]), lambda r, g: (r, 0, 0)),
        ],
        out_specs=pl.BlockSpec((1, n_cols + n_local, block, LANES), lambda r, g: (r, 0, g, 0)),
        out_shape=jax.ShapeDtypeStruct((rows, n_cols + n_local, queries, LANES), BF),
        scratch_shapes=[pltpu.VMEM((pad, block, LANES), F32)],
        compiler_params=pltpu.CompilerParams(vmem_limit_bytes=VMEM_BYTES),
        cost_estimate=pl.CostEstimate(flops=12000000000, bytes_accessed=3000000, transcendentals=0),
        name="mask_build",
    )(columns, live)


def project_kernel(x_ref, wa_ref, wb_ref, cos_ref, sin_ref, q_ref, k_ref, v_ref, h_ref, inv_ref, gain_ref):
    quarter = q_ref.shape[2]

    @pl.when(pl.program_id(0) == 0)
    def gains():
        gain_ref[...] = jnp.transpose(wb_ref[:, quarter:].astype(F32), (1, 0))[0:8]

    x = x_ref[0].astype(F32)
    inverse = lax.rsqrt(jnp.mean(x * x, axis=-1, keepdims=True) + EPSILON)
    h = (x * inverse * gain_ref[0:1, :]).astype(BF)
    h_ref[0] = h
    inv_ref[0] = inverse
    turned = matmul(h, wa_ref[:, : 2 * quarter])
    for head in range(2 * quarter // HD):
        value = turned[:, head * HD : (head + 1) * HD]
        value = (value * cos_ref[...] + pltpu.roll(value, HD // 2, 1) * sin_ref[...]).astype(BF)
        if head < quarter // HD:
            q_ref[0, :, head * HD : (head + 1) * HD] = value
        else:
            at = head * HD - quarter
            k_ref[0, :, at : at + HD] = value
    v_ref[0] = matmul(h, wa_ref[:, 2 * quarter :]).astype(BF)


def project(x_all, w_a, w_b, cosine, sine):
    blocks, seg_len, width = x_all.shape
    quarter = w_a.shape[1] // 3
    whole = lambda array: pl.BlockSpec(array.shape, lambda r: (0, 0))
    head = pl.BlockSpec((1, seg_len, quarter), lambda r: (r, 0, 0))
    full = pl.BlockSpec((1, seg_len, width), lambda r: (r, 0, 0))
    out = jax.ShapeDtypeStruct((blocks, seg_len, quarter), BF)
    return pl.pallas_call(
        project_kernel,
        grid=(blocks,),
        in_specs=[full, whole(w_a), whole(w_b), whole(cosine), whole(sine)],
        out_specs=[head, head, head, full, pl.BlockSpec((1, seg_len, 1), lambda r: (r, 0, 0))],
        out_shape=[out, out, out, jax.ShapeDtypeStruct(x_all.shape, BF), jax.ShapeDtypeStruct((blocks, seg_len, 1), F32)],
        scratch_shapes=[pltpu.VMEM((8, width), F32)],
        compiler_params=pltpu.CompilerParams(vmem_limit_bytes=VMEM_BYTES),
        cost_estimate=SHORT,
        name="project",
    )(x_all, w_a, w_b, cosine, sine)


def plane_place():
    x, low, unused, y, core = place()
    return jnp.stack([x, y, 2 * low + core]).astype(jnp.int32)


def gradient(*entries):
    tokens, width = entries[0][0].shape
    n_blocks = lax.axis_size("seg")
    rows = width // n_blocks
    half = rows // 2
    sizes = [[entry[3] or right.shape[1] for right in entry[1]] for entry in entries]
    if rows % LANES:
        x, unused, unused, y, unused = place()
        outs = []
        for left, rights, way, columns in entries:
            if columns:
                rights = [cut(right, plane_place()[2] * columns, columns) for right in rights]
            full = jnp.concatenate([matmul_rows(left, right).astype(BF) for right in rights], 1)
            full = full.reshape(-1, 2, 2, half, full.shape[1])
            if way == "xy":
                near, side = halves(full, 1, x)
                near, side = halves(near, 1, y), halves(side, 1, y)
                parts = [near[0], side[0], near[1], side[1]]
            else:
                parts = halves(full, 1, x) if way == "x" else halves(full, 2, y)
            outs.append([part.reshape(-1, half, part.shape[-1]) for part in parts])
        return outs
    lefts = []
    for entry in entries:
        if not any(entry[0] is left for left in lefts):
            lefts.append(entry[0])
    which = [[entry[0] is left for left in lefts].index(True) for entry in entries]
    counts = [4 if entry[2] == "xy" else 2 for entry in entries]
    shapes = []
    for entry, size, count in zip(entries, sizes, counts):
        blocks = n_blocks // 2 if entry[2] == "xy" else n_blocks
        shapes += [(blocks, half, sum(size))] * count
    n_rights = sum(len(size) for size in sizes)

    def body(at_ref, *refs):
        left_refs, right_refs = refs[: len(lefts)], list(refs[len(lefts) : len(lefts) + n_rights])
        out_refs = list(refs[len(lefts) + n_rights :])
        pair = pl.program_id(0)
        turned = [jnp.transpose(ref[...]) for ref in left_refs]

        def by_row(value):
            upper, lower = value[:half], value[half:]
            return jnp.where(at_ref[1] == 0, upper, lower), jnp.where(at_ref[1] == 0, lower, upper)

        for entry, i, size, count in zip(entries, which, sizes, counts):
            outs, out_refs = out_refs[:count], out_refs[count:]
            start = 0
            for width_here in size:
                product = matmul(turned[i], right_refs.pop(0)[...]).astype(BF)
                span = slice(start, start + width_here)
                start += width_here
                first, second = product[:rows], product[rows:]
                if entry[2] == "y":
                    for side, value in enumerate((first, second)):
                        outs[0][2 * pair + side, :, span], outs[1][2 * pair + side, :, span] = by_row(value)
                    continue
                same = jnp.where(at_ref[0] == 0, first, second)
                other = jnp.where(at_ref[0] == 0, second, first)
                if entry[2] == "x":
                    for ref, value in zip(outs, (same, other)):
                        ref[2 * pair, :, span] = value[:half]
                        ref[2 * pair + 1, :, span] = value[half:]
                else:
                    outs[0][pair, :, span], outs[2][pair, :, span] = by_row(same)
                    outs[1][pair, :, span], outs[3][pair, :, span] = by_row(other)

    in_specs = [pl.BlockSpec((tokens, 2 * rows), lambda i, at: (0, i))] * len(lefts)
    for entry, size in zip(entries, sizes):
        column = (lambda i, at: (0, at[2])) if entry[3] else (lambda i, at: (0, 0))
        in_specs += [pl.BlockSpec((tokens, width_here), column) for width_here in size]
    outs = pl.pallas_call(
        body,
        grid_spec=pltpu.PrefetchScalarGridSpec(
            num_scalar_prefetch=1,
            grid=(n_blocks // 2,),
            in_specs=in_specs,
            out_specs=[pl.BlockSpec(shape, lambda i, at: (0, 0, 0)) for shape in shapes],
        ),
        out_shape=[jax.ShapeDtypeStruct(shape, BF) for shape in shapes],
        compiler_params=pltpu.CompilerParams(vmem_limit_bytes=VMEM_BYTES),
        cost_estimate=SHORT,
        name="gradient",
    )(plane_place(), *lefts, *[right for entry in entries for right in entry[1]])
    groups = []
    for count in counts:
        groups.append(outs[:count])
        outs = outs[count:]
    return groups


def split_sums(keep, recv, way):
    n_blocks, rows, cols = keep.shape

    def body(at_ref, keep_ref, recv_ref, mine_ref, give_ref):
        side = at_ref[1] if way == "y" else at_ref[0]
        for block in range(n_blocks // 2):
            for at, out_ref in ((2 * block + side, mine_ref), (2 * block + 1 - side, give_ref)):
                out_ref[block] = (keep_ref[at].astype(F32) + recv_ref[at].astype(F32)).astype(BF)

    vmem = pl.BlockSpec(memory_space=pltpu.VMEM)
    return pl.pallas_call(
        body,
        in_specs=[pl.BlockSpec(memory_space=pltpu.SMEM)] + [vmem] * 2,
        out_specs=[vmem] * 2,
        out_shape=[jax.ShapeDtypeStruct((n_blocks // 2, rows, cols), BF)] * 2,
        compiler_params=pltpu.CompilerParams(vmem_limit_bytes=VMEM_BYTES),
        cost_estimate=SHORT,
        name="split_sums",
    )(plane_place(), keep, recv)


def gradient_units(left, right):
    tokens, width = left.shape
    n_high = lax.axis_size("seg") // 4
    rows = width // (4 * n_high)
    cols = right.shape[1]
    step = 256
    if rows % 8:
        full = matmul_rows(left, right).astype(BF).reshape(-1, 2, 2, rows, cols)
        return halves(full, 1, place()[0])

    def body(at_ref, left_ref, right_ref, keep_ref, give_ref):
        product = matmul_rows(left_ref[...], right_ref[...])
        for high in range(n_high):
            for y in range(2):
                zero, one = [
                    product[(high * 4 + x * 2 + y) * rows : (high * 4 + x * 2 + y + 1) * rows] for x in range(2)
                ]
                keep_ref[high, y] = jnp.where(at_ref[0] == 0, zero, one).astype(BF)
                give_ref[high, y] = jnp.where(at_ref[0] == 0, one, zero).astype(BF)

    shape = (n_high, 2, rows, cols)
    return pl.pallas_call(
        body,
        grid_spec=pltpu.PrefetchScalarGridSpec(
            num_scalar_prefetch=1,
            grid=(cols // step,),
            in_specs=[
                pl.BlockSpec((tokens, width), lambda i, at: (0, 0)),
                pl.BlockSpec((tokens, step), lambda i, at: (0, i)),
            ],
            out_specs=[pl.BlockSpec((n_high, 2, rows, step), lambda i, at: (0, 0, 0, i))] * 2,
        ),
        out_shape=[jax.ShapeDtypeStruct(shape, BF)] * 2,
        compiler_params=pltpu.CompilerParams(vmem_limit_bytes=VMEM_BYTES),
        cost_estimate=SHORT,
        name="gradient_units",
    )(plane_place(), left, right)


def group_place():
    unused, low, high, unused, core = place()
    return jnp.stack([2 * high + low, low, core]).astype(jnp.int32)


def plane_sort(*groups, units=()):
    sizes = [group[0].shape[-1] for group in groups]
    rows, cols = groups[0][0].shape[1], sum(sizes)
    shapes = [(rows, cols)] * 4
    if units:
        unit_rows = units[0].shape[1]
        below = cdiv(unit_rows, 16) * 16
        shapes = [(rows + below if way == 2 else rows, cols) for way in range(4)] + [(unit_rows, cols)]

    def body(at_ref, *refs):
        in_refs, out_refs = list(refs[: -len(shapes)]), refs[-len(shapes) :]
        unit_refs = in_refs[len(in_refs) - len(units) :]
        for way in range(4):
            start = 0
            left = list(in_refs)
            for size, group in zip(sizes, groups):
                total = None
                for unused in group:
                    part = left.pop(0)[at_ref[0] ^ way].astype(F32)
                    total = part if total is None else total + part
                out_refs[way][0:rows, start : start + size] = total.astype(BF)
                start += size
        if units:
            high = lax.shift_right_logical(at_ref[0], 1)
            own = sum(ref[high].astype(F32) for ref in unit_refs)
            give = sum(ref[1 - high].astype(F32) for ref in unit_refs)
            out_refs[4][...] = own.astype(BF)
            give = jnp.concatenate([give, jnp.zeros((below - unit_rows, cols), F32)], 0)
            out_refs[2][rows : rows + below, :] = give.astype(BF)

    vmem = pl.BlockSpec(memory_space=pltpu.VMEM)
    arrays = [array for group in groups for array in group] + list(units)
    return pl.pallas_call(
        body,
        in_specs=[pl.BlockSpec(memory_space=pltpu.SMEM)] + [vmem] * len(arrays),
        out_specs=[vmem] * len(shapes),
        out_shape=[jax.ShapeDtypeStruct(shape, BF) for shape in shapes],
        compiler_params=pltpu.CompilerParams(vmem_limit_bytes=VMEM_BYTES),
        cost_estimate=SHORT,
        name="plane_sort",
    )(group_place(), *arrays)


def z_merge(kept, from_1, from_2, from_3):
    rows, cols = kept.shape
    half = rows // 2

    def body(at_ref, kept_ref, one_ref, two_ref, three_ref, keep_ref, give_ref):
        same = kept_ref[...].astype(F32) + two_ref[0:rows, :].astype(F32)
        other = one_ref[...].astype(F32) + three_ref[...].astype(F32)
        for quarter, value in ((at_ref[1], same), (1 - at_ref[1], other)):
            upper, lower = value[:half], value[half:]
            keep_ref[quarter] = jnp.where(at_ref[2] == 0, upper, lower).astype(BF)
            give_ref[quarter] = jnp.where(at_ref[2] == 0, lower, upper).astype(BF)

    vmem = pl.BlockSpec(memory_space=pltpu.VMEM)
    return pl.pallas_call(
        body,
        in_specs=[pl.BlockSpec(memory_space=pltpu.SMEM)] + [vmem] * 4,
        out_specs=[vmem] * 2,
        out_shape=[jax.ShapeDtypeStruct((2, half, cols), BF)] * 2,
        compiler_params=pltpu.CompilerParams(vmem_limit_bytes=VMEM_BYTES),
        cost_estimate=SHORT,
        name="z_merge",
    )(group_place(), kept, from_1, from_2, from_3)


def join_quarters(mine, recv, core_ref, start, size, z_low, core):
    return jnp.where(
        core_ref[2] == core, mine[z_low, :, start : start + size], recv[z_low, :, start : start + size]
    ).astype(F32)


def join_columns(mine, recv, weights, gain, n_matrices):
    rows, cols = mine.shape[1:]
    size = cols // n_matrices

    def body(at_ref, mine_ref, recv_ref, gain_ref, *refs):
        weight_refs, out_refs = refs[: len(weights)], refs[len(weights) :]
        total = jnp.zeros((rows, 1), F32)
        for i in range(n_matrices):
            for z_low in range(2):
                for core in range(2):
                    at = (2 * z_low + core) * size
                    value = join_quarters(mine_ref, recv_ref, at_ref, i * size, size, z_low, core)
                    out_refs[i][:, at : at + size] = value
                    if i < len(weights):
                        product = value * weight_refs[i][:, at : at + size].astype(F32)
                        total = total + jnp.sum(product, axis=1, keepdims=True)
        out_refs[-1][...] = total / gain_ref[...]

    vmem = pl.BlockSpec(memory_space=pltpu.VMEM)
    outs = pl.pallas_call(
        body,
        in_specs=[pl.BlockSpec(memory_space=pltpu.SMEM)] + [vmem] * (3 + len(weights)),
        out_specs=[vmem] * (n_matrices + 1),
        out_shape=[jax.ShapeDtypeStruct((rows, 4 * size), F32)] * n_matrices + [jax.ShapeDtypeStruct((rows, 1), F32)],
        cost_estimate=SHORT,
        name="join_columns",
    )(group_place(), mine, recv, gain.astype(F32)[:, None], *weights)
    return outs[:-1] + [outs[-1][:, 0]] if isinstance(outs, list) else list(outs[:-1]) + [outs[-1][:, 0]]


def join_units(mine, recv, weights, gain, n_blocks):
    rows, both = mine.shape[1:]
    quarter_size = both // 2
    size = 4 * quarter_size // n_blocks

    def body(at_ref, mine_ref, recv_ref, gain_ref, one_weight, two_weight, one_ref, two_ref, total_ref):
        total = jnp.zeros((rows, 1), F32)
        for half, (out_ref, weight_ref) in enumerate(((one_ref, one_weight), (two_ref, two_weight))):
            for block, (quarter, at) in enumerate(unit_blocks(n_blocks)):
                start = half * quarter_size + at * size
                out_ref[:, block * size : (block + 1) * size] = join_quarters(
                    mine_ref, recv_ref, at_ref, start, size, quarter // 2, quarter % 2
                )
            total = total + jnp.sum(out_ref[...] * weight_ref[...].astype(F32), axis=1, keepdims=True)
        total_ref[...] = total / gain_ref[...]

    vmem = pl.BlockSpec(memory_space=pltpu.VMEM)
    one, two, total = pl.pallas_call(
        body,
        in_specs=[pl.BlockSpec(memory_space=pltpu.SMEM)] + [vmem] * 5,
        out_specs=[vmem] * 3,
        out_shape=[jax.ShapeDtypeStruct((rows, 4 * quarter_size), F32)] * 2 + [jax.ShapeDtypeStruct((rows, 1), F32)],
        cost_estimate=SHORT,
        name="join_units",
    )(group_place(), mine, recv, gain.astype(F32)[:, None], *weights)
    return one, two, total[:, 0]


def pair_add(one, two):
    def body(at_ref, one_ref, two_ref, own_ref, give_ref):
        for way, out_ref in enumerate((own_ref, give_ref)):
            at = at_ref[1] ^ way
            out_ref[...] = (one_ref[at].astype(F32) + two_ref[at].astype(F32)).astype(BF)

    vmem = pl.BlockSpec(memory_space=pltpu.VMEM)
    return pl.pallas_call(
        body,
        in_specs=[pl.BlockSpec(memory_space=pltpu.SMEM)] + [vmem] * 2,
        out_specs=[vmem] * 2,
        out_shape=[jax.ShapeDtypeStruct(one.shape[1:], BF)] * 2,
        compiler_params=pltpu.CompilerParams(vmem_limit_bytes=VMEM_BYTES),
        cost_estimate=SHORT,
        name="pair_add",
    )(group_place(), one, two)


def back_project(lefts, weights, transposed=True):
    block = lefts[0].shape[0] // 4
    out = weights[0].shape[0] if transposed else weights[0].shape[1]

    def body(*refs):
        left_refs, weight_refs = refs[: len(lefts)], refs[len(lefts) : 2 * len(lefts)]
        keep_ref, give_ref = refs[2 * len(lefts) :]
        total = None
        for left_ref, weight_ref in zip(left_refs, weight_refs):
            part = (matmul_cols if transposed else matmul)(left_ref[...], weight_ref[...])
            total = part if total is None else total + part
        total = total.astype(BF)
        for i in range(4):
            (keep_ref, give_ref)[i % 2][i // 2] = total[i * block : (i + 1) * block]

    return pl.pallas_call(
        body,
        in_specs=[pl.BlockSpec(memory_space=pltpu.VMEM)] * (2 * len(lefts)),
        out_specs=[pl.BlockSpec(memory_space=pltpu.VMEM)] * 2,
        out_shape=[jax.ShapeDtypeStruct((2, block, out), BF)] * 2,
        compiler_params=pltpu.CompilerParams(vmem_limit_bytes=VMEM_BYTES),
        cost_estimate=SHORT,
        name="back_project",
    )(*lefts, *weights)


def join_four(mine, recv, of_tokens):
    rows, size = mine.shape[1:]
    block = rows // 4

    def body(at_ref, mine_ref, recv_ref, out_ref):
        for z_low in range(2):
            side = at_ref[1] ^ z_low
            for core in range(2):
                at = (2 * z_low + core) * size
                for i in range(4):
                    j = i ^ 1 if of_tokens else i
                    ours = mine_ref[side, i * block : (i + 1) * block]
                    theirs = recv_ref[side, j * block : (j + 1) * block]
                    out_ref[i * block : (i + 1) * block, at : at + size] = jnp.where(at_ref[2] == core, ours, theirs)

    vmem = pl.BlockSpec(memory_space=pltpu.VMEM)
    return pl.pallas_call(
        body,
        in_specs=[pl.BlockSpec(memory_space=pltpu.SMEM)] + [vmem] * 2,
        out_specs=vmem,
        out_shape=jax.ShapeDtypeStruct((rows, 4 * size), mine.dtype),
        compiler_params=pltpu.CompilerParams(vmem_limit_bytes=VMEM_BYTES),
        cost_estimate=SHORT,
        name="join_four",
    )(group_place(), mine, recv)


def branch_back(mine, recv, x_one, gain, g_mine, g_recv, w_out):
    blocks, seg_len, width = x_one.shape
    quarter = width // 4

    def body(at_ref, mine_ref, recv_ref, x_ref, gain_ref, g_ref, g_recv_ref, w_ref, branch_ref, att_ref, own_ref):
        block = pl.program_id(0)
        grad = jnp.where(block % 2 == 0, mine_ref[0], recv_ref[0]).astype(F32)
        passed = jnp.where(block % 2 == 0, g_ref[0], g_recv_ref[0]).astype(F32)
        values = x_ref[0]
        inverse = lax.rsqrt(jnp.mean(values * values, axis=-1, keepdims=True) + EPSILON)
        normed = values * inverse
        scaled = grad * gain_ref[...]
        mean = jnp.mean(scaled * normed, axis=-1, keepdims=True)
        total = passed + inverse * (scaled - normed * mean)
        low = total.astype(BF)
        branch_ref[0] = low
        att_ref[0] = matmul_cols(low, w_ref[...]).astype(BF)

        @pl.when(block == 2 * at_ref[1])
        def own():
            own_ref[...] = total

    pair = pl.BlockSpec((1, seg_len, width), lambda i, at: (i // 2, 0, 0))
    full = pl.BlockSpec((1, seg_len, width), lambda i, at: (i, 0, 0))
    return pl.pallas_call(
        body,
        grid_spec=pltpu.PrefetchScalarGridSpec(
            num_scalar_prefetch=1,
            grid=(blocks,),
            in_specs=[
                pair,
                pair,
                full,
                pl.BlockSpec((1, width), lambda i, at: (0, 0)),
                pair,
                pair,
                pl.BlockSpec((quarter, width), lambda i, at: (2 * at[1] + at[2], 0)),
            ],
            out_specs=[
                full,
                pl.BlockSpec((1, seg_len, quarter), lambda i, at: (i, 0, 0)),
                pl.BlockSpec((seg_len, width), lambda i, at: (0, 0)),
            ],
        ),
        out_shape=[
            jax.ShapeDtypeStruct((blocks, seg_len, width), BF),
            jax.ShapeDtypeStruct((blocks, seg_len, quarter), BF),
            jax.ShapeDtypeStruct((seg_len, width), F32),
        ],
        compiler_params=pltpu.CompilerParams(vmem_limit_bytes=VMEM_BYTES),
        cost_estimate=SHORT,
        name="branch_back",
    )(group_place(), mine, recv, x_one, gain, g_mine, g_recv, w_out)


def add_kernel(one, two):
    def body(one_ref, two_ref, out_ref):
        out_ref[...] = (one_ref[...].astype(F32) + two_ref[...].astype(F32)).astype(BF)

    return pl.pallas_call(
        body,
        in_specs=[pl.BlockSpec(memory_space=pltpu.VMEM)] * 2,
        out_specs=pl.BlockSpec(memory_space=pltpu.VMEM),
        out_shape=jax.ShapeDtypeStruct(one.shape, BF),
        compiler_params=pltpu.CompilerParams(vmem_limit_bytes=VMEM_BYTES),
        cost_estimate=SHORT,
        name="add_kernel",
    )(one, two)


def add_low(one, two):
    return (one.astype(F32) + two.astype(F32)).astype(BF)


def lane_blocks(value):
    return [value[:, i : i + LANES] for i in range(0, value.shape[1], LANES)]


PIECES = ((0, 0), (0, 1), (1, 0), (1, 1), (2, 0), (3, 0), (2, 1))
N_COMMON = 5
N_GROUPS = 4


def forward_kernel(q_ref, k_ref, v_ref, mine_ref, other_ref, *refs):
    key_refs, value_refs = refs[:N_GROUPS], refs[N_GROUPS : 2 * N_GROUPS]
    o_ref, of_ref, p_ref, pl_ref, inv_ref, s_ref, top_ref, total_ref, acc_ref = refs[2 * N_GROUPS :]
    scale = HD ** (-0.5)
    upper = pl.program_id(1) >= 2
    queries = q_ref[0]
    seg_len = queries.shape[0]
    per = key_refs[0].shape[1] // LANES
    first = pl.program_id(1) % 2 == 0

    def bias(at):
        return jnp.where(first, mine_ref[0, at], other_ref[0, at]).astype(F32)

    local_bias = jnp.concatenate([bias(len(PIECES) * per + i) for i in range(cdiv(seg_len, LANES))], 1)
    s_local = jnp.minimum(matmul_cols(queries, k_ref[0]) * scale, local_bias[:, :seg_len])

    def score(t, top):
        group, low = PIECES[t]
        parts = lane_blocks(matmul_cols(queries, key_refs[group][low]) * scale)
        for i in range(per):
            part = jnp.minimum(parts[i], bias(t * per + i))
            s_ref[t, :, i * LANES : (i + 1) * LANES] = part
            top = part if top is None else jnp.maximum(top, part)
        return top

    top = None
    for t in range(N_COMMON):
        top = score(t, top)
    top_ref[...] = top

    @pl.when(upper)
    def more_scores():
        more = top_ref[...]
        for t in range(N_COMMON, len(PIECES)):
            more = score(t, more)
        top_ref[...] = more

    row_max = jnp.maximum(
        jnp.max(s_local, axis=-1, keepdims=True), jnp.max(top_ref[...], axis=-1, keepdims=True)
    )
    e_local = jnp.exp(s_local - row_max)
    low_local = e_local.astype(BF)
    pl_ref[0, 0] = low_local

    def weigh(t, total, acc):
        group, low = PIECES[t]
        expo = jnp.exp(s_ref[t] - row_max)
        for part in lane_blocks(expo):
            total = part if total is None else total + part
        chances = expo.astype(BF)
        p_ref[0, 0, t] = chances
        return total, acc + matmul(chances, value_refs[group][low])

    total, acc = None, matmul(low_local, v_ref[0])
    for t in range(N_COMMON):
        total, acc = weigh(t, total, acc)
    total_ref[...] = total
    acc_ref[...] = acc

    @pl.when(upper)
    def more_values():
        total, acc = total_ref[...], acc_ref[...]
        for t in range(N_COMMON, len(PIECES)):
            total, acc = weigh(t, total, acc)
        total_ref[...] = total
        acc_ref[...] = acc

    row_total = jnp.sum(e_local, axis=-1, keepdims=True) + jnp.sum(total_ref[...], axis=-1, keepdims=True)
    inverse = 1.0 / row_total
    out = acc_ref[...] * inverse
    of_ref[0] = out
    o_ref[0] = out.astype(BF)
    inv_ref[0, 0] = inverse


def backward_local_kernel(do_ref, of_ref, q_ref, k_ref, v_ref, inv_ref, pl_ref, cos_ref, sin_ref, dkv_ref, dq_ref):
    scale = HD ** (-0.5)
    d_out = do_ref[0]
    delta = jnp.sum(d_out.astype(F32) * of_ref[0], axis=-1, keepdims=True)
    chances = pl_ref[0, 0].astype(F32) * inv_ref[0, 0]
    ds = (chances * (matmul_cols(d_out, v_ref[0]) - delta)).astype(BF)
    dq_ref[0] = matmul(ds, k_ref[0])
    dk = matmul_rows(ds, q_ref[0])
    dkv_ref[0, 0] = ((dk * cos_ref[...] - pltpu.roll(dk, HD // 2, 1) * sin_ref[...]) * scale).astype(BF)
    dkv_ref[1, 0] = matmul_rows(chances.astype(BF), d_out).astype(BF)


def backward_kernel(do_ref, of_ref, local_ref, inv_ref, p_ref, cos_ref, sin_ref, *refs):
    key_refs, value_refs = refs[:N_GROUPS], refs[N_GROUPS : 2 * N_GROUPS]
    out_ref, dq_ref = refs[2 * N_GROUPS :]
    scale = HD ** (-0.5)
    upper = pl.program_id(1) >= 2
    d_out = do_ref[0]
    inverse = inv_ref[0, 0]
    delta = jnp.sum(d_out.astype(F32) * of_ref[0], axis=-1, keepdims=True)

    def piece(t, dq):
        group, low = PIECES[t]
        dp = matmul_cols(d_out, value_refs[group][low])
        ds = (p_ref[0, 0, t].astype(F32) * ((dp - delta) * inverse)).astype(BF)
        return dq + matmul(ds, key_refs[group][low])

    dq = local_ref[0]
    for t in range(N_COMMON):
        dq = piece(t, dq)
    dq_ref[...] = dq

    @pl.when(upper)
    def more():
        dq = dq_ref[...]
        for t in range(N_COMMON, len(PIECES)):
            dq = piece(t, dq)
        dq_ref[...] = dq

    dq = dq_ref[...]
    out_ref[0] = ((dq * cos_ref[...] - pltpu.roll(dq, HD // 2, 1) * sin_ref[...]) * scale).astype(BF)


def attention_specs(piece_rows, seg_len):
    head = pl.BlockSpec((1, seg_len, HD), lambda h, r: (r, 0, h))
    piece = pl.BlockSpec((2, piece_rows, HD), lambda h, r: (0, 0, h))
    p_spec = pl.BlockSpec((1, 1, len(PIECES), seg_len, piece_rows), lambda h, r: (r, h, 0, 0, 0))
    pl_spec = pl.BlockSpec((1, 1, seg_len, seg_len), lambda h, r: (r, h, 0, 0))
    inv_spec = pl.BlockSpec((1, 1, seg_len, 1), lambda h, r: (r, h, 0, 0))
    return head, piece, p_spec, pl_spec, inv_spec


def attention_forward(queries, keys, values, mask, other_mask, key_pieces, value_pieces):
    blocks, seg_len, width = queries.shape
    heads = width // HD
    piece_rows = key_pieces[0].shape[1]
    head, piece, p_spec, pl_spec, inv_spec = attention_specs(piece_rows, seg_len)
    return pl.pallas_call(
        forward_kernel,
        grid=(heads, blocks),
        in_specs=[
            head,
            head,
            head,
            pl.BlockSpec((1,) + mask.shape[1:], lambda h, r: (r // 2, 0, 0, 0)),
            pl.BlockSpec((1,) + mask.shape[1:], lambda h, r: (r // 2, 0, 0, 0)),
        ]
        + [piece] * (2 * N_GROUPS),
        out_specs=[head, head, p_spec, pl_spec, inv_spec],
        out_shape=[
            jax.ShapeDtypeStruct(queries.shape, BF),
            jax.ShapeDtypeStruct(queries.shape, F32),
            jax.ShapeDtypeStruct((blocks, heads, len(PIECES), seg_len, piece_rows), BF),
            jax.ShapeDtypeStruct((blocks, heads, seg_len, seg_len), BF),
            jax.ShapeDtypeStruct((blocks, heads, seg_len, 1), F32),
        ],
        scratch_shapes=[
            pltpu.VMEM((len(PIECES), seg_len, piece_rows), F32),
            pltpu.VMEM((seg_len, LANES), F32),
            pltpu.VMEM((seg_len, LANES), F32),
            pltpu.VMEM((seg_len, HD), F32),
        ],
        compiler_params=pltpu.CompilerParams(vmem_limit_bytes=VMEM_BYTES),
        cost_estimate=SHORT,
        name="attention_forward",
    )(queries, keys, values, mask, other_mask, *key_pieces, *value_pieces)


def attention_backward_local(d_out, out_f32, queries, keys, values, inverse, p_local, cosine, sine):
    blocks, seg_len, width = queries.shape
    head, unused, unused, pl_spec, inv_spec = attention_specs(seg_len, seg_len)
    table = pl.BlockSpec((seg_len, HD), lambda h, r: (0, 0))
    return pl.pallas_call(
        backward_local_kernel,
        grid=(width // HD, blocks),
        in_specs=[head, head, head, head, head, inv_spec, pl_spec, table, table],
        out_specs=[pl.BlockSpec((2, 1, seg_len, HD), lambda h, r: (0, r, 0, h)), head],
        out_shape=[
            jax.ShapeDtypeStruct((2, blocks, seg_len, width), BF),
            jax.ShapeDtypeStruct(queries.shape, F32),
        ],
        compiler_params=pltpu.CompilerParams(vmem_limit_bytes=VMEM_BYTES),
        cost_estimate=SHORT,
        name="attention_backward_local",
    )(d_out, out_f32, queries, keys, values, inverse, p_local, cosine, sine)


def attention_backward(d_out, out_f32, dq_local, inverse, p_memory, cosine, sine, key_pieces, value_pieces):
    blocks, seg_len, width = d_out.shape
    heads = width // HD
    piece_rows = key_pieces[0].shape[1]
    head, piece, p_spec, unused, inv_spec = attention_specs(piece_rows, seg_len)
    table = pl.BlockSpec((seg_len, HD), lambda h, r: (0, 0))
    return pl.pallas_call(
        backward_kernel,
        grid=(heads, blocks),
        in_specs=[head, head, head, inv_spec, p_spec, table, table] + [piece] * (2 * N_GROUPS),
        out_specs=head,
        out_shape=jax.ShapeDtypeStruct((blocks, seg_len, width), BF),
        scratch_shapes=[pltpu.VMEM((seg_len, HD), F32)],
        compiler_params=pltpu.CompilerParams(vmem_limit_bytes=VMEM_BYTES),
        cost_estimate=SHORT,
        name="attention_backward",
    )(d_out, out_f32, dq_local, inverse, p_memory, cosine, sine, *key_pieces, *value_pieces)


def allow_local_of(live):
    seg_len = live.shape[-1]
    position = jnp.arange(seg_len, dtype=jnp.int32)
    same = position[None, :] == position[:, None]
    return same[None] | ((position[None, :] < position[:, None])[None] & (live == 1))


def split_heads(value):
    rows, seg_len, width = value.shape
    return value.reshape(rows, seg_len, width // HD, HD)


def stream_forward(queries, keys, values, live, allow, memory):
    scale = HD ** (-0.5)
    q4, k4, v4 = split_heads(queries), split_heads(keys), split_heads(values)
    scores = jnp.einsum("rqhd,rkhd->rhqk", q4, k4, preferred_element_type=F32) * scale
    scores = jnp.where(allow_local_of(live)[:, None], scores, NEG_BIG)
    row_max = jnp.max(scores, axis=-1)
    expo = jnp.exp(scores - row_max[..., None])
    state = (
        row_max,
        jnp.sum(expo, axis=-1),
        jnp.einsum("rhqk,rkhd->rhqd", expo.astype(BF), v4, preferred_element_type=F32),
    )

    def step(running, item):
        row_max, row_total, acc = running
        block, allowed = item
        k3 = block[0].reshape(block.shape[1], -1, HD)
        v3 = block[1].reshape(block.shape[1], -1, HD)
        scores = jnp.einsum("rqhd,khd->rhqk", q4, k3, preferred_element_type=F32) * scale
        scores = jnp.where(allowed[:, None] > 0, scores, NEG_BIG)
        new_max = jnp.maximum(row_max, jnp.max(scores, axis=-1))
        shrink = jnp.exp(row_max - new_max)
        expo = jnp.exp(scores - new_max[..., None])
        acc = acc * shrink[..., None] + jnp.einsum(
            "rhqk,khd->rhqd", expo.astype(BF), v3, preferred_element_type=F32
        )
        return (new_max, row_total * shrink + jnp.sum(expo, axis=-1), acc), None

    (row_max, row_total, acc), unused = lax.scan(step, state, (memory, allow))
    out = (acc / row_total[..., None]).transpose(0, 2, 1, 3).reshape(queries.shape)
    return out.astype(BF), out, row_max + jnp.log(row_total)


def stream_backward(d_out, out_f32, queries, keys, values, live, log_total, allow, memory, cosine, sine):
    scale = HD ** (-0.5)
    q4, k4, v4, d4 = split_heads(queries), split_heads(keys), split_heads(values), split_heads(d_out)
    delta = jnp.sum(d4.astype(F32) * split_heads(out_f32), axis=-1).transpose(0, 2, 1)
    scores = jnp.einsum("rqhd,rkhd->rhqk", q4, k4, preferred_element_type=F32) * scale
    scores = jnp.where(allow_local_of(live)[:, None], scores, NEG_BIG)
    chances = jnp.exp(scores - log_total[..., None])
    dp = jnp.einsum("rqhd,rkhd->rhqk", d4, v4, preferred_element_type=F32)
    ds = (chances * (dp - delta[..., None])).astype(BF)
    dq = jnp.einsum("rhqk,rkhd->rqhd", ds, k4, preferred_element_type=F32)
    dk = jnp.einsum("rhqk,rqhd->rkhd", ds, q4, preferred_element_type=F32)
    dv = jnp.einsum("rhqk,rqhd->rkhd", chances.astype(BF), d4, preferred_element_type=F32)

    def step(running, item):
        block, allowed = item
        k3 = block[0].reshape(block.shape[1], -1, HD)
        v3 = block[1].reshape(block.shape[1], -1, HD)
        scores = jnp.einsum("rqhd,khd->rhqk", q4, k3, preferred_element_type=F32) * scale
        scores = jnp.where(allowed[:, None] > 0, scores, NEG_BIG)
        chances = jnp.exp(scores - log_total[..., None])
        dp = jnp.einsum("rqhd,khd->rhqk", d4, v3, preferred_element_type=F32)
        ds = (chances * (dp - delta[..., None])).astype(BF)
        return running + jnp.einsum("rhqk,khd->rqhd", ds, k3, preferred_element_type=F32), None

    dq, unused = lax.scan(step, dq, (memory, allow))

    def back(value):
        turned = rope_heads(value.reshape((-1,) + value.shape[2:]), jnp.tile(cosine, (value.shape[0], 1)), -jnp.tile(sine, (value.shape[0], 1)))
        return (turned * scale).reshape(queries.shape).astype(BF)

    return jnp.stack([back(dq), back(dk), dv.reshape(queries.shape).astype(BF)])


def local(
    layer_input,
    live,
    knn_index,
    mem_keys,
    mem_values,
    gain_attn,
    w_query,
    w_key,
    w_value,
    w_out,
    gain_ffn,
    w_gate,
    w_up,
    w_down,
    cotangent,
):
    seg_len, width = layer_input.shape[1:]
    quarter = width // 4
    n_seg = lax.axis_size("seg")
    n_devices = n_seg * lax.axis_size("rep")
    tokens = seg_len * n_seg
    n_high = n_seg // 4
    x, low, high, y, core = place()
    use_kernel = n_high <= KERNEL_HIGH
    kv_rows = 2 * seg_len
    group_tokens = 4 * seg_len

    def by_quarter(value):
        return [value[:, i * quarter : (i + 1) * quarter] for i in range(4)]

    gains = jnp.concatenate(
        [gain_attn[:, None], gain_ffn[:, None], jnp.zeros((gain_attn.shape[0], LANES - 2), BF)], 1
    )
    stacked = [by_quarter(w) for w in (w_query, w_key, w_value, w_out)]
    qo = jnp.stack([jnp.concatenate([s[i] for s in stacked] + [gains], 1) for i in range(4)])

    def core_quarters(value, side):
        return jnp.stack([cut(value, side * quarter, quarter), cut(value, (2 + side) * quarter, quarter)])

    def core_memory(side):
        return jnp.stack([core_quarters(mem_keys[0], side), core_quarters(mem_values[0], side)])

    coded = knn_index[0] * 2 + live[0][:, None]
    qo = qo.reshape(2, 2, -1, qo.shape[-1])
    qo_keep, qo_give = halves(qo, 1, core)
    kv_keep, kv_give = core_memory(core), core_memory(1 - core)
    qo_recv, kv_recv, coded_recv = flip_core(qo_give), flip_core(kv_give), flip_z(coded)
    qo_keep, kv_keep, coded, qo_recv, kv_recv, coded_recv, w_gate_, w_up_ = fence(
        qo_keep, kv_keep, coded, qo_recv, kv_recv, coded_recv, w_gate, w_up
    )

    qo_keep, qo_give = halves(ordered(qo_keep, qo_recv, core, 1), 0, low)
    kv_keep, kv_give = halves(ordered(kv_keep, kv_recv, core, 2), 1, low)
    coded = ordered(coded[None], coded_recv[None], low, 0)
    kv_recv = flip_z(kv_give)
    qo_near = flip_z(qo_give)
    down_w = w_down[None, None, None, None]
    x_own = layer_input[0]
    gate_up = split_units(w_gate_, w_up_, n_devices).reshape(2, 2, 2, -1, w_gate.shape[1] // 4)

    def places_of(codes, row_core):
        picks = lax.shift_right_arithmetic(codes, 1)
        pair = picks >= tokens
        slot = jnp.where(pair, picks - tokens, picks)
        slot_seg = slot // seg_len
        kv_row = jnp.bitwise_xor(pair.astype(jnp.int32), row_core)
        return picks, slot_seg, kv_row * seg_len + (slot - slot_seg * seg_len)

    split = 3 * quarter
    g_own = cotangent[0]
    cosine, sine = rope_tables(seg_len)
    if use_kernel:
        qo_far, qo_side = flip(qo_keep, "seg", 4), flip(qo_give, "seg", 6)
        picks, slot_seg, within = places_of(coded, core)
        slot_x, slot_low = slot_seg % 2, (slot_seg // 2) % 2
        same_x = slot_x == x
        in_group = jnp.where(same_x, 5, 4 + 2 * slot_low)
        before = jnp.where(same_x, 0, 2) + slot_low
        piece_no = jnp.where(slot_seg // 4 == high, in_group, before)
        columns = jnp.where(picks >= 0, piece_no * kv_rows + within, -1)
        live_two = jnp.bitwise_and(coded[:, :, 0], 1)[:, None, :]
        live_two = jnp.pad(live_two, ((0, 0), (0, 0), (0, cdiv(seg_len, LANES) * LANES - seg_len)))
        down_recv = flip(down_w, "seg", 4)
        (
            qo_keep, qo_near, qo_far, qo_side, kv_keep, kv_recv, x_own, gate_up, columns, live_two, down_w, down_recv
        ) = fence(
            qo_keep, qo_near, qo_far, qo_side, kv_keep, kv_recv, x_own, gate_up, columns, live_two, down_w, down_recv
        )

        pieces = ordered(kv_keep[:, None], kv_recv[:, None], low, 1)
        own_k, own_v = pieces[0], pieces[1]
        near = ordered(qo_keep[None, None], qo_near[None, None], low, 1)
        far = ordered(qo_far[None, None], qo_side[None, None], low, 1)
        qo = ordered(near, far, high, 0)[:, :, None, None]
        qo_a, qo_b = qo[..., :split], qo[..., split:]
        up_high = [(i, i + 4) for i in range(n_seg - 4)]

        def cross(value):
            return lax.ppermute(value, "seg", up_high)

        cross_k, side_k = cross(own_k), flip_x(own_k)
        a_recv, b_recv = flip_x(qo_a), flip_y(qo_b)
        x_recv = flip_z(x_own)
        gu_keep, gu_give = halves(gate_up, 1, core)
        gu_recv = flip_core(gu_give)
        mask = build_mask(columns, live_two, len(PIECES) * kv_rows // LANES)
        qo_a, qo_b, a_recv, b_recv, cross_k, side_k, own_v, x_own, x_recv, gu_keep, gu_recv, mask, down_w, down_recv = fence(
            qo_a, qo_b, a_recv, b_recv, cross_k, side_k, own_v, x_own, x_recv, gu_keep, gu_recv, mask, down_w, down_recv
        )

        cross_v, cross_side_k = cross(own_v), flip_x(cross_k)
        qo_a, qo_b = ordered(qo_a, a_recv, x, 2), ordered(qo_b, b_recv, y, 3)
        a_recv, b_recv = flip_y(qo_a), flip_x(qo_b)
        gu_keep, gu_give = halves(ordered(gu_keep, gu_recv, core, 2), 0, low)
        gu_recv = flip_z(gu_give)
        x_two = ordered(x_own[None], x_recv[None], low, 0)
        x_recv = flip_core(x_two)
        qo_a, qo_b, a_recv, b_recv, cross_v, cross_side_k, own_v, gu_keep, gu_recv, x_two, x_recv, mask, down_w, down_recv = fence(
            qo_a, qo_b, a_recv, b_recv, cross_v, cross_side_k, own_v, gu_keep, gu_recv, x_two, x_recv, mask, down_w, down_recv
        )

        cross_side_v, side_v = flip_x(cross_v), flip_x(own_v)
        other_mask = flip_core(mask)
        w_a, w_b = flat(ordered(qo_a, a_recv, y, 3)), flat(ordered(qo_b, b_recv, x, 2))
        gate_up = ordered(gu_keep[:, None], gu_recv[:, None], low, 1)[:, None]
        gu_recv = flip(gate_up, "seg", 4)
        down_w = ordered(down_w, down_recv, high, 0)
        down_recv = flip_y(down_w)
        x_all = jnp.stack([x_two, x_recv], 1).reshape(4, seg_len, width)
        queries, keys, values, h_one, inv_one = project(x_all, w_a, w_b, cosine, sine)
        wo_near = w_b[:, :quarter]
        queries, keys, values, cross_side_v, side_v, gate_up, gu_recv, down_w, down_recv, wo_near, g_own, other_mask = fence(
            queries, keys, values, cross_side_v, side_v, gate_up, gu_recv, down_w, down_recv, wo_near, g_own, other_mask
        )

        key_pieces = (cross_k, cross_side_k, side_k, own_k)
        value_pieces = (cross_v, cross_side_v, side_v, own_v)
        gate, upw = [ordered(gate_up[i], gu_recv[i], high, 0)[:, :, None, None] for i in range(2)]
        down_w = ordered(down_w, down_recv, y, 3)
        down_a, down_b = down_w[..., : width // 2], down_w[..., width // 2 :]
        g_recv, u_recv, a_recv, wo_far = flip_x(gate), flip_y(upw), flip_x(down_a), flip_z(wo_near)
        out_low, out_f32, p_memory, p_local, inverse = attention_forward(
            queries, keys, values, mask, other_mask, key_pieces, value_pieces
        )
        out_low, gate, upw, g_recv, u_recv, down_a, a_recv, down_b, wo_near, wo_far, g_own = fence(
            out_low, gate, upw, g_recv, u_recv, down_a, a_recv, down_b, wo_near, wo_far, g_own
        )
    else:
        qo = gather_high(ordered(qo_keep[None], qo_near[None], low, 0)[None, :, None, None])
        kv = ordered(kv_keep[:, None], kv_recv[:, None], low, 1)
        w_a, w_b = flat(gather_y(gather_x(qo[..., :split]))), flat(gather_x(gather_y(qo[..., split:])))
        x_all = all_blocks(two_rows(x_own))
        gu_keep, gu_give = halves(gate_up, 1, core)
        gu_keep, gu_give = halves(ordered(gu_keep, flip_core(gu_give), core, 2), 0, low)
        gate, upw = gather_high_pair(ordered(gu_keep[:, None], flip_z(gu_give)[:, None], low, 1))
        down_w = gather_y(gather_high(down_w))
        down_a, down_b = down_w[..., : width // 2], down_w[..., width // 2 :]
        coded = all_blocks(coded)
        row_core = jnp.bitwise_xor(core, jnp.arange(4, dtype=jnp.int32) % 2)[:, None, None]
        picks, slot_seg, within = places_of(coded, row_core)
        live_all = jnp.bitwise_and(coded[:, :, 0], 1)[:, None, :]
        columns = jnp.where(picks >= 0, slot_seg * kv_rows + within, n_seg * kv_rows)
        blocks_at = jnp.arange(4)[:, None, None]
        queries_at = jnp.arange(seg_len)[None, :, None]
        allow = jnp.zeros((4, seg_len, n_seg * kv_rows), BF).at[blocks_at, queries_at, columns].set(1.0, mode="drop")
        allow = allow.reshape(4, seg_len, n_seg, kv_rows).transpose(2, 0, 1, 3)
        memory = jnp.swapaxes(kv, 0, 1)[None, :, None]
        memory = gather_x(gather_high(memory)).reshape(n_seg, 2, kv_rows, quarter)
        queries, keys, values, h_one, inv_one = project(x_all, w_a, w_b, cosine, sine)
        wo_near = w_b[:, :quarter]
        out_low, out_f32, log_total = stream_forward(queries, keys, values, live_all, allow, memory)
        g_recv, u_recv, a_recv, wo_far = flip_x(gate), flip_y(upw), flip_x(down_a), flip_z(wo_near)

    h_one = h_one.reshape(group_tokens, width)
    inv_one = inv_one.reshape(group_tokens, 1)
    x_float = x_all.reshape(group_tokens, width).astype(F32)
    g_attn = w_b[:, quarter].astype(F32)
    g_ffn = w_b[:, quarter + 1].astype(F32)
    att_near = out_low.reshape(group_tokens, quarter)
    att_far = flip_z(att_near)
    gate, upw = ordered(gate, g_recv, x, 2), ordered(upw, u_recv, y, 3)
    g_recv, u_recv = flip_y(gate), flip_x(upw)
    wo_both = jnp.stack([wo_near, wo_far])
    wo_recv = flip_core(wo_both)
    g_far = flip_z(g_own)
    wo = join_four(wo_both, wo_recv, False)
    att_near, att_far, gate, upw, g_recv, u_recv, down_b, wo, g_own, g_far = fence(
        att_near, att_far, gate, upw, g_recv, u_recv, down_b, wo, g_own, g_far
    )

    att_both = jnp.stack([att_near, att_far])
    att_recv = flip_core(att_both)
    down_recv = flip_x(down_b)
    g_two = ordered(g_own[None], g_far[None], low, 0)
    g_recv_core = flip_core(g_two)
    wg, wu = flat(ordered(gate, g_recv, y, 3)), flat(ordered(upw, u_recv, x, 2))
    attended = join_four(att_both, att_recv, True)
    x_one = x_float + matmul(attended, wo)
    h_two_f, inv_two = norm_forward(x_one, g_ffn)
    h_two = h_two_f.astype(BF)
    gate_out = matmul(h_two, wg)
    up_out = matmul(h_two, wu)
    sigma = jax.nn.sigmoid(gate_out)
    swish = gate_out * sigma
    hidden = (swish * up_out).astype(BF)
    grad_out = jnp.stack([g_two, g_recv_core], 1).reshape(group_tokens, width)

    down_b, hidden = fence(down_b, hidden)
    wd = jnp.concatenate([flat(ordered(down_a, a_recv, x, 2)), flat(ordered(down_b, down_recv, x, 2))], 1)
    d_hidden = matmul_cols(grad_out, wd)
    d_gate = (d_hidden * up_out * sigma * (1.0 + gate_out * (1.0 - sigma))).astype(BF)
    d_up = (d_hidden * swish).astype(BF)
    sums_keep, sums_give = back_project([d_gate, d_up], [wg, wu])
    sums = add_low(sums_keep, flip_core(sums_give))
    sums, hidden, h_two, d_gate, d_up, wd = fence(sums, hidden, h_two, d_gate, d_up, wd)

    far_sums = flip_z(sums)
    (keep_g, give_g), (keep_u, give_u) = gradient((h_two, [d_gate], "x", None), (h_two, [d_up], "y", None))
    keep_g, give_g, keep_u, give_u, hidden, wd = fence(keep_g, give_g, keep_u, give_u, hidden, wd)
    recv_g, recv_u = flip_x(give_g), flip_y(give_u)
    down_keep, down_give = back_project([hidden], [wd], False)
    down_recv = flip_core(down_give)
    keep_wd, give_wd = gradient_units(hidden, grad_out)
    sums, far_sums, keep_g, keep_u, recv_g, recv_u, down_keep, down_recv, keep_wd, give_wd = fence(
        sums, far_sums, keep_g, keep_u, recv_g, recv_u, down_keep, down_recv, keep_wd, give_wd
    )

    own = 2 * low * seg_len
    summed = add_kernel(sums, far_sums)
    summed_recv = flip_core(summed)
    d_branch, d_att, d_x_own = branch_back(
        summed,
        summed_recv,
        x_one.reshape(4, seg_len, width),
        g_ffn[None],
        g_two,
        g_recv_core,
        wo,
    )
    d_branch = d_branch.reshape(group_tokens, width)
    keep_g, keep_u, recv_g, recv_u, d_att, d_branch, down_keep, down_recv = fence(
        keep_g, keep_u, recv_g, recv_u, d_att, d_branch, down_keep, down_recv
    )

    keep_g, give_g = split_sums(keep_g, recv_g, "y")
    keep_u, give_u = split_sums(keep_u, recv_u, "x")
    down_own, down_give = pair_add(down_keep, down_recv)
    w_thirds = [w_a[:, i * quarter : (i + 1) * quarter] for i in range(3)]
    if use_kernel:
        recv_g, recv_u = flip_y(give_g), flip_x(give_u)
        down_recv = flip_z(down_give)
        d_kv, dq_local = attention_backward_local(
            d_att, out_f32, queries, keys, values, inverse, p_local, cosine, sine
        )
        d_kv = d_kv.reshape(2, group_tokens, quarter)
        (keep_kv, give_kv), (keep_wo, give_wo) = gradient(
            (h_one, [d_kv[0], d_kv[1]], "y", None), (attended, [d_branch], "y", quarter)
        )
        give_kvo = jnp.concatenate([give_kv, give_wo], -1)
        keep_kvo = jnp.concatenate([keep_kv, keep_wo], -1)
        keep_kvo, give_kvo, keep_g, recv_g, keep_u, recv_u, dq_local, keep_wd, give_wd, down_own, down_recv = fence(
            keep_kvo, give_kvo, keep_g, recv_g, keep_u, recv_u, dq_local, keep_wd, give_wd, down_own, down_recv
        )
        gu_parts = plane_sort((keep_g, recv_g), (keep_u, recv_u))
        recv_kvo = flip_y(give_kvo)
        gu_flips = z_flips(gu_parts)
        recv_wd = flip_x(give_wd)
        d_q = attention_backward(
            d_att, out_f32, dq_local, inverse, p_memory, cosine, sine, key_pieces, value_pieces
        )
        d_q, keep_kvo = fence(d_q, keep_kvo)

        d_q = d_q.reshape(group_tokens, quarter)
        ((keep_q, *give_q),) = gradient((h_one, [d_q], "xy", None))
        keep_q, give_q, d_q, keep_kvo, recv_kvo, keep_wd, recv_wd, gu_kept, gu_flips = fence(
            keep_q, give_q, d_q, keep_kvo, recv_kvo, keep_wd, recv_wd, gu_parts[0], gu_flips
        )
        recv_q = plane_flips(give_q)
        keep_kvo, give_kvo = split_sums(keep_kvo, recv_kvo, "x")
        keep_wd, give_wd = split_sums(
            keep_wd.reshape((-1,) + keep_wd.shape[2:]), recv_wd.reshape((-1,) + keep_wd.shape[2:]), "y"
        )
        recv_wd = flip_y(give_wd)
        recv_kvo = flip_x(give_kvo)
        d_h_keep, d_h_give = back_project([d_q, d_kv[0], d_kv[1]], w_thirds)
        gu_keep, gu_give = z_merge(gu_kept, *gu_flips)
        keep_q, recv_q, keep_kvo, recv_kvo, keep_wd, recv_wd, d_h_keep, d_h_give, gu_keep, gu_give = fence(
            keep_q, recv_q, keep_kvo, recv_kvo, keep_wd, recv_wd, d_h_keep, d_h_give, gu_keep, gu_give
        )
        d_h_recv = flip_core(d_h_give)
        *parts, wd_own = plane_sort((keep_q,) + tuple(recv_q), (keep_kvo, recv_kvo), units=(keep_wd, recv_wd))
        flips = z_flips(parts)
        d_h_own, d_h_give = pair_add(d_h_keep, d_h_recv)
        d_h_recv = flip_z(d_h_give)
        gu_recv = flip_core(gu_give)
        sum_wg, sum_wu, grad_g_ffn = join_units(gu_keep, gu_recv, (w_gate, w_up), gain_ffn, n_devices)
        kept, flips, d_h_own, d_h_recv, wd_own, sum_wg, sum_wu = fence(
            parts[0], flips, d_h_own, d_h_recv, wd_own, sum_wg, sum_wu
        )
        qkvo_keep, qkvo_give = z_merge(kept, *flips)
        qkvo_recv = flip_core(qkvo_give)
        wd_recv = flips[1][kept.shape[0] : kept.shape[0] + wd_own.shape[0]]
        sum_wd = wd_own.astype(F32) + wd_recv.astype(F32)
    else:
        down_recv = flip_z(down_give)
        recv_wd = flip_x(give_wd)
        d_q, *d_kv = stream_backward(
            d_att, out_f32, queries, keys, values, live_all, log_total, allow, memory, cosine, sine
        ).reshape(3, group_tokens, quarter)

        def by_chip(value):
            return value.reshape(n_high, 2, -1, value.shape[-1])

        (keep_qkv, *give_qkv), (keep_wo, *give_wo) = gradient(
            (h_one, [d_q, d_kv[0], d_kv[1]], "xy", None), (attended, [d_branch], "xy", quarter)
        )
        plane_gu = [add_low(keep_g, flip_y(give_g)), add_low(keep_u, flip_x(give_u))]
        z_gu = z_plain(by_chip(jnp.concatenate(plane_gu, -1)))
        plane_qkvo = [add_all(keep_qkv, *plane_flips(give_qkv)), add_all(keep_wo, *plane_flips(give_wo))]
        z_qkvo = z_plain(by_chip(jnp.concatenate(plane_qkvo, -1)))
        (gu_keep, gu_give), (qkvo_keep, qkvo_give) = core_halves(z_gu), core_halves(z_qkvo)
        qkvo_recv, gu_recv = flip_core(qkvo_give), flip_core(gu_give)
        keep_wd, give_wd = halves(add_low(keep_wd, recv_wd), 1, y)
        recv_wd = flip_y(give_wd)
        d_h_keep, d_h_give = back_project([d_q, d_kv[0], d_kv[1]], w_thirds)
        d_h_own, d_h_give = pair_add(d_h_keep, flip_core(d_h_give))
        d_h_recv = flip_z(d_h_give)
        sum_wd = reduce_high(add_low(keep_wd, recv_wd)[:, None])[0].astype(F32)
        sum_wg, sum_wu, grad_g_ffn = join_units(gu_keep, gu_recv, (w_gate, w_up), gain_ffn, n_devices)
    layer_output = (cut(x_one, own, seg_len, 0) + down_own.astype(F32) + down_recv.astype(F32)).astype(BF)
    sum_q, sum_k, sum_v, sum_o, grad_g_attn = join_columns(
        qkvo_keep, qkvo_recv, (w_query, w_key, w_value), gain_attn, 4
    )
    d_h_one = d_h_own.astype(F32) + d_h_recv.astype(F32)
    x_own = cut(x_float, own, seg_len, 0)
    d_x_first, unused = norm_backward(x_own, cut(inv_one, own, seg_len, 0), g_attn, d_h_one)
    grad_x = (d_x_own + d_x_first).astype(BF)
    return (
        layer_output[None],
        grad_x[None],
        grad_g_attn,
        sum_q,
        sum_k,
        sum_v,
        sum_o,
        grad_g_ffn,
        sum_wg,
        sum_wu,
        sum_wd,
    )


def solution(mesh):
    tokens = P("rep", "seg", None)
    vector = P(("seg", "rep"))
    matrix = P(("seg", "rep"), None)
    return jax.shard_map(
        local,
        mesh=mesh,
        in_specs=(
            tokens,
            P("rep", "seg"),
            tokens,
            tokens,
            tokens,
            vector,
            matrix,
            matrix,
            matrix,
            matrix,
            vector,
            matrix,
            matrix,
            matrix,
            tokens,
        ),
        out_specs=(tokens, tokens, vector, matrix, matrix, matrix, matrix, vector, matrix, matrix, matrix),
        check_vma=False,
    )
```

```python
import jax
import jax.numpy as jnp
from jax import lax
from jax.experimental import pallas as pl
from jax.experimental.pallas import tpu as pltpu
from jax.sharding import PartitionSpec as P

H = 8
HD = 128
EPSILON = 1e-05
NEG_BIG = -1e30
POS_BIG = 1e30
ROPE_BASE = 10000.0
LANES = 128
KERNEL_HIGH = 2
LOG2_E = 1.4426950408889634
VMEM_BYTES = 44 * 1024 * 1024

SHORT = pl.CostEstimate(flops=1000, bytes_accessed=1000, transcendentals=0)

BF = jnp.bfloat16
F32 = jnp.float32


def cdiv(a, b):
    return -(-a // b)


def flip(value, axis, bit):
    count = lax.axis_size(axis)
    return lax.ppermute(value, axis, [(i, i ^ bit) for i in range(count)])


def flip_core(value):
    return flip(value, "rep", 1)


def flip_y(value):
    return flip(value, "rep", 2)


def flip_x(value):
    return flip(value, "seg", 1)


def flip_z(value):
    return flip(value, "seg", 2)


def ordered(mine, other, bit, axis):
    first = jnp.where(bit == 0, mine, other)
    second = jnp.where(bit == 0, other, mine)
    return jnp.concatenate([first, second], axis)


def pick(value, index, axis):
    return lax.dynamic_index_in_dim(value, index, axis, keepdims=False)


def cut(value, start, size, axis=-1):
    return lax.dynamic_slice_in_dim(value, start, size, axis % value.ndim)


def fence(*values):
    return lax.optimization_barrier(values)


def place():
    seg = lax.axis_index("seg")
    rep = lax.axis_index("rep")
    return seg % 2, (seg // 2) % 2, seg // 4, rep // 2, rep % 2


def high_bits():
    bit = 4
    out = []
    while bit < lax.axis_size("seg"):
        out.append(bit)
        bit *= 2
    return out


def gather_high(cur):
    seg = lax.axis_index("seg")
    for bit in high_bits():
        cur = ordered(cur, flip(cur, "seg", bit), (seg // bit) % 2, 0)
    return cur


def gather_x(cur):
    return ordered(cur, flip_x(cur), place()[0], 2)


def gather_y(cur):
    return ordered(cur, flip_y(cur), place()[3], 3)


def gather_high_pair(cur):
    seg = lax.axis_index("seg")
    cur = cur[:, None]
    bits = high_bits()
    for bit in bits[:-1]:
        cur = ordered(cur, flip(cur, "seg", bit), (seg // bit) % 2, 1)
    recv = flip(cur, "seg", bits[-1])
    side = (seg // bits[-1]) % 2
    return [ordered(cur[i], recv[i], side, 0)[:, :, None, None] for i in range(2)]


def flat(cur):
    return cur.reshape(-1, cur.shape[-1])


def halve(value, axis_name, bit, side, axis):
    recv = flip(pick(value, 1 - side, axis), axis_name, bit)
    kept = pick(value, side, axis)
    return (kept.astype(F32) + recv.astype(F32)).astype(BF)


def plane_shape(value, low):
    high = lax.axis_size("seg") // 4
    return value.reshape(high, low, 2, -1, value.shape[-1])


def halves(cur, axis, side):
    return pick(cur, side, axis), pick(cur, 1 - side, axis)


def plane_flips(parts):
    n_rep = lax.axis_size("rep")
    count = lax.axis_size("seg") * n_rep
    far = [(i, i ^ n_rep ^ 2) for i in range(count)]
    return flip_x(parts[0]), flip_y(parts[1]), lax.ppermute(parts[2], ("seg", "rep"), far)


def add_all(first, *others):
    total = first.astype(F32)
    for other in others:
        total = total + other.astype(F32)
    return total.astype(BF)


def z_flips(parts):
    return flip_z(parts[1]), flip(parts[2], "seg", 4), flip(parts[3], "seg", 6)


def z_plain(cur):
    low = place()[1]
    sums = reduce_high(cur)
    return ordered(pick(sums, low, 0)[None], flip_z(pick(sums, 1 - low, 0))[None], low, 0)


def reduce_high(cur):
    seg = lax.axis_index("seg")
    for bit in reversed(high_bits()):
        cur = cur.reshape((2, cur.shape[0] // 2) + cur.shape[1:])
        cur = halve(cur, "seg", bit, (seg // bit) % 2, 0)
    return cur[0]


def trade_core(quarters):
    core = place()[4]
    low, unused, rows, cols = 2, 2, quarters.shape[1], quarters.shape[2]
    four = quarters.reshape(2, 2, rows, cols)
    return ordered(pick(four, core, 1), flip_core(pick(four, 1 - core, 1)), core, 1)


def trade_z(halves):
    low = place()[1]
    return ordered(pick(halves, low, 0)[None], flip_z(pick(halves, 1 - low, 0))[None], low, 0)


def gather_z_four(halves):
    seg = lax.axis_index("seg")
    low = (seg // 2) % 2
    keep, give = pick(halves, low, 0)[None, None], pick(halves, 1 - low, 0)[None, None]
    near = ordered(keep, flip(give, "seg", 2), low, 1)
    far = ordered(flip(keep, "seg", 4), flip(give, "seg", 6), low, 1)
    return ordered(near, far, (seg // 4) % 2, 0)[:, :, None, None]


def start_gather(traded):
    return traded[None, :, None, None]


def core_halves(mine):
    core = place()[4]
    four = mine.reshape(2, 2, mine.shape[1] // 2, mine.shape[2])
    return halves(four, 1, core)


def all_blocks(by_low):
    both = jnp.stack([by_low, flip_core(by_low)], 1)
    return both.reshape((-1,) + by_low.shape[1:])


def two_rows(value):
    return ordered(value[None], flip_z(value)[None], place()[1], 0)


def core_parts(part):
    blocks = part.reshape((2, 2, part.shape[0] // 4) + part.shape[1:])
    return blocks[:, 0].astype(BF), blocks[:, 1].astype(BF)


def core_sums(part):
    blocks = part.reshape((2, 2, part.shape[0] // 4) + part.shape[1:])
    return (blocks[:, 0] + flip_core(blocks[:, 1].astype(BF)).astype(F32)).astype(BF)


def own_sums(sums):
    low = place()[1]
    return pick(sums, low, 0).astype(F32) + flip_z(pick(sums, 1 - low, 0)).astype(F32)


def z_sums(sums):
    return (sums.astype(F32) + flip_z(sums).astype(F32)).astype(BF)


def both_cores(sums):
    return jnp.stack([sums, flip_core(sums)], 1).astype(F32)


def unit_blocks(n_blocks):
    order = []
    for block in range(n_blocks):
        high, low, rest, core = block // 16, (block // 8) % 2, (block // 2) % 4, block % 2
        order.append((low * 2 + core, high * 4 + rest))
    return order


def split_units(one, two, n_blocks):
    rows, total = one.shape
    size = total // n_blocks

    def body(one_ref, two_ref, out_ref):
        for half, in_ref in enumerate((one_ref, two_ref)):
            for block, (quarter, at) in enumerate(unit_blocks(n_blocks)):
                out_ref[quarter, half * rows : (half + 1) * rows, at * size : (at + 1) * size] = in_ref[
                    :, block * size : (block + 1) * size
                ]

    return pl.pallas_call(
        body,
        out_shape=jax.ShapeDtypeStruct((4, 2 * rows, total // 4), one.dtype),
        cost_estimate=SHORT,
        name="split_units",
    )(one, two)


def matmul(left, right):
    return jnp.dot(left, right, preferred_element_type=F32)


def matmul_rows(left, right):
    return lax.dot_general(left, right, (((0,), (0,)), ((), ())), preferred_element_type=F32)


def matmul_cols(left, right):
    return lax.dot_general(left, right, (((1,), (1,)), ((), ())), preferred_element_type=F32)


def norm_forward(values, gain):
    inverse = lax.rsqrt(jnp.mean(values * values, axis=-1, keepdims=True) + EPSILON)
    return (values * inverse * gain, inverse)


def norm_backward(values, inverse, gain, grad_out):
    normed = values * inverse
    scaled = grad_out * gain
    grad_values = inverse * (scaled - normed * jnp.mean(scaled * normed, axis=-1, keepdims=True))
    return (grad_values, normed)


def rope_tables(seg_len):
    position = jnp.arange(seg_len).astype(F32)
    freqs = ROPE_BASE ** (-(2.0 * jnp.arange(HD // 2).astype(F32)) / HD)
    angle = position[:, None] * freqs[None, :]
    cosine, sine = jnp.cos(angle), jnp.sin(angle)
    return (jnp.concatenate([cosine, cosine], -1), jnp.concatenate([-sine, sine], -1))


def rope_heads(values, cosine, sine):
    half = HD // 2
    swapped = jnp.concatenate([values[..., half:], values[..., :half]], -1)
    return values * cosine[:, None, :] + swapped * sine[:, None, :]


def mask_kernel(n_cols, cols_ref, live_ref, out_ref, scratch):
    queries = cols_ref.shape[1]
    picks = cols_ref[0]
    pad = scratch.shape[0]
    high = lax.shift_right_arithmetic(picks, 7)
    low = jnp.bitwise_and(picks, LANES - 1)
    iota_high = lax.broadcasted_iota(jnp.int32, (pad, picks.shape[1]), 0)
    iota_low = lax.broadcasted_iota(jnp.int32, (LANES, picks.shape[1]), 0)
    for i in range(queries):
        hot_high = jnp.where(iota_high == high[i : i + 1, :], 1.0, 0.0).astype(BF)
        hot_low = jnp.where(iota_low == low[i : i + 1, :], 1.0, 0.0).astype(BF)
        scratch[:, i, :] = matmul_cols(hot_high, hot_low)
    out_ref[0, 0:n_cols] = jnp.where(scratch[0:n_cols] > 0.5, POS_BIG, NEG_BIG).astype(BF)
    row = lax.broadcasted_iota(jnp.int32, (queries, LANES), 0) + pl.program_id(1) * queries
    for part in range(out_ref.shape[1] - n_cols):
        col = lax.broadcasted_iota(jnp.int32, (queries, LANES), 1) + part * LANES
        live = live_ref[0, :, part * LANES : (part + 1) * LANES]
        allow = (col == row) | ((col < row) & (live == 1))
        out_ref[0, n_cols + part] = jnp.where(allow, POS_BIG, NEG_BIG).astype(BF)


def build_mask(columns, live, n_cols):
    rows, queries, picks = columns.shape
    block = 16
    pad = cdiv(n_cols, 8) * 8
    n_local = live.shape[2] // LANES
    return pl.pallas_call(
        lambda *refs: mask_kernel(n_cols, *refs),
        grid=(rows, queries // block),
        in_specs=[
            pl.BlockSpec((1, block, picks), lambda r, g: (r, g, 0)),
            pl.BlockSpec((1, 1, live.shape[2]), lambda r, g: (r, 0, 0)),
        ],
        out_specs=pl.BlockSpec((1, n_cols + n_local, block, LANES), lambda r, g: (r, 0, g, 0)),
        out_shape=jax.ShapeDtypeStruct((rows, n_cols + n_local, queries, LANES), BF),
        scratch_shapes=[pltpu.VMEM((pad, block, LANES), F32)],
        compiler_params=pltpu.CompilerParams(vmem_limit_bytes=VMEM_BYTES),
        cost_estimate=pl.CostEstimate(flops=12000000000, bytes_accessed=3000000, transcendentals=0),
        name="mask_build",
    )(columns, live)


def project_kernel(x_ref, wa_ref, wb_ref, cos_ref, sin_ref, q_ref, k_ref, v_ref, h_ref, inv_ref, gain_ref):
    quarter = q_ref.shape[2]

    @pl.when(pl.program_id(0) == 0)
    def gains():
        gain_ref[...] = jnp.transpose(wb_ref[:, quarter:].astype(F32), (1, 0))[0:8]

    x = x_ref[0].astype(F32)
    inverse = lax.rsqrt(jnp.mean(x * x, axis=-1, keepdims=True) + EPSILON)
    h = (x * inverse * gain_ref[0:1, :]).astype(BF)
    h_ref[0] = h
    inv_ref[0] = inverse
    turned = matmul(h, wa_ref[:, : 2 * quarter])
    for head in range(2 * quarter // HD):
        value = turned[:, head * HD : (head + 1) * HD]
        value = (value * cos_ref[...] + pltpu.roll(value, HD // 2, 1) * sin_ref[...]).astype(BF)
        if head < quarter // HD:
            q_ref[0, :, head * HD : (head + 1) * HD] = value
        else:
            at = head * HD - quarter
            k_ref[0, :, at : at + HD] = value
    v_ref[0] = matmul(h, wa_ref[:, 2 * quarter :]).astype(BF)


def project(x_all, w_a, w_b, cosine, sine):
    blocks, seg_len, width = x_all.shape
    quarter = w_a.shape[1] // 3
    whole = lambda array: pl.BlockSpec(array.shape, lambda r: (0, 0))
    head = pl.BlockSpec((1, seg_len, quarter), lambda r: (r, 0, 0))
    full = pl.BlockSpec((1, seg_len, width), lambda r: (r, 0, 0))
    out = jax.ShapeDtypeStruct((blocks, seg_len, quarter), BF)
    return pl.pallas_call(
        project_kernel,
        grid=(blocks,),
        in_specs=[full, whole(w_a), whole(w_b), whole(cosine), whole(sine)],
        out_specs=[head, head, head, full, pl.BlockSpec((1, seg_len, 1), lambda r: (r, 0, 0))],
        out_shape=[out, out, out, jax.ShapeDtypeStruct(x_all.shape, BF), jax.ShapeDtypeStruct((blocks, seg_len, 1), F32)],
        scratch_shapes=[pltpu.VMEM((8, width), F32)],
        compiler_params=pltpu.CompilerParams(vmem_limit_bytes=VMEM_BYTES),
        cost_estimate=SHORT,
        name="project",
    )(x_all, w_a, w_b, cosine, sine)


def plane_place():
    x, low, unused, y, core = place()
    return jnp.stack([x, y, 2 * low + core]).astype(jnp.int32)


def gradient(*entries):
    tokens, width = entries[0][0].shape
    n_blocks = lax.axis_size("seg")
    rows = width // n_blocks
    half = rows // 2
    sizes = [[entry[3] or right.shape[1] for right in entry[1]] for entry in entries]
    if rows % LANES:
        x, unused, unused, y, unused = place()
        outs = []
        for left, rights, way, columns in entries:
            if columns:
                rights = [cut(right, plane_place()[2] * columns, columns) for right in rights]
            full = jnp.concatenate([matmul_rows(left, right).astype(BF) for right in rights], 1)
            full = full.reshape(-1, 2, 2, half, full.shape[1])
            if way == "xy":
                near, side = halves(full, 1, x)
                near, side = halves(near, 1, y), halves(side, 1, y)
                parts = [near[0], side[0], near[1], side[1]]
            else:
                parts = halves(full, 1, x) if way == "x" else halves(full, 2, y)
            outs.append([part.reshape(-1, half, part.shape[-1]) for part in parts])
        return outs
    lefts = []
    for entry in entries:
        if not any(entry[0] is left for left in lefts):
            lefts.append(entry[0])
    which = [[entry[0] is left for left in lefts].index(True) for entry in entries]
    counts = [4 if entry[2] == "xy" else 2 for entry in entries]
    shapes = []
    for entry, size, count in zip(entries, sizes, counts):
        blocks = n_blocks // 2 if entry[2] == "xy" else n_blocks
        shapes += [(blocks, half, sum(size))] * count
    n_rights = sum(len(size) for size in sizes)

    def body(at_ref, *refs):
        left_refs, right_refs = refs[: len(lefts)], list(refs[len(lefts) : len(lefts) + n_rights])
        out_refs = list(refs[len(lefts) + n_rights :])
        pair = pl.program_id(0)
        turned = [jnp.transpose(ref[...]) for ref in left_refs]

        def by_row(value):
            upper, lower = value[:half], value[half:]
            return jnp.where(at_ref[1] == 0, upper, lower), jnp.where(at_ref[1] == 0, lower, upper)

        for entry, i, size, count in zip(entries, which, sizes, counts):
            outs, out_refs = out_refs[:count], out_refs[count:]
            start = 0
            for width_here in size:
                product = matmul(turned[i], right_refs.pop(0)[...]).astype(BF)
                span = slice(start, start + width_here)
                start += width_here
                first, second = product[:rows], product[rows:]
                if entry[2] == "y":
                    for side, value in enumerate((first, second)):
                        outs[0][2 * pair + side, :, span], outs[1][2 * pair + side, :, span] = by_row(value)
                    continue
                same = jnp.where(at_ref[0] == 0, first, second)
                other = jnp.where(at_ref[0] == 0, second, first)
                if entry[2] == "x":
                    for ref, value in zip(outs, (same, other)):
                        ref[2 * pair, :, span] = value[:half]
                        ref[2 * pair + 1, :, span] = value[half:]
                else:
                    outs[0][pair, :, span], outs[2][pair, :, span] = by_row(same)
                    outs[1][pair, :, span], outs[3][pair, :, span] = by_row(other)

    in_specs = [pl.BlockSpec((tokens, 2 * rows), lambda i, at: (0, i))] * len(lefts)
    for entry, size in zip(entries, sizes):
        column = (lambda i, at: (0, at[2])) if entry[3] else (lambda i, at: (0, 0))
        in_specs += [pl.BlockSpec((tokens, width_here), column) for width_here in size]
    outs = pl.pallas_call(
        body,
        grid_spec=pltpu.PrefetchScalarGridSpec(
            num_scalar_prefetch=1,
            grid=(n_blocks // 2,),
            in_specs=in_specs,
            out_specs=[pl.BlockSpec(shape, lambda i, at: (0, 0, 0)) for shape in shapes],
        ),
        out_shape=[jax.ShapeDtypeStruct(shape, BF) for shape in shapes],
        compiler_params=pltpu.CompilerParams(vmem_limit_bytes=VMEM_BYTES),
        cost_estimate=SHORT,
        name="gradient",
    )(plane_place(), *lefts, *[right for entry in entries for right in entry[1]])
    groups = []
    for count in counts:
        groups.append(outs[:count])
        outs = outs[count:]
    return groups


def split_sums(keep, recv, way):
    n_blocks, rows, cols = keep.shape

    def body(at_ref, keep_ref, recv_ref, mine_ref, give_ref):
        side = at_ref[1] if way == "y" else at_ref[0]
        for block in range(n_blocks // 2):
            for at, out_ref in ((2 * block + side, mine_ref), (2 * block + 1 - side, give_ref)):
                out_ref[block] = (keep_ref[at].astype(F32) + recv_ref[at].astype(F32)).astype(BF)

    vmem = pl.BlockSpec(memory_space=pltpu.VMEM)
    return pl.pallas_call(
        body,
        in_specs=[pl.BlockSpec(memory_space=pltpu.SMEM)] + [vmem] * 2,
        out_specs=[vmem] * 2,
        out_shape=[jax.ShapeDtypeStruct((n_blocks // 2, rows, cols), BF)] * 2,
        compiler_params=pltpu.CompilerParams(vmem_limit_bytes=VMEM_BYTES),
        cost_estimate=SHORT,
        name="split_sums",
    )(plane_place(), keep, recv)


def gradient_units(left, right):
    tokens, width = left.shape
    n_high = lax.axis_size("seg") // 4
    rows = width // (4 * n_high)
    cols = right.shape[1]
    step = 256
    if rows % 8:
        full = matmul_rows(left, right).astype(BF).reshape(-1, 2, 2, rows, cols)
        return halves(full, 1, place()[0])

    def body(at_ref, left_ref, right_ref, keep_ref, give_ref):
        product = matmul_rows(left_ref[...], right_ref[...])
        for high in range(n_high):
            for y in range(2):
                zero, one = [
                    product[(high * 4 + x * 2 + y) * rows : (high * 4 + x * 2 + y + 1) * rows] for x in range(2)
                ]
                keep_ref[high, y] = jnp.where(at_ref[0] == 0, zero, one).astype(BF)
                give_ref[high, y] = jnp.where(at_ref[0] == 0, one, zero).astype(BF)

    shape = (n_high, 2, rows, cols)
    return pl.pallas_call(
        body,
        grid_spec=pltpu.PrefetchScalarGridSpec(
            num_scalar_prefetch=1,
            grid=(cols // step,),
            in_specs=[
                pl.BlockSpec((tokens, width), lambda i, at: (0, 0)),
                pl.BlockSpec((tokens, step), lambda i, at: (0, i)),
            ],
            out_specs=[pl.BlockSpec((n_high, 2, rows, step), lambda i, at: (0, 0, 0, i))] * 2,
        ),
        out_shape=[jax.ShapeDtypeStruct(shape, BF)] * 2,
        compiler_params=pltpu.CompilerParams(vmem_limit_bytes=VMEM_BYTES),
        cost_estimate=SHORT,
        name="gradient_units",
    )(plane_place(), left, right)


def gather_columns(matrices, gain_one, gain_two):
    rows, width = matrices[0].shape
    quarter = width // 4

    def body(one_ref, two_ref, *refs):
        out_ref = refs[-1]
        pair = jnp.concatenate([one_ref[...], two_ref[...], jnp.zeros((6, rows), F32)], 0)
        square = jnp.concatenate([pair, jnp.zeros((8, LANES - rows), F32)], 1)
        square = jnp.concatenate([square, jnp.zeros((LANES - 8, LANES), F32)], 0)
        gains = jnp.transpose(square)[:rows].astype(BF)
        for i in range(4):
            for at, ref in enumerate(refs[:-1]):
                out_ref[i, :, at * quarter : (at + 1) * quarter] = ref[:, i * quarter : (i + 1) * quarter]
            out_ref[i, :, len(matrices) * quarter :] = gains

    return pl.pallas_call(
        body,
        out_shape=jax.ShapeDtypeStruct((4, rows, len(matrices) * quarter + LANES), BF),
        cost_estimate=SHORT,
        name="gather_columns",
    )(gain_one.astype(F32)[None], gain_two.astype(F32)[None], *matrices)


def group_place():
    unused, low, high, unused, core = place()
    return jnp.stack([2 * high + low, low, core]).astype(jnp.int32)


def plane_sort(*groups, units=()):
    sizes = [group[0].shape[-1] for group in groups]
    rows, cols = groups[0][0].shape[1], sum(sizes)
    shapes = [(rows, cols)] * 4
    if units:
        unit_rows = units[0].shape[1]
        below = cdiv(unit_rows, 16) * 16
        shapes = [(rows + below if way == 2 else rows, cols) for way in range(4)] + [(unit_rows, cols)]

    def body(at_ref, *refs):
        in_refs, out_refs = list(refs[: -len(shapes)]), refs[-len(shapes) :]
        unit_refs = in_refs[len(in_refs) - len(units) :]
        for way in range(4):
            start = 0
            left = list(in_refs)
            for size, group in zip(sizes, groups):
                total = None
                for unused in group:
                    part = left.pop(0)[at_ref[0] ^ way].astype(F32)
                    total = part if total is None else total + part
                out_refs[way][0:rows, start : start + size] = total.astype(BF)
                start += size
        if units:
            high = lax.shift_right_logical(at_ref[0], 1)
            own = sum(ref[high].astype(F32) for ref in unit_refs)
            give = sum(ref[1 - high].astype(F32) for ref in unit_refs)
            out_refs[4][...] = own.astype(BF)
            give = jnp.concatenate([give, jnp.zeros((below - unit_rows, cols), F32)], 0)
            out_refs[2][rows : rows + below, :] = give.astype(BF)

    vmem = pl.BlockSpec(memory_space=pltpu.VMEM)
    arrays = [array for group in groups for array in group] + list(units)
    return pl.pallas_call(
        body,
        in_specs=[pl.BlockSpec(memory_space=pltpu.SMEM)] + [vmem] * len(arrays),
        out_specs=[vmem] * len(shapes),
        out_shape=[jax.ShapeDtypeStruct(shape, BF) for shape in shapes],
        compiler_params=pltpu.CompilerParams(vmem_limit_bytes=VMEM_BYTES),
        cost_estimate=SHORT,
        name="plane_sort",
    )(group_place(), *arrays)


def z_merge(kept, from_1, from_2, from_3):
    rows, cols = kept.shape
    half = rows // 2

    def body(at_ref, kept_ref, one_ref, two_ref, three_ref, keep_ref, give_ref):
        same = kept_ref[...].astype(F32) + two_ref[0:rows, :].astype(F32)
        other = one_ref[...].astype(F32) + three_ref[...].astype(F32)
        for quarter, value in ((at_ref[1], same), (1 - at_ref[1], other)):
            upper, lower = value[:half], value[half:]
            keep_ref[quarter] = jnp.where(at_ref[2] == 0, upper, lower).astype(BF)
            give_ref[quarter] = jnp.where(at_ref[2] == 0, lower, upper).astype(BF)

    vmem = pl.BlockSpec(memory_space=pltpu.VMEM)
    return pl.pallas_call(
        body,
        in_specs=[pl.BlockSpec(memory_space=pltpu.SMEM)] + [vmem] * 4,
        out_specs=[vmem] * 2,
        out_shape=[jax.ShapeDtypeStruct((2, half, cols), BF)] * 2,
        compiler_params=pltpu.CompilerParams(vmem_limit_bytes=VMEM_BYTES),
        cost_estimate=SHORT,
        name="z_merge",
    )(group_place(), kept, from_1, from_2, from_3)


def join_quarters(mine, recv, core_ref, start, size, z_low, core):
    return jnp.where(
        core_ref[2] == core, mine[z_low, :, start : start + size], recv[z_low, :, start : start + size]
    ).astype(F32)


def lane_sums(value):
    total = value[:, :LANES]
    for part in lane_blocks(value)[1:]:
        total = total + part
    return total


def sums_as_row(value):
    rows = value.shape[0]
    padded = jnp.concatenate([value, jnp.zeros((LANES - rows, LANES), F32)], 0)
    return jnp.sum(jnp.transpose(padded), axis=0, keepdims=True)[:, :rows]


def join_columns(mine, recv, weights, gain, n_matrices):
    rows, cols = mine.shape[1:]
    size = cols // n_matrices

    def body(at_ref, mine_ref, recv_ref, gain_ref, *refs):
        weight_refs, out_refs = refs[: len(weights)], refs[len(weights) :]
        total = jnp.zeros((rows, LANES), F32)
        for i in range(n_matrices):
            for z_low in range(2):
                for core in range(2):
                    at = (2 * z_low + core) * size
                    value = join_quarters(mine_ref, recv_ref, at_ref, i * size, size, z_low, core)
                    out_refs[i][:, at : at + size] = value
                    if i < len(weights):
                        total = total + lane_sums(value * weight_refs[i][:, at : at + size].astype(F32))
        out_refs[-1][...] = sums_as_row(total) / gain_ref[...]

    vmem = pl.BlockSpec(memory_space=pltpu.VMEM)
    outs = pl.pallas_call(
        body,
        in_specs=[pl.BlockSpec(memory_space=pltpu.SMEM)] + [vmem] * (3 + len(weights)),
        out_specs=[vmem] * (n_matrices + 1),
        out_shape=[jax.ShapeDtypeStruct((rows, 4 * size), F32)] * n_matrices + [jax.ShapeDtypeStruct((1, rows), F32)],
        cost_estimate=SHORT,
        name="join_columns",
    )(group_place(), mine, recv, gain.astype(F32)[None], *weights)
    return list(outs[:-1]) + [outs[-1][0]]


def join_units(mine, recv, weights, gain, n_blocks):
    rows, both = mine.shape[1:]
    quarter_size = both // 2
    size = 4 * quarter_size // n_blocks

    def body(at_ref, mine_ref, recv_ref, gain_ref, one_weight, two_weight, one_ref, two_ref, total_ref):
        total = jnp.zeros((rows, LANES), F32)
        for half, (out_ref, weight_ref) in enumerate(((one_ref, one_weight), (two_ref, two_weight))):
            for block, (quarter, at) in enumerate(unit_blocks(n_blocks)):
                start = half * quarter_size + at * size
                out_ref[:, block * size : (block + 1) * size] = join_quarters(
                    mine_ref, recv_ref, at_ref, start, size, quarter // 2, quarter % 2
                )
            total = total + lane_sums(out_ref[...] * weight_ref[...].astype(F32))
        total_ref[...] = sums_as_row(total) / gain_ref[...]

    vmem = pl.BlockSpec(memory_space=pltpu.VMEM)
    one, two, total = pl.pallas_call(
        body,
        in_specs=[pl.BlockSpec(memory_space=pltpu.SMEM)] + [vmem] * 5,
        out_specs=[vmem] * 3,
        out_shape=[jax.ShapeDtypeStruct((rows, 4 * quarter_size), F32)] * 2 + [jax.ShapeDtypeStruct((1, rows), F32)],
        cost_estimate=SHORT,
        name="join_units",
    )(group_place(), mine, recv, gain.astype(F32)[None], *weights)
    return one, two, total[0]


def pair_add(one, two):
    def body(at_ref, one_ref, two_ref, own_ref, give_ref):
        for way, out_ref in enumerate((own_ref, give_ref)):
            at = at_ref[1] ^ way
            out_ref[...] = (one_ref[at].astype(F32) + two_ref[at].astype(F32)).astype(BF)

    vmem = pl.BlockSpec(memory_space=pltpu.VMEM)
    return pl.pallas_call(
        body,
        in_specs=[pl.BlockSpec(memory_space=pltpu.SMEM)] + [vmem] * 2,
        out_specs=[vmem] * 2,
        out_shape=[jax.ShapeDtypeStruct(one.shape[1:], BF)] * 2,
        compiler_params=pltpu.CompilerParams(vmem_limit_bytes=VMEM_BYTES),
        cost_estimate=SHORT,
        name="pair_add",
    )(group_place(), one, two)


def back_project(lefts, weights, transposed=True):
    block = lefts[0].shape[0] // 4
    out = weights[0].shape[0] if transposed else weights[0].shape[1]

    def body(*refs):
        left_refs, weight_refs = refs[: len(lefts)], refs[len(lefts) : 2 * len(lefts)]
        keep_ref, give_ref = refs[2 * len(lefts) :]
        total = None
        for left_ref, weight_ref in zip(left_refs, weight_refs):
            part = (matmul_cols if transposed else matmul)(left_ref[...], weight_ref[...])
            total = part if total is None else total + part
        total = total.astype(BF)
        for i in range(4):
            (keep_ref, give_ref)[i % 2][i // 2] = total[i * block : (i + 1) * block]

    return pl.pallas_call(
        body,
        in_specs=[pl.BlockSpec(memory_space=pltpu.VMEM)] * (2 * len(lefts)),
        out_specs=[pl.BlockSpec(memory_space=pltpu.VMEM)] * 2,
        out_shape=[jax.ShapeDtypeStruct((2, block, out), BF)] * 2,
        compiler_params=pltpu.CompilerParams(vmem_limit_bytes=VMEM_BYTES),
        cost_estimate=SHORT,
        name="back_project",
    )(*lefts, *weights)


def join_four(mine, recv, of_tokens):
    rows, size = mine.shape[1:]
    block = rows // 4

    def body(at_ref, mine_ref, recv_ref, out_ref):
        for z_low in range(2):
            side = at_ref[1] ^ z_low
            for core in range(2):
                at = (2 * z_low + core) * size
                for i in range(4):
                    j = i ^ 1 if of_tokens else i
                    ours = mine_ref[side, i * block : (i + 1) * block]
                    theirs = recv_ref[side, j * block : (j + 1) * block]
                    out_ref[i * block : (i + 1) * block, at : at + size] = jnp.where(at_ref[2] == core, ours, theirs)

    vmem = pl.BlockSpec(memory_space=pltpu.VMEM)
    return pl.pallas_call(
        body,
        in_specs=[pl.BlockSpec(memory_space=pltpu.SMEM)] + [vmem] * 2,
        out_specs=vmem,
        out_shape=jax.ShapeDtypeStruct((rows, 4 * size), mine.dtype),
        compiler_params=pltpu.CompilerParams(vmem_limit_bytes=VMEM_BYTES),
        cost_estimate=SHORT,
        name="join_four",
    )(group_place(), mine, recv)


def branch_back(mine, recv, x_one, gain, g_mine, g_recv, w_out):
    blocks, seg_len, width = x_one.shape
    quarter = width // 4

    def body(at_ref, mine_ref, recv_ref, x_ref, gain_ref, g_ref, g_recv_ref, w_ref, branch_ref, att_ref, own_ref):
        block = pl.program_id(0)
        grad = jnp.where(block % 2 == 0, mine_ref[0], recv_ref[0]).astype(F32)
        passed = jnp.where(block % 2 == 0, g_ref[0], g_recv_ref[0]).astype(F32)
        values = x_ref[0]
        inverse = lax.rsqrt(jnp.mean(values * values, axis=-1, keepdims=True) + EPSILON)
        normed = values * inverse
        scaled = grad * gain_ref[...]
        mean = jnp.mean(scaled * normed, axis=-1, keepdims=True)
        total = passed + inverse * (scaled - normed * mean)
        low = total.astype(BF)
        branch_ref[0] = low
        att_ref[0] = matmul_cols(low, w_ref[...]).astype(BF)

        @pl.when(block == 2 * at_ref[1])
        def own():
            own_ref[...] = total

    pair = pl.BlockSpec((1, seg_len, width), lambda i, at: (i // 2, 0, 0))
    full = pl.BlockSpec((1, seg_len, width), lambda i, at: (i, 0, 0))
    return pl.pallas_call(
        body,
        grid_spec=pltpu.PrefetchScalarGridSpec(
            num_scalar_prefetch=1,
            grid=(blocks,),
            in_specs=[
                pair,
                pair,
                full,
                pl.BlockSpec((1, width), lambda i, at: (0, 0)),
                pair,
                pair,
                pl.BlockSpec((quarter, width), lambda i, at: (2 * at[1] + at[2], 0)),
            ],
            out_specs=[
                full,
                pl.BlockSpec((1, seg_len, quarter), lambda i, at: (i, 0, 0)),
                pl.BlockSpec((seg_len, width), lambda i, at: (0, 0)),
            ],
        ),
        out_shape=[
            jax.ShapeDtypeStruct((blocks, seg_len, width), BF),
            jax.ShapeDtypeStruct((blocks, seg_len, quarter), BF),
            jax.ShapeDtypeStruct((seg_len, width), F32),
        ],
        compiler_params=pltpu.CompilerParams(vmem_limit_bytes=VMEM_BYTES),
        cost_estimate=SHORT,
        name="branch_back",
    )(group_place(), mine, recv, x_one, gain, g_mine, g_recv, w_out)


def input_back(mine, recv, x_all, gain, passed):
    unused, seg_len, width = x_all.shape

    def body(at_ref, mine_ref, recv_ref, x_ref, gain_ref, passed_ref, out_ref):
        values = x_ref[0].astype(F32)
        inverse = lax.rsqrt(jnp.mean(values * values, axis=-1, keepdims=True) + EPSILON)
        normed = values * inverse
        scaled = (mine_ref[...].astype(F32) + recv_ref[...].astype(F32)) * gain_ref[...]
        mean = jnp.mean(scaled * normed, axis=-1, keepdims=True)
        out_ref[...] = (passed_ref[...] + inverse * (scaled - normed * mean)).astype(BF)

    tokens = pl.BlockSpec((seg_len, width), lambda i, at: (0, 0))
    return pl.pallas_call(
        body,
        grid_spec=pltpu.PrefetchScalarGridSpec(
            num_scalar_prefetch=1,
            grid=(1,),
            in_specs=[
                tokens,
                tokens,
                pl.BlockSpec((1, seg_len, width), lambda i, at: (2 * at[1], 0, 0)),
                pl.BlockSpec((1, width), lambda i, at: (0, 0)),
                tokens,
            ],
            out_specs=tokens,
        ),
        out_shape=jax.ShapeDtypeStruct((seg_len, width), BF),
        compiler_params=pltpu.CompilerParams(vmem_limit_bytes=VMEM_BYTES),
        cost_estimate=SHORT,
        name="input_back",
    )(group_place(), mine, recv, x_all, gain, passed)


def add_kernel(one, two):
    def body(one_ref, two_ref, out_ref):
        out_ref[...] = (one_ref[...].astype(F32) + two_ref[...].astype(F32)).astype(BF)

    return pl.pallas_call(
        body,
        in_specs=[pl.BlockSpec(memory_space=pltpu.VMEM)] * 2,
        out_specs=pl.BlockSpec(memory_space=pltpu.VMEM),
        out_shape=jax.ShapeDtypeStruct(one.shape, BF),
        compiler_params=pltpu.CompilerParams(vmem_limit_bytes=VMEM_BYTES),
        cost_estimate=SHORT,
        name="add_kernel",
    )(one, two)


def add_low(one, two):
    return (one.astype(F32) + two.astype(F32)).astype(BF)


def lane_blocks(value):
    return [value[:, i : i + LANES] for i in range(0, value.shape[1], LANES)]


PIECES = ((0, 0), (0, 1), (1, 0), (1, 1), (2, 0), (3, 0), (2, 1))
N_COMMON = 5
N_GROUPS = 4


def head_of(value, head):
    return value[:, head * HD : (head + 1) * HD]


def forward_kernel(q_ref, k_ref, v_ref, mine_ref, other_ref, *refs):
    key_refs, value_refs = refs[:N_GROUPS], refs[N_GROUPS : 2 * N_GROUPS]
    o_ref, of_ref, p_ref, pl_ref, inv_ref, s_ref, top_ref, total_ref, acc_ref = refs[2 * N_GROUPS :]
    heads = range(q_ref.shape[2] // HD)
    scale = HD ** (-0.5) * LOG2_E
    block = pl.program_id(0)
    upper = block >= 2
    queries = q_ref[0]
    seg_len = queries.shape[0]
    per = key_refs[0].shape[1] // LANES
    first = block % 2 == 0

    def bias(at):
        return jnp.where(first, mine_ref[0, at], other_ref[0, at]).astype(F32)

    local_bias = jnp.concatenate([bias(len(PIECES) * per + i) for i in range(cdiv(seg_len, LANES))], 1)[:, :seg_len]
    s_local = [
        jnp.minimum(matmul_cols(head_of(queries, h), head_of(k_ref[0], h)) * scale, local_bias) for h in heads
    ]

    def score(t, tops):
        group, low = PIECES[t]
        keys = key_refs[group][low]
        parts = [lane_blocks(matmul_cols(head_of(queries, h), head_of(keys, h)) * scale) for h in heads]
        for i in range(per):
            limit = bias(t * per + i)
            for h in heads:
                part = jnp.minimum(parts[h][i], limit)
                s_ref[h, t, :, i * LANES : (i + 1) * LANES] = part
                tops[h] = part if tops[h] is None else jnp.maximum(tops[h], part)
        return tops

    tops = [None for h in heads]
    for t in range(N_COMMON):
        tops = score(t, tops)
    for h in heads:
        top_ref[h] = tops[h]

    @pl.when(upper)
    def more_scores():
        tops = [top_ref[h] for h in heads]
        for t in range(N_COMMON, len(PIECES)):
            tops = score(t, tops)
        for h in heads:
            top_ref[h] = tops[h]

    row_max, e_local = [], []
    for h in heads:
        row_max.append(
            jnp.maximum(
                jnp.max(s_local[h], axis=-1, keepdims=True), jnp.max(top_ref[h], axis=-1, keepdims=True)
            )
        )
        expo = jnp.exp2(s_local[h] - row_max[h])
        e_local.append(jnp.sum(expo, axis=-1, keepdims=True))
        chances = expo.astype(BF)
        pl_ref[0, h] = chances
        acc_ref[h] = matmul(chances, head_of(v_ref[0], h))

    def weigh(t, h, total, acc):
        group, low = PIECES[t]
        expo = jnp.exp2(s_ref[h, t] - row_max[h])
        for part in lane_blocks(expo):
            total = part if total is None else total + part
        chances = expo.astype(BF)
        p_ref[0, h, t] = chances
        return total, acc + matmul(chances, head_of(value_refs[group][low], h))

    for h in heads:
        total, acc = None, acc_ref[h]
        for t in range(N_COMMON):
            total, acc = weigh(t, h, total, acc)
        total_ref[h] = total
        acc_ref[h] = acc

    @pl.when(upper)
    def more_values():
        for h in heads:
            total, acc = total_ref[h], acc_ref[h]
            for t in range(N_COMMON, len(PIECES)):
                total, acc = weigh(t, h, total, acc)
            total_ref[h] = total
            acc_ref[h] = acc

    for h in heads:
        inverse = 1.0 / (e_local[h] + jnp.sum(total_ref[h], axis=-1, keepdims=True))
        out = acc_ref[h] * inverse
        of_ref[0, :, h * HD : (h + 1) * HD] = out
        o_ref[0, :, h * HD : (h + 1) * HD] = out.astype(BF)
        inv_ref[0, h] = inverse


def backward_local_kernel(do_ref, of_ref, q_ref, k_ref, v_ref, inv_ref, pl_ref, cos_ref, sin_ref, dkv_ref, dq_ref):
    scale = HD ** (-0.5)
    for h in range(q_ref.shape[2] // HD):
        span = slice(h * HD, (h + 1) * HD)
        d_out = do_ref[0, :, span]
        delta = jnp.sum(d_out.astype(F32) * of_ref[0, :, span], axis=-1, keepdims=True)
        chances = pl_ref[0, h].astype(F32) * inv_ref[0, h]
        ds = (chances * (matmul_cols(d_out, v_ref[0, :, span]) - delta)).astype(BF)
        dq_ref[0, :, span] = matmul(ds, k_ref[0, :, span])
        dk = matmul_rows(ds, q_ref[0, :, span])
        dkv_ref[0, 0, :, span] = (
            (dk * cos_ref[...] - pltpu.roll(dk, HD // 2, 1) * sin_ref[...]) * scale
        ).astype(BF)
        dkv_ref[1, 0, :, span] = matmul_rows(chances.astype(BF), d_out).astype(BF)


def backward_kernel(do_ref, of_ref, local_ref, inv_ref, p_ref, cos_ref, sin_ref, *refs):
    key_refs, value_refs = refs[:N_GROUPS], refs[N_GROUPS : 2 * N_GROUPS]
    out_ref, dq_ref = refs[2 * N_GROUPS :]
    heads = range(do_ref.shape[2] // HD)
    scale = HD ** (-0.5)
    upper = pl.program_id(0) >= 2
    d_out = [do_ref[0, :, h * HD : (h + 1) * HD] for h in heads]
    inverse = [inv_ref[0, h] for h in heads]
    delta = [
        jnp.sum(d_out[h].astype(F32) * of_ref[0, :, h * HD : (h + 1) * HD], axis=-1, keepdims=True) for h in heads
    ]

    def piece(t, h, dq):
        group, low = PIECES[t]
        dp = matmul_cols(d_out[h], head_of(value_refs[group][low], h))
        ds = (p_ref[0, h, t].astype(F32) * ((dp - delta[h]) * inverse[h])).astype(BF)
        return dq + matmul(ds, head_of(key_refs[group][low], h))

    for h in heads:
        dq = local_ref[0, :, h * HD : (h + 1) * HD]
        for t in range(N_COMMON):
            dq = piece(t, h, dq)
        dq_ref[h] = dq

    @pl.when(upper)
    def more():
        for h in heads:
            dq = dq_ref[h]
            for t in range(N_COMMON, len(PIECES)):
                dq = piece(t, h, dq)
            dq_ref[h] = dq

    for h in heads:
        dq = dq_ref[h]
        out_ref[0, :, h * HD : (h + 1) * HD] = (
            (dq * cos_ref[...] - pltpu.roll(dq, HD // 2, 1) * sin_ref[...]) * scale
        ).astype(BF)


def attention_specs(piece_rows, seg_len, width):
    heads = width // HD
    tokens = pl.BlockSpec((1, seg_len, width), lambda r: (r, 0, 0))
    piece = pl.BlockSpec((2, piece_rows, width), lambda r: (0, 0, 0))
    p_spec = pl.BlockSpec((1, heads, len(PIECES), seg_len, piece_rows), lambda r: (r, 0, 0, 0, 0))
    pl_spec = pl.BlockSpec((1, heads, seg_len, seg_len), lambda r: (r, 0, 0, 0))
    inv_spec = pl.BlockSpec((1, heads, seg_len, 1), lambda r: (r, 0, 0, 0))
    return tokens, piece, p_spec, pl_spec, inv_spec


def attention_forward(queries, keys, values, mask, other_mask, key_pieces, value_pieces):
    blocks, seg_len, width = queries.shape
    heads = width // HD
    piece_rows = key_pieces[0].shape[1]
    tokens, piece, p_spec, pl_spec, inv_spec = attention_specs(piece_rows, seg_len, width)
    mask_spec = pl.BlockSpec((1,) + mask.shape[1:], lambda r: (r // 2, 0, 0, 0))
    return pl.pallas_call(
        forward_kernel,
        grid=(blocks,),
        in_specs=[tokens, tokens, tokens, mask_spec, mask_spec] + [piece] * (2 * N_GROUPS),
        out_specs=[tokens, tokens, p_spec, pl_spec, inv_spec],
        out_shape=[
            jax.ShapeDtypeStruct(queries.shape, BF),
            jax.ShapeDtypeStruct(queries.shape, F32),
            jax.ShapeDtypeStruct((blocks, heads, len(PIECES), seg_len, piece_rows), BF),
            jax.ShapeDtypeStruct((blocks, heads, seg_len, seg_len), BF),
            jax.ShapeDtypeStruct((blocks, heads, seg_len, 1), F32),
        ],
        scratch_shapes=[
            pltpu.VMEM((heads, len(PIECES), seg_len, piece_rows), F32),
            pltpu.VMEM((heads, seg_len, LANES), F32),
            pltpu.VMEM((heads, seg_len, LANES), F32),
            pltpu.VMEM((heads, seg_len, HD), F32),
        ],
        compiler_params=pltpu.CompilerParams(vmem_limit_bytes=VMEM_BYTES),
        cost_estimate=SHORT,
        name="attention_forward",
    )(queries, keys, values, mask, other_mask, *key_pieces, *value_pieces)


def attention_backward_local(d_out, out_f32, queries, keys, values, inverse, p_local, cosine, sine):
    blocks, seg_len, width = queries.shape
    tokens, unused, unused, pl_spec, inv_spec = attention_specs(seg_len, seg_len, width)
    table = pl.BlockSpec((seg_len, HD), lambda r: (0, 0))
    return pl.pallas_call(
        backward_local_kernel,
        grid=(blocks,),
        in_specs=[tokens, tokens, tokens, tokens, tokens, inv_spec, pl_spec, table, table],
        out_specs=[pl.BlockSpec((2, 1, seg_len, width), lambda r: (0, r, 0, 0)), tokens],
        out_shape=[
            jax.ShapeDtypeStruct((2, blocks, seg_len, width), BF),
            jax.ShapeDtypeStruct(queries.shape, F32),
        ],
        compiler_params=pltpu.CompilerParams(vmem_limit_bytes=VMEM_BYTES),
        cost_estimate=SHORT,
        name="attention_backward_local",
    )(d_out, out_f32, queries, keys, values, inverse, p_local, cosine, sine)


def attention_backward(d_out, out_f32, dq_local, inverse, p_memory, cosine, sine, key_pieces, value_pieces):
    blocks, seg_len, width = d_out.shape
    piece_rows = key_pieces[0].shape[1]
    tokens, piece, p_spec, unused, inv_spec = attention_specs(piece_rows, seg_len, width)
    table = pl.BlockSpec((seg_len, HD), lambda r: (0, 0))
    return pl.pallas_call(
        backward_kernel,
        grid=(blocks,),
        in_specs=[tokens, tokens, tokens, inv_spec, p_spec, table, table] + [piece] * (2 * N_GROUPS),
        out_specs=tokens,
        out_shape=jax.ShapeDtypeStruct((blocks, seg_len, width), BF),
        scratch_shapes=[pltpu.VMEM((width // HD, seg_len, HD), F32)],
        compiler_params=pltpu.CompilerParams(vmem_limit_bytes=VMEM_BYTES),
        cost_estimate=SHORT,
        name="attention_backward",
    )(d_out, out_f32, dq_local, inverse, p_memory, cosine, sine, *key_pieces, *value_pieces)


def allow_local_of(live):
    seg_len = live.shape[-1]
    position = jnp.arange(seg_len, dtype=jnp.int32)
    same = position[None, :] == position[:, None]
    return same[None] | ((position[None, :] < position[:, None])[None] & (live == 1))


def split_heads(value):
    rows, seg_len, width = value.shape
    return value.reshape(rows, seg_len, width // HD, HD)


def stream_forward(queries, keys, values, live, allow, memory):
    scale = HD ** (-0.5)
    q4, k4, v4 = split_heads(queries), split_heads(keys), split_heads(values)
    scores = jnp.einsum("rqhd,rkhd->rhqk", q4, k4, preferred_element_type=F32) * scale
    scores = jnp.where(allow_local_of(live)[:, None], scores, NEG_BIG)
    row_max = jnp.max(scores, axis=-1)
    expo = jnp.exp(scores - row_max[..., None])
    state = (
        row_max,
        jnp.sum(expo, axis=-1),
        jnp.einsum("rhqk,rkhd->rhqd", expo.astype(BF), v4, preferred_element_type=F32),
    )

    def step(running, item):
        row_max, row_total, acc = running
        block, allowed = item
        k3 = block[0].reshape(block.shape[1], -1, HD)
        v3 = block[1].reshape(block.shape[1], -1, HD)
        scores = jnp.einsum("rqhd,khd->rhqk", q4, k3, preferred_element_type=F32) * scale
        scores = jnp.where(allowed[:, None] > 0, scores, NEG_BIG)
        new_max = jnp.maximum(row_max, jnp.max(scores, axis=-1))
        shrink = jnp.exp(row_max - new_max)
        expo = jnp.exp(scores - new_max[..., None])
        acc = acc * shrink[..., None] + jnp.einsum(
            "rhqk,khd->rhqd", expo.astype(BF), v3, preferred_element_type=F32
        )
        return (new_max, row_total * shrink + jnp.sum(expo, axis=-1), acc), None

    (row_max, row_total, acc), unused = lax.scan(step, state, (memory, allow))
    out = (acc / row_total[..., None]).transpose(0, 2, 1, 3).reshape(queries.shape)
    return out.astype(BF), out, row_max + jnp.log(row_total)


def stream_backward(d_out, out_f32, queries, keys, values, live, log_total, allow, memory, cosine, sine):
    scale = HD ** (-0.5)
    q4, k4, v4, d4 = split_heads(queries), split_heads(keys), split_heads(values), split_heads(d_out)
    delta = jnp.sum(d4.astype(F32) * split_heads(out_f32), axis=-1).transpose(0, 2, 1)
    scores = jnp.einsum("rqhd,rkhd->rhqk", q4, k4, preferred_element_type=F32) * scale
    scores = jnp.where(allow_local_of(live)[:, None], scores, NEG_BIG)
    chances = jnp.exp(scores - log_total[..., None])
    dp = jnp.einsum("rqhd,rkhd->rhqk", d4, v4, preferred_element_type=F32)
    ds = (chances * (dp - delta[..., None])).astype(BF)
    dq = jnp.einsum("rhqk,rkhd->rqhd", ds, k4, preferred_element_type=F32)
    dk = jnp.einsum("rhqk,rqhd->rkhd", ds, q4, preferred_element_type=F32)
    dv = jnp.einsum("rhqk,rqhd->rkhd", chances.astype(BF), d4, preferred_element_type=F32)

    def step(running, item):
        block, allowed = item
        k3 = block[0].reshape(block.shape[1], -1, HD)
        v3 = block[1].reshape(block.shape[1], -1, HD)
        scores = jnp.einsum("rqhd,khd->rhqk", q4, k3, preferred_element_type=F32) * scale
        scores = jnp.where(allowed[:, None] > 0, scores, NEG_BIG)
        chances = jnp.exp(scores - log_total[..., None])
        dp = jnp.einsum("rqhd,khd->rhqk", d4, v3, preferred_element_type=F32)
        ds = (chances * (dp - delta[..., None])).astype(BF)
        return running + jnp.einsum("rhqk,khd->rqhd", ds, k3, preferred_element_type=F32), None

    dq, unused = lax.scan(step, dq, (memory, allow))

    def back(value):
        turned = rope_heads(value.reshape((-1,) + value.shape[2:]), jnp.tile(cosine, (value.shape[0], 1)), -jnp.tile(sine, (value.shape[0], 1)))
        return (turned * scale).reshape(queries.shape).astype(BF)

    return jnp.stack([back(dq), back(dk), dv.reshape(queries.shape).astype(BF)])


def local(
    layer_input,
    live,
    knn_index,
    mem_keys,
    mem_values,
    gain_attn,
    w_query,
    w_key,
    w_value,
    w_out,
    gain_ffn,
    w_gate,
    w_up,
    w_down,
    cotangent,
):
    seg_len, width = layer_input.shape[1:]
    quarter = width // 4
    n_seg = lax.axis_size("seg")
    n_devices = n_seg * lax.axis_size("rep")
    tokens = seg_len * n_seg
    n_high = n_seg // 4
    x, low, high, y, core = place()
    use_kernel = n_high <= KERNEL_HIGH
    kv_rows = 2 * seg_len
    group_tokens = 4 * seg_len

    def by_quarter(value):
        return [value[:, i * quarter : (i + 1) * quarter] for i in range(4)]

    gains = None if width // n_devices % 16 == 0 else jnp.concatenate(
        [gain_attn[:, None], gain_ffn[:, None], jnp.zeros((gain_attn.shape[0], LANES - 2), BF)], 1
    )
    if gains is None:
        qo = gather_columns((w_query, w_key, w_value, w_out), gain_attn, gain_ffn)
    else:
        stacked = [by_quarter(w) for w in (w_query, w_key, w_value, w_out)]
        qo = jnp.stack([jnp.concatenate([s[i] for s in stacked] + [gains], 1) for i in range(4)])

    def core_quarters(value, side):
        return jnp.stack([cut(value, side * quarter, quarter), cut(value, (2 + side) * quarter, quarter)])

    def core_memory(side):
        return jnp.stack([core_quarters(mem_keys[0], side), core_quarters(mem_values[0], side)])

    coded = knn_index[0] * 2 + live[0][:, None]
    qo = qo.reshape(2, 2, -1, qo.shape[-1])
    qo_keep, qo_give = halves(qo, 1, core)
    kv_keep, kv_give = core_memory(core), core_memory(1 - core)
    qo_recv, kv_recv, coded_recv = flip_core(qo_give), flip_core(kv_give), flip_z(coded)
    qo_keep, kv_keep, coded, qo_recv, kv_recv, coded_recv, w_gate_, w_up_ = fence(
        qo_keep, kv_keep, coded, qo_recv, kv_recv, coded_recv, w_gate, w_up
    )

    qo_keep, qo_give = halves(ordered(qo_keep, qo_recv, core, 1), 0, low)
    kv_keep, kv_give = halves(ordered(kv_keep, kv_recv, core, 2), 1, low)
    coded = ordered(coded[None], coded_recv[None], low, 0)
    kv_recv = flip_z(kv_give)
    qo_near = flip_z(qo_give)
    down_w = w_down[None, None, None, None]
    x_own = layer_input[0]
    gate_up = split_units(w_gate_, w_up_, n_devices).reshape(2, 2, 2, -1, w_gate.shape[1] // 4)

    def places_of(codes, row_core):
        picks = lax.shift_right_arithmetic(codes, 1)
        pair = picks >= tokens
        slot = jnp.where(pair, picks - tokens, picks)
        slot_seg = slot // seg_len
        kv_row = jnp.bitwise_xor(pair.astype(jnp.int32), row_core)
        return picks, slot_seg, kv_row * seg_len + (slot - slot_seg * seg_len)

    split = 3 * quarter
    g_own = cotangent[0]
    cosine, sine = rope_tables(seg_len)
    if use_kernel:
        qo_far, qo_side = flip(qo_keep, "seg", 4), flip(qo_give, "seg", 6)
        picks, slot_seg, within = places_of(coded, core)
        slot_x, slot_low = slot_seg % 2, (slot_seg // 2) % 2
        same_x = slot_x == x
        in_group = jnp.where(same_x, 5, 4 + 2 * slot_low)
        before = jnp.where(same_x, 0, 2) + slot_low
        piece_no = jnp.where(slot_seg // 4 == high, in_group, before)
        columns = jnp.where(picks >= 0, piece_no * kv_rows + within, -1)
        live_two = jnp.bitwise_and(coded[:, :, 0], 1)[:, None, :]
        live_two = jnp.pad(live_two, ((0, 0), (0, 0), (0, cdiv(seg_len, LANES) * LANES - seg_len)))
        down_recv = flip(down_w, "seg", 4)
        (
            qo_keep, qo_near, qo_far, qo_side, kv_keep, kv_recv, x_own, gate_up, columns, live_two, down_w, down_recv
        ) = fence(
            qo_keep, qo_near, qo_far, qo_side, kv_keep, kv_recv, x_own, gate_up, columns, live_two, down_w, down_recv
        )

        pieces = ordered(kv_keep[:, None], kv_recv[:, None], low, 1)
        own_k, own_v = pieces[0], pieces[1]
        near = ordered(qo_keep[None, None], qo_near[None, None], low, 1)
        far = ordered(qo_far[None, None], qo_side[None, None], low, 1)
        qo = ordered(near, far, high, 0)[:, :, None, None]
        qo_a, qo_b = qo[..., :split], qo[..., split:]
        up_high = [(i, i + 4) for i in range(n_seg - 4)]

        def cross(value):
            return lax.ppermute(value, "seg", up_high)

        cross_k, side_k = cross(own_k), flip_x(own_k)
        a_recv, b_recv = flip_x(qo_a), flip_y(qo_b)
        x_recv = flip_z(x_own)
        gu_keep, gu_give = halves(gate_up, 1, core)
        gu_recv = flip_core(gu_give)
        mask = build_mask(columns, live_two, len(PIECES) * kv_rows // LANES)
        qo_a, qo_b, a_recv, b_recv, cross_k, side_k, own_v, x_own, x_recv, gu_keep, gu_recv, mask, down_w, down_recv = fence(
            qo_a, qo_b, a_recv, b_recv, cross_k, side_k, own_v, x_own, x_recv, gu_keep, gu_recv, mask, down_w, down_recv
        )

        cross_v, cross_side_k = cross(own_v), flip_x(cross_k)
        qo_a, qo_b = ordered(qo_a, a_recv, x, 2), ordered(qo_b, b_recv, y, 3)
        a_recv, b_recv = flip_y(qo_a), flip_x(qo_b)
        gu_keep, gu_give = halves(ordered(gu_keep, gu_recv, core, 2), 0, low)
        gu_recv = flip_z(gu_give)
        x_two = ordered(x_own[None], x_recv[None], low, 0)
        x_recv = flip_core(x_two)
        qo_a, qo_b, a_recv, b_recv, cross_v, cross_side_k, own_v, gu_keep, gu_recv, x_two, x_recv, mask, down_w, down_recv = fence(
            qo_a, qo_b, a_recv, b_recv, cross_v, cross_side_k, own_v, gu_keep, gu_recv, x_two, x_recv, mask, down_w, down_recv
        )

        cross_side_v, side_v = flip_x(cross_v), flip_x(own_v)
        other_mask = flip_core(mask)
        w_a, w_b = flat(ordered(qo_a, a_recv, y, 3)), flat(ordered(qo_b, b_recv, x, 2))
        gate_up = ordered(gu_keep[:, None], gu_recv[:, None], low, 1)[:, None]
        gu_recv = flip(gate_up, "seg", 4)
        down_w = ordered(down_w, down_recv, high, 0)
        down_recv = flip_y(down_w)
        x_all = jnp.stack([x_two, x_recv], 1).reshape(4, seg_len, width)
        queries, keys, values, h_one, inv_one = project(x_all, w_a, w_b, cosine, sine)
        wo_near = w_b[:, :quarter]
        queries, keys, values, cross_side_v, side_v, gate_up, gu_recv, down_w, down_recv, wo_near, g_own, other_mask = fence(
            queries, keys, values, cross_side_v, side_v, gate_up, gu_recv, down_w, down_recv, wo_near, g_own, other_mask
        )

        key_pieces = (cross_k, cross_side_k, side_k, own_k)
        value_pieces = (cross_v, cross_side_v, side_v, own_v)
        gate, upw = [ordered(gate_up[i], gu_recv[i], high, 0)[:, :, None, None] for i in range(2)]
        down_w = ordered(down_w, down_recv, y, 3)
        down_a, down_b = down_w[..., : width // 2], down_w[..., width // 2 :]
        g_recv, u_recv, a_recv, wo_far = flip_x(gate), flip_y(upw), flip_x(down_a), flip_z(wo_near)
        out_low, out_f32, p_memory, p_local, inverse = attention_forward(
            queries, keys, values, mask, other_mask, key_pieces, value_pieces
        )
        g_far = flip_z(g_own)
        out_low, gate, upw, g_recv, u_recv, down_a, a_recv, down_b, wo_near, wo_far, g_own, g_far = fence(
            out_low, gate, upw, g_recv, u_recv, down_a, a_recv, down_b, wo_near, wo_far, g_own, g_far
        )
    else:
        qo = gather_high(ordered(qo_keep[None], qo_near[None], low, 0)[None, :, None, None])
        kv = ordered(kv_keep[:, None], kv_recv[:, None], low, 1)
        w_a, w_b = flat(gather_y(gather_x(qo[..., :split]))), flat(gather_x(gather_y(qo[..., split:])))
        x_all = all_blocks(two_rows(x_own))
        gu_keep, gu_give = halves(gate_up, 1, core)
        gu_keep, gu_give = halves(ordered(gu_keep, flip_core(gu_give), core, 2), 0, low)
        gate, upw = gather_high_pair(ordered(gu_keep[:, None], flip_z(gu_give)[:, None], low, 1))
        down_w = gather_y(gather_high(down_w))
        down_a, down_b = down_w[..., : width // 2], down_w[..., width // 2 :]
        coded = all_blocks(coded)
        row_core = jnp.bitwise_xor(core, jnp.arange(4, dtype=jnp.int32) % 2)[:, None, None]
        picks, slot_seg, within = places_of(coded, row_core)
        live_all = jnp.bitwise_and(coded[:, :, 0], 1)[:, None, :]
        columns = jnp.where(picks >= 0, slot_seg * kv_rows + within, n_seg * kv_rows)
        blocks_at = jnp.arange(4)[:, None, None]
        queries_at = jnp.arange(seg_len)[None, :, None]
        allow = jnp.zeros((4, seg_len, n_seg * kv_rows), BF).at[blocks_at, queries_at, columns].set(1.0, mode="drop")
        allow = allow.reshape(4, seg_len, n_seg, kv_rows).transpose(2, 0, 1, 3)
        memory = jnp.swapaxes(kv, 0, 1)[None, :, None]
        memory = gather_x(gather_high(memory)).reshape(n_seg, 2, kv_rows, quarter)
        queries, keys, values, h_one, inv_one = project(x_all, w_a, w_b, cosine, sine)
        wo_near = w_b[:, :quarter]
        out_low, out_f32, log_total = stream_forward(queries, keys, values, live_all, allow, memory)
        g_recv, u_recv, a_recv, wo_far = flip_x(gate), flip_y(upw), flip_x(down_a), flip_z(wo_near)
        g_far = flip_z(g_own)

    h_one = h_one.reshape(group_tokens, width)
    inv_one = inv_one.reshape(group_tokens, 1)
    x_float = x_all.reshape(group_tokens, width).astype(F32)
    g_attn = w_b[:, quarter].astype(F32)
    g_ffn = w_b[:, quarter + 1].astype(F32)
    att_near = out_low.reshape(group_tokens, quarter)
    att_far = flip_z(att_near)
    gate, upw = ordered(gate, g_recv, x, 2), ordered(upw, u_recv, y, 3)
    g_recv, u_recv = flip_y(gate), flip_x(upw)
    wo_both = jnp.stack([wo_near, wo_far])
    wo_recv = flip_core(wo_both)
    wo = join_four(wo_both, wo_recv, False)
    att_near, att_far, gate, upw, g_recv, u_recv, down_b, wo, g_own, g_far = fence(
        att_near, att_far, gate, upw, g_recv, u_recv, down_b, wo, g_own, g_far
    )

    att_both = jnp.stack([att_near, att_far])
    att_recv = flip_core(att_both)
    down_recv = flip_x(down_b)
    g_two = ordered(g_own[None], g_far[None], low, 0)
    g_recv_core = flip_core(g_two)
    wg, wu = flat(ordered(gate, g_recv, y, 3)), flat(ordered(upw, u_recv, x, 2))
    attended = join_four(att_both, att_recv, True)
    x_one = x_float + matmul(attended, wo)
    h_two_f, inv_two = norm_forward(x_one, g_ffn)
    h_two = h_two_f.astype(BF)
    gate_out = matmul(h_two, wg)
    up_out = matmul(h_two, wu)
    sigma = jax.nn.sigmoid(gate_out)
    swish = gate_out * sigma
    hidden = (swish * up_out).astype(BF)
    grad_out = jnp.stack([g_two, g_recv_core], 1).reshape(group_tokens, width)

    down_b, hidden = fence(down_b, hidden)
    wd = jnp.concatenate([flat(ordered(down_a, a_recv, x, 2)), flat(ordered(down_b, down_recv, x, 2))], 1)
    d_hidden = matmul_cols(grad_out, wd)
    d_gate = (d_hidden * up_out * sigma * (1.0 + gate_out * (1.0 - sigma))).astype(BF)
    d_up = (d_hidden * swish).astype(BF)
    sums_keep, sums_give = back_project([d_gate, d_up], [wg, wu])
    sums_recv = flip_core(sums_give)
    (keep_g, give_g), (keep_u, give_u) = gradient((h_two, [d_gate], "x", None), (h_two, [d_up], "y", None))
    sums_keep, sums_recv, keep_g, give_g, keep_u, give_u, hidden, wd = fence(
        sums_keep, sums_recv, keep_g, give_g, keep_u, give_u, hidden, wd
    )

    sums = add_kernel(sums_keep, sums_recv)
    far_sums = flip_z(sums)
    recv_g, recv_u = flip_x(give_g), flip_y(give_u)
    down_keep, down_give = back_project([hidden], [wd], False)
    down_recv = flip_core(down_give)
    keep_wd, give_wd = gradient_units(hidden, grad_out)
    sums, far_sums, keep_g, keep_u, recv_g, recv_u, down_keep, down_recv, keep_wd, give_wd = fence(
        sums, far_sums, keep_g, keep_u, recv_g, recv_u, down_keep, down_recv, keep_wd, give_wd
    )

    own = 2 * low * seg_len
    summed = add_kernel(sums, far_sums)
    summed_recv = flip_core(summed)
    d_branch, d_att, d_x_own = branch_back(
        summed,
        summed_recv,
        x_one.reshape(4, seg_len, width),
        g_ffn[None],
        g_two,
        g_recv_core,
        wo,
    )
    d_branch = d_branch.reshape(group_tokens, width)
    keep_g, keep_u, recv_g, recv_u, d_att, d_branch, down_keep, down_recv = fence(
        keep_g, keep_u, recv_g, recv_u, d_att, d_branch, down_keep, down_recv
    )

    keep_g, give_g = split_sums(keep_g, recv_g, "y")
    keep_u, give_u = split_sums(keep_u, recv_u, "x")
    down_own, down_give = pair_add(down_keep, down_recv)
    w_thirds = [w_a[:, i * quarter : (i + 1) * quarter] for i in range(3)]
    if use_kernel:
        recv_g, recv_u = flip_y(give_g), flip_x(give_u)
        down_recv = flip_z(down_give)
        d_kv, dq_local = attention_backward_local(
            d_att, out_f32, queries, keys, values, inverse, p_local, cosine, sine
        )
        d_kv = d_kv.reshape(2, group_tokens, quarter)
        (keep_kv, give_kv), (keep_wo, give_wo) = gradient(
            (h_one, [d_kv[0], d_kv[1]], "y", None), (attended, [d_branch], "y", quarter)
        )
        give_kvo = jnp.concatenate([give_kv, give_wo], -1)
        keep_kvo = jnp.concatenate([keep_kv, keep_wo], -1)
        keep_kvo, give_kvo, keep_g, recv_g, keep_u, recv_u, dq_local, keep_wd, give_wd, down_own, down_recv = fence(
            keep_kvo, give_kvo, keep_g, recv_g, keep_u, recv_u, dq_local, keep_wd, give_wd, down_own, down_recv
        )
        gu_parts = plane_sort((keep_g, recv_g), (keep_u, recv_u))
        recv_kvo = flip_y(give_kvo)
        gu_flips = z_flips(gu_parts)
        recv_wd = flip_x(give_wd)
        d_q = attention_backward(
            d_att, out_f32, dq_local, inverse, p_memory, cosine, sine, key_pieces, value_pieces
        )
        d_q, keep_kvo = fence(d_q, keep_kvo)

        d_q = d_q.reshape(group_tokens, quarter)
        ((keep_q, *give_q),) = gradient((h_one, [d_q], "xy", None))
        keep_q, give_q, d_q, keep_kvo, recv_kvo, keep_wd, recv_wd, gu_kept, gu_flips = fence(
            keep_q, give_q, d_q, keep_kvo, recv_kvo, keep_wd, recv_wd, gu_parts[0], gu_flips
        )
        recv_q = plane_flips(give_q)
        keep_kvo, give_kvo = split_sums(keep_kvo, recv_kvo, "x")
        keep_wd, give_wd = split_sums(
            keep_wd.reshape((-1,) + keep_wd.shape[2:]), recv_wd.reshape((-1,) + keep_wd.shape[2:]), "y"
        )
        recv_wd = flip_y(give_wd)
        recv_kvo = flip_x(give_kvo)
        d_h_keep, d_h_give = back_project([d_q, d_kv[0], d_kv[1]], w_thirds)
        gu_keep, gu_give = z_merge(gu_kept, *gu_flips)
        keep_q, recv_q, keep_kvo, recv_kvo, keep_wd, recv_wd, d_h_keep, d_h_give, gu_keep, gu_give = fence(
            keep_q, recv_q, keep_kvo, recv_kvo, keep_wd, recv_wd, d_h_keep, d_h_give, gu_keep, gu_give
        )
        *parts, wd_own = plane_sort((keep_q,) + tuple(recv_q), (keep_kvo, recv_kvo), units=(keep_wd, recv_wd))
        parts, d_h_give, wd_own = fence(parts, d_h_give, wd_own)
        d_h_recv = flip_core(d_h_give)
        flips = z_flips(parts)
        d_h_own, d_h_give = pair_add(d_h_keep, d_h_recv)
        d_h_recv = flip_z(d_h_give)
        gu_recv = flip_core(gu_give)
        sum_wg, sum_wu, grad_g_ffn = join_units(gu_keep, gu_recv, (w_gate, w_up), gain_ffn, n_devices)
        grad_x = input_back(d_h_own, d_h_recv, x_all, g_attn[None], d_x_own)
        kept, flips, grad_x, wd_own, sum_wg, sum_wu = fence(parts[0], flips, grad_x, wd_own, sum_wg, sum_wu)
        qkvo_keep, qkvo_give = z_merge(kept, *flips)
        qkvo_recv = flip_core(qkvo_give)
        wd_recv = flips[1][kept.shape[0] : kept.shape[0] + wd_own.shape[0]]
        sum_wd = wd_own.astype(F32) + wd_recv.astype(F32)
    else:
        down_recv = flip_z(down_give)
        recv_wd = flip_x(give_wd)
        d_q, *d_kv = stream_backward(
            d_att, out_f32, queries, keys, values, live_all, log_total, allow, memory, cosine, sine
        ).reshape(3, group_tokens, quarter)

        def by_chip(value):
            return value.reshape(n_high, 2, -1, value.shape[-1])

        (keep_qkv, *give_qkv), (keep_wo, *give_wo) = gradient(
            (h_one, [d_q, d_kv[0], d_kv[1]], "xy", None), (attended, [d_branch], "xy", quarter)
        )
        plane_gu = [add_low(keep_g, flip_y(give_g)), add_low(keep_u, flip_x(give_u))]
        z_gu = z_plain(by_chip(jnp.concatenate(plane_gu, -1)))
        plane_qkvo = [add_all(keep_qkv, *plane_flips(give_qkv)), add_all(keep_wo, *plane_flips(give_wo))]
        z_qkvo = z_plain(by_chip(jnp.concatenate(plane_qkvo, -1)))
        (gu_keep, gu_give), (qkvo_keep, qkvo_give) = core_halves(z_gu), core_halves(z_qkvo)
        qkvo_recv, gu_recv = flip_core(qkvo_give), flip_core(gu_give)
        keep_wd, give_wd = halves(add_low(keep_wd, recv_wd), 1, y)
        recv_wd = flip_y(give_wd)
        d_h_keep, d_h_give = back_project([d_q, d_kv[0], d_kv[1]], w_thirds)
        d_h_own, d_h_give = pair_add(d_h_keep, flip_core(d_h_give))
        d_h_recv = flip_z(d_h_give)
        grad_x = input_back(d_h_own, d_h_recv, x_all, g_attn[None], d_x_own)
        sum_wd = reduce_high(add_low(keep_wd, recv_wd)[:, None])[0].astype(F32)
        sum_wg, sum_wu, grad_g_ffn = join_units(gu_keep, gu_recv, (w_gate, w_up), gain_ffn, n_devices)
    layer_output = (cut(x_one, own, seg_len, 0) + down_own.astype(F32) + down_recv.astype(F32)).astype(BF)
    sum_q, sum_k, sum_v, sum_o, grad_g_attn = join_columns(
        qkvo_keep, qkvo_recv, (w_query, w_key, w_value), gain_attn, 4
    )
    return (
        layer_output[None],
        grad_x[None],
        grad_g_attn,
        sum_q,
        sum_k,
        sum_v,
        sum_o,
        grad_g_ffn,
        sum_wg,
        sum_wu,
        sum_wd,
    )


def solution(mesh):
    tokens = P("rep", "seg", None)
    vector = P(("seg", "rep"))
    matrix = P(("seg", "rep"), None)
    return jax.shard_map(
        local,
        mesh=mesh,
        in_specs=(
            tokens,
            P("rep", "seg"),
            tokens,
            tokens,
            tokens,
            vector,
            matrix,
            matrix,
            matrix,
            matrix,
            vector,
            matrix,
            matrix,
            matrix,
            tokens,
        ),
        out_specs=(tokens, tokens, vector, matrix, matrix, matrix, matrix, vector, matrix, matrix, matrix),
        check_vma=False,
    )
```

```python
import jax
import jax.numpy as jnp
from jax import lax
from jax.experimental import pallas as pl
from jax.experimental.pallas import tpu as pltpu
from jax.sharding import PartitionSpec as P

H = 8
HD = 128
EPSILON = 1e-05
NEG_BIG = -1e30
POS_BIG = 1e30
ROPE_BASE = 10000.0
LANES = 128
KERNEL_HIGH = 2
LOG2_E = 1.4426950408889634
VMEM_BYTES = 44 * 1024 * 1024

SHORT = pl.CostEstimate(flops=1000, bytes_accessed=1000, transcendentals=0)

BF = jnp.bfloat16
F32 = jnp.float32


def cdiv(a, b):
    return -(-a // b)


def flip(value, axis, bit):
    count = lax.axis_size(axis)
    return lax.ppermute(value, axis, [(i, i ^ bit) for i in range(count)])


def flip_core(value):
    return flip(value, "rep", 1)


def flip_y(value):
    return flip(value, "rep", 2)


def flip_x(value):
    return flip(value, "seg", 1)


def flip_z(value):
    return flip(value, "seg", 2)


def ordered(mine, other, bit, axis):
    first = jnp.where(bit == 0, mine, other)
    second = jnp.where(bit == 0, other, mine)
    return jnp.concatenate([first, second], axis)


def pick(value, index, axis):
    return lax.dynamic_index_in_dim(value, index, axis, keepdims=False)


def cut(value, start, size, axis=-1):
    return lax.dynamic_slice_in_dim(value, start, size, axis % value.ndim)


def fence(*values):
    return lax.optimization_barrier(values)


def place():
    seg = lax.axis_index("seg")
    rep = lax.axis_index("rep")
    return seg % 2, (seg // 2) % 2, seg // 4, rep // 2, rep % 2


def high_bits():
    bit = 4
    out = []
    while bit < lax.axis_size("seg"):
        out.append(bit)
        bit *= 2
    return out


def gather_high(cur):
    seg = lax.axis_index("seg")
    for bit in high_bits():
        cur = ordered(cur, flip(cur, "seg", bit), (seg // bit) % 2, 0)
    return cur


def gather_x(cur):
    return ordered(cur, flip_x(cur), place()[0], 2)


def gather_y(cur):
    return ordered(cur, flip_y(cur), place()[3], 3)


def gather_high_pair(cur):
    seg = lax.axis_index("seg")
    cur = cur[:, None]
    bits = high_bits()
    for bit in bits[:-1]:
        cur = ordered(cur, flip(cur, "seg", bit), (seg // bit) % 2, 1)
    recv = flip(cur, "seg", bits[-1])
    side = (seg // bits[-1]) % 2
    return [ordered(cur[i], recv[i], side, 0)[:, :, None, None] for i in range(2)]


def flat(cur):
    return cur.reshape(-1, cur.shape[-1])


def halve(value, axis_name, bit, side, axis):
    recv = flip(pick(value, 1 - side, axis), axis_name, bit)
    kept = pick(value, side, axis)
    return (kept.astype(F32) + recv.astype(F32)).astype(BF)


def plane_shape(value, low):
    high = lax.axis_size("seg") // 4
    return value.reshape(high, low, 2, -1, value.shape[-1])


def halves(cur, axis, side):
    return pick(cur, side, axis), pick(cur, 1 - side, axis)


def plane_flips(parts):
    n_rep = lax.axis_size("rep")
    count = lax.axis_size("seg") * n_rep
    far = [(i, i ^ n_rep ^ 2) for i in range(count)]
    return flip_x(parts[0]), flip_y(parts[1]), lax.ppermute(parts[2], ("seg", "rep"), far)


def add_all(first, *others):
    total = first.astype(F32)
    for other in others:
        total = total + other.astype(F32)
    return total.astype(BF)


def z_flips(parts):
    return flip_z(parts[1]), flip(parts[2], "seg", 4), flip(parts[3], "seg", 6)


def z_plain(cur):
    low = place()[1]
    sums = reduce_high(cur)
    return ordered(pick(sums, low, 0)[None], flip_z(pick(sums, 1 - low, 0))[None], low, 0)


def reduce_high(cur):
    seg = lax.axis_index("seg")
    for bit in reversed(high_bits()):
        cur = cur.reshape((2, cur.shape[0] // 2) + cur.shape[1:])
        cur = halve(cur, "seg", bit, (seg // bit) % 2, 0)
    return cur[0]


def trade_core(quarters):
    core = place()[4]
    low, unused, rows, cols = 2, 2, quarters.shape[1], quarters.shape[2]
    four = quarters.reshape(2, 2, rows, cols)
    return ordered(pick(four, core, 1), flip_core(pick(four, 1 - core, 1)), core, 1)


def trade_z(halves):
    low = place()[1]
    return ordered(pick(halves, low, 0)[None], flip_z(pick(halves, 1 - low, 0))[None], low, 0)


def gather_z_four(halves):
    seg = lax.axis_index("seg")
    low = (seg // 2) % 2
    keep, give = pick(halves, low, 0)[None, None], pick(halves, 1 - low, 0)[None, None]
    near = ordered(keep, flip(give, "seg", 2), low, 1)
    far = ordered(flip(keep, "seg", 4), flip(give, "seg", 6), low, 1)
    return ordered(near, far, (seg // 4) % 2, 0)[:, :, None, None]


def start_gather(traded):
    return traded[None, :, None, None]


def core_halves(mine):
    core = place()[4]
    four = mine.reshape(2, 2, mine.shape[1] // 2, mine.shape[2])
    return halves(four, 1, core)


def all_blocks(by_low):
    both = jnp.stack([by_low, flip_core(by_low)], 1)
    return both.reshape((-1,) + by_low.shape[1:])


def two_rows(value):
    return ordered(value[None], flip_z(value)[None], place()[1], 0)


def core_parts(part):
    blocks = part.reshape((2, 2, part.shape[0] // 4) + part.shape[1:])
    return blocks[:, 0].astype(BF), blocks[:, 1].astype(BF)


def core_sums(part):
    blocks = part.reshape((2, 2, part.shape[0] // 4) + part.shape[1:])
    return (blocks[:, 0] + flip_core(blocks[:, 1].astype(BF)).astype(F32)).astype(BF)


def own_sums(sums):
    low = place()[1]
    return pick(sums, low, 0).astype(F32) + flip_z(pick(sums, 1 - low, 0)).astype(F32)


def z_sums(sums):
    return (sums.astype(F32) + flip_z(sums).astype(F32)).astype(BF)


def both_cores(sums):
    return jnp.stack([sums, flip_core(sums)], 1).astype(F32)


def unit_blocks(n_blocks):
    order = []
    for block in range(n_blocks):
        high, low, rest, core = block // 16, (block // 8) % 2, (block // 2) % 4, block % 2
        order.append((low * 2 + core, high * 4 + rest))
    return order


def split_units(one, two, n_blocks):
    rows, total = one.shape
    size = total // n_blocks

    def body(one_ref, two_ref, out_ref):
        for half, in_ref in enumerate((one_ref, two_ref)):
            for block, (quarter, at) in enumerate(unit_blocks(n_blocks)):
                out_ref[quarter, half * rows : (half + 1) * rows, at * size : (at + 1) * size] = in_ref[
                    :, block * size : (block + 1) * size
                ]

    return pl.pallas_call(
        body,
        out_shape=jax.ShapeDtypeStruct((4, 2 * rows, total // 4), one.dtype),
        cost_estimate=SHORT,
        name="split_units",
    )(one, two)


def matmul(left, right):
    return jnp.dot(left, right, preferred_element_type=F32)


def matmul_rows(left, right):
    return lax.dot_general(left, right, (((0,), (0,)), ((), ())), preferred_element_type=F32)


def matmul_cols(left, right):
    return lax.dot_general(left, right, (((1,), (1,)), ((), ())), preferred_element_type=F32)


def norm_forward(values, gain):
    inverse = lax.rsqrt(jnp.mean(values * values, axis=-1, keepdims=True) + EPSILON)
    return (values * inverse * gain, inverse)


def norm_backward(values, inverse, gain, grad_out):
    normed = values * inverse
    scaled = grad_out * gain
    grad_values = inverse * (scaled - normed * jnp.mean(scaled * normed, axis=-1, keepdims=True))
    return (grad_values, normed)


def rope_tables(seg_len):
    position = jnp.arange(seg_len).astype(F32)
    freqs = ROPE_BASE ** (-(2.0 * jnp.arange(HD // 2).astype(F32)) / HD)
    angle = position[:, None] * freqs[None, :]
    cosine, sine = jnp.cos(angle), jnp.sin(angle)
    return (jnp.concatenate([cosine, cosine], -1), jnp.concatenate([-sine, sine], -1))


def rope_heads(values, cosine, sine):
    half = HD // 2
    swapped = jnp.concatenate([values[..., half:], values[..., :half]], -1)
    return values * cosine[:, None, :] + swapped * sine[:, None, :]


def mask_kernel(n_cols, cols_ref, live_ref, out_ref, scratch):
    queries = cols_ref.shape[1]
    picks = cols_ref[0]
    pad = scratch.shape[0]
    high = lax.shift_right_arithmetic(picks, 7)
    low = jnp.bitwise_and(picks, LANES - 1)
    iota_high = lax.broadcasted_iota(jnp.int32, (pad, picks.shape[1]), 0)
    iota_low = lax.broadcasted_iota(jnp.int32, (LANES, picks.shape[1]), 0)
    for i in range(queries):
        hot_high = jnp.where(iota_high == high[i : i + 1, :], 1.0, 0.0).astype(BF)
        hot_low = jnp.where(iota_low == low[i : i + 1, :], 1.0, 0.0).astype(BF)
        scratch[:, i, :] = matmul_cols(hot_high, hot_low)
    out_ref[0, 0:n_cols] = jnp.where(scratch[0:n_cols] > 0.5, POS_BIG, NEG_BIG).astype(BF)
    row = lax.broadcasted_iota(jnp.int32, (queries, LANES), 0) + pl.program_id(1) * queries
    for part in range(out_ref.shape[1] - n_cols):
        col = lax.broadcasted_iota(jnp.int32, (queries, LANES), 1) + part * LANES
        live = live_ref[0, :, part * LANES : (part + 1) * LANES]
        allow = (col == row) | ((col < row) & (live == 1))
        out_ref[0, n_cols + part] = jnp.where(allow, POS_BIG, NEG_BIG).astype(BF)


def build_mask(columns, live, n_cols):
    rows, queries, picks = columns.shape
    block = 16
    pad = cdiv(n_cols, 8) * 8
    n_local = live.shape[2] // LANES
    return pl.pallas_call(
        lambda *refs: mask_kernel(n_cols, *refs),
        grid=(rows, queries // block),
        in_specs=[
            pl.BlockSpec((1, block, picks), lambda r, g: (r, g, 0)),
            pl.BlockSpec((1, 1, live.shape[2]), lambda r, g: (r, 0, 0)),
        ],
        out_specs=pl.BlockSpec((1, n_cols + n_local, block, LANES), lambda r, g: (r, 0, g, 0)),
        out_shape=jax.ShapeDtypeStruct((rows, n_cols + n_local, queries, LANES), BF),
        scratch_shapes=[pltpu.VMEM((pad, block, LANES), F32)],
        compiler_params=pltpu.CompilerParams(vmem_limit_bytes=VMEM_BYTES),
        cost_estimate=pl.CostEstimate(flops=12000000000, bytes_accessed=3000000, transcendentals=0),
        name="mask_build",
    )(columns, live)


def project_kernel(x_ref, wa_ref, wb_ref, cos_ref, sin_ref, q_ref, k_ref, v_ref, h_ref, inv_ref, gain_ref):
    quarter = q_ref.shape[2]

    @pl.when(pl.program_id(0) == 0)
    def gains():
        gain_ref[...] = jnp.transpose(wb_ref[:, quarter:].astype(F32), (1, 0))[0:8]

    x = x_ref[0].astype(F32)
    inverse = lax.rsqrt(jnp.mean(x * x, axis=-1, keepdims=True) + EPSILON)
    h = (x * inverse * gain_ref[0:1, :]).astype(BF)
    h_ref[0] = h
    inv_ref[0] = inverse
    turned = matmul(h, wa_ref[:, : 2 * quarter])
    for head in range(2 * quarter // HD):
        value = turned[:, head * HD : (head + 1) * HD]
        value = (value * cos_ref[...] + pltpu.roll(value, HD // 2, 1) * sin_ref[...]).astype(BF)
        if head < quarter // HD:
            q_ref[0, :, head * HD : (head + 1) * HD] = value
        else:
            at = head * HD - quarter
            k_ref[0, :, at : at + HD] = value
    v_ref[0] = matmul(h, wa_ref[:, 2 * quarter :]).astype(BF)


def project(x_all, w_a, w_b, cosine, sine):
    blocks, seg_len, width = x_all.shape
    quarter = w_a.shape[1] // 3
    whole = lambda array: pl.BlockSpec(array.shape, lambda r: (0, 0))
    head = pl.BlockSpec((1, seg_len, quarter), lambda r: (r, 0, 0))
    full = pl.BlockSpec((1, seg_len, width), lambda r: (r, 0, 0))
    out = jax.ShapeDtypeStruct((blocks, seg_len, quarter), BF)
    return pl.pallas_call(
        project_kernel,
        grid=(blocks,),
        in_specs=[full, whole(w_a), whole(w_b), whole(cosine), whole(sine)],
        out_specs=[head, head, head, full, pl.BlockSpec((1, seg_len, 1), lambda r: (r, 0, 0))],
        out_shape=[out, out, out, jax.ShapeDtypeStruct(x_all.shape, BF), jax.ShapeDtypeStruct((blocks, seg_len, 1), F32)],
        scratch_shapes=[pltpu.VMEM((8, width), F32)],
        compiler_params=pltpu.CompilerParams(vmem_limit_bytes=VMEM_BYTES),
        cost_estimate=SHORT,
        name="project",
    )(x_all, w_a, w_b, cosine, sine)


def plane_place():
    x, low, unused, y, core = place()
    return jnp.stack([x, y, 2 * low + core]).astype(jnp.int32)


def gradient(*entries):
    tokens, width = entries[0][0].shape
    n_blocks = lax.axis_size("seg")
    rows = width // n_blocks
    half = rows // 2
    sizes = [[entry[3] or right.shape[1] for right in entry[1]] for entry in entries]
    if rows % LANES:
        x, unused, unused, y, unused = place()
        outs = []
        for left, rights, way, columns in entries:
            if columns:
                rights = [cut(right, plane_place()[2] * columns, columns) for right in rights]
            full = jnp.concatenate([matmul_rows(left, right).astype(BF) for right in rights], 1)
            full = full.reshape(-1, 2, 2, half, full.shape[1])
            if way == "xy":
                near, side = halves(full, 1, x)
                near, side = halves(near, 1, y), halves(side, 1, y)
                parts = [near[0], side[0], near[1], side[1]]
            else:
                parts = halves(full, 1, x) if way == "x" else halves(full, 2, y)
            outs.append([part.reshape(-1, half, part.shape[-1]) for part in parts])
        return outs
    lefts = []
    for entry in entries:
        if not any(entry[0] is left for left in lefts):
            lefts.append(entry[0])
    which = [[entry[0] is left for left in lefts].index(True) for entry in entries]
    counts = [4 if entry[2] == "xy" else 2 for entry in entries]
    shapes = []
    for entry, size, count in zip(entries, sizes, counts):
        blocks = n_blocks // 2 if entry[2] == "xy" else n_blocks
        shapes += [(blocks, half, sum(size))] * count
    n_rights = sum(len(size) for size in sizes)

    def body(at_ref, *refs):
        left_refs, right_refs = refs[: len(lefts)], list(refs[len(lefts) : len(lefts) + n_rights])
        out_refs = list(refs[len(lefts) + n_rights :])
        pair = pl.program_id(0)
        turned = [jnp.transpose(ref[...]) for ref in left_refs]

        def by_row(value):
            upper, lower = value[:half], value[half:]
            return jnp.where(at_ref[1] == 0, upper, lower), jnp.where(at_ref[1] == 0, lower, upper)

        for entry, i, size, count in zip(entries, which, sizes, counts):
            outs, out_refs = out_refs[:count], out_refs[count:]
            start = 0
            for width_here in size:
                product = matmul(turned[i], right_refs.pop(0)[...]).astype(BF)
                span = slice(start, start + width_here)
                start += width_here
                first, second = product[:rows], product[rows:]
                if entry[2] == "y":
                    for side, value in enumerate((first, second)):
                        outs[0][2 * pair + side, :, span], outs[1][2 * pair + side, :, span] = by_row(value)
                    continue
                same = jnp.where(at_ref[0] == 0, first, second)
                other = jnp.where(at_ref[0] == 0, second, first)
                if entry[2] == "x":
                    for ref, value in zip(outs, (same, other)):
                        ref[2 * pair, :, span] = value[:half]
                        ref[2 * pair + 1, :, span] = value[half:]
                else:
                    outs[0][pair, :, span], outs[2][pair, :, span] = by_row(same)
                    outs[1][pair, :, span], outs[3][pair, :, span] = by_row(other)

    in_specs = [pl.BlockSpec((tokens, 2 * rows), lambda i, at: (0, i))] * len(lefts)
    for entry, size in zip(entries, sizes):
        column = (lambda i, at: (0, at[2])) if entry[3] else (lambda i, at: (0, 0))
        in_specs += [pl.BlockSpec((tokens, width_here), column) for width_here in size]
    outs = pl.pallas_call(
        body,
        grid_spec=pltpu.PrefetchScalarGridSpec(
            num_scalar_prefetch=1,
            grid=(n_blocks // 2,),
            in_specs=in_specs,
            out_specs=[pl.BlockSpec(shape, lambda i, at: (0, 0, 0)) for shape in shapes],
        ),
        out_shape=[jax.ShapeDtypeStruct(shape, BF) for shape in shapes],
        compiler_params=pltpu.CompilerParams(vmem_limit_bytes=VMEM_BYTES),
        cost_estimate=SHORT,
        name="gradient",
    )(plane_place(), *lefts, *[right for entry in entries for right in entry[1]])
    groups = []
    for count in counts:
        groups.append(outs[:count])
        outs = outs[count:]
    return groups


def split_sums(keep, recv, way):
    n_blocks, rows, cols = keep.shape

    def body(at_ref, keep_ref, recv_ref, mine_ref, give_ref):
        side = at_ref[1] if way == "y" else at_ref[0]
        for block in range(n_blocks // 2):
            for at, out_ref in ((2 * block + side, mine_ref), (2 * block + 1 - side, give_ref)):
                out_ref[block] = (keep_ref[at].astype(F32) + recv_ref[at].astype(F32)).astype(BF)

    vmem = pl.BlockSpec(memory_space=pltpu.VMEM)
    return pl.pallas_call(
        body,
        in_specs=[pl.BlockSpec(memory_space=pltpu.SMEM)] + [vmem] * 2,
        out_specs=[vmem] * 2,
        out_shape=[jax.ShapeDtypeStruct((n_blocks // 2, rows, cols), BF)] * 2,
        compiler_params=pltpu.CompilerParams(vmem_limit_bytes=VMEM_BYTES),
        cost_estimate=SHORT,
        name="split_sums",
    )(plane_place(), keep, recv)


def gradient_units(left, right):
    tokens, width = left.shape
    n_high = lax.axis_size("seg") // 4
    rows = width // (4 * n_high)
    cols = right.shape[1]
    step = 256
    if rows % 8:
        full = matmul_rows(left, right).astype(BF).reshape(-1, 2, 2, rows, cols)
        return halves(full, 1, place()[0])

    def body(at_ref, left_ref, right_ref, keep_ref, give_ref):
        product = matmul_rows(left_ref[...], right_ref[...])
        for high in range(n_high):
            for y in range(2):
                zero, one = [
                    product[(high * 4 + x * 2 + y) * rows : (high * 4 + x * 2 + y + 1) * rows] for x in range(2)
                ]
                keep_ref[high, y] = jnp.where(at_ref[0] == 0, zero, one).astype(BF)
                give_ref[high, y] = jnp.where(at_ref[0] == 0, one, zero).astype(BF)

    shape = (n_high, 2, rows, cols)
    return pl.pallas_call(
        body,
        grid_spec=pltpu.PrefetchScalarGridSpec(
            num_scalar_prefetch=1,
            grid=(cols // step,),
            in_specs=[
                pl.BlockSpec((tokens, width), lambda i, at: (0, 0)),
                pl.BlockSpec((tokens, step), lambda i, at: (0, i)),
            ],
            out_specs=[pl.BlockSpec((n_high, 2, rows, step), lambda i, at: (0, 0, 0, i))] * 2,
        ),
        out_shape=[jax.ShapeDtypeStruct(shape, BF)] * 2,
        compiler_params=pltpu.CompilerParams(vmem_limit_bytes=VMEM_BYTES),
        cost_estimate=SHORT,
        name="gradient_units",
    )(plane_place(), left, right)


def gather_columns(matrices, gain_one, gain_two):
    rows, width = matrices[0].shape
    quarter = width // 4

    def body(one_ref, two_ref, *refs):
        out_ref = refs[-1]
        pair = jnp.concatenate([one_ref[...], two_ref[...], jnp.zeros((6, rows), F32)], 0)
        square = jnp.concatenate([pair, jnp.zeros((8, LANES - rows), F32)], 1)
        square = jnp.concatenate([square, jnp.zeros((LANES - 8, LANES), F32)], 0)
        gains = jnp.transpose(square)[:rows].astype(BF)
        for i in range(4):
            for at, ref in enumerate(refs[:-1]):
                out_ref[i, :, at * quarter : (at + 1) * quarter] = ref[:, i * quarter : (i + 1) * quarter]
            out_ref[i, :, len(matrices) * quarter :] = gains

    return pl.pallas_call(
        body,
        out_shape=jax.ShapeDtypeStruct((4, rows, len(matrices) * quarter + LANES), BF),
        cost_estimate=SHORT,
        name="gather_columns",
    )(gain_one.astype(F32)[None], gain_two.astype(F32)[None], *matrices)


def group_place():
    unused, low, high, unused, core = place()
    return jnp.stack([2 * high + low, low, core]).astype(jnp.int32)


def plane_sort(*groups, units=()):
    sizes = [group[0].shape[-1] for group in groups]
    rows, cols = groups[0][0].shape[1], sum(sizes)
    shapes = [(rows, cols)] * 4
    if units:
        unit_rows = units[0].shape[1]
        below = cdiv(unit_rows, 16) * 16
        shapes = [(rows + below if way == 2 else rows, cols) for way in range(4)] + [(unit_rows, cols)]

    def body(at_ref, *refs):
        in_refs, out_refs = list(refs[: -len(shapes)]), refs[-len(shapes) :]
        unit_refs = in_refs[len(in_refs) - len(units) :]
        for way in range(4):
            start = 0
            left = list(in_refs)
            for size, group in zip(sizes, groups):
                total = None
                for unused in group:
                    part = left.pop(0)[at_ref[0] ^ way].astype(F32)
                    total = part if total is None else total + part
                out_refs[way][0:rows, start : start + size] = total.astype(BF)
                start += size
        if units:
            high = lax.shift_right_logical(at_ref[0], 1)
            own = sum(ref[high].astype(F32) for ref in unit_refs)
            give = sum(ref[1 - high].astype(F32) for ref in unit_refs)
            out_refs[4][...] = own.astype(BF)
            give = jnp.concatenate([give, jnp.zeros((below - unit_rows, cols), F32)], 0)
            out_refs[2][rows : rows + below, :] = give.astype(BF)

    vmem = pl.BlockSpec(memory_space=pltpu.VMEM)
    arrays = [array for group in groups for array in group] + list(units)
    return pl.pallas_call(
        body,
        in_specs=[pl.BlockSpec(memory_space=pltpu.SMEM)] + [vmem] * len(arrays),
        out_specs=[vmem] * len(shapes),
        out_shape=[jax.ShapeDtypeStruct(shape, BF) for shape in shapes],
        compiler_params=pltpu.CompilerParams(vmem_limit_bytes=VMEM_BYTES),
        cost_estimate=SHORT,
        name="plane_sort",
    )(group_place(), *arrays)


def z_merge(kept, from_1, from_2, from_3):
    rows, cols = kept.shape
    half = rows // 2

    def body(at_ref, kept_ref, one_ref, two_ref, three_ref, keep_ref, give_ref):
        same = kept_ref[...].astype(F32) + two_ref[0:rows, :].astype(F32)
        other = one_ref[...].astype(F32) + three_ref[...].astype(F32)
        for quarter, value in ((at_ref[1], same), (1 - at_ref[1], other)):
            upper, lower = value[:half], value[half:]
            keep_ref[quarter] = jnp.where(at_ref[2] == 0, upper, lower).astype(BF)
            give_ref[quarter] = jnp.where(at_ref[2] == 0, lower, upper).astype(BF)

    vmem = pl.BlockSpec(memory_space=pltpu.VMEM)
    return pl.pallas_call(
        body,
        in_specs=[pl.BlockSpec(memory_space=pltpu.SMEM)] + [vmem] * 4,
        out_specs=[vmem] * 2,
        out_shape=[jax.ShapeDtypeStruct((2, half, cols), BF)] * 2,
        compiler_params=pltpu.CompilerParams(vmem_limit_bytes=VMEM_BYTES),
        cost_estimate=SHORT,
        name="z_merge",
    )(group_place(), kept, from_1, from_2, from_3)


def join_quarters(mine, recv, core_ref, start, size, z_low, core):
    return jnp.where(
        core_ref[2] == core, mine[z_low, :, start : start + size], recv[z_low, :, start : start + size]
    ).astype(F32)


def lane_sums(value):
    total = value[:, :LANES]
    for part in lane_blocks(value)[1:]:
        total = total + part
    return total


def sums_as_row(value):
    rows = value.shape[0]
    padded = jnp.concatenate([value, jnp.zeros((LANES - rows, LANES), F32)], 0)
    return jnp.sum(jnp.transpose(padded), axis=0, keepdims=True)[:, :rows]


def join_columns(mine, recv, weights, gain, n_matrices):
    rows, cols = mine.shape[1:]
    size = cols // n_matrices

    def body(at_ref, mine_ref, recv_ref, gain_ref, *refs):
        weight_refs, out_refs = refs[: len(weights)], refs[len(weights) :]
        total = jnp.zeros((rows, LANES), F32)
        for i in range(n_matrices):
            for z_low in range(2):
                for core in range(2):
                    at = (2 * z_low + core) * size
                    value = join_quarters(mine_ref, recv_ref, at_ref, i * size, size, z_low, core)
                    out_refs[i][:, at : at + size] = value
                    if i < len(weights):
                        total = total + lane_sums(value * weight_refs[i][:, at : at + size].astype(F32))
        out_refs[-1][...] = sums_as_row(total) / gain_ref[...]

    vmem = pl.BlockSpec(memory_space=pltpu.VMEM)
    outs = pl.pallas_call(
        body,
        in_specs=[pl.BlockSpec(memory_space=pltpu.SMEM)] + [vmem] * (3 + len(weights)),
        out_specs=[vmem] * (n_matrices + 1),
        out_shape=[jax.ShapeDtypeStruct((rows, 4 * size), F32)] * n_matrices + [jax.ShapeDtypeStruct((1, rows), F32)],
        cost_estimate=SHORT,
        name="join_columns",
    )(group_place(), mine, recv, gain.astype(F32)[None], *weights)
    return list(outs[:-1]) + [outs[-1][0]]


def join_units(mine, recv, weights, gain, n_blocks):
    rows, both = mine.shape[1:]
    quarter_size = both // 2
    size = 4 * quarter_size // n_blocks

    def body(at_ref, mine_ref, recv_ref, gain_ref, one_weight, two_weight, one_ref, two_ref, total_ref):
        total = jnp.zeros((rows, LANES), F32)
        for half, (out_ref, weight_ref) in enumerate(((one_ref, one_weight), (two_ref, two_weight))):
            for block, (quarter, at) in enumerate(unit_blocks(n_blocks)):
                start = half * quarter_size + at * size
                out_ref[:, block * size : (block + 1) * size] = join_quarters(
                    mine_ref, recv_ref, at_ref, start, size, quarter // 2, quarter % 2
                )
            total = total + lane_sums(out_ref[...] * weight_ref[...].astype(F32))
        total_ref[...] = sums_as_row(total) / gain_ref[...]

    vmem = pl.BlockSpec(memory_space=pltpu.VMEM)
    one, two, total = pl.pallas_call(
        body,
        in_specs=[pl.BlockSpec(memory_space=pltpu.SMEM)] + [vmem] * 5,
        out_specs=[vmem] * 3,
        out_shape=[jax.ShapeDtypeStruct((rows, 4 * quarter_size), F32)] * 2 + [jax.ShapeDtypeStruct((1, rows), F32)],
        cost_estimate=SHORT,
        name="join_units",
    )(group_place(), mine, recv, gain.astype(F32)[None], *weights)
    return one, two, total[0]


def pair_add(one, two):
    def body(at_ref, one_ref, two_ref, own_ref, give_ref):
        for way, out_ref in enumerate((own_ref, give_ref)):
            at = at_ref[1] ^ way
            out_ref[...] = (one_ref[at].astype(F32) + two_ref[at].astype(F32)).astype(BF)

    vmem = pl.BlockSpec(memory_space=pltpu.VMEM)
    return pl.pallas_call(
        body,
        in_specs=[pl.BlockSpec(memory_space=pltpu.SMEM)] + [vmem] * 2,
        out_specs=[vmem] * 2,
        out_shape=[jax.ShapeDtypeStruct(one.shape[1:], BF)] * 2,
        compiler_params=pltpu.CompilerParams(vmem_limit_bytes=VMEM_BYTES),
        cost_estimate=SHORT,
        name="pair_add",
    )(group_place(), one, two)


def back_project(lefts, weights, transposed=True):
    block = lefts[0].shape[0] // 4
    out = weights[0].shape[0] if transposed else weights[0].shape[1]

    def body(*refs):
        left_refs, weight_refs = refs[: len(lefts)], refs[len(lefts) : 2 * len(lefts)]
        keep_ref, give_ref = refs[2 * len(lefts) :]
        total = None
        for left_ref, weight_ref in zip(left_refs, weight_refs):
            part = (matmul_cols if transposed else matmul)(left_ref[...], weight_ref[...])
            total = part if total is None else total + part
        total = total.astype(BF)
        for i in range(4):
            (keep_ref, give_ref)[i % 2][i // 2] = total[i * block : (i + 1) * block]

    return pl.pallas_call(
        body,
        in_specs=[pl.BlockSpec(memory_space=pltpu.VMEM)] * (2 * len(lefts)),
        out_specs=[pl.BlockSpec(memory_space=pltpu.VMEM)] * 2,
        out_shape=[jax.ShapeDtypeStruct((2, block, out), BF)] * 2,
        compiler_params=pltpu.CompilerParams(vmem_limit_bytes=VMEM_BYTES),
        cost_estimate=SHORT,
        name="back_project",
    )(*lefts, *weights)


def join_four(near, far, near_recv, far_recv, of_tokens):
    rows, size = near.shape
    block = rows // 4

    def body(at_ref, near_ref, far_ref, near_recv_ref, far_recv_ref, out_ref):
        for z_low in range(2):
            here = at_ref[1] == z_low
            for core in range(2):
                at = (2 * z_low + core) * size
                for i in range(4):
                    j = i ^ 1 if of_tokens else i
                    mine, other = slice(i * block, (i + 1) * block), slice(j * block, (j + 1) * block)
                    ours = jnp.where(here, near_ref[mine], far_ref[mine])
                    theirs = jnp.where(here, near_recv_ref[other], far_recv_ref[other])
                    out_ref[mine, at : at + size] = jnp.where(at_ref[2] == core, ours, theirs)

    vmem = pl.BlockSpec(memory_space=pltpu.VMEM)
    return pl.pallas_call(
        body,
        in_specs=[pl.BlockSpec(memory_space=pltpu.SMEM)] + [vmem] * 4,
        out_specs=vmem,
        out_shape=jax.ShapeDtypeStruct((rows, 4 * size), near.dtype),
        compiler_params=pltpu.CompilerParams(vmem_limit_bytes=VMEM_BYTES),
        cost_estimate=SHORT,
        name="join_four",
    )(group_place(), near, far, near_recv, far_recv)


def branch_back(mine, recv, x_one, gain, g_mine, g_recv, w_out):
    blocks, seg_len, width = x_one.shape
    quarter = width // 4

    def body(at_ref, mine_ref, recv_ref, x_ref, gain_ref, g_ref, g_recv_ref, w_ref, branch_ref, att_ref, own_ref):
        block = pl.program_id(0)
        grad = jnp.where(block % 2 == 0, mine_ref[0], recv_ref[0]).astype(F32)
        passed = jnp.where(block % 2 == 0, g_ref[0], g_recv_ref[0]).astype(F32)
        values = x_ref[0]
        inverse = lax.rsqrt(jnp.mean(values * values, axis=-1, keepdims=True) + EPSILON)
        normed = values * inverse
        scaled = grad * gain_ref[...]
        mean = jnp.mean(scaled * normed, axis=-1, keepdims=True)
        total = passed + inverse * (scaled - normed * mean)
        low = total.astype(BF)
        branch_ref[0] = low
        att_ref[0] = matmul_cols(low, w_ref[...]).astype(BF)

        @pl.when(block == 2 * at_ref[1])
        def own():
            own_ref[...] = total

    pair = pl.BlockSpec((1, seg_len, width), lambda i, at: (i // 2, 0, 0))
    full = pl.BlockSpec((1, seg_len, width), lambda i, at: (i, 0, 0))
    return pl.pallas_call(
        body,
        grid_spec=pltpu.PrefetchScalarGridSpec(
            num_scalar_prefetch=1,
            grid=(blocks,),
            in_specs=[
                pair,
                pair,
                full,
                pl.BlockSpec((1, width), lambda i, at: (0, 0)),
                pair,
                pair,
                pl.BlockSpec((quarter, width), lambda i, at: (2 * at[1] + at[2], 0)),
            ],
            out_specs=[
                full,
                pl.BlockSpec((1, seg_len, quarter), lambda i, at: (i, 0, 0)),
                pl.BlockSpec((seg_len, width), lambda i, at: (0, 0)),
            ],
        ),
        out_shape=[
            jax.ShapeDtypeStruct((blocks, seg_len, width), BF),
            jax.ShapeDtypeStruct((blocks, seg_len, quarter), BF),
            jax.ShapeDtypeStruct((seg_len, width), F32),
        ],
        compiler_params=pltpu.CompilerParams(vmem_limit_bytes=VMEM_BYTES),
        cost_estimate=SHORT,
        name="branch_back",
    )(group_place(), mine, recv, x_one, gain, g_mine, g_recv, w_out)


def input_back(mine, recv, x_all, gain, passed):
    unused, seg_len, width = x_all.shape

    def body(at_ref, mine_ref, recv_ref, x_ref, gain_ref, passed_ref, out_ref):
        values = x_ref[0].astype(F32)
        inverse = lax.rsqrt(jnp.mean(values * values, axis=-1, keepdims=True) + EPSILON)
        normed = values * inverse
        scaled = (mine_ref[...].astype(F32) + recv_ref[...].astype(F32)) * gain_ref[...]
        mean = jnp.mean(scaled * normed, axis=-1, keepdims=True)
        out_ref[...] = (passed_ref[...] + inverse * (scaled - normed * mean)).astype(BF)

    tokens = pl.BlockSpec((seg_len, width), lambda i, at: (0, 0))
    return pl.pallas_call(
        body,
        grid_spec=pltpu.PrefetchScalarGridSpec(
            num_scalar_prefetch=1,
            grid=(1,),
            in_specs=[
                tokens,
                tokens,
                pl.BlockSpec((1, seg_len, width), lambda i, at: (2 * at[1], 0, 0)),
                pl.BlockSpec((1, width), lambda i, at: (0, 0)),
                tokens,
            ],
            out_specs=tokens,
        ),
        out_shape=jax.ShapeDtypeStruct((seg_len, width), BF),
        compiler_params=pltpu.CompilerParams(vmem_limit_bytes=VMEM_BYTES),
        cost_estimate=SHORT,
        name="input_back",
    )(group_place(), mine, recv, x_all, gain, passed)


def add_kernel(one, two):
    def body(one_ref, two_ref, out_ref):
        out_ref[...] = (one_ref[...].astype(F32) + two_ref[...].astype(F32)).astype(BF)

    return pl.pallas_call(
        body,
        in_specs=[pl.BlockSpec(memory_space=pltpu.VMEM)] * 2,
        out_specs=pl.BlockSpec(memory_space=pltpu.VMEM),
        out_shape=jax.ShapeDtypeStruct(one.shape, BF),
        compiler_params=pltpu.CompilerParams(vmem_limit_bytes=VMEM_BYTES),
        cost_estimate=SHORT,
        name="add_kernel",
    )(one, two)


def add_low(one, two):
    return (one.astype(F32) + two.astype(F32)).astype(BF)


def lane_blocks(value):
    return [value[:, i : i + LANES] for i in range(0, value.shape[1], LANES)]


PIECES = ((0, 0), (0, 1), (1, 0), (1, 1), (2, 0), (3, 0), (2, 1))
N_COMMON = 5
N_GROUPS = 4


def head_of(value, head):
    return value[:, head * HD : (head + 1) * HD]


def forward_kernel(q_ref, k_ref, v_ref, mine_ref, other_ref, *refs):
    key_refs, value_refs = refs[:N_GROUPS], refs[N_GROUPS : 2 * N_GROUPS]
    o_ref, of_ref, p_ref, pl_ref, inv_ref, s_ref, top_ref, total_ref, acc_ref = refs[2 * N_GROUPS :]
    heads = range(q_ref.shape[2] // HD)
    scale = HD ** (-0.5) * LOG2_E
    block = pl.program_id(0)
    upper = block >= 2
    queries = q_ref[0]
    seg_len = queries.shape[0]
    per = key_refs[0].shape[1] // LANES
    first = block % 2 == 0

    def bias(at):
        return jnp.where(first, mine_ref[0, at], other_ref[0, at]).astype(F32)

    local_bias = jnp.concatenate([bias(len(PIECES) * per + i) for i in range(cdiv(seg_len, LANES))], 1)[:, :seg_len]
    s_local = [
        jnp.minimum(matmul_cols(head_of(queries, h), head_of(k_ref[0], h)) * scale, local_bias) for h in heads
    ]

    def score(t, tops):
        group, low = PIECES[t]
        keys = key_refs[group][low]
        parts = [lane_blocks(matmul_cols(head_of(queries, h), head_of(keys, h)) * scale) for h in heads]
        for i in range(per):
            limit = bias(t * per + i)
            for h in heads:
                part = jnp.minimum(parts[h][i], limit)
                s_ref[h, t, :, i * LANES : (i + 1) * LANES] = part
                tops[h] = part if tops[h] is None else jnp.maximum(tops[h], part)
        return tops

    tops = [None for h in heads]
    for t in range(N_COMMON):
        tops = score(t, tops)
    for h in heads:
        top_ref[h] = tops[h]

    @pl.when(upper)
    def more_scores():
        tops = [top_ref[h] for h in heads]
        for t in range(N_COMMON, len(PIECES)):
            tops = score(t, tops)
        for h in heads:
            top_ref[h] = tops[h]

    row_max, e_local = [], []
    for h in heads:
        row_max.append(
            jnp.maximum(
                jnp.max(s_local[h], axis=-1, keepdims=True), jnp.max(top_ref[h], axis=-1, keepdims=True)
            )
        )
        expo = jnp.exp2(s_local[h] - row_max[h])
        e_local.append(jnp.sum(expo, axis=-1, keepdims=True))
        chances = expo.astype(BF)
        pl_ref[0, h] = chances
        acc_ref[h] = matmul(chances, head_of(v_ref[0], h))

    def weigh(t, h, total, acc):
        group, low = PIECES[t]
        expo = jnp.exp2(s_ref[h, t] - row_max[h])
        for part in lane_blocks(expo):
            total = part if total is None else total + part
        chances = expo.astype(BF)
        p_ref[0, h, t] = chances
        return total, acc + matmul(chances, head_of(value_refs[group][low], h))

    for h in heads:
        total, acc = None, acc_ref[h]
        for t in range(N_COMMON):
            total, acc = weigh(t, h, total, acc)
        total_ref[h] = total
        acc_ref[h] = acc

    @pl.when(upper)
    def more_values():
        for h in heads:
            total, acc = total_ref[h], acc_ref[h]
            for t in range(N_COMMON, len(PIECES)):
                total, acc = weigh(t, h, total, acc)
            total_ref[h] = total
            acc_ref[h] = acc

    for h in heads:
        inverse = 1.0 / (e_local[h] + jnp.sum(total_ref[h], axis=-1, keepdims=True))
        out = acc_ref[h] * inverse
        of_ref[0, :, h * HD : (h + 1) * HD] = out
        o_ref[0, :, h * HD : (h + 1) * HD] = out.astype(BF)
        inv_ref[0, h] = inverse


def backward_local_kernel(do_ref, of_ref, q_ref, k_ref, v_ref, inv_ref, pl_ref, cos_ref, sin_ref, dkv_ref, dq_ref):
    scale = HD ** (-0.5)
    for h in range(q_ref.shape[2] // HD):
        span = slice(h * HD, (h + 1) * HD)
        d_out = do_ref[0, :, span]
        delta = jnp.sum(d_out.astype(F32) * of_ref[0, :, span], axis=-1, keepdims=True)
        chances = pl_ref[0, h].astype(F32) * inv_ref[0, h]
        ds = (chances * (matmul_cols(d_out, v_ref[0, :, span]) - delta)).astype(BF)
        dq_ref[0, :, span] = matmul(ds, k_ref[0, :, span])
        dk = matmul_rows(ds, q_ref[0, :, span])
        dkv_ref[0, 0, :, span] = (
            (dk * cos_ref[...] - pltpu.roll(dk, HD // 2, 1) * sin_ref[...]) * scale
        ).astype(BF)
        dkv_ref[1, 0, :, span] = matmul_rows(chances.astype(BF), d_out).astype(BF)


def backward_kernel(do_ref, of_ref, local_ref, inv_ref, p_ref, cos_ref, sin_ref, *refs):
    key_refs, value_refs = refs[:N_GROUPS], refs[N_GROUPS : 2 * N_GROUPS]
    out_ref, dq_ref = refs[2 * N_GROUPS :]
    heads = range(do_ref.shape[2] // HD)
    scale = HD ** (-0.5)
    upper = pl.program_id(0) >= 2
    d_out = [do_ref[0, :, h * HD : (h + 1) * HD] for h in heads]
    inverse = [inv_ref[0, h] for h in heads]
    delta = [
        jnp.sum(d_out[h].astype(F32) * of_ref[0, :, h * HD : (h + 1) * HD], axis=-1, keepdims=True) for h in heads
    ]

    def piece(t, h, dq):
        group, low = PIECES[t]
        dp = matmul_cols(d_out[h], head_of(value_refs[group][low], h))
        ds = (p_ref[0, h, t].astype(F32) * ((dp - delta[h]) * inverse[h])).astype(BF)
        return dq + matmul(ds, head_of(key_refs[group][low], h))

    for h in heads:
        dq = local_ref[0, :, h * HD : (h + 1) * HD]
        for t in range(N_COMMON):
            dq = piece(t, h, dq)
        dq_ref[h] = dq

    @pl.when(upper)
    def more():
        for h in heads:
            dq = dq_ref[h]
            for t in range(N_COMMON, len(PIECES)):
                dq = piece(t, h, dq)
            dq_ref[h] = dq

    for h in heads:
        dq = dq_ref[h]
        out_ref[0, :, h * HD : (h + 1) * HD] = (
            (dq * cos_ref[...] - pltpu.roll(dq, HD // 2, 1) * sin_ref[...]) * scale
        ).astype(BF)


def attention_specs(piece_rows, seg_len, width):
    heads = width // HD
    tokens = pl.BlockSpec((1, seg_len, width), lambda r: (r, 0, 0))
    piece = pl.BlockSpec((2, piece_rows, width), lambda r: (0, 0, 0))
    p_spec = pl.BlockSpec((1, heads, len(PIECES), seg_len, piece_rows), lambda r: (r, 0, 0, 0, 0))
    pl_spec = pl.BlockSpec((1, heads, seg_len, seg_len), lambda r: (r, 0, 0, 0))
    inv_spec = pl.BlockSpec((1, heads, seg_len, 1), lambda r: (r, 0, 0, 0))
    return tokens, piece, p_spec, pl_spec, inv_spec


def attention_forward(queries, keys, values, mask, other_mask, key_pieces, value_pieces):
    blocks, seg_len, width = queries.shape
    heads = width // HD
    piece_rows = key_pieces[0].shape[1]
    tokens, piece, p_spec, pl_spec, inv_spec = attention_specs(piece_rows, seg_len, width)
    mask_spec = pl.BlockSpec((1,) + mask.shape[1:], lambda r: (r // 2, 0, 0, 0))
    return pl.pallas_call(
        forward_kernel,
        grid=(blocks,),
        in_specs=[tokens, tokens, tokens, mask_spec, mask_spec] + [piece] * (2 * N_GROUPS),
        out_specs=[tokens, tokens, p_spec, pl_spec, inv_spec],
        out_shape=[
            jax.ShapeDtypeStruct(queries.shape, BF),
            jax.ShapeDtypeStruct(queries.shape, F32),
            jax.ShapeDtypeStruct((blocks, heads, len(PIECES), seg_len, piece_rows), BF),
            jax.ShapeDtypeStruct((blocks, heads, seg_len, seg_len), BF),
            jax.ShapeDtypeStruct((blocks, heads, seg_len, 1), F32),
        ],
        scratch_shapes=[
            pltpu.VMEM((heads, len(PIECES), seg_len, piece_rows), F32),
            pltpu.VMEM((heads, seg_len, LANES), F32),
            pltpu.VMEM((heads, seg_len, LANES), F32),
            pltpu.VMEM((heads, seg_len, HD), F32),
        ],
        compiler_params=pltpu.CompilerParams(vmem_limit_bytes=VMEM_BYTES),
        cost_estimate=SHORT,
        name="attention_forward",
    )(queries, keys, values, mask, other_mask, *key_pieces, *value_pieces)


def attention_backward_local(d_out, out_f32, queries, keys, values, inverse, p_local, cosine, sine):
    blocks, seg_len, width = queries.shape
    tokens, unused, unused, pl_spec, inv_spec = attention_specs(seg_len, seg_len, width)
    table = pl.BlockSpec((seg_len, HD), lambda r: (0, 0))
    return pl.pallas_call(
        backward_local_kernel,
        grid=(blocks,),
        in_specs=[tokens, tokens, tokens, tokens, tokens, inv_spec, pl_spec, table, table],
        out_specs=[pl.BlockSpec((2, 1, seg_len, width), lambda r: (0, r, 0, 0)), tokens],
        out_shape=[
            jax.ShapeDtypeStruct((2, blocks, seg_len, width), BF),
            jax.ShapeDtypeStruct(queries.shape, F32),
        ],
        compiler_params=pltpu.CompilerParams(vmem_limit_bytes=VMEM_BYTES),
        cost_estimate=SHORT,
        name="attention_backward_local",
    )(d_out, out_f32, queries, keys, values, inverse, p_local, cosine, sine)


def attention_backward(d_out, out_f32, dq_local, inverse, p_memory, cosine, sine, key_pieces, value_pieces):
    blocks, seg_len, width = d_out.shape
    piece_rows = key_pieces[0].shape[1]
    tokens, piece, p_spec, unused, inv_spec = attention_specs(piece_rows, seg_len, width)
    table = pl.BlockSpec((seg_len, HD), lambda r: (0, 0))
    return pl.pallas_call(
        backward_kernel,
        grid=(blocks,),
        in_specs=[tokens, tokens, tokens, inv_spec, p_spec, table, table] + [piece] * (2 * N_GROUPS),
        out_specs=tokens,
        out_shape=jax.ShapeDtypeStruct((blocks, seg_len, width), BF),
        scratch_shapes=[pltpu.VMEM((width // HD, seg_len, HD), F32)],
        compiler_params=pltpu.CompilerParams(vmem_limit_bytes=VMEM_BYTES),
        cost_estimate=SHORT,
        name="attention_backward",
    )(d_out, out_f32, dq_local, inverse, p_memory, cosine, sine, *key_pieces, *value_pieces)


def allow_local_of(live):
    seg_len = live.shape[-1]
    position = jnp.arange(seg_len, dtype=jnp.int32)
    same = position[None, :] == position[:, None]
    return same[None] | ((position[None, :] < position[:, None])[None] & (live == 1))


def split_heads(value):
    rows, seg_len, width = value.shape
    return value.reshape(rows, seg_len, width // HD, HD)


def stream_forward(queries, keys, values, live, allow, memory):
    scale = HD ** (-0.5)
    q4, k4, v4 = split_heads(queries), split_heads(keys), split_heads(values)
    scores = jnp.einsum("rqhd,rkhd->rhqk", q4, k4, preferred_element_type=F32) * scale
    scores = jnp.where(allow_local_of(live)[:, None], scores, NEG_BIG)
    row_max = jnp.max(scores, axis=-1)
    expo = jnp.exp(scores - row_max[..., None])
    state = (
        row_max,
        jnp.sum(expo, axis=-1),
        jnp.einsum("rhqk,rkhd->rhqd", expo.astype(BF), v4, preferred_element_type=F32),
    )

    def step(running, item):
        row_max, row_total, acc = running
        block, allowed = item
        k3 = block[0].reshape(block.shape[1], -1, HD)
        v3 = block[1].reshape(block.shape[1], -1, HD)
        scores = jnp.einsum("rqhd,khd->rhqk", q4, k3, preferred_element_type=F32) * scale
        scores = jnp.where(allowed[:, None] > 0, scores, NEG_BIG)
        new_max = jnp.maximum(row_max, jnp.max(scores, axis=-1))
        shrink = jnp.exp(row_max - new_max)
        expo = jnp.exp(scores - new_max[..., None])
        acc = acc * shrink[..., None] + jnp.einsum(
            "rhqk,khd->rhqd", expo.astype(BF), v3, preferred_element_type=F32
        )
        return (new_max, row_total * shrink + jnp.sum(expo, axis=-1), acc), None

    (row_max, row_total, acc), unused = lax.scan(step, state, (memory, allow))
    out = (acc / row_total[..., None]).transpose(0, 2, 1, 3).reshape(queries.shape)
    return out.astype(BF), out, row_max + jnp.log(row_total)


def stream_backward(d_out, out_f32, queries, keys, values, live, log_total, allow, memory, cosine, sine):
    scale = HD ** (-0.5)
    q4, k4, v4, d4 = split_heads(queries), split_heads(keys), split_heads(values), split_heads(d_out)
    delta = jnp.sum(d4.astype(F32) * split_heads(out_f32), axis=-1).transpose(0, 2, 1)
    scores = jnp.einsum("rqhd,rkhd->rhqk", q4, k4, preferred_element_type=F32) * scale
    scores = jnp.where(allow_local_of(live)[:, None], scores, NEG_BIG)
    chances = jnp.exp(scores - log_total[..., None])
    dp = jnp.einsum("rqhd,rkhd->rhqk", d4, v4, preferred_element_type=F32)
    ds = (chances * (dp - delta[..., None])).astype(BF)
    dq = jnp.einsum("rhqk,rkhd->rqhd", ds, k4, preferred_element_type=F32)
    dk = jnp.einsum("rhqk,rqhd->rkhd", ds, q4, preferred_element_type=F32)
    dv = jnp.einsum("rhqk,rqhd->rkhd", chances.astype(BF), d4, preferred_element_type=F32)

    def step(running, item):
        block, allowed = item
        k3 = block[0].reshape(block.shape[1], -1, HD)
        v3 = block[1].reshape(block.shape[1], -1, HD)
        scores = jnp.einsum("rqhd,khd->rhqk", q4, k3, preferred_element_type=F32) * scale
        scores = jnp.where(allowed[:, None] > 0, scores, NEG_BIG)
        chances = jnp.exp(scores - log_total[..., None])
        dp = jnp.einsum("rqhd,khd->rhqk", d4, v3, preferred_element_type=F32)
        ds = (chances * (dp - delta[..., None])).astype(BF)
        return running + jnp.einsum("rhqk,khd->rqhd", ds, k3, preferred_element_type=F32), None

    dq, unused = lax.scan(step, dq, (memory, allow))

    def back(value):
        turned = rope_heads(value.reshape((-1,) + value.shape[2:]), jnp.tile(cosine, (value.shape[0], 1)), -jnp.tile(sine, (value.shape[0], 1)))
        return (turned * scale).reshape(queries.shape).astype(BF)

    return jnp.stack([back(dq), back(dk), dv.reshape(queries.shape).astype(BF)])


def local(
    layer_input,
    live,
    knn_index,
    mem_keys,
    mem_values,
    gain_attn,
    w_query,
    w_key,
    w_value,
    w_out,
    gain_ffn,
    w_gate,
    w_up,
    w_down,
    cotangent,
):
    seg_len, width = layer_input.shape[1:]
    quarter = width // 4
    n_seg = lax.axis_size("seg")
    n_devices = n_seg * lax.axis_size("rep")
    tokens = seg_len * n_seg
    n_high = n_seg // 4
    x, low, high, y, core = place()
    use_kernel = n_high <= KERNEL_HIGH
    kv_rows = 2 * seg_len
    group_tokens = 4 * seg_len

    def by_quarter(value):
        return [value[:, i * quarter : (i + 1) * quarter] for i in range(4)]

    gains = None if width // n_devices % 16 == 0 else jnp.concatenate(
        [gain_attn[:, None], gain_ffn[:, None], jnp.zeros((gain_attn.shape[0], LANES - 2), BF)], 1
    )
    if gains is None:
        qo = gather_columns((w_query, w_key, w_value, w_out), gain_attn, gain_ffn)
    else:
        stacked = [by_quarter(w) for w in (w_query, w_key, w_value, w_out)]
        qo = jnp.stack([jnp.concatenate([s[i] for s in stacked] + [gains], 1) for i in range(4)])

    def core_quarters(value, side):
        return jnp.stack([cut(value, side * quarter, quarter), cut(value, (2 + side) * quarter, quarter)])

    def core_memory(side):
        return jnp.stack([core_quarters(mem_keys[0], side), core_quarters(mem_values[0], side)])

    coded = knn_index[0] * 2 + live[0][:, None]
    qo = qo.reshape(2, 2, -1, qo.shape[-1])
    qo_keep, qo_give = halves(qo, 1, core)
    kv_keep, kv_give = core_memory(core), core_memory(1 - core)
    qo_recv, kv_recv, coded_recv = flip_core(qo_give), flip_core(kv_give), flip_z(coded)
    qo_keep, kv_keep, coded, qo_recv, kv_recv, coded_recv, w_gate_, w_up_ = fence(
        qo_keep, kv_keep, coded, qo_recv, kv_recv, coded_recv, w_gate, w_up
    )

    qo_keep, qo_give = halves(ordered(qo_keep, qo_recv, core, 1), 0, low)
    kv_keep, kv_give = halves(ordered(kv_keep, kv_recv, core, 2), 1, low)
    coded = ordered(coded[None], coded_recv[None], low, 0)
    kv_recv = flip_z(kv_give)
    qo_near = flip_z(qo_give)
    down_w = w_down[None, None, None, None]
    x_own = layer_input[0]
    gate_up = split_units(w_gate_, w_up_, n_devices).reshape(2, 2, 2, -1, w_gate.shape[1] // 4)

    def places_of(codes, row_core):
        picks = lax.shift_right_arithmetic(codes, 1)
        pair = picks >= tokens
        slot = jnp.where(pair, picks - tokens, picks)
        slot_seg = slot // seg_len
        kv_row = jnp.bitwise_xor(pair.astype(jnp.int32), row_core)
        return picks, slot_seg, kv_row * seg_len + (slot - slot_seg * seg_len)

    split = 3 * quarter
    g_own = cotangent[0]
    cosine, sine = rope_tables(seg_len)
    if use_kernel:
        qo_far, qo_side = flip(qo_keep, "seg", 4), flip(qo_give, "seg", 6)
        picks, slot_seg, within = places_of(coded, core)
        slot_x, slot_low = slot_seg % 2, (slot_seg // 2) % 2
        same_x = slot_x == x
        in_group = jnp.where(same_x, 5, 4 + 2 * slot_low)
        before = jnp.where(same_x, 0, 2) + slot_low
        piece_no = jnp.where(slot_seg // 4 == high, in_group, before)
        columns = jnp.where(picks >= 0, piece_no * kv_rows + within, -1)
        live_two = jnp.bitwise_and(coded[:, :, 0], 1)[:, None, :]
        live_two = jnp.pad(live_two, ((0, 0), (0, 0), (0, cdiv(seg_len, LANES) * LANES - seg_len)))
        down_recv = flip(down_w, "seg", 4)
        (
            qo_keep, qo_near, qo_far, qo_side, kv_keep, kv_recv, x_own, gate_up, columns, live_two, down_w, down_recv
        ) = fence(
            qo_keep, qo_near, qo_far, qo_side, kv_keep, kv_recv, x_own, gate_up, columns, live_two, down_w, down_recv
        )

        pieces = ordered(kv_keep[:, None], kv_recv[:, None], low, 1)
        own_k, own_v = pieces[0], pieces[1]
        near = ordered(qo_keep[None, None], qo_near[None, None], low, 1)
        far = ordered(qo_far[None, None], qo_side[None, None], low, 1)
        qo = ordered(near, far, high, 0)[:, :, None, None]
        qo_a, qo_b = qo[..., :split], qo[..., split:]
        up_high = [(i, i + 4) for i in range(n_seg - 4)]

        def cross(value):
            return lax.ppermute(value, "seg", up_high)

        cross_k, side_k = cross(own_k), flip_x(own_k)
        a_recv, b_recv = flip_x(qo_a), flip_y(qo_b)
        x_recv = flip_z(x_own)
        gu_keep, gu_give = halves(gate_up, 1, core)
        gu_recv = flip_core(gu_give)
        mask = build_mask(columns, live_two, len(PIECES) * kv_rows // LANES)
        qo_a, qo_b, a_recv, b_recv, cross_k, side_k, own_v, x_own, x_recv, gu_keep, gu_recv, mask, down_w, down_recv = fence(
            qo_a, qo_b, a_recv, b_recv, cross_k, side_k, own_v, x_own, x_recv, gu_keep, gu_recv, mask, down_w, down_recv
        )

        cross_v, cross_side_k = cross(own_v), flip_x(cross_k)
        qo_a, qo_b = ordered(qo_a, a_recv, x, 2), ordered(qo_b, b_recv, y, 3)
        a_recv, b_recv = flip_y(qo_a), flip_x(qo_b)
        gu_keep, gu_give = halves(ordered(gu_keep, gu_recv, core, 2), 0, low)
        gu_recv = flip_z(gu_give)
        x_two = ordered(x_own[None], x_recv[None], low, 0)
        x_recv = flip_core(x_two)
        qo_a, qo_b, a_recv, b_recv, cross_v, cross_side_k, own_v, gu_keep, gu_recv, x_two, x_recv, mask, down_w, down_recv = fence(
            qo_a, qo_b, a_recv, b_recv, cross_v, cross_side_k, own_v, gu_keep, gu_recv, x_two, x_recv, mask, down_w, down_recv
        )

        cross_side_v, side_v = flip_x(cross_v), flip_x(own_v)
        other_mask = flip_core(mask)
        g_far = flip_z(g_own)
        w_a, w_b = flat(ordered(qo_a, a_recv, y, 3)), flat(ordered(qo_b, b_recv, x, 2))
        gate_up = ordered(gu_keep[:, None], gu_recv[:, None], low, 1)[:, None]
        gu_recv = flip(gate_up, "seg", 4)
        down_w = ordered(down_w, down_recv, high, 0)
        down_recv = flip_y(down_w)
        x_all = jnp.stack([x_two, x_recv], 1).reshape(4, seg_len, width)
        queries, keys, values, h_one, inv_one = project(x_all, w_a, w_b, cosine, sine)
        wo_near = w_b[:, :quarter]
        (
            queries, keys, values, cross_side_v, side_v, gate_up, gu_recv, down_w, down_recv, wo_near, g_own, g_far, other_mask
        ) = fence(
            queries, keys, values, cross_side_v, side_v, gate_up, gu_recv, down_w, down_recv, wo_near, g_own, g_far, other_mask
        )

        key_pieces = (cross_k, cross_side_k, side_k, own_k)
        value_pieces = (cross_v, cross_side_v, side_v, own_v)
        gate, upw = [ordered(gate_up[i], gu_recv[i], high, 0)[:, :, None, None] for i in range(2)]
        down_w = ordered(down_w, down_recv, y, 3)
        down_a, down_b = down_w[..., : width // 4], down_w[..., width // 4 :]
        g_recv, u_recv, a_recv, wo_far = flip_x(gate), flip_y(upw), flip_x(down_a), flip_z(wo_near)
        out_low, out_f32, p_memory, p_local, inverse = attention_forward(
            queries, keys, values, mask, other_mask, key_pieces, value_pieces
        )
        wo_recv = flip_core(wo_near)
        out_low, gate, upw, g_recv, u_recv, down_a, a_recv, down_b, wo_near, wo_far, wo_recv, g_own, g_far = fence(
            out_low, gate, upw, g_recv, u_recv, down_a, a_recv, down_b, wo_near, wo_far, wo_recv, g_own, g_far
        )
    else:
        qo = gather_high(ordered(qo_keep[None], qo_near[None], low, 0)[None, :, None, None])
        kv = ordered(kv_keep[:, None], kv_recv[:, None], low, 1)
        w_a, w_b = flat(gather_y(gather_x(qo[..., :split]))), flat(gather_x(gather_y(qo[..., split:])))
        x_all = all_blocks(two_rows(x_own))
        gu_keep, gu_give = halves(gate_up, 1, core)
        gu_keep, gu_give = halves(ordered(gu_keep, flip_core(gu_give), core, 2), 0, low)
        gate, upw = gather_high_pair(ordered(gu_keep[:, None], flip_z(gu_give)[:, None], low, 1))
        down_w = gather_y(gather_high(down_w))
        down_a, down_b = down_w[..., : width // 4], down_w[..., width // 4 :]
        coded = all_blocks(coded)
        row_core = jnp.bitwise_xor(core, jnp.arange(4, dtype=jnp.int32) % 2)[:, None, None]
        picks, slot_seg, within = places_of(coded, row_core)
        live_all = jnp.bitwise_and(coded[:, :, 0], 1)[:, None, :]
        columns = jnp.where(picks >= 0, slot_seg * kv_rows + within, n_seg * kv_rows)
        blocks_at = jnp.arange(4)[:, None, None]
        queries_at = jnp.arange(seg_len)[None, :, None]
        allow = jnp.zeros((4, seg_len, n_seg * kv_rows), BF).at[blocks_at, queries_at, columns].set(1.0, mode="drop")
        allow = allow.reshape(4, seg_len, n_seg, kv_rows).transpose(2, 0, 1, 3)
        memory = jnp.swapaxes(kv, 0, 1)[None, :, None]
        memory = gather_x(gather_high(memory)).reshape(n_seg, 2, kv_rows, quarter)
        queries, keys, values, h_one, inv_one = project(x_all, w_a, w_b, cosine, sine)
        wo_near = w_b[:, :quarter]
        out_low, out_f32, log_total = stream_forward(queries, keys, values, live_all, allow, memory)
        g_recv, u_recv, a_recv, wo_far = flip_x(gate), flip_y(upw), flip_x(down_a), flip_z(wo_near)
        g_far = flip_z(g_own)
        wo_recv = flip_core(wo_near)

    h_one = h_one.reshape(group_tokens, width)
    inv_one = inv_one.reshape(group_tokens, 1)
    x_float = x_all.reshape(group_tokens, width).astype(F32)
    g_attn = w_b[:, quarter].astype(F32)
    g_ffn = w_b[:, quarter + 1].astype(F32)
    att_near = out_low.reshape(group_tokens, quarter)
    att_far = flip_z(att_near)
    gate, upw = ordered(gate, g_recv, x, 2), ordered(upw, u_recv, y, 3)
    g_recv, u_recv = flip_y(gate), flip_x(upw)
    wo = join_four(wo_near, wo_far, wo_recv, flip_core(wo_far), False)
    att_recv = flip_core(att_near)
    att_near, att_far, att_recv, gate, upw, g_recv, u_recv, down_b, wo, g_own, g_far = fence(
        att_near, att_far, att_recv, gate, upw, g_recv, u_recv, down_b, wo, g_own, g_far
    )

    att_far_recv = flip_core(att_far)
    down_recv = flip_x(down_b)
    g_two = ordered(g_own[None], g_far[None], low, 0)
    g_recv_core = flip_core(g_two)
    wg, wu = flat(ordered(gate, g_recv, y, 3)), flat(ordered(upw, u_recv, x, 2))
    attended = join_four(att_near, att_far, att_recv, att_far_recv, True)
    x_one = x_float + matmul(attended, wo)
    h_two_f, inv_two = norm_forward(x_one, g_ffn)
    h_two = h_two_f.astype(BF)
    gate_out = matmul(h_two, wg)
    up_out = matmul(h_two, wu)
    sigma = jax.nn.sigmoid(gate_out)
    swish = gate_out * sigma
    hidden = (swish * up_out).astype(BF)
    grad_out = jnp.stack([g_two, g_recv_core], 1).reshape(group_tokens, width)

    down_b, hidden = fence(down_b, hidden)
    wd = jnp.concatenate([flat(ordered(down_a, a_recv, x, 2)), flat(ordered(down_b, down_recv, x, 2))], 1)
    d_hidden = matmul_cols(grad_out, wd)
    d_gate = (d_hidden * up_out * sigma * (1.0 + gate_out * (1.0 - sigma))).astype(BF)
    d_up = (d_hidden * swish).astype(BF)
    sums_keep, sums_give = back_project([d_gate, d_up], [wg, wu])
    sums_recv = flip_core(sums_give)
    (keep_g, give_g), (keep_u, give_u) = gradient((h_two, [d_gate], "x", None), (h_two, [d_up], "y", None))
    sums_keep, sums_recv, keep_g, give_g, keep_u, give_u, hidden, wd = fence(
        sums_keep, sums_recv, keep_g, give_g, keep_u, give_u, hidden, wd
    )

    sums = add_kernel(sums_keep, sums_recv)
    far_sums = flip_z(sums)
    recv_g, recv_u = flip_x(give_g), flip_y(give_u)
    down_keep, down_give = back_project([hidden], [wd], False)
    down_recv = flip_core(down_give)
    keep_wd, give_wd = gradient_units(hidden, grad_out)
    sums, far_sums, keep_g, keep_u, recv_g, recv_u, down_keep, down_recv, keep_wd, give_wd = fence(
        sums, far_sums, keep_g, keep_u, recv_g, recv_u, down_keep, down_recv, keep_wd, give_wd
    )

    own = 2 * low * seg_len
    summed = add_kernel(sums, far_sums)
    summed_recv = flip_core(summed)
    d_branch, d_att, d_x_own = branch_back(
        summed,
        summed_recv,
        x_one.reshape(4, seg_len, width),
        g_ffn[None],
        g_two,
        g_recv_core,
        wo,
    )
    d_branch = d_branch.reshape(group_tokens, width)
    keep_g, keep_u, recv_g, recv_u, d_att, d_branch, down_keep, down_recv = fence(
        keep_g, keep_u, recv_g, recv_u, d_att, d_branch, down_keep, down_recv
    )

    keep_g, give_g = split_sums(keep_g, recv_g, "y")
    keep_u, give_u = split_sums(keep_u, recv_u, "x")
    down_own, down_give = pair_add(down_keep, down_recv)
    w_thirds = [w_a[:, i * quarter : (i + 1) * quarter] for i in range(3)]
    if use_kernel:
        recv_g, recv_u = flip_y(give_g), flip_x(give_u)
        down_recv = flip_z(down_give)
        d_kv, dq_local = attention_backward_local(
            d_att, out_f32, queries, keys, values, inverse, p_local, cosine, sine
        )
        d_kv = d_kv.reshape(2, group_tokens, quarter)
        (keep_kv, give_kv), (keep_wo, give_wo) = gradient(
            (h_one, [d_kv[0], d_kv[1]], "y", None), (attended, [d_branch], "y", quarter)
        )
        give_kvo = jnp.concatenate([give_kv, give_wo], -1)
        keep_kvo = jnp.concatenate([keep_kv, keep_wo], -1)
        keep_kvo, give_kvo, keep_g, recv_g, keep_u, recv_u, dq_local, keep_wd, give_wd, down_own, down_recv = fence(
            keep_kvo, give_kvo, keep_g, recv_g, keep_u, recv_u, dq_local, keep_wd, give_wd, down_own, down_recv
        )
        gu_parts = plane_sort((keep_g, recv_g), (keep_u, recv_u))
        recv_kvo = flip_y(give_kvo)
        gu_flips = z_flips(gu_parts)
        recv_wd = flip_x(give_wd)
        d_q = attention_backward(
            d_att, out_f32, dq_local, inverse, p_memory, cosine, sine, key_pieces, value_pieces
        )
        d_q, keep_kvo = fence(d_q, keep_kvo)

        d_q = d_q.reshape(group_tokens, quarter)
        ((keep_q, *give_q),) = gradient((h_one, [d_q], "xy", None))
        keep_q, give_q, d_q, keep_kvo, recv_kvo, keep_wd, recv_wd, gu_kept, gu_flips = fence(
            keep_q, give_q, d_q, keep_kvo, recv_kvo, keep_wd, recv_wd, gu_parts[0], gu_flips
        )
        recv_q = plane_flips(give_q)
        keep_kvo, give_kvo = split_sums(keep_kvo, recv_kvo, "x")
        keep_wd, give_wd = split_sums(
            keep_wd.reshape((-1,) + keep_wd.shape[2:]), recv_wd.reshape((-1,) + keep_wd.shape[2:]), "y"
        )
        recv_wd = flip_y(give_wd)
        recv_kvo = flip_x(give_kvo)
        d_h_keep, d_h_give = back_project([d_q, d_kv[0], d_kv[1]], w_thirds)
        gu_keep, gu_give = z_merge(gu_kept, *gu_flips)
        keep_q, recv_q, keep_kvo, recv_kvo, keep_wd, recv_wd, d_h_keep, d_h_give, gu_keep, gu_give = fence(
            keep_q, recv_q, keep_kvo, recv_kvo, keep_wd, recv_wd, d_h_keep, d_h_give, gu_keep, gu_give
        )
        *parts, wd_own = plane_sort((keep_q,) + tuple(recv_q), (keep_kvo, recv_kvo), units=(keep_wd, recv_wd))
        parts, d_h_give, wd_own = fence(parts, d_h_give, wd_own)
        d_h_recv = flip_core(d_h_give)
        flips = z_flips(parts)
        d_h_own, d_h_give = pair_add(d_h_keep, d_h_recv)
        d_h_recv = flip_z(d_h_give)
        gu_recv = flip_core(gu_give)
        sum_wg, sum_wu, grad_g_ffn = join_units(gu_keep, gu_recv, (w_gate, w_up), gain_ffn, n_devices)
        grad_x = input_back(d_h_own, d_h_recv, x_all, g_attn[None], d_x_own)
        kept, flips, grad_x, wd_own, sum_wg, sum_wu = fence(parts[0], flips, grad_x, wd_own, sum_wg, sum_wu)
        qkvo_keep, qkvo_give = z_merge(kept, *flips)
        qkvo_recv = flip_core(qkvo_give)
        wd_recv = flips[1][kept.shape[0] : kept.shape[0] + wd_own.shape[0]]
        sum_wd = wd_own.astype(F32) + wd_recv.astype(F32)
    else:
        down_recv = flip_z(down_give)
        recv_wd = flip_x(give_wd)
        d_q, *d_kv = stream_backward(
            d_att, out_f32, queries, keys, values, live_all, log_total, allow, memory, cosine, sine
        ).reshape(3, group_tokens, quarter)

        def by_chip(value):
            return value.reshape(n_high, 2, -1, value.shape[-1])

        (keep_qkv, *give_qkv), (keep_wo, *give_wo) = gradient(
            (h_one, [d_q, d_kv[0], d_kv[1]], "xy", None), (attended, [d_branch], "xy", quarter)
        )
        plane_gu = [add_low(keep_g, flip_y(give_g)), add_low(keep_u, flip_x(give_u))]
        z_gu = z_plain(by_chip(jnp.concatenate(plane_gu, -1)))
        plane_qkvo = [add_all(keep_qkv, *plane_flips(give_qkv)), add_all(keep_wo, *plane_flips(give_wo))]
        z_qkvo = z_plain(by_chip(jnp.concatenate(plane_qkvo, -1)))
        (gu_keep, gu_give), (qkvo_keep, qkvo_give) = core_halves(z_gu), core_halves(z_qkvo)
        qkvo_recv, gu_recv = flip_core(qkvo_give), flip_core(gu_give)
        keep_wd, give_wd = halves(add_low(keep_wd, recv_wd), 1, y)
        recv_wd = flip_y(give_wd)
        d_h_keep, d_h_give = back_project([d_q, d_kv[0], d_kv[1]], w_thirds)
        d_h_own, d_h_give = pair_add(d_h_keep, flip_core(d_h_give))
        d_h_recv = flip_z(d_h_give)
        grad_x = input_back(d_h_own, d_h_recv, x_all, g_attn[None], d_x_own)
        sum_wd = reduce_high(add_low(keep_wd, recv_wd)[:, None])[0].astype(F32)
        sum_wg, sum_wu, grad_g_ffn = join_units(gu_keep, gu_recv, (w_gate, w_up), gain_ffn, n_devices)
    layer_output = (cut(x_one, own, seg_len, 0) + down_own.astype(F32) + down_recv.astype(F32)).astype(BF)
    sum_q, sum_k, sum_v, sum_o, grad_g_attn = join_columns(
        qkvo_keep, qkvo_recv, (w_query, w_key, w_value), gain_attn, 4
    )
    return (
        layer_output[None],
        grad_x[None],
        grad_g_attn,
        sum_q,
        sum_k,
        sum_v,
        sum_o,
        grad_g_ffn,
        sum_wg,
        sum_wu,
        sum_wd,
    )


def solution(mesh):
    tokens = P("rep", "seg", None)
    vector = P(("seg", "rep"))
    matrix = P(("seg", "rep"), None)
    return jax.shard_map(
        local,
        mesh=mesh,
        in_specs=(
            tokens,
            P("rep", "seg"),
            tokens,
            tokens,
            tokens,
            vector,
            matrix,
            matrix,
            matrix,
            matrix,
            vector,
            matrix,
            matrix,
            matrix,
            tokens,
        ),
        out_specs=(tokens, tokens, vector, matrix, matrix, matrix, matrix, vector, matrix, matrix, matrix),
        check_vma=False,
    )
```

```python
import jax
import jax.numpy as jnp
from jax import lax
from jax.experimental import pallas as pl
from jax.experimental.pallas import tpu as pltpu
from jax.sharding import PartitionSpec as P

H = 8
HD = 128
EPSILON = 1e-05
NEG_BIG = -1e30
POS_BIG = 1e30
ROPE_BASE = 10000.0
LANES = 128
KERNEL_HIGH = 2
LOG2_E = 1.4426950408889634
VMEM_BYTES = 44 * 1024 * 1024

SHORT = pl.CostEstimate(flops=1000, bytes_accessed=1000, transcendentals=0)

BF = jnp.bfloat16
F32 = jnp.float32


def cdiv(a, b):
    return -(-a // b)


def flip(value, axis, bit):
    count = lax.axis_size(axis)
    return lax.ppermute(value, axis, [(i, i ^ bit) for i in range(count)])


def flip_core(value):
    return flip(value, "rep", 1)


def flip_y(value):
    return flip(value, "rep", 2)


def flip_x(value):
    return flip(value, "seg", 1)


def flip_z(value):
    return flip(value, "seg", 2)


def ordered(mine, other, bit, axis):
    first = jnp.where(bit == 0, mine, other)
    second = jnp.where(bit == 0, other, mine)
    return jnp.concatenate([first, second], axis)


def pick(value, index, axis):
    return lax.dynamic_index_in_dim(value, index, axis, keepdims=False)


def cut(value, start, size, axis=-1):
    return lax.dynamic_slice_in_dim(value, start, size, axis % value.ndim)


def fence(*values):
    return lax.optimization_barrier(values)


def place():
    seg = lax.axis_index("seg")
    rep = lax.axis_index("rep")
    return seg % 2, (seg // 2) % 2, seg // 4, rep // 2, rep % 2


def high_bits():
    bit = 4
    out = []
    while bit < lax.axis_size("seg"):
        out.append(bit)
        bit *= 2
    return out


def gather_high(cur):
    seg = lax.axis_index("seg")
    for bit in high_bits():
        cur = ordered(cur, flip(cur, "seg", bit), (seg // bit) % 2, 0)
    return cur


def gather_x(cur):
    return ordered(cur, flip_x(cur), place()[0], 2)


def gather_y(cur):
    return ordered(cur, flip_y(cur), place()[3], 3)


def gather_high_pair(cur):
    seg = lax.axis_index("seg")
    cur = cur[:, None]
    bits = high_bits()
    for bit in bits[:-1]:
        cur = ordered(cur, flip(cur, "seg", bit), (seg // bit) % 2, 1)
    recv = flip(cur, "seg", bits[-1])
    side = (seg // bits[-1]) % 2
    return [ordered(cur[i], recv[i], side, 0)[:, :, None, None] for i in range(2)]


def flat(cur):
    return cur.reshape(-1, cur.shape[-1])


def halve(value, axis_name, bit, side, axis):
    recv = flip(pick(value, 1 - side, axis), axis_name, bit)
    kept = pick(value, side, axis)
    return (kept.astype(F32) + recv.astype(F32)).astype(BF)


def plane_shape(value, low):
    high = lax.axis_size("seg") // 4
    return value.reshape(high, low, 2, -1, value.shape[-1])


def halves(cur, axis, side):
    return pick(cur, side, axis), pick(cur, 1 - side, axis)


def plane_flips(parts):
    n_rep = lax.axis_size("rep")
    count = lax.axis_size("seg") * n_rep
    far = [(i, i ^ n_rep ^ 2) for i in range(count)]
    return flip_x(parts[0]), flip_y(parts[1]), lax.ppermute(parts[2], ("seg", "rep"), far)


def add_all(first, *others):
    total = first.astype(F32)
    for other in others:
        total = total + other.astype(F32)
    return total.astype(BF)


def z_flips(parts):
    return flip_z(parts[1]), flip(parts[2], "seg", 4), flip(parts[3], "seg", 6)


def z_plain(cur):
    low = place()[1]
    sums = reduce_high(cur)
    return ordered(pick(sums, low, 0)[None], flip_z(pick(sums, 1 - low, 0))[None], low, 0)


def reduce_high(cur):
    seg = lax.axis_index("seg")
    for bit in reversed(high_bits()):
        cur = cur.reshape((2, cur.shape[0] // 2) + cur.shape[1:])
        cur = halve(cur, "seg", bit, (seg // bit) % 2, 0)
    return cur[0]


def trade_core(quarters):
    core = place()[4]
    low, unused, rows, cols = 2, 2, quarters.shape[1], quarters.shape[2]
    four = quarters.reshape(2, 2, rows, cols)
    return ordered(pick(four, core, 1), flip_core(pick(four, 1 - core, 1)), core, 1)


def trade_z(halves):
    low = place()[1]
    return ordered(pick(halves, low, 0)[None], flip_z(pick(halves, 1 - low, 0))[None], low, 0)


def gather_z_four(halves):
    seg = lax.axis_index("seg")
    low = (seg // 2) % 2
    keep, give = pick(halves, low, 0)[None, None], pick(halves, 1 - low, 0)[None, None]
    near = ordered(keep, flip(give, "seg", 2), low, 1)
    far = ordered(flip(keep, "seg", 4), flip(give, "seg", 6), low, 1)
    return ordered(near, far, (seg // 4) % 2, 0)[:, :, None, None]


def start_gather(traded):
    return traded[None, :, None, None]


def core_halves(mine):
    core = place()[4]
    four = mine.reshape(2, 2, mine.shape[1] // 2, mine.shape[2])
    return halves(four, 1, core)


def all_blocks(by_low):
    both = jnp.stack([by_low, flip_core(by_low)], 1)
    return both.reshape((-1,) + by_low.shape[1:])


def two_rows(value):
    return ordered(value[None], flip_z(value)[None], place()[1], 0)


def core_parts(part):
    blocks = part.reshape((2, 2, part.shape[0] // 4) + part.shape[1:])
    return blocks[:, 0].astype(BF), blocks[:, 1].astype(BF)


def core_sums(part):
    blocks = part.reshape((2, 2, part.shape[0] // 4) + part.shape[1:])
    return (blocks[:, 0] + flip_core(blocks[:, 1].astype(BF)).astype(F32)).astype(BF)


def own_sums(sums):
    low = place()[1]
    return pick(sums, low, 0).astype(F32) + flip_z(pick(sums, 1 - low, 0)).astype(F32)


def z_sums(sums):
    return (sums.astype(F32) + flip_z(sums).astype(F32)).astype(BF)


def both_cores(sums):
    return jnp.stack([sums, flip_core(sums)], 1).astype(F32)


def unit_blocks(n_blocks):
    order = []
    for block in range(n_blocks):
        high, low, rest, core = block // 16, (block // 8) % 2, (block // 2) % 4, block % 2
        order.append((low * 2 + core, high * 4 + rest))
    return order


def split_units(one, two, n_blocks):
    rows, total = one.shape
    size = total // n_blocks

    def body(one_ref, two_ref, out_ref):
        for half, in_ref in enumerate((one_ref, two_ref)):
            for block, (quarter, at) in enumerate(unit_blocks(n_blocks)):
                out_ref[quarter, half * rows : (half + 1) * rows, at * size : (at + 1) * size] = in_ref[
                    :, block * size : (block + 1) * size
                ]

    return pl.pallas_call(
        body,
        out_shape=jax.ShapeDtypeStruct((4, 2 * rows, total // 4), one.dtype),
        cost_estimate=SHORT,
        name="split_units",
    )(one, two)


def matmul(left, right):
    return jnp.dot(left, right, preferred_element_type=F32)


def matmul_rows(left, right):
    return lax.dot_general(left, right, (((0,), (0,)), ((), ())), preferred_element_type=F32)


def matmul_cols(left, right):
    return lax.dot_general(left, right, (((1,), (1,)), ((), ())), preferred_element_type=F32)


def norm_forward(values, gain):
    inverse = lax.rsqrt(jnp.mean(values * values, axis=-1, keepdims=True) + EPSILON)
    return (values * inverse * gain, inverse)


def norm_backward(values, inverse, gain, grad_out):
    normed = values * inverse
    scaled = grad_out * gain
    grad_values = inverse * (scaled - normed * jnp.mean(scaled * normed, axis=-1, keepdims=True))
    return (grad_values, normed)


def rope_tables(seg_len):
    position = jnp.arange(seg_len).astype(F32)
    freqs = ROPE_BASE ** (-(2.0 * jnp.arange(HD // 2).astype(F32)) / HD)
    angle = position[:, None] * freqs[None, :]
    cosine, sine = jnp.cos(angle), jnp.sin(angle)
    return (jnp.concatenate([cosine, cosine], -1), jnp.concatenate([-sine, sine], -1))


def rope_heads(values, cosine, sine):
    half = HD // 2
    swapped = jnp.concatenate([values[..., half:], values[..., :half]], -1)
    return values * cosine[:, None, :] + swapped * sine[:, None, :]


def mask_kernel(n_cols, cols_ref, live_ref, out_ref, scratch):
    queries = cols_ref.shape[1]
    picks = cols_ref[0]
    pad = scratch.shape[0]
    high = lax.shift_right_arithmetic(picks, 7)
    low = jnp.bitwise_and(picks, LANES - 1)
    iota_high = lax.broadcasted_iota(jnp.int32, (pad, picks.shape[1]), 0)
    iota_low = lax.broadcasted_iota(jnp.int32, (LANES, picks.shape[1]), 0)
    for i in range(queries):
        hot_high = jnp.where(iota_high == high[i : i + 1, :], 1.0, 0.0).astype(BF)
        hot_low = jnp.where(iota_low == low[i : i + 1, :], 1.0, 0.0).astype(BF)
        scratch[:, i, :] = matmul_cols(hot_high, hot_low)
    out_ref[0, 0:n_cols] = jnp.where(scratch[0:n_cols] > 0.5, POS_BIG, NEG_BIG).astype(BF)
    row = lax.broadcasted_iota(jnp.int32, (queries, LANES), 0) + pl.program_id(1) * queries
    for part in range(out_ref.shape[1] - n_cols):
        col = lax.broadcasted_iota(jnp.int32, (queries, LANES), 1) + part * LANES
        live = live_ref[0, :, part * LANES : (part + 1) * LANES]
        allow = (col == row) | ((col < row) & (live == 1))
        out_ref[0, n_cols + part] = jnp.where(allow, POS_BIG, NEG_BIG).astype(BF)


def build_mask(columns, live, n_cols):
    rows, queries, picks = columns.shape
    block = 16
    pad = cdiv(n_cols, 8) * 8
    n_local = live.shape[2] // LANES
    return pl.pallas_call(
        lambda *refs: mask_kernel(n_cols, *refs),
        grid=(rows, queries // block),
        in_specs=[
            pl.BlockSpec((1, block, picks), lambda r, g: (r, g, 0)),
            pl.BlockSpec((1, 1, live.shape[2]), lambda r, g: (r, 0, 0)),
        ],
        out_specs=pl.BlockSpec((1, n_cols + n_local, block, LANES), lambda r, g: (r, 0, g, 0)),
        out_shape=jax.ShapeDtypeStruct((rows, n_cols + n_local, queries, LANES), BF),
        scratch_shapes=[pltpu.VMEM((pad, block, LANES), F32)],
        compiler_params=pltpu.CompilerParams(vmem_limit_bytes=VMEM_BYTES),
        cost_estimate=SHORT,
        name="mask_build",
    )(columns, live)


def project_kernel(x_ref, wa_ref, wb_ref, cos_ref, sin_ref, q_ref, k_ref, v_ref, h_ref, inv_ref, gain_ref):
    quarter = q_ref.shape[2]

    @pl.when(pl.program_id(0) == 0)
    def gains():
        gain_ref[...] = jnp.transpose(wb_ref[:, quarter:].astype(F32), (1, 0))[0:8]

    x = x_ref[0].astype(F32)
    inverse = lax.rsqrt(jnp.mean(x * x, axis=-1, keepdims=True) + EPSILON)
    h = (x * inverse * gain_ref[0:1, :]).astype(BF)
    h_ref[0] = h
    inv_ref[0] = inverse
    turned = matmul(h, wa_ref[:, : 2 * quarter])
    for head in range(2 * quarter // HD):
        value = turned[:, head * HD : (head + 1) * HD]
        value = (value * cos_ref[...] + pltpu.roll(value, HD // 2, 1) * sin_ref[...]).astype(BF)
        if head < quarter // HD:
            q_ref[0, :, head * HD : (head + 1) * HD] = value
        else:
            at = head * HD - quarter
            k_ref[0, :, at : at + HD] = value
    v_ref[0] = matmul(h, wa_ref[:, 2 * quarter :]).astype(BF)


def project(x_all, w_a, w_b, cosine, sine):
    blocks, seg_len, width = x_all.shape
    quarter = w_a.shape[1] // 3
    whole = lambda array: pl.BlockSpec(array.shape, lambda r: (0, 0))
    head = pl.BlockSpec((1, seg_len, quarter), lambda r: (r, 0, 0))
    full = pl.BlockSpec((1, seg_len, width), lambda r: (r, 0, 0))
    out = jax.ShapeDtypeStruct((blocks, seg_len, quarter), BF)
    return pl.pallas_call(
        project_kernel,
        grid=(blocks,),
        in_specs=[full, whole(w_a), whole(w_b), whole(cosine), whole(sine)],
        out_specs=[head, head, head, full, pl.BlockSpec((1, seg_len, 1), lambda r: (r, 0, 0))],
        out_shape=[out, out, out, jax.ShapeDtypeStruct(x_all.shape, BF), jax.ShapeDtypeStruct((blocks, seg_len, 1), F32)],
        scratch_shapes=[pltpu.VMEM((8, width), F32)],
        compiler_params=pltpu.CompilerParams(vmem_limit_bytes=VMEM_BYTES),
        cost_estimate=SHORT,
        name="project",
    )(x_all, w_a, w_b, cosine, sine)


def plane_place():
    x, low, unused, y, core = place()
    return jnp.stack([x, y, 2 * low + core]).astype(jnp.int32)


def gradient(*entries):
    tokens, width = entries[0][0].shape
    n_blocks = lax.axis_size("seg")
    rows = width // n_blocks
    half = rows // 2
    sizes = [[entry[3] or right.shape[1] for right in entry[1]] for entry in entries]
    if rows % LANES:
        x, unused, unused, y, unused = place()
        outs = []
        for left, rights, way, columns in entries:
            if columns:
                rights = [cut(right, plane_place()[2] * columns, columns) for right in rights]
            full = jnp.concatenate([matmul_rows(left, right).astype(BF) for right in rights], 1)
            full = full.reshape(-1, 2, 2, half, full.shape[1])
            if way == "xy":
                near, side = halves(full, 1, x)
                near, side = halves(near, 1, y), halves(side, 1, y)
                parts = [near[0], side[0], near[1], side[1]]
            else:
                parts = halves(full, 1, x) if way == "x" else halves(full, 2, y)
            outs.append([part.reshape(-1, half, part.shape[-1]) for part in parts])
        return outs
    lefts = []
    for entry in entries:
        if not any(entry[0] is left for left in lefts):
            lefts.append(entry[0])
    which = [[entry[0] is left for left in lefts].index(True) for entry in entries]
    counts = [4 if entry[2] == "xy" else 2 for entry in entries]
    shapes = []
    for entry, size, count in zip(entries, sizes, counts):
        blocks = n_blocks // 2 if entry[2] == "xy" else n_blocks
        shapes += [(blocks, half, sum(size))] * count
    n_rights = sum(len(size) for size in sizes)

    def body(at_ref, *refs):
        left_refs, right_refs = refs[: len(lefts)], list(refs[len(lefts) : len(lefts) + n_rights])
        out_refs = list(refs[len(lefts) + n_rights :])
        pair = pl.program_id(0)
        turned = [jnp.transpose(ref[...]) for ref in left_refs]

        def by_row(value):
            upper, lower = value[:half], value[half:]
            return jnp.where(at_ref[1] == 0, upper, lower), jnp.where(at_ref[1] == 0, lower, upper)

        for entry, i, size, count in zip(entries, which, sizes, counts):
            outs, out_refs = out_refs[:count], out_refs[count:]
            start = 0
            for width_here in size:
                product = matmul(turned[i], right_refs.pop(0)[...]).astype(BF)
                span = slice(start, start + width_here)
                start += width_here
                first, second = product[:rows], product[rows:]
                if entry[2] == "y":
                    for side, value in enumerate((first, second)):
                        outs[0][2 * pair + side, :, span], outs[1][2 * pair + side, :, span] = by_row(value)
                    continue
                same = jnp.where(at_ref[0] == 0, first, second)
                other = jnp.where(at_ref[0] == 0, second, first)
                if entry[2] == "x":
                    for ref, value in zip(outs, (same, other)):
                        ref[2 * pair, :, span] = value[:half]
                        ref[2 * pair + 1, :, span] = value[half:]
                else:
                    outs[0][pair, :, span], outs[2][pair, :, span] = by_row(same)
                    outs[1][pair, :, span], outs[3][pair, :, span] = by_row(other)

    in_specs = [pl.BlockSpec((tokens, 2 * rows), lambda i, at: (0, i))] * len(lefts)
    for entry, size in zip(entries, sizes):
        column = (lambda i, at: (0, at[2])) if entry[3] else (lambda i, at: (0, 0))
        in_specs += [pl.BlockSpec((tokens, width_here), column) for width_here in size]
    outs = pl.pallas_call(
        body,
        grid_spec=pltpu.PrefetchScalarGridSpec(
            num_scalar_prefetch=1,
            grid=(n_blocks // 2,),
            in_specs=in_specs,
            out_specs=[pl.BlockSpec(shape, lambda i, at: (0, 0, 0)) for shape in shapes],
        ),
        out_shape=[jax.ShapeDtypeStruct(shape, BF) for shape in shapes],
        compiler_params=pltpu.CompilerParams(vmem_limit_bytes=VMEM_BYTES),
        cost_estimate=SHORT,
        name="gradient",
    )(plane_place(), *lefts, *[right for entry in entries for right in entry[1]])
    groups = []
    for count in counts:
        groups.append(outs[:count])
        outs = outs[count:]
    return groups


def split_sums(keep, recv, way):
    n_blocks, rows, cols = keep.shape

    def body(at_ref, keep_ref, recv_ref, mine_ref, give_ref):
        side = at_ref[1] if way == "y" else at_ref[0]
        for block in range(n_blocks // 2):
            for at, out_ref in ((2 * block + side, mine_ref), (2 * block + 1 - side, give_ref)):
                out_ref[block] = (keep_ref[at].astype(F32) + recv_ref[at].astype(F32)).astype(BF)

    vmem = pl.BlockSpec(memory_space=pltpu.VMEM)
    return pl.pallas_call(
        body,
        in_specs=[pl.BlockSpec(memory_space=pltpu.SMEM)] + [vmem] * 2,
        out_specs=[vmem] * 2,
        out_shape=[jax.ShapeDtypeStruct((n_blocks // 2, rows, cols), BF)] * 2,
        compiler_params=pltpu.CompilerParams(vmem_limit_bytes=VMEM_BYTES),
        cost_estimate=SHORT,
        name="split_sums",
    )(plane_place(), keep, recv)


def gradient_units(left, right):
    tokens, width = left.shape
    n_high = lax.axis_size("seg") // 4
    rows = width // (4 * n_high)
    cols = right.shape[1]
    step = 256
    if rows % 8:
        full = matmul_rows(left, right).astype(BF).reshape(-1, 2, 2, rows, cols)
        return halves(full, 1, place()[0])

    def body(at_ref, left_ref, right_ref, keep_ref, give_ref):
        product = matmul_rows(left_ref[...], right_ref[...])
        for high in range(n_high):
            for y in range(2):
                zero, one = [
                    product[(high * 4 + x * 2 + y) * rows : (high * 4 + x * 2 + y + 1) * rows] for x in range(2)
                ]
                keep_ref[high, y] = jnp.where(at_ref[0] == 0, zero, one).astype(BF)
                give_ref[high, y] = jnp.where(at_ref[0] == 0, one, zero).astype(BF)

    shape = (n_high, 2, rows, cols)
    return pl.pallas_call(
        body,
        grid_spec=pltpu.PrefetchScalarGridSpec(
            num_scalar_prefetch=1,
            grid=(cols // step,),
            in_specs=[
                pl.BlockSpec((tokens, width), lambda i, at: (0, 0)),
                pl.BlockSpec((tokens, step), lambda i, at: (0, i)),
            ],
            out_specs=[pl.BlockSpec((n_high, 2, rows, step), lambda i, at: (0, 0, 0, i))] * 2,
        ),
        out_shape=[jax.ShapeDtypeStruct(shape, BF)] * 2,
        compiler_params=pltpu.CompilerParams(vmem_limit_bytes=VMEM_BYTES),
        cost_estimate=SHORT,
        name="gradient_units",
    )(plane_place(), left, right)


def gather_columns(matrices, gain_one, gain_two):
    rows, width = matrices[0].shape
    quarter = width // 4

    def body(one_ref, two_ref, *refs):
        out_ref = refs[-1]
        pair = jnp.concatenate([one_ref[...], two_ref[...], jnp.zeros((6, rows), F32)], 0)
        square = jnp.concatenate([pair, jnp.zeros((8, LANES - rows), F32)], 1)
        square = jnp.concatenate([square, jnp.zeros((LANES - 8, LANES), F32)], 0)
        gains = jnp.transpose(square)[:rows].astype(BF)
        for i in range(4):
            for at, ref in enumerate(refs[:-1]):
                out_ref[i, :, at * quarter : (at + 1) * quarter] = ref[:, i * quarter : (i + 1) * quarter]
            out_ref[i, :, len(matrices) * quarter :] = gains

    return pl.pallas_call(
        body,
        out_shape=jax.ShapeDtypeStruct((4, rows, len(matrices) * quarter + LANES), BF),
        cost_estimate=SHORT,
        name="gather_columns",
    )(gain_one.astype(F32)[None], gain_two.astype(F32)[None], *matrices)


def group_place():
    unused, low, high, unused, core = place()
    return jnp.stack([2 * high + low, low, core]).astype(jnp.int32)


def plane_sort(*groups, units=()):
    sizes = [group[0].shape[-1] for group in groups]
    rows, cols = groups[0][0].shape[1], sum(sizes)
    shapes = [(rows, cols)] * 4
    if units:
        unit_rows = units[0].shape[1]
        below = cdiv(unit_rows, 16) * 16
        shapes = [(rows + below if way == 2 else rows, cols) for way in range(4)] + [(unit_rows, cols)]

    def body(at_ref, *refs):
        in_refs, out_refs = list(refs[: -len(shapes)]), refs[-len(shapes) :]
        unit_refs = in_refs[len(in_refs) - len(units) :]
        for way in range(4):
            start = 0
            left = list(in_refs)
            for size, group in zip(sizes, groups):
                total = None
                for unused in group:
                    part = left.pop(0)[at_ref[0] ^ way].astype(F32)
                    total = part if total is None else total + part
                out_refs[way][0:rows, start : start + size] = total.astype(BF)
                start += size
        if units:
            high = lax.shift_right_logical(at_ref[0], 1)
            own = sum(ref[high].astype(F32) for ref in unit_refs)
            give = sum(ref[1 - high].astype(F32) for ref in unit_refs)
            out_refs[4][...] = own.astype(BF)
            give = jnp.concatenate([give, jnp.zeros((below - unit_rows, cols), F32)], 0)
            out_refs[2][rows : rows + below, :] = give.astype(BF)

    vmem = pl.BlockSpec(memory_space=pltpu.VMEM)
    arrays = [array for group in groups for array in group] + list(units)
    return pl.pallas_call(
        body,
        in_specs=[pl.BlockSpec(memory_space=pltpu.SMEM)] + [vmem] * len(arrays),
        out_specs=[vmem] * len(shapes),
        out_shape=[jax.ShapeDtypeStruct(shape, BF) for shape in shapes],
        compiler_params=pltpu.CompilerParams(vmem_limit_bytes=VMEM_BYTES),
        cost_estimate=SHORT,
        name="plane_sort",
    )(group_place(), *arrays)


def z_merge(kept, from_1, from_2, from_3):
    rows, cols = kept.shape
    half = rows // 2

    def body(at_ref, kept_ref, one_ref, two_ref, three_ref, keep_ref, give_ref):
        same = kept_ref[...].astype(F32) + two_ref[0:rows, :].astype(F32)
        other = one_ref[...].astype(F32) + three_ref[...].astype(F32)
        for quarter, value in ((at_ref[1], same), (1 - at_ref[1], other)):
            upper, lower = value[:half], value[half:]
            keep_ref[quarter] = jnp.where(at_ref[2] == 0, upper, lower).astype(BF)
            give_ref[quarter] = jnp.where(at_ref[2] == 0, lower, upper).astype(BF)

    vmem = pl.BlockSpec(memory_space=pltpu.VMEM)
    return pl.pallas_call(
        body,
        in_specs=[pl.BlockSpec(memory_space=pltpu.SMEM)] + [vmem] * 4,
        out_specs=[vmem] * 2,
        out_shape=[jax.ShapeDtypeStruct((2, half, cols), BF)] * 2,
        compiler_params=pltpu.CompilerParams(vmem_limit_bytes=VMEM_BYTES),
        cost_estimate=SHORT,
        name="z_merge",
    )(group_place(), kept, from_1, from_2, from_3)


def join_quarters(mine, recv, core_ref, start, size, z_low, core):
    return jnp.where(
        core_ref[2] == core, mine[z_low, :, start : start + size], recv[z_low, :, start : start + size]
    ).astype(F32)


def lane_sums(value):
    total = value[:, :LANES]
    for part in lane_blocks(value)[1:]:
        total = total + part
    return total


def sums_as_row(value):
    rows = value.shape[0]
    padded = jnp.concatenate([value, jnp.zeros((LANES - rows, LANES), F32)], 0)
    return jnp.sum(jnp.transpose(padded), axis=0, keepdims=True)[:, :rows]


def join_columns(mine, recv, weights, gain, n_matrices):
    rows, cols = mine.shape[1:]
    size = cols // n_matrices

    def body(at_ref, mine_ref, recv_ref, gain_ref, *refs):
        weight_refs, out_refs = refs[: len(weights)], refs[len(weights) :]
        total = jnp.zeros((rows, LANES), F32)
        for i in range(n_matrices):
            for z_low in range(2):
                for core in range(2):
                    at = (2 * z_low + core) * size
                    value = join_quarters(mine_ref, recv_ref, at_ref, i * size, size, z_low, core)
                    out_refs[i][:, at : at + size] = value
                    if i < len(weights):
                        total = total + lane_sums(value * weight_refs[i][:, at : at + size].astype(F32))
        out_refs[-1][...] = sums_as_row(total) / gain_ref[...]

    vmem = pl.BlockSpec(memory_space=pltpu.VMEM)
    outs = pl.pallas_call(
        body,
        in_specs=[pl.BlockSpec(memory_space=pltpu.SMEM)] + [vmem] * (3 + len(weights)),
        out_specs=[vmem] * (n_matrices + 1),
        out_shape=[jax.ShapeDtypeStruct((rows, 4 * size), F32)] * n_matrices + [jax.ShapeDtypeStruct((1, rows), F32)],
        cost_estimate=SHORT,
        name="join_columns",
    )(group_place(), mine, recv, gain.astype(F32)[None], *weights)
    return list(outs[:-1]) + [outs[-1][0]]


def join_units(mine, recv, weights, gain, n_blocks):
    rows, both = mine.shape[1:]
    quarter_size = both // 2
    size = 4 * quarter_size // n_blocks

    def body(at_ref, mine_ref, recv_ref, gain_ref, one_weight, two_weight, one_ref, two_ref, total_ref):
        total = jnp.zeros((rows, LANES), F32)
        for half, (out_ref, weight_ref) in enumerate(((one_ref, one_weight), (two_ref, two_weight))):
            for block, (quarter, at) in enumerate(unit_blocks(n_blocks)):
                start = half * quarter_size + at * size
                out_ref[:, block * size : (block + 1) * size] = join_quarters(
                    mine_ref, recv_ref, at_ref, start, size, quarter // 2, quarter % 2
                )
            total = total + lane_sums(out_ref[...] * weight_ref[...].astype(F32))
        total_ref[...] = sums_as_row(total) / gain_ref[...]

    vmem = pl.BlockSpec(memory_space=pltpu.VMEM)
    one, two, total = pl.pallas_call(
        body,
        in_specs=[pl.BlockSpec(memory_space=pltpu.SMEM)] + [vmem] * 5,
        out_specs=[vmem] * 3,
        out_shape=[jax.ShapeDtypeStruct((rows, 4 * quarter_size), F32)] * 2 + [jax.ShapeDtypeStruct((1, rows), F32)],
        cost_estimate=SHORT,
        name="join_units",
    )(group_place(), mine, recv, gain.astype(F32)[None], *weights)
    return one, two, total[0]


def pair_add(one, two):
    def body(at_ref, one_ref, two_ref, own_ref, give_ref):
        for way, out_ref in enumerate((own_ref, give_ref)):
            at = at_ref[1] ^ way
            out_ref[...] = (one_ref[at].astype(F32) + two_ref[at].astype(F32)).astype(BF)

    vmem = pl.BlockSpec(memory_space=pltpu.VMEM)
    return pl.pallas_call(
        body,
        in_specs=[pl.BlockSpec(memory_space=pltpu.SMEM)] + [vmem] * 2,
        out_specs=[vmem] * 2,
        out_shape=[jax.ShapeDtypeStruct(one.shape[1:], BF)] * 2,
        compiler_params=pltpu.CompilerParams(vmem_limit_bytes=VMEM_BYTES),
        cost_estimate=SHORT,
        name="pair_add",
    )(group_place(), one, two)


def back_project(lefts, weights, transposed=True):
    block = lefts[0].shape[0] // 4
    out = weights[0].shape[0] if transposed else weights[0].shape[1]

    def body(*refs):
        left_refs, weight_refs = refs[: len(lefts)], refs[len(lefts) : 2 * len(lefts)]
        keep_ref, give_ref = refs[2 * len(lefts) :]
        total = None
        for left_ref, weight_ref in zip(left_refs, weight_refs):
            part = (matmul_cols if transposed else matmul)(left_ref[...], weight_ref[...])
            total = part if total is None else total + part
        total = total.astype(BF)
        for i in range(4):
            (keep_ref, give_ref)[i % 2][i // 2] = total[i * block : (i + 1) * block]

    return pl.pallas_call(
        body,
        in_specs=[pl.BlockSpec(memory_space=pltpu.VMEM)] * (2 * len(lefts)),
        out_specs=[pl.BlockSpec(memory_space=pltpu.VMEM)] * 2,
        out_shape=[jax.ShapeDtypeStruct((2, block, out), BF)] * 2,
        compiler_params=pltpu.CompilerParams(vmem_limit_bytes=VMEM_BYTES),
        cost_estimate=SHORT,
        name="back_project",
    )(*lefts, *weights)


def join_four(near, far, near_recv, far_recv, of_tokens):
    rows, size = near.shape
    block = rows // 4

    def body(at_ref, near_ref, far_ref, near_recv_ref, far_recv_ref, out_ref):
        for z_low in range(2):
            here = at_ref[1] == z_low
            for core in range(2):
                at = (2 * z_low + core) * size
                for i in range(4):
                    j = i ^ 1 if of_tokens else i
                    mine, other = slice(i * block, (i + 1) * block), slice(j * block, (j + 1) * block)
                    ours = jnp.where(here, near_ref[mine], far_ref[mine])
                    theirs = jnp.where(here, near_recv_ref[other], far_recv_ref[other])
                    out_ref[mine, at : at + size] = jnp.where(at_ref[2] == core, ours, theirs)

    vmem = pl.BlockSpec(memory_space=pltpu.VMEM)
    return pl.pallas_call(
        body,
        in_specs=[pl.BlockSpec(memory_space=pltpu.SMEM)] + [vmem] * 4,
        out_specs=vmem,
        out_shape=jax.ShapeDtypeStruct((rows, 4 * size), near.dtype),
        compiler_params=pltpu.CompilerParams(vmem_limit_bytes=VMEM_BYTES),
        cost_estimate=SHORT,
        name="join_four",
    )(group_place(), near, far, near_recv, far_recv)


def branch_back(mine, recv, x_one, gain, g_mine, g_recv, w_out):
    blocks, seg_len, width = x_one.shape
    quarter = width // 4

    def body(at_ref, mine_ref, recv_ref, x_ref, gain_ref, g_ref, g_recv_ref, w_ref, branch_ref, att_ref, own_ref):
        block = pl.program_id(0)
        grad = jnp.where(block % 2 == 0, mine_ref[0], recv_ref[0]).astype(F32)
        passed = jnp.where(block % 2 == 0, g_ref[0], g_recv_ref[0]).astype(F32)
        values = x_ref[0]
        inverse = lax.rsqrt(jnp.mean(values * values, axis=-1, keepdims=True) + EPSILON)
        normed = values * inverse
        scaled = grad * gain_ref[...]
        mean = jnp.mean(scaled * normed, axis=-1, keepdims=True)
        total = passed + inverse * (scaled - normed * mean)
        low = total.astype(BF)
        branch_ref[0] = low
        att_ref[0] = matmul_cols(low, w_ref[...]).astype(BF)

        @pl.when(block == 2 * at_ref[1])
        def own():
            own_ref[...] = total

    pair = pl.BlockSpec((1, seg_len, width), lambda i, at: (i // 2, 0, 0))
    full = pl.BlockSpec((1, seg_len, width), lambda i, at: (i, 0, 0))
    return pl.pallas_call(
        body,
        grid_spec=pltpu.PrefetchScalarGridSpec(
            num_scalar_prefetch=1,
            grid=(blocks,),
            in_specs=[
                pair,
                pair,
                full,
                pl.BlockSpec((1, width), lambda i, at: (0, 0)),
                pair,
                pair,
                pl.BlockSpec((quarter, width), lambda i, at: (2 * at[1] + at[2], 0)),
            ],
            out_specs=[
                full,
                pl.BlockSpec((1, seg_len, quarter), lambda i, at: (i, 0, 0)),
                pl.BlockSpec((seg_len, width), lambda i, at: (0, 0)),
            ],
        ),
        out_shape=[
            jax.ShapeDtypeStruct((blocks, seg_len, width), BF),
            jax.ShapeDtypeStruct((blocks, seg_len, quarter), BF),
            jax.ShapeDtypeStruct((seg_len, width), F32),
        ],
        compiler_params=pltpu.CompilerParams(vmem_limit_bytes=VMEM_BYTES),
        cost_estimate=SHORT,
        name="branch_back",
    )(group_place(), mine, recv, x_one, gain, g_mine, g_recv, w_out)


def input_back(mine, recv, x_all, gain, passed):
    unused, seg_len, width = x_all.shape

    def body(at_ref, mine_ref, recv_ref, x_ref, gain_ref, passed_ref, out_ref):
        values = x_ref[0].astype(F32)
        inverse = lax.rsqrt(jnp.mean(values * values, axis=-1, keepdims=True) + EPSILON)
        normed = values * inverse
        scaled = (mine_ref[...].astype(F32) + recv_ref[...].astype(F32)) * gain_ref[...]
        mean = jnp.mean(scaled * normed, axis=-1, keepdims=True)
        out_ref[...] = (passed_ref[...] + inverse * (scaled - normed * mean)).astype(BF)

    tokens = pl.BlockSpec((seg_len, width), lambda i, at: (0, 0))
    return pl.pallas_call(
        body,
        grid_spec=pltpu.PrefetchScalarGridSpec(
            num_scalar_prefetch=1,
            grid=(1,),
            in_specs=[
                tokens,
                tokens,
                pl.BlockSpec((1, seg_len, width), lambda i, at: (2 * at[1], 0, 0)),
                pl.BlockSpec((1, width), lambda i, at: (0, 0)),
                tokens,
            ],
            out_specs=tokens,
        ),
        out_shape=jax.ShapeDtypeStruct((seg_len, width), BF),
        compiler_params=pltpu.CompilerParams(vmem_limit_bytes=VMEM_BYTES),
        cost_estimate=SHORT,
        name="input_back",
    )(group_place(), mine, recv, x_all, gain, passed)


def add_kernel(one, two):
    def body(one_ref, two_ref, out_ref):
        out_ref[...] = (one_ref[...].astype(F32) + two_ref[...].astype(F32)).astype(BF)

    return pl.pallas_call(
        body,
        in_specs=[pl.BlockSpec(memory_space=pltpu.VMEM)] * 2,
        out_specs=pl.BlockSpec(memory_space=pltpu.VMEM),
        out_shape=jax.ShapeDtypeStruct(one.shape, BF),
        compiler_params=pltpu.CompilerParams(vmem_limit_bytes=VMEM_BYTES),
        cost_estimate=SHORT,
        name="add_kernel",
    )(one, two)


def add_low(one, two):
    return (one.astype(F32) + two.astype(F32)).astype(BF)


def lane_blocks(value):
    return [value[:, i : i + LANES] for i in range(0, value.shape[1], LANES)]


PIECES = ((0, 0), (0, 1), (1, 0), (1, 1), (2, 0), (3, 0), (2, 1))
N_COMMON = 5
N_GROUPS = 4


def head_of(value, head):
    return value[:, head * HD : (head + 1) * HD]


def forward_kernel(q_ref, k_ref, v_ref, mine_ref, other_ref, *refs):
    key_refs, value_refs = refs[:N_GROUPS], refs[N_GROUPS : 2 * N_GROUPS]
    o_ref, of_ref, p_ref, pl_ref, inv_ref, s_ref, top_ref, total_ref, acc_ref = refs[2 * N_GROUPS :]
    heads = range(q_ref.shape[2] // HD)
    scale = HD ** (-0.5) * LOG2_E
    block = pl.program_id(0)
    upper = block >= 2
    queries = q_ref[0]
    seg_len = queries.shape[0]
    per = key_refs[0].shape[1] // LANES
    first = block % 2 == 0

    def bias(at):
        return jnp.where(first, mine_ref[0, at], other_ref[0, at]).astype(F32)

    local_bias = jnp.concatenate([bias(len(PIECES) * per + i) for i in range(cdiv(seg_len, LANES))], 1)[:, :seg_len]
    s_local = [
        jnp.minimum(matmul_cols(head_of(queries, h), head_of(k_ref[0], h)) * scale, local_bias) for h in heads
    ]

    def score(t, tops):
        group, low = PIECES[t]
        keys = key_refs[group][low]
        parts = [lane_blocks(matmul_cols(head_of(queries, h), head_of(keys, h)) * scale) for h in heads]
        for i in range(per):
            limit = bias(t * per + i)
            for h in heads:
                part = jnp.minimum(parts[h][i], limit)
                s_ref[h, t, :, i * LANES : (i + 1) * LANES] = part
                tops[h] = part if tops[h] is None else jnp.maximum(tops[h], part)
        return tops

    tops = [None for h in heads]
    for t in range(N_COMMON):
        tops = score(t, tops)
    for h in heads:
        top_ref[h] = tops[h]

    @pl.when(upper)
    def more_scores():
        tops = [top_ref[h] for h in heads]
        for t in range(N_COMMON, len(PIECES)):
            tops = score(t, tops)
        for h in heads:
            top_ref[h] = tops[h]

    row_max, e_local = [], []
    for h in heads:
        row_max.append(
            jnp.maximum(
                jnp.max(s_local[h], axis=-1, keepdims=True), jnp.max(top_ref[h], axis=-1, keepdims=True)
            )
        )
        expo = jnp.exp2(s_local[h] - row_max[h])
        e_local.append(jnp.sum(expo, axis=-1, keepdims=True))
        chances = expo.astype(BF)
        pl_ref[0, h] = chances
        acc_ref[h] = matmul(chances, head_of(v_ref[0], h))

    def weigh(t, h, total, acc):
        group, low = PIECES[t]
        expo = jnp.exp2(s_ref[h, t] - row_max[h])
        for part in lane_blocks(expo):
            total = part if total is None else total + part
        chances = expo.astype(BF)
        p_ref[0, h, t] = chances
        return total, acc + matmul(chances, head_of(value_refs[group][low], h))

    for h in heads:
        total, acc = None, acc_ref[h]
        for t in range(N_COMMON):
            total, acc = weigh(t, h, total, acc)
        total_ref[h] = total
        acc_ref[h] = acc

    @pl.when(upper)
    def more_values():
        for h in heads:
            total, acc = total_ref[h], acc_ref[h]
            for t in range(N_COMMON, len(PIECES)):
                total, acc = weigh(t, h, total, acc)
            total_ref[h] = total
            acc_ref[h] = acc

    for h in heads:
        inverse = 1.0 / (e_local[h] + jnp.sum(total_ref[h], axis=-1, keepdims=True))
        out = acc_ref[h] * inverse
        of_ref[0, :, h * HD : (h + 1) * HD] = out
        o_ref[0, :, h * HD : (h + 1) * HD] = out.astype(BF)
        inv_ref[0, h] = inverse


def backward_local_kernel(do_ref, of_ref, q_ref, k_ref, v_ref, inv_ref, pl_ref, cos_ref, sin_ref, dkv_ref, dq_ref):
    scale = HD ** (-0.5)
    for h in range(q_ref.shape[2] // HD):
        span = slice(h * HD, (h + 1) * HD)
        d_out = do_ref[0, :, span]
        delta = jnp.sum(d_out.astype(F32) * of_ref[0, :, span], axis=-1, keepdims=True)
        chances = pl_ref[0, h].astype(F32) * inv_ref[0, h]
        ds = (chances * (matmul_cols(d_out, v_ref[0, :, span]) - delta)).astype(BF)
        dq_ref[0, :, span] = matmul(ds, k_ref[0, :, span])
        dk = matmul_rows(ds, q_ref[0, :, span])
        dkv_ref[0, 0, :, span] = (
            (dk * cos_ref[...] - pltpu.roll(dk, HD // 2, 1) * sin_ref[...]) * scale
        ).astype(BF)
        dkv_ref[1, 0, :, span] = matmul_rows(chances.astype(BF), d_out).astype(BF)


def backward_kernel(do_ref, of_ref, local_ref, inv_ref, p_ref, cos_ref, sin_ref, *refs):
    key_refs, value_refs = refs[:N_GROUPS], refs[N_GROUPS : 2 * N_GROUPS]
    out_ref, dq_ref = refs[2 * N_GROUPS :]
    heads = range(do_ref.shape[2] // HD)
    scale = HD ** (-0.5)
    upper = pl.program_id(0) >= 2
    d_out = [do_ref[0, :, h * HD : (h + 1) * HD] for h in heads]
    inverse = [inv_ref[0, h] for h in heads]
    delta = [
        jnp.sum(d_out[h].astype(F32) * of_ref[0, :, h * HD : (h + 1) * HD], axis=-1, keepdims=True) for h in heads
    ]

    def piece(t, h, dq):
        group, low = PIECES[t]
        dp = matmul_cols(d_out[h], head_of(value_refs[group][low], h))
        ds = (p_ref[0, h, t].astype(F32) * ((dp - delta[h]) * inverse[h])).astype(BF)
        return dq + matmul(ds, head_of(key_refs[group][low], h))

    for h in heads:
        dq = local_ref[0, :, h * HD : (h + 1) * HD]
        for t in range(N_COMMON):
            dq = piece(t, h, dq)
        dq_ref[h] = dq

    @pl.when(upper)
    def more():
        for h in heads:
            dq = dq_ref[h]
            for t in range(N_COMMON, len(PIECES)):
                dq = piece(t, h, dq)
            dq_ref[h] = dq

    for h in heads:
        dq = dq_ref[h]
        out_ref[0, :, h * HD : (h + 1) * HD] = (
            (dq * cos_ref[...] - pltpu.roll(dq, HD // 2, 1) * sin_ref[...]) * scale
        ).astype(BF)


def attention_specs(piece_rows, seg_len, width):
    heads = width // HD
    tokens = pl.BlockSpec((1, seg_len, width), lambda r: (r, 0, 0))
    piece = pl.BlockSpec((2, piece_rows, width), lambda r: (0, 0, 0))
    p_spec = pl.BlockSpec((1, heads, len(PIECES), seg_len, piece_rows), lambda r: (r, 0, 0, 0, 0))
    pl_spec = pl.BlockSpec((1, heads, seg_len, seg_len), lambda r: (r, 0, 0, 0))
    inv_spec = pl.BlockSpec((1, heads, seg_len, 1), lambda r: (r, 0, 0, 0))
    return tokens, piece, p_spec, pl_spec, inv_spec


def attention_forward(queries, keys, values, mask, other_mask, key_pieces, value_pieces):
    blocks, seg_len, width = queries.shape
    heads = width // HD
    piece_rows = key_pieces[0].shape[1]
    tokens, piece, p_spec, pl_spec, inv_spec = attention_specs(piece_rows, seg_len, width)
    mask_spec = pl.BlockSpec((1,) + mask.shape[1:], lambda r: (r // 2, 0, 0, 0))
    return pl.pallas_call(
        forward_kernel,
        grid=(blocks,),
        in_specs=[tokens, tokens, tokens, mask_spec, mask_spec] + [piece] * (2 * N_GROUPS),
        out_specs=[tokens, tokens, p_spec, pl_spec, inv_spec],
        out_shape=[
            jax.ShapeDtypeStruct(queries.shape, BF),
            jax.ShapeDtypeStruct(queries.shape, F32),
            jax.ShapeDtypeStruct((blocks, heads, len(PIECES), seg_len, piece_rows), BF),
            jax.ShapeDtypeStruct((blocks, heads, seg_len, seg_len), BF),
            jax.ShapeDtypeStruct((blocks, heads, seg_len, 1), F32),
        ],
        scratch_shapes=[
            pltpu.VMEM((heads, len(PIECES), seg_len, piece_rows), F32),
            pltpu.VMEM((heads, seg_len, LANES), F32),
            pltpu.VMEM((heads, seg_len, LANES), F32),
            pltpu.VMEM((heads, seg_len, HD), F32),
        ],
        compiler_params=pltpu.CompilerParams(vmem_limit_bytes=VMEM_BYTES),
        cost_estimate=SHORT,
        name="attention_forward",
    )(queries, keys, values, mask, other_mask, *key_pieces, *value_pieces)


def attention_backward_local(d_out, out_f32, queries, keys, values, inverse, p_local, cosine, sine):
    blocks, seg_len, width = queries.shape
    tokens, unused, unused, pl_spec, inv_spec = attention_specs(seg_len, seg_len, width)
    table = pl.BlockSpec((seg_len, HD), lambda r: (0, 0))
    return pl.pallas_call(
        backward_local_kernel,
        grid=(blocks,),
        in_specs=[tokens, tokens, tokens, tokens, tokens, inv_spec, pl_spec, table, table],
        out_specs=[pl.BlockSpec((2, 1, seg_len, width), lambda r: (0, r, 0, 0)), tokens],
        out_shape=[
            jax.ShapeDtypeStruct((2, blocks, seg_len, width), BF),
            jax.ShapeDtypeStruct(queries.shape, F32),
        ],
        compiler_params=pltpu.CompilerParams(vmem_limit_bytes=VMEM_BYTES),
        cost_estimate=SHORT,
        name="attention_backward_local",
    )(d_out, out_f32, queries, keys, values, inverse, p_local, cosine, sine)


def attention_backward(d_out, out_f32, dq_local, inverse, p_memory, cosine, sine, key_pieces, value_pieces):
    blocks, seg_len, width = d_out.shape
    piece_rows = key_pieces[0].shape[1]
    tokens, piece, p_spec, unused, inv_spec = attention_specs(piece_rows, seg_len, width)
    table = pl.BlockSpec((seg_len, HD), lambda r: (0, 0))
    return pl.pallas_call(
        backward_kernel,
        grid=(blocks,),
        in_specs=[tokens, tokens, tokens, inv_spec, p_spec, table, table] + [piece] * (2 * N_GROUPS),
        out_specs=tokens,
        out_shape=jax.ShapeDtypeStruct((blocks, seg_len, width), BF),
        scratch_shapes=[pltpu.VMEM((width // HD, seg_len, HD), F32)],
        compiler_params=pltpu.CompilerParams(vmem_limit_bytes=VMEM_BYTES),
        cost_estimate=SHORT,
        name="attention_backward",
    )(d_out, out_f32, dq_local, inverse, p_memory, cosine, sine, *key_pieces, *value_pieces)


def allow_local_of(live):
    seg_len = live.shape[-1]
    position = jnp.arange(seg_len, dtype=jnp.int32)
    same = position[None, :] == position[:, None]
    return same[None] | ((position[None, :] < position[:, None])[None] & (live == 1))


def split_heads(value):
    rows, seg_len, width = value.shape
    return value.reshape(rows, seg_len, width // HD, HD)


def stream_forward(queries, keys, values, live, allow, memory):
    scale = HD ** (-0.5)
    q4, k4, v4 = split_heads(queries), split_heads(keys), split_heads(values)
    scores = jnp.einsum("rqhd,rkhd->rhqk", q4, k4, preferred_element_type=F32) * scale
    scores = jnp.where(allow_local_of(live)[:, None], scores, NEG_BIG)
    row_max = jnp.max(scores, axis=-1)
    expo = jnp.exp(scores - row_max[..., None])
    state = (
        row_max,
        jnp.sum(expo, axis=-1),
        jnp.einsum("rhqk,rkhd->rhqd", expo.astype(BF), v4, preferred_element_type=F32),
    )

    def step(running, item):
        row_max, row_total, acc = running
        block, allowed = item
        k3 = block[0].reshape(block.shape[1], -1, HD)
        v3 = block[1].reshape(block.shape[1], -1, HD)
        scores = jnp.einsum("rqhd,khd->rhqk", q4, k3, preferred_element_type=F32) * scale
        scores = jnp.where(allowed[:, None] > 0, scores, NEG_BIG)
        new_max = jnp.maximum(row_max, jnp.max(scores, axis=-1))
        shrink = jnp.exp(row_max - new_max)
        expo = jnp.exp(scores - new_max[..., None])
        acc = acc * shrink[..., None] + jnp.einsum(
            "rhqk,khd->rhqd", expo.astype(BF), v3, preferred_element_type=F32
        )
        return (new_max, row_total * shrink + jnp.sum(expo, axis=-1), acc), None

    (row_max, row_total, acc), unused = lax.scan(step, state, (memory, allow))
    out = (acc / row_total[..., None]).transpose(0, 2, 1, 3).reshape(queries.shape)
    return out.astype(BF), out, row_max + jnp.log(row_total)


def stream_backward(d_out, out_f32, queries, keys, values, live, log_total, allow, memory, cosine, sine):
    scale = HD ** (-0.5)
    q4, k4, v4, d4 = split_heads(queries), split_heads(keys), split_heads(values), split_heads(d_out)
    delta = jnp.sum(d4.astype(F32) * split_heads(out_f32), axis=-1).transpose(0, 2, 1)
    scores = jnp.einsum("rqhd,rkhd->rhqk", q4, k4, preferred_element_type=F32) * scale
    scores = jnp.where(allow_local_of(live)[:, None], scores, NEG_BIG)
    chances = jnp.exp(scores - log_total[..., None])
    dp = jnp.einsum("rqhd,rkhd->rhqk", d4, v4, preferred_element_type=F32)
    ds = (chances * (dp - delta[..., None])).astype(BF)
    dq = jnp.einsum("rhqk,rkhd->rqhd", ds, k4, preferred_element_type=F32)
    dk = jnp.einsum("rhqk,rqhd->rkhd", ds, q4, preferred_element_type=F32)
    dv = jnp.einsum("rhqk,rqhd->rkhd", chances.astype(BF), d4, preferred_element_type=F32)

    def step(running, item):
        block, allowed = item
        k3 = block[0].reshape(block.shape[1], -1, HD)
        v3 = block[1].reshape(block.shape[1], -1, HD)
        scores = jnp.einsum("rqhd,khd->rhqk", q4, k3, preferred_element_type=F32) * scale
        scores = jnp.where(allowed[:, None] > 0, scores, NEG_BIG)
        chances = jnp.exp(scores - log_total[..., None])
        dp = jnp.einsum("rqhd,khd->rhqk", d4, v3, preferred_element_type=F32)
        ds = (chances * (dp - delta[..., None])).astype(BF)
        return running + jnp.einsum("rhqk,khd->rqhd", ds, k3, preferred_element_type=F32), None

    dq, unused = lax.scan(step, dq, (memory, allow))

    def back(value):
        turned = rope_heads(value.reshape((-1,) + value.shape[2:]), jnp.tile(cosine, (value.shape[0], 1)), -jnp.tile(sine, (value.shape[0], 1)))
        return (turned * scale).reshape(queries.shape).astype(BF)

    return jnp.stack([back(dq), back(dk), dv.reshape(queries.shape).astype(BF)])


def local(
    layer_input,
    live,
    knn_index,
    mem_keys,
    mem_values,
    gain_attn,
    w_query,
    w_key,
    w_value,
    w_out,
    gain_ffn,
    w_gate,
    w_up,
    w_down,
    cotangent,
):
    seg_len, width = layer_input.shape[1:]
    quarter = width // 4
    n_seg = lax.axis_size("seg")
    n_devices = n_seg * lax.axis_size("rep")
    tokens = seg_len * n_seg
    n_high = n_seg // 4
    x, low, high, y, core = place()
    use_kernel = n_high <= KERNEL_HIGH
    kv_rows = 2 * seg_len
    group_tokens = 4 * seg_len

    def by_quarter(value):
        return [value[:, i * quarter : (i + 1) * quarter] for i in range(4)]

    gains = None if width // n_devices % 16 == 0 else jnp.concatenate(
        [gain_attn[:, None], gain_ffn[:, None], jnp.zeros((gain_attn.shape[0], LANES - 2), BF)], 1
    )
    if gains is None:
        qo = gather_columns((w_query, w_key, w_value, w_out), gain_attn, gain_ffn)
    else:
        stacked = [by_quarter(w) for w in (w_query, w_key, w_value, w_out)]
        qo = jnp.stack([jnp.concatenate([s[i] for s in stacked] + [gains], 1) for i in range(4)])

    def core_quarters(value, side):
        return jnp.stack([cut(value, side * quarter, quarter), cut(value, (2 + side) * quarter, quarter)])

    def core_memory(side):
        return jnp.stack([core_quarters(mem_keys[0], side), core_quarters(mem_values[0], side)])

    coded = knn_index[0] * 2 + live[0][:, None]
    qo = qo.reshape(2, 2, -1, qo.shape[-1])
    qo_keep, qo_give = halves(qo, 1, core)
    kv_keep, kv_give = core_memory(core), core_memory(1 - core)
    qo_recv, kv_recv, coded_recv = flip_core(qo_give), flip_core(kv_give), flip_z(coded)
    qo_keep, kv_keep, coded, qo_recv, kv_recv, coded_recv, w_gate_, w_up_ = fence(
        qo_keep, kv_keep, coded, qo_recv, kv_recv, coded_recv, w_gate, w_up
    )

    qo_keep, qo_give = halves(ordered(qo_keep, qo_recv, core, 1), 0, low)
    kv_keep, kv_give = halves(ordered(kv_keep, kv_recv, core, 2), 1, low)
    coded = ordered(coded[None], coded_recv[None], low, 0)
    kv_recv = flip_z(kv_give)
    qo_near = flip_z(qo_give)
    down_w = w_down[None, None, None, None]
    x_own = layer_input[0]
    gate_up = split_units(w_gate_, w_up_, n_devices).reshape(2, 2, 2, -1, w_gate.shape[1] // 4)

    def places_of(codes, row_core):
        picks = lax.shift_right_arithmetic(codes, 1)
        pair = picks >= tokens
        slot = jnp.where(pair, picks - tokens, picks)
        slot_seg = slot // seg_len
        kv_row = jnp.bitwise_xor(pair.astype(jnp.int32), row_core)
        return picks, slot_seg, kv_row * seg_len + (slot - slot_seg * seg_len)

    split = 3 * quarter
    g_own = cotangent[0]
    cosine, sine = rope_tables(seg_len)
    if use_kernel:
        qo_far, qo_side = flip(qo_keep, "seg", 4), flip(qo_give, "seg", 6)
        picks, slot_seg, within = places_of(coded, core)
        slot_x, slot_low = slot_seg % 2, (slot_seg // 2) % 2
        same_x = slot_x == x
        in_group = jnp.where(same_x, 5, 4 + 2 * slot_low)
        before = jnp.where(same_x, 0, 2) + slot_low
        piece_no = jnp.where(slot_seg // 4 == high, in_group, before)
        columns = jnp.where(picks >= 0, piece_no * kv_rows + within, -1)
        live_two = jnp.bitwise_and(coded[:, :, 0], 1)[:, None, :]
        live_two = jnp.pad(live_two, ((0, 0), (0, 0), (0, cdiv(seg_len, LANES) * LANES - seg_len)))
        down_recv = flip(down_w, "seg", 4)
        (
            qo_keep, qo_near, qo_far, qo_side, kv_keep, kv_recv, x_own, gate_up, columns, live_two, down_w, down_recv
        ) = fence(
            qo_keep, qo_near, qo_far, qo_side, kv_keep, kv_recv, x_own, gate_up, columns, live_two, down_w, down_recv
        )

        pieces = ordered(kv_keep[:, None], kv_recv[:, None], low, 1)
        own_k, own_v = pieces[0], pieces[1]
        near = ordered(qo_keep[None, None], qo_near[None, None], low, 1)
        far = ordered(qo_far[None, None], qo_side[None, None], low, 1)
        qo = ordered(near, far, high, 0)[:, :, None, None]
        qo_a, qo_b = qo[..., :split], qo[..., split:]
        up_high = [(i, i + 4) for i in range(n_seg - 4)]

        def cross(value):
            return lax.ppermute(value, "seg", up_high)

        cross_k, side_k = cross(own_k), flip_x(own_k)
        a_recv, b_recv = flip_x(qo_a), flip_y(qo_b)
        x_recv = flip_z(x_own)
        gu_keep, gu_give = halves(gate_up, 1, core)
        gu_recv = flip_core(gu_give)
        mask = build_mask(columns, live_two, len(PIECES) * kv_rows // LANES)
        qo_a, qo_b, a_recv, b_recv, cross_k, side_k, own_v, x_own, x_recv, gu_keep, gu_recv, mask, down_w, down_recv = fence(
            qo_a, qo_b, a_recv, b_recv, cross_k, side_k, own_v, x_own, x_recv, gu_keep, gu_recv, mask, down_w, down_recv
        )

        cross_v, cross_side_k = cross(own_v), flip_x(cross_k)
        qo_a, qo_b = ordered(qo_a, a_recv, x, 2), ordered(qo_b, b_recv, y, 3)
        a_recv, b_recv = flip_y(qo_a), flip_x(qo_b)
        gu_keep, gu_give = halves(ordered(gu_keep, gu_recv, core, 2), 0, low)
        gu_recv = flip_z(gu_give)
        x_two = ordered(x_own[None], x_recv[None], low, 0)
        x_recv = flip_core(x_two)
        qo_a, qo_b, a_recv, b_recv, cross_v, cross_side_k, own_v, gu_keep, gu_recv, x_two, x_recv, mask, down_w, down_recv = fence(
            qo_a, qo_b, a_recv, b_recv, cross_v, cross_side_k, own_v, gu_keep, gu_recv, x_two, x_recv, mask, down_w, down_recv
        )

        cross_side_v, side_v = flip_x(cross_v), flip_x(own_v)
        other_mask = flip_core(mask)
        g_far = flip_z(g_own)
        w_a, w_b = flat(ordered(qo_a, a_recv, y, 3)), flat(ordered(qo_b, b_recv, x, 2))
        gate_up = ordered(gu_keep[:, None], gu_recv[:, None], low, 1)[:, None]
        gu_recv = flip(gate_up, "seg", 4)
        down_w = ordered(down_w, down_recv, high, 0)
        down_recv = flip_y(down_w)
        x_all = jnp.stack([x_two, x_recv], 1).reshape(4, seg_len, width)
        queries, keys, values, h_one, inv_one = project(x_all, w_a, w_b, cosine, sine)
        wo_near = w_b[:, :quarter]
        (
            queries, keys, values, cross_side_v, side_v, gate_up, gu_recv, down_w, down_recv, wo_near, g_own, g_far, other_mask
        ) = fence(
            queries, keys, values, cross_side_v, side_v, gate_up, gu_recv, down_w, down_recv, wo_near, g_own, g_far, other_mask
        )

        key_pieces = (cross_k, cross_side_k, side_k, own_k)
        value_pieces = (cross_v, cross_side_v, side_v, own_v)
        gate, upw = [ordered(gate_up[i], gu_recv[i], high, 0)[:, :, None, None] for i in range(2)]
        down_w = ordered(down_w, down_recv, y, 3)
        down_a, down_b = down_w[..., : width // 4], down_w[..., width // 4 :]
        g_recv, u_recv, a_recv, wo_far = flip_x(gate), flip_y(upw), flip_x(down_a), flip_z(wo_near)
        out_low, out_f32, p_memory, p_local, inverse = attention_forward(
            queries, keys, values, mask, other_mask, key_pieces, value_pieces
        )
        wo_recv = flip_core(wo_near)
        out_low, gate, upw, g_recv, u_recv, down_a, a_recv, down_b, wo_near, wo_far, wo_recv, g_own, g_far = fence(
            out_low, gate, upw, g_recv, u_recv, down_a, a_recv, down_b, wo_near, wo_far, wo_recv, g_own, g_far
        )
    else:
        qo = gather_high(ordered(qo_keep[None], qo_near[None], low, 0)[None, :, None, None])
        kv = ordered(kv_keep[:, None], kv_recv[:, None], low, 1)
        w_a, w_b = flat(gather_y(gather_x(qo[..., :split]))), flat(gather_x(gather_y(qo[..., split:])))
        x_all = all_blocks(two_rows(x_own))
        gu_keep, gu_give = halves(gate_up, 1, core)
        gu_keep, gu_give = halves(ordered(gu_keep, flip_core(gu_give), core, 2), 0, low)
        gate, upw = gather_high_pair(ordered(gu_keep[:, None], flip_z(gu_give)[:, None], low, 1))
        down_w = gather_y(gather_high(down_w))
        down_a, down_b = down_w[..., : width // 4], down_w[..., width // 4 :]
        coded = all_blocks(coded)
        row_core = jnp.bitwise_xor(core, jnp.arange(4, dtype=jnp.int32) % 2)[:, None, None]
        picks, slot_seg, within = places_of(coded, row_core)
        live_all = jnp.bitwise_and(coded[:, :, 0], 1)[:, None, :]
        columns = jnp.where(picks >= 0, slot_seg * kv_rows + within, n_seg * kv_rows)
        blocks_at = jnp.arange(4)[:, None, None]
        queries_at = jnp.arange(seg_len)[None, :, None]
        allow = jnp.zeros((4, seg_len, n_seg * kv_rows), BF).at[blocks_at, queries_at, columns].set(1.0, mode="drop")
        allow = allow.reshape(4, seg_len, n_seg, kv_rows).transpose(2, 0, 1, 3)
        memory = jnp.swapaxes(kv, 0, 1)[None, :, None]
        memory = gather_x(gather_high(memory)).reshape(n_seg, 2, kv_rows, quarter)
        queries, keys, values, h_one, inv_one = project(x_all, w_a, w_b, cosine, sine)
        wo_near = w_b[:, :quarter]
        out_low, out_f32, log_total = stream_forward(queries, keys, values, live_all, allow, memory)
        g_recv, u_recv, a_recv, wo_far = flip_x(gate), flip_y(upw), flip_x(down_a), flip_z(wo_near)
        g_far = flip_z(g_own)
        wo_recv = flip_core(wo_near)

    h_one = h_one.reshape(group_tokens, width)
    inv_one = inv_one.reshape(group_tokens, 1)
    x_float = x_all.reshape(group_tokens, width).astype(F32)
    g_attn = w_b[:, quarter].astype(F32)
    g_ffn = w_b[:, quarter + 1].astype(F32)
    att_near = out_low.reshape(group_tokens, quarter)
    att_far = flip_z(att_near)
    gate, upw = ordered(gate, g_recv, x, 2), ordered(upw, u_recv, y, 3)
    g_recv, u_recv = flip_y(gate), flip_x(upw)
    wo = join_four(wo_near, wo_far, wo_recv, flip_core(wo_far), False)
    att_recv = flip_core(att_near)
    att_near, att_far, att_recv, gate, upw, g_recv, u_recv, down_b, wo, g_own, g_far = fence(
        att_near, att_far, att_recv, gate, upw, g_recv, u_recv, down_b, wo, g_own, g_far
    )

    att_far_recv = flip_core(att_far)
    down_recv = flip_x(down_b)
    g_two = ordered(g_own[None], g_far[None], low, 0)
    g_recv_core = flip_core(g_two)
    wg, wu = flat(ordered(gate, g_recv, y, 3)), flat(ordered(upw, u_recv, x, 2))
    attended = join_four(att_near, att_far, att_recv, att_far_recv, True)
    x_one = x_float + matmul(attended, wo)
    h_two_f, inv_two = norm_forward(x_one, g_ffn)
    h_two = h_two_f.astype(BF)
    gate_out = matmul(h_two, wg)
    up_out = matmul(h_two, wu)
    sigma = jax.nn.sigmoid(gate_out)
    swish = gate_out * sigma
    hidden = (swish * up_out).astype(BF)
    grad_out = jnp.stack([g_two, g_recv_core], 1).reshape(group_tokens, width)

    down_b, hidden = fence(down_b, hidden)
    wd = jnp.concatenate([flat(ordered(down_a, a_recv, x, 2)), flat(ordered(down_b, down_recv, x, 2))], 1)
    d_hidden = matmul_cols(grad_out, wd)
    d_gate = (d_hidden * up_out * sigma * (1.0 + gate_out * (1.0 - sigma))).astype(BF)
    d_up = (d_hidden * swish).astype(BF)
    sums_keep, sums_give = back_project([d_gate, d_up], [wg, wu])
    sums_recv = flip_core(sums_give)
    (keep_g, give_g), (keep_u, give_u) = gradient((h_two, [d_gate], "x", None), (h_two, [d_up], "y", None))
    sums_keep, sums_recv, keep_g, give_g, keep_u, give_u, hidden, wd = fence(
        sums_keep, sums_recv, keep_g, give_g, keep_u, give_u, hidden, wd
    )

    sums = add_kernel(sums_keep, sums_recv)
    far_sums = flip_z(sums)
    recv_g, recv_u = flip_x(give_g), flip_y(give_u)
    down_keep, down_give = back_project([hidden], [wd], False)
    down_recv = flip_core(down_give)
    keep_wd, give_wd = gradient_units(hidden, grad_out)
    sums, far_sums, keep_g, keep_u, recv_g, recv_u, down_keep, down_recv, keep_wd, give_wd = fence(
        sums, far_sums, keep_g, keep_u, recv_g, recv_u, down_keep, down_recv, keep_wd, give_wd
    )

    own = 2 * low * seg_len
    summed = add_kernel(sums, far_sums)
    summed_recv = flip_core(summed)
    d_branch, d_att, d_x_own = branch_back(
        summed,
        summed_recv,
        x_one.reshape(4, seg_len, width),
        g_ffn[None],
        g_two,
        g_recv_core,
        wo,
    )
    d_branch = d_branch.reshape(group_tokens, width)
    keep_g, keep_u, recv_g, recv_u, d_att, d_branch, down_keep, down_recv = fence(
        keep_g, keep_u, recv_g, recv_u, d_att, d_branch, down_keep, down_recv
    )

    keep_g, give_g = split_sums(keep_g, recv_g, "y")
    keep_u, give_u = split_sums(keep_u, recv_u, "x")
    down_own, down_give = pair_add(down_keep, down_recv)
    w_thirds = [w_a[:, i * quarter : (i + 1) * quarter] for i in range(3)]
    if use_kernel:
        recv_g, recv_u = flip_y(give_g), flip_x(give_u)
        down_recv = flip_z(down_give)
        d_kv, dq_local = attention_backward_local(
            d_att, out_f32, queries, keys, values, inverse, p_local, cosine, sine
        )
        d_kv = d_kv.reshape(2, group_tokens, quarter)
        (keep_kv, give_kv), (keep_wo, give_wo) = gradient(
            (h_one, [d_kv[0], d_kv[1]], "y", None), (attended, [d_branch], "y", quarter)
        )
        give_kvo = jnp.concatenate([give_kv, give_wo], -1)
        keep_kvo = jnp.concatenate([keep_kv, keep_wo], -1)
        keep_kvo, give_kvo, keep_g, recv_g, keep_u, recv_u, dq_local, keep_wd, give_wd, down_own, down_recv = fence(
            keep_kvo, give_kvo, keep_g, recv_g, keep_u, recv_u, dq_local, keep_wd, give_wd, down_own, down_recv
        )
        gu_parts = plane_sort((keep_g, recv_g), (keep_u, recv_u))
        recv_kvo = flip_y(give_kvo)
        gu_flips = z_flips(gu_parts)
        recv_wd = flip_x(give_wd)
        d_q = attention_backward(
            d_att, out_f32, dq_local, inverse, p_memory, cosine, sine, key_pieces, value_pieces
        )
        d_q, keep_kvo = fence(d_q, keep_kvo)

        d_q = d_q.reshape(group_tokens, quarter)
        ((keep_q, *give_q),) = gradient((h_one, [d_q], "xy", None))
        keep_q, give_q, d_q, keep_kvo, recv_kvo, keep_wd, recv_wd, gu_kept, gu_flips = fence(
            keep_q, give_q, d_q, keep_kvo, recv_kvo, keep_wd, recv_wd, gu_parts[0], gu_flips
        )
        recv_q = plane_flips(give_q)
        keep_kvo, give_kvo = split_sums(keep_kvo, recv_kvo, "x")
        keep_wd, give_wd = split_sums(
            keep_wd.reshape((-1,) + keep_wd.shape[2:]), recv_wd.reshape((-1,) + keep_wd.shape[2:]), "y"
        )
        recv_wd = flip_y(give_wd)
        recv_kvo = flip_x(give_kvo)
        d_h_keep, d_h_give = back_project([d_q, d_kv[0], d_kv[1]], w_thirds)
        gu_keep, gu_give = z_merge(gu_kept, *gu_flips)
        keep_q, recv_q, keep_kvo, recv_kvo, keep_wd, recv_wd, d_h_keep, d_h_give, gu_keep, gu_give = fence(
            keep_q, recv_q, keep_kvo, recv_kvo, keep_wd, recv_wd, d_h_keep, d_h_give, gu_keep, gu_give
        )
        *parts, wd_own = plane_sort((keep_q,) + tuple(recv_q), (keep_kvo, recv_kvo), units=(keep_wd, recv_wd))
        parts, d_h_give, wd_own = fence(parts, d_h_give, wd_own)
        d_h_recv = flip_core(d_h_give)
        flips = z_flips(parts)
        d_h_own, d_h_give = pair_add(d_h_keep, d_h_recv)
        d_h_recv = flip_z(d_h_give)
        gu_recv = flip_core(gu_give)
        sum_wg, sum_wu, grad_g_ffn = join_units(gu_keep, gu_recv, (w_gate, w_up), gain_ffn, n_devices)
        grad_x = input_back(d_h_own, d_h_recv, x_all, g_attn[None], d_x_own)
        kept, flips, grad_x, wd_own, sum_wg, sum_wu = fence(parts[0], flips, grad_x, wd_own, sum_wg, sum_wu)
        qkvo_keep, qkvo_give = z_merge(kept, *flips)
        qkvo_recv = flip_core(qkvo_give)
        wd_recv = flips[1][kept.shape[0] : kept.shape[0] + wd_own.shape[0]]
        sum_wd = wd_own.astype(F32) + wd_recv.astype(F32)
    else:
        down_recv = flip_z(down_give)
        recv_wd = flip_x(give_wd)
        d_q, *d_kv = stream_backward(
            d_att, out_f32, queries, keys, values, live_all, log_total, allow, memory, cosine, sine
        ).reshape(3, group_tokens, quarter)

        def by_chip(value):
            return value.reshape(n_high, 2, -1, value.shape[-1])

        (keep_qkv, *give_qkv), (keep_wo, *give_wo) = gradient(
            (h_one, [d_q, d_kv[0], d_kv[1]], "xy", None), (attended, [d_branch], "xy", quarter)
        )
        plane_gu = [add_low(keep_g, flip_y(give_g)), add_low(keep_u, flip_x(give_u))]
        z_gu = z_plain(by_chip(jnp.concatenate(plane_gu, -1)))
        plane_qkvo = [add_all(keep_qkv, *plane_flips(give_qkv)), add_all(keep_wo, *plane_flips(give_wo))]
        z_qkvo = z_plain(by_chip(jnp.concatenate(plane_qkvo, -1)))
        (gu_keep, gu_give), (qkvo_keep, qkvo_give) = core_halves(z_gu), core_halves(z_qkvo)
        qkvo_recv, gu_recv = flip_core(qkvo_give), flip_core(gu_give)
        keep_wd, give_wd = halves(add_low(keep_wd, recv_wd), 1, y)
        recv_wd = flip_y(give_wd)
        d_h_keep, d_h_give = back_project([d_q, d_kv[0], d_kv[1]], w_thirds)
        d_h_own, d_h_give = pair_add(d_h_keep, flip_core(d_h_give))
        d_h_recv = flip_z(d_h_give)
        grad_x = input_back(d_h_own, d_h_recv, x_all, g_attn[None], d_x_own)
        sum_wd = reduce_high(add_low(keep_wd, recv_wd)[:, None])[0].astype(F32)
        sum_wg, sum_wu, grad_g_ffn = join_units(gu_keep, gu_recv, (w_gate, w_up), gain_ffn, n_devices)
    layer_output = (cut(x_one, own, seg_len, 0) + down_own.astype(F32) + down_recv.astype(F32)).astype(BF)
    sum_q, sum_k, sum_v, sum_o, grad_g_attn = join_columns(
        qkvo_keep, qkvo_recv, (w_query, w_key, w_value), gain_attn, 4
    )
    return (
        layer_output[None],
        grad_x[None],
        grad_g_attn,
        sum_q,
        sum_k,
        sum_v,
        sum_o,
        grad_g_ffn,
        sum_wg,
        sum_wu,
        sum_wd,
    )


def solution(mesh):
    tokens = P("rep", "seg", None)
    vector = P(("seg", "rep"))
    matrix = P(("seg", "rep"), None)
    return jax.shard_map(
        local,
        mesh=mesh,
        in_specs=(
            tokens,
            P("rep", "seg"),
            tokens,
            tokens,
            tokens,
            vector,
            matrix,
            matrix,
            matrix,
            matrix,
            vector,
            matrix,
            matrix,
            matrix,
            tokens,
        ),
        out_specs=(tokens, tokens, vector, matrix, matrix, matrix, matrix, vector, matrix, matrix, matrix),
        check_vma=False,
    )
```

```python
import jax
import jax.numpy as jnp
from jax import lax
from jax.experimental import pallas as pl
from jax.experimental.pallas import tpu as pltpu
from jax.sharding import PartitionSpec as P

H = 8
HD = 128
EPSILON = 1e-05
NEG_BIG = -1e30
POS_BIG = 1e30
ROPE_BASE = 10000.0
LANES = 128
KERNEL_HIGH = 2
LOG2_E = 1.4426950408889634
VMEM_BYTES = 44 * 1024 * 1024

SHORT = pl.CostEstimate(flops=1000, bytes_accessed=1000, transcendentals=0)

BF = jnp.bfloat16
F32 = jnp.float32


def cdiv(a, b):
    return -(-a // b)


def flip(value, axis, bit):
    count = lax.axis_size(axis)
    return lax.ppermute(value, axis, [(i, i ^ bit) for i in range(count)])


def flip_core(value):
    return flip(value, "rep", 1)


def flip_y(value):
    return flip(value, "rep", 2)


def flip_x(value):
    return flip(value, "seg", 1)


def flip_z(value):
    return flip(value, "seg", 2)


def ordered(mine, other, bit, axis):
    first = jnp.where(bit == 0, mine, other)
    second = jnp.where(bit == 0, other, mine)
    return jnp.concatenate([first, second], axis)


def pick(value, index, axis):
    return lax.dynamic_index_in_dim(value, index, axis, keepdims=False)


def cut(value, start, size, axis=-1):
    return lax.dynamic_slice_in_dim(value, start, size, axis % value.ndim)


def fence(*values):
    return lax.optimization_barrier(values)


def place():
    seg = lax.axis_index("seg")
    rep = lax.axis_index("rep")
    return seg % 2, (seg // 2) % 2, seg // 4, rep // 2, rep % 2


def high_bits():
    bit = 4
    out = []
    while bit < lax.axis_size("seg"):
        out.append(bit)
        bit *= 2
    return out


def gather_high(cur):
    seg = lax.axis_index("seg")
    for bit in high_bits():
        cur = ordered(cur, flip(cur, "seg", bit), (seg // bit) % 2, 0)
    return cur


def gather_x(cur):
    return ordered(cur, flip_x(cur), place()[0], 2)


def gather_y(cur):
    return ordered(cur, flip_y(cur), place()[3], 3)


def gather_high_pair(cur):
    seg = lax.axis_index("seg")
    cur = cur[:, None]
    bits = high_bits()
    for bit in bits[:-1]:
        cur = ordered(cur, flip(cur, "seg", bit), (seg // bit) % 2, 1)
    recv = flip(cur, "seg", bits[-1])
    side = (seg // bits[-1]) % 2
    return [ordered(cur[i], recv[i], side, 0)[:, :, None, None] for i in range(2)]


def flat(cur):
    return cur.reshape(-1, cur.shape[-1])


def halve(value, axis_name, bit, side, axis):
    recv = flip(pick(value, 1 - side, axis), axis_name, bit)
    kept = pick(value, side, axis)
    return (kept.astype(F32) + recv.astype(F32)).astype(BF)


def plane_shape(value, low):
    high = lax.axis_size("seg") // 4
    return value.reshape(high, low, 2, -1, value.shape[-1])


def halves(cur, axis, side):
    return pick(cur, side, axis), pick(cur, 1 - side, axis)


def plane_flips(parts):
    n_rep = lax.axis_size("rep")
    count = lax.axis_size("seg") * n_rep
    far = [(i, i ^ n_rep ^ 2) for i in range(count)]
    return flip_x(parts[0]), flip_y(parts[1]), lax.ppermute(parts[2], ("seg", "rep"), far)


def add_all(first, *others):
    total = first.astype(F32)
    for other in others:
        total = total + other.astype(F32)
    return total.astype(BF)


def z_flips(parts):
    return flip_z(parts[1]), flip(parts[2], "seg", 4), flip(parts[3], "seg", 6)


def z_plain(cur):
    low = place()[1]
    sums = reduce_high(cur)
    return ordered(pick(sums, low, 0)[None], flip_z(pick(sums, 1 - low, 0))[None], low, 0)


def reduce_high(cur):
    seg = lax.axis_index("seg")
    for bit in reversed(high_bits()):
        cur = cur.reshape((2, cur.shape[0] // 2) + cur.shape[1:])
        cur = halve(cur, "seg", bit, (seg // bit) % 2, 0)
    return cur[0]


def trade_core(quarters):
    core = place()[4]
    low, unused, rows, cols = 2, 2, quarters.shape[1], quarters.shape[2]
    four = quarters.reshape(2, 2, rows, cols)
    return ordered(pick(four, core, 1), flip_core(pick(four, 1 - core, 1)), core, 1)


def trade_z(halves):
    low = place()[1]
    return ordered(pick(halves, low, 0)[None], flip_z(pick(halves, 1 - low, 0))[None], low, 0)


def gather_z_four(halves):
    seg = lax.axis_index("seg")
    low = (seg // 2) % 2
    keep, give = pick(halves, low, 0)[None, None], pick(halves, 1 - low, 0)[None, None]
    near = ordered(keep, flip(give, "seg", 2), low, 1)
    far = ordered(flip(keep, "seg", 4), flip(give, "seg", 6), low, 1)
    return ordered(near, far, (seg // 4) % 2, 0)[:, :, None, None]


def start_gather(traded):
    return traded[None, :, None, None]


def core_halves(mine):
    core = place()[4]
    four = mine.reshape(2, 2, mine.shape[1] // 2, mine.shape[2])
    return halves(four, 1, core)


def all_blocks(by_low):
    both = jnp.stack([by_low, flip_core(by_low)], 1)
    return both.reshape((-1,) + by_low.shape[1:])


def two_rows(value):
    return ordered(value[None], flip_z(value)[None], place()[1], 0)


def core_parts(part):
    blocks = part.reshape((2, 2, part.shape[0] // 4) + part.shape[1:])
    return blocks[:, 0].astype(BF), blocks[:, 1].astype(BF)


def core_sums(part):
    blocks = part.reshape((2, 2, part.shape[0] // 4) + part.shape[1:])
    return (blocks[:, 0] + flip_core(blocks[:, 1].astype(BF)).astype(F32)).astype(BF)


def own_sums(sums):
    low = place()[1]
    return pick(sums, low, 0).astype(F32) + flip_z(pick(sums, 1 - low, 0)).astype(F32)


def z_sums(sums):
    return (sums.astype(F32) + flip_z(sums).astype(F32)).astype(BF)


def both_cores(sums):
    return jnp.stack([sums, flip_core(sums)], 1).astype(F32)


def unit_blocks(n_blocks):
    order = []
    for block in range(n_blocks):
        high, low, rest, core = block // 16, (block // 8) % 2, (block // 2) % 4, block % 2
        order.append((low * 2 + core, high * 4 + rest))
    return order


def split_units(one, two, n_blocks):
    rows, total = one.shape
    size = total // n_blocks

    def body(one_ref, two_ref, out_ref):
        for half, in_ref in enumerate((one_ref, two_ref)):
            for block, (quarter, at) in enumerate(unit_blocks(n_blocks)):
                out_ref[quarter, half * rows : (half + 1) * rows, at * size : (at + 1) * size] = in_ref[
                    :, block * size : (block + 1) * size
                ]

    return pl.pallas_call(
        body,
        out_shape=jax.ShapeDtypeStruct((4, 2 * rows, total // 4), one.dtype),
        cost_estimate=SHORT,
        name="split_units",
    )(one, two)


def matmul(left, right):
    return jnp.dot(left, right, preferred_element_type=F32)


def matmul_rows(left, right):
    return lax.dot_general(left, right, (((0,), (0,)), ((), ())), preferred_element_type=F32)


def matmul_cols(left, right):
    return lax.dot_general(left, right, (((1,), (1,)), ((), ())), preferred_element_type=F32)


def norm_forward(values, gain):
    inverse = lax.rsqrt(jnp.mean(values * values, axis=-1, keepdims=True) + EPSILON)
    return (values * inverse * gain, inverse)


def norm_backward(values, inverse, gain, grad_out):
    normed = values * inverse
    scaled = grad_out * gain
    grad_values = inverse * (scaled - normed * jnp.mean(scaled * normed, axis=-1, keepdims=True))
    return (grad_values, normed)


def rope_tables(seg_len):
    position = jnp.arange(seg_len).astype(F32)
    freqs = ROPE_BASE ** (-(2.0 * jnp.arange(HD // 2).astype(F32)) / HD)
    angle = position[:, None] * freqs[None, :]
    cosine, sine = jnp.cos(angle), jnp.sin(angle)
    return (jnp.concatenate([cosine, cosine], -1), jnp.concatenate([-sine, sine], -1))


def rope_heads(values, cosine, sine):
    half = HD // 2
    swapped = jnp.concatenate([values[..., half:], values[..., :half]], -1)
    return values * cosine[:, None, :] + swapped * sine[:, None, :]


def mask_kernel(n_cols, cols_ref, live_ref, out_ref, scratch):
    queries = cols_ref.shape[1]
    picks = cols_ref[0]
    pad = scratch.shape[0]
    high = lax.shift_right_arithmetic(picks, 7)
    low = jnp.bitwise_and(picks, LANES - 1)
    iota_high = lax.broadcasted_iota(jnp.int32, (pad, picks.shape[1]), 0)
    iota_low = lax.broadcasted_iota(jnp.int32, (LANES, picks.shape[1]), 0)
    for i in range(queries):
        hot_high = jnp.where(iota_high == high[i : i + 1, :], 1.0, 0.0).astype(BF)
        hot_low = jnp.where(iota_low == low[i : i + 1, :], 1.0, 0.0).astype(BF)
        scratch[:, i, :] = matmul_cols(hot_high, hot_low)
    out_ref[0, 0:n_cols] = jnp.where(scratch[0:n_cols] > 0.5, POS_BIG, NEG_BIG).astype(BF)
    row = lax.broadcasted_iota(jnp.int32, (queries, LANES), 0) + pl.program_id(1) * queries
    for part in range(out_ref.shape[1] - n_cols):
        col = lax.broadcasted_iota(jnp.int32, (queries, LANES), 1) + part * LANES
        live = live_ref[0, :, part * LANES : (part + 1) * LANES]
        allow = (col == row) | ((col < row) & (live == 1))
        out_ref[0, n_cols + part] = jnp.where(allow, POS_BIG, NEG_BIG).astype(BF)


def build_mask(columns, live, n_cols):
    rows, queries, picks = columns.shape
    block = 16
    pad = cdiv(n_cols, 8) * 8
    n_local = live.shape[2] // LANES
    return pl.pallas_call(
        lambda *refs: mask_kernel(n_cols, *refs),
        grid=(rows, queries // block),
        in_specs=[
            pl.BlockSpec((1, block, picks), lambda r, g: (r, g, 0)),
            pl.BlockSpec((1, 1, live.shape[2]), lambda r, g: (r, 0, 0)),
        ],
        out_specs=pl.BlockSpec((1, n_cols + n_local, block, LANES), lambda r, g: (r, 0, g, 0)),
        out_shape=jax.ShapeDtypeStruct((rows, n_cols + n_local, queries, LANES), BF),
        scratch_shapes=[pltpu.VMEM((pad, block, LANES), F32)],
        compiler_params=pltpu.CompilerParams(vmem_limit_bytes=VMEM_BYTES),
        cost_estimate=SHORT,
        name="mask_build",
    )(columns, live)


def project_kernel(x_ref, wa_ref, wb_ref, cos_ref, sin_ref, q_ref, k_ref, v_ref, h_ref, inv_ref, gain_ref):
    quarter = q_ref.shape[2]

    @pl.when(pl.program_id(0) == 0)
    def gains():
        gain_ref[...] = jnp.transpose(wb_ref[:, quarter:].astype(F32), (1, 0))[0:8]

    x = x_ref[0].astype(F32)
    inverse = lax.rsqrt(jnp.mean(x * x, axis=-1, keepdims=True) + EPSILON)
    h = (x * inverse * gain_ref[0:1, :]).astype(BF)
    h_ref[0] = h
    inv_ref[0] = inverse
    turned = matmul(h, wa_ref[:, : 2 * quarter])
    for head in range(2 * quarter // HD):
        value = turned[:, head * HD : (head + 1) * HD]
        value = (value * cos_ref[...] + pltpu.roll(value, HD // 2, 1) * sin_ref[...]).astype(BF)
        if head < quarter // HD:
            q_ref[0, :, head * HD : (head + 1) * HD] = value
        else:
            at = head * HD - quarter
            k_ref[0, :, at : at + HD] = value
    v_ref[0] = matmul(h, wa_ref[:, 2 * quarter :]).astype(BF)


def project(x_all, w_a, w_b, cosine, sine):
    blocks, seg_len, width = x_all.shape
    quarter = w_a.shape[1] // 3
    whole = lambda array: pl.BlockSpec(array.shape, lambda r: (0, 0))
    head = pl.BlockSpec((1, seg_len, quarter), lambda r: (r, 0, 0))
    full = pl.BlockSpec((1, seg_len, width), lambda r: (r, 0, 0))
    out = jax.ShapeDtypeStruct((blocks, seg_len, quarter), BF)
    return pl.pallas_call(
        project_kernel,
        grid=(blocks,),
        in_specs=[full, whole(w_a), whole(w_b), whole(cosine), whole(sine)],
        out_specs=[head, head, head, full, pl.BlockSpec((1, seg_len, 1), lambda r: (r, 0, 0))],
        out_shape=[out, out, out, jax.ShapeDtypeStruct(x_all.shape, BF), jax.ShapeDtypeStruct((blocks, seg_len, 1), F32)],
        scratch_shapes=[pltpu.VMEM((8, width), F32)],
        compiler_params=pltpu.CompilerParams(vmem_limit_bytes=VMEM_BYTES),
        cost_estimate=SHORT,
        name="project",
    )(x_all, w_a, w_b, cosine, sine)


def plane_place():
    x, low, unused, y, core = place()
    return jnp.stack([x, y, 2 * low + core]).astype(jnp.int32)


def gradient(*entries):
    tokens, width = entries[0][0].shape
    n_blocks = lax.axis_size("seg")
    rows = width // n_blocks
    half = rows // 2
    sizes = [[entry[3] or right.shape[1] for right in entry[1]] for entry in entries]
    if rows % LANES:
        x, unused, unused, y, unused = place()
        outs = []
        for left, rights, way, columns in entries:
            if columns:
                rights = [cut(right, plane_place()[2] * columns, columns) for right in rights]
            full = jnp.concatenate([matmul_rows(left, right).astype(BF) for right in rights], 1)
            full = full.reshape(-1, 2, 2, half, full.shape[1])
            if way == "xy":
                near, side = halves(full, 1, x)
                near, side = halves(near, 1, y), halves(side, 1, y)
                parts = [near[0], side[0], near[1], side[1]]
            else:
                parts = halves(full, 1, x) if way == "x" else halves(full, 2, y)
            outs.append([part.reshape(-1, half, part.shape[-1]) for part in parts])
        return outs
    lefts = []
    for entry in entries:
        if not any(entry[0] is left for left in lefts):
            lefts.append(entry[0])
    which = [[entry[0] is left for left in lefts].index(True) for entry in entries]
    counts = [4 if entry[2] == "xy" else 2 for entry in entries]
    shapes = []
    for entry, size, count in zip(entries, sizes, counts):
        blocks = n_blocks // 2 if entry[2] == "xy" else n_blocks
        shapes += [(blocks, half, sum(size))] * count
    n_rights = sum(len(size) for size in sizes)

    def body(at_ref, *refs):
        left_refs, right_refs = refs[: len(lefts)], list(refs[len(lefts) : len(lefts) + n_rights])
        out_refs = list(refs[len(lefts) + n_rights :])
        pair = pl.program_id(0)
        turned = [jnp.transpose(ref[...]) for ref in left_refs]

        def by_row(value):
            upper, lower = value[:half], value[half:]
            return jnp.where(at_ref[1] == 0, upper, lower), jnp.where(at_ref[1] == 0, lower, upper)

        for entry, i, size, count in zip(entries, which, sizes, counts):
            outs, out_refs = out_refs[:count], out_refs[count:]
            start = 0
            for width_here in size:
                product = matmul(turned[i], right_refs.pop(0)[...]).astype(BF)
                span = slice(start, start + width_here)
                start += width_here
                first, second = product[:rows], product[rows:]
                if entry[2] == "y":
                    for side, value in enumerate((first, second)):
                        outs[0][2 * pair + side, :, span], outs[1][2 * pair + side, :, span] = by_row(value)
                    continue
                same = jnp.where(at_ref[0] == 0, first, second)
                other = jnp.where(at_ref[0] == 0, second, first)
                if entry[2] == "x":
                    for ref, value in zip(outs, (same, other)):
                        ref[2 * pair, :, span] = value[:half]
                        ref[2 * pair + 1, :, span] = value[half:]
                else:
                    outs[0][pair, :, span], outs[2][pair, :, span] = by_row(same)
                    outs[1][pair, :, span], outs[3][pair, :, span] = by_row(other)

    in_specs = [pl.BlockSpec((tokens, 2 * rows), lambda i, at: (0, i))] * len(lefts)
    for entry, size in zip(entries, sizes):
        column = (lambda i, at: (0, at[2])) if entry[3] else (lambda i, at: (0, 0))
        in_specs += [pl.BlockSpec((tokens, width_here), column) for width_here in size]
    outs = pl.pallas_call(
        body,
        grid_spec=pltpu.PrefetchScalarGridSpec(
            num_scalar_prefetch=1,
            grid=(n_blocks // 2,),
            in_specs=in_specs,
            out_specs=[pl.BlockSpec(shape, lambda i, at: (0, 0, 0)) for shape in shapes],
        ),
        out_shape=[jax.ShapeDtypeStruct(shape, BF) for shape in shapes],
        compiler_params=pltpu.CompilerParams(vmem_limit_bytes=VMEM_BYTES),
        cost_estimate=SHORT,
        name="gradient",
    )(plane_place(), *lefts, *[right for entry in entries for right in entry[1]])
    groups = []
    for count in counts:
        groups.append(outs[:count])
        outs = outs[count:]
    return groups


def split_sums(keep, recv, way):
    n_blocks, rows, cols = keep.shape

    def body(at_ref, keep_ref, recv_ref, mine_ref, give_ref):
        side = at_ref[1] if way == "y" else at_ref[0]
        for block in range(n_blocks // 2):
            for at, out_ref in ((2 * block + side, mine_ref), (2 * block + 1 - side, give_ref)):
                out_ref[block] = (keep_ref[at].astype(F32) + recv_ref[at].astype(F32)).astype(BF)

    vmem = pl.BlockSpec(memory_space=pltpu.VMEM)
    return pl.pallas_call(
        body,
        in_specs=[pl.BlockSpec(memory_space=pltpu.SMEM)] + [vmem] * 2,
        out_specs=[vmem] * 2,
        out_shape=[jax.ShapeDtypeStruct((n_blocks // 2, rows, cols), BF)] * 2,
        compiler_params=pltpu.CompilerParams(vmem_limit_bytes=VMEM_BYTES),
        cost_estimate=SHORT,
        name="split_sums",
    )(plane_place(), keep, recv)


def gradient_units(left, right):
    tokens, width = left.shape
    n_high = lax.axis_size("seg") // 4
    rows = width // (4 * n_high)
    cols = right.shape[1]
    step = 256
    if rows % 8:
        full = matmul_rows(left, right).astype(BF).reshape(-1, 2, 2, rows, cols)
        return halves(full, 1, place()[0])

    def body(at_ref, left_ref, right_ref, keep_ref, give_ref):
        product = matmul_rows(left_ref[...], right_ref[...])
        for high in range(n_high):
            for y in range(2):
                zero, one = [
                    product[(high * 4 + x * 2 + y) * rows : (high * 4 + x * 2 + y + 1) * rows] for x in range(2)
                ]
                keep_ref[high, y] = jnp.where(at_ref[0] == 0, zero, one).astype(BF)
                give_ref[high, y] = jnp.where(at_ref[0] == 0, one, zero).astype(BF)

    shape = (n_high, 2, rows, cols)
    return pl.pallas_call(
        body,
        grid_spec=pltpu.PrefetchScalarGridSpec(
            num_scalar_prefetch=1,
            grid=(cols // step,),
            in_specs=[
                pl.BlockSpec((tokens, width), lambda i, at: (0, 0)),
                pl.BlockSpec((tokens, step), lambda i, at: (0, i)),
            ],
            out_specs=[pl.BlockSpec((n_high, 2, rows, step), lambda i, at: (0, 0, 0, i))] * 2,
        ),
        out_shape=[jax.ShapeDtypeStruct(shape, BF)] * 2,
        compiler_params=pltpu.CompilerParams(vmem_limit_bytes=VMEM_BYTES),
        cost_estimate=SHORT,
        name="gradient_units",
    )(plane_place(), left, right)


def gather_columns(matrices, gain_one, gain_two):
    rows, width = matrices[0].shape
    quarter = width // 4

    def body(one_ref, two_ref, *refs):
        out_ref = refs[-1]
        pair = jnp.concatenate([one_ref[...], two_ref[...], jnp.zeros((6, rows), F32)], 0)
        square = jnp.concatenate([pair, jnp.zeros((8, LANES - rows), F32)], 1)
        square = jnp.concatenate([square, jnp.zeros((LANES - 8, LANES), F32)], 0)
        gains = jnp.transpose(square)[:rows].astype(BF)
        for i in range(4):
            for at, ref in enumerate(refs[:-1]):
                out_ref[i, :, at * quarter : (at + 1) * quarter] = ref[:, i * quarter : (i + 1) * quarter]
            out_ref[i, :, len(matrices) * quarter :] = gains

    return pl.pallas_call(
        body,
        out_shape=jax.ShapeDtypeStruct((4, rows, len(matrices) * quarter + LANES), BF),
        cost_estimate=SHORT,
        name="gather_columns",
    )(gain_one.astype(F32)[None], gain_two.astype(F32)[None], *matrices)


def group_place():
    unused, low, high, unused, core = place()
    return jnp.stack([2 * high + low, low, core]).astype(jnp.int32)


def plane_sort(*groups, units=()):
    sizes = [group[0].shape[-1] for group in groups]
    rows, cols = groups[0][0].shape[1], sum(sizes)
    shapes = [(rows, cols)] * 4
    if units:
        unit_rows = units[0].shape[1]
        below = cdiv(unit_rows, 16) * 16
        shapes = [(rows + below if way == 2 else rows, cols) for way in range(4)] + [(unit_rows, cols)]

    def body(at_ref, *refs):
        in_refs, out_refs = list(refs[: -len(shapes)]), refs[-len(shapes) :]
        unit_refs = in_refs[len(in_refs) - len(units) :]
        for way in range(4):
            start = 0
            left = list(in_refs)
            for size, group in zip(sizes, groups):
                total = None
                for unused in group:
                    part = left.pop(0)[at_ref[0] ^ way].astype(F32)
                    total = part if total is None else total + part
                out_refs[way][0:rows, start : start + size] = total.astype(BF)
                start += size
        if units:
            high = lax.shift_right_logical(at_ref[0], 1)
            own = sum(ref[high].astype(F32) for ref in unit_refs)
            give = sum(ref[1 - high].astype(F32) for ref in unit_refs)
            out_refs[4][...] = own.astype(BF)
            give = jnp.concatenate([give, jnp.zeros((below - unit_rows, cols), F32)], 0)
            out_refs[2][rows : rows + below, :] = give.astype(BF)

    vmem = pl.BlockSpec(memory_space=pltpu.VMEM)
    arrays = [array for group in groups for array in group] + list(units)
    return pl.pallas_call(
        body,
        in_specs=[pl.BlockSpec(memory_space=pltpu.SMEM)] + [vmem] * len(arrays),
        out_specs=[vmem] * len(shapes),
        out_shape=[jax.ShapeDtypeStruct(shape, BF) for shape in shapes],
        compiler_params=pltpu.CompilerParams(vmem_limit_bytes=VMEM_BYTES),
        cost_estimate=SHORT,
        name="plane_sort",
    )(group_place(), *arrays)


def z_merge(kept, from_1, from_2, from_3):
    rows, cols = kept.shape
    half = rows // 2

    def body(at_ref, kept_ref, one_ref, two_ref, three_ref, keep_ref, give_ref):
        same = kept_ref[...].astype(F32) + two_ref[0:rows, :].astype(F32)
        other = one_ref[...].astype(F32) + three_ref[...].astype(F32)
        for quarter, value in ((at_ref[1], same), (1 - at_ref[1], other)):
            upper, lower = value[:half], value[half:]
            keep_ref[quarter] = jnp.where(at_ref[2] == 0, upper, lower).astype(BF)
            give_ref[quarter] = jnp.where(at_ref[2] == 0, lower, upper).astype(BF)

    vmem = pl.BlockSpec(memory_space=pltpu.VMEM)
    return pl.pallas_call(
        body,
        in_specs=[pl.BlockSpec(memory_space=pltpu.SMEM)] + [vmem] * 4,
        out_specs=[vmem] * 2,
        out_shape=[jax.ShapeDtypeStruct((2, half, cols), BF)] * 2,
        compiler_params=pltpu.CompilerParams(vmem_limit_bytes=VMEM_BYTES),
        cost_estimate=SHORT,
        name="z_merge",
    )(group_place(), kept, from_1, from_2, from_3)


def join_quarters(mine, recv, core_ref, start, size, z_low, core):
    return jnp.where(
        core_ref[2] == core, mine[z_low, :, start : start + size], recv[z_low, :, start : start + size]
    ).astype(F32)


def lane_sums(value):
    total = value[:, :LANES]
    for part in lane_blocks(value)[1:]:
        total = total + part
    return total


def sums_as_row(value):
    rows = value.shape[0]
    padded = jnp.concatenate([value, jnp.zeros((LANES - rows, LANES), F32)], 0)
    return jnp.sum(jnp.transpose(padded), axis=0, keepdims=True)[:, :rows]


def join_columns(mine, recv, weights, gain, n_matrices):
    rows, cols = mine.shape[1:]
    size = cols // n_matrices

    def body(at_ref, mine_ref, recv_ref, gain_ref, *refs):
        weight_refs, out_refs = refs[: len(weights)], refs[len(weights) :]
        total = jnp.zeros((rows, LANES), F32)
        for i in range(n_matrices):
            for z_low in range(2):
                for core in range(2):
                    at = (2 * z_low + core) * size
                    value = join_quarters(mine_ref, recv_ref, at_ref, i * size, size, z_low, core)
                    out_refs[i][:, at : at + size] = value
                    if i < len(weights):
                        total = total + lane_sums(value * weight_refs[i][:, at : at + size].astype(F32))
        out_refs[-1][...] = sums_as_row(total) / gain_ref[...]

    vmem = pl.BlockSpec(memory_space=pltpu.VMEM)
    outs = pl.pallas_call(
        body,
        in_specs=[pl.BlockSpec(memory_space=pltpu.SMEM)] + [vmem] * (3 + len(weights)),
        out_specs=[vmem] * (n_matrices + 1),
        out_shape=[jax.ShapeDtypeStruct((rows, 4 * size), F32)] * n_matrices + [jax.ShapeDtypeStruct((1, rows), F32)],
        cost_estimate=SHORT,
        name="join_columns",
    )(group_place(), mine, recv, gain.astype(F32)[None], *weights)
    return list(outs[:-1]) + [outs[-1][0]]


def join_units(mine, recv, weights, gain, n_blocks):
    rows, both = mine.shape[1:]
    quarter_size = both // 2
    size = 4 * quarter_size // n_blocks

    def body(at_ref, mine_ref, recv_ref, gain_ref, one_weight, two_weight, one_ref, two_ref, total_ref):
        total = jnp.zeros((rows, LANES), F32)
        for half, (out_ref, weight_ref) in enumerate(((one_ref, one_weight), (two_ref, two_weight))):
            for block, (quarter, at) in enumerate(unit_blocks(n_blocks)):
                start = half * quarter_size + at * size
                out_ref[:, block * size : (block + 1) * size] = join_quarters(
                    mine_ref, recv_ref, at_ref, start, size, quarter // 2, quarter % 2
                )
            total = total + lane_sums(out_ref[...] * weight_ref[...].astype(F32))
        total_ref[...] = sums_as_row(total) / gain_ref[...]

    vmem = pl.BlockSpec(memory_space=pltpu.VMEM)
    one, two, total = pl.pallas_call(
        body,
        in_specs=[pl.BlockSpec(memory_space=pltpu.SMEM)] + [vmem] * 5,
        out_specs=[vmem] * 3,
        out_shape=[jax.ShapeDtypeStruct((rows, 4 * quarter_size), F32)] * 2 + [jax.ShapeDtypeStruct((1, rows), F32)],
        cost_estimate=SHORT,
        name="join_units",
    )(group_place(), mine, recv, gain.astype(F32)[None], *weights)
    return one, two, total[0]


def pair_add(one, two):
    def body(at_ref, one_ref, two_ref, own_ref, give_ref):
        for way, out_ref in enumerate((own_ref, give_ref)):
            at = at_ref[1] ^ way
            out_ref[...] = (one_ref[at].astype(F32) + two_ref[at].astype(F32)).astype(BF)

    vmem = pl.BlockSpec(memory_space=pltpu.VMEM)
    return pl.pallas_call(
        body,
        in_specs=[pl.BlockSpec(memory_space=pltpu.SMEM)] + [vmem] * 2,
        out_specs=[vmem] * 2,
        out_shape=[jax.ShapeDtypeStruct(one.shape[1:], BF)] * 2,
        compiler_params=pltpu.CompilerParams(vmem_limit_bytes=VMEM_BYTES),
        cost_estimate=SHORT,
        name="pair_add",
    )(group_place(), one, two)


def back_project(lefts, weights, transposed=True):
    block = lefts[0].shape[0] // 4
    out = weights[0].shape[0] if transposed else weights[0].shape[1]

    def body(*refs):
        left_refs, weight_refs = refs[: len(lefts)], refs[len(lefts) : 2 * len(lefts)]
        keep_ref, give_ref = refs[2 * len(lefts) :]
        total = None
        for left_ref, weight_ref in zip(left_refs, weight_refs):
            part = (matmul_cols if transposed else matmul)(left_ref[...], weight_ref[...])
            total = part if total is None else total + part
        total = total.astype(BF)
        for i in range(4):
            (keep_ref, give_ref)[i % 2][i // 2] = total[i * block : (i + 1) * block]

    return pl.pallas_call(
        body,
        in_specs=[pl.BlockSpec(memory_space=pltpu.VMEM)] * (2 * len(lefts)),
        out_specs=[pl.BlockSpec(memory_space=pltpu.VMEM)] * 2,
        out_shape=[jax.ShapeDtypeStruct((2, block, out), BF)] * 2,
        compiler_params=pltpu.CompilerParams(vmem_limit_bytes=VMEM_BYTES),
        cost_estimate=SHORT,
        name="back_project",
    )(*lefts, *weights)


def join_four(near, far, near_recv, far_recv, of_tokens):
    rows, size = near.shape
    block = rows // 4

    def body(at_ref, near_ref, far_ref, near_recv_ref, far_recv_ref, out_ref):
        for z_low in range(2):
            here = at_ref[1] == z_low
            for core in range(2):
                at = (2 * z_low + core) * size
                for i in range(4):
                    j = i ^ 1 if of_tokens else i
                    mine, other = slice(i * block, (i + 1) * block), slice(j * block, (j + 1) * block)
                    ours = jnp.where(here, near_ref[mine], far_ref[mine])
                    theirs = jnp.where(here, near_recv_ref[other], far_recv_ref[other])
                    out_ref[mine, at : at + size] = jnp.where(at_ref[2] == core, ours, theirs)

    vmem = pl.BlockSpec(memory_space=pltpu.VMEM)
    return pl.pallas_call(
        body,
        in_specs=[pl.BlockSpec(memory_space=pltpu.SMEM)] + [vmem] * 4,
        out_specs=vmem,
        out_shape=jax.ShapeDtypeStruct((rows, 4 * size), near.dtype),
        compiler_params=pltpu.CompilerParams(vmem_limit_bytes=VMEM_BYTES),
        cost_estimate=SHORT,
        name="join_four",
    )(group_place(), near, far, near_recv, far_recv)


def branch_back(mine, recv, x_one, gain, g_mine, g_recv, w_out):
    blocks, seg_len, width = x_one.shape
    quarter = width // 4

    def body(at_ref, mine_ref, recv_ref, x_ref, gain_ref, g_ref, g_recv_ref, w_ref, branch_ref, att_ref, own_ref):
        block = pl.program_id(0)
        grad = jnp.where(block % 2 == 0, mine_ref[0], recv_ref[0]).astype(F32)
        passed = jnp.where(block % 2 == 0, g_ref[0], g_recv_ref[0]).astype(F32)
        values = x_ref[0]
        inverse = lax.rsqrt(jnp.mean(values * values, axis=-1, keepdims=True) + EPSILON)
        normed = values * inverse
        scaled = grad * gain_ref[...]
        mean = jnp.mean(scaled * normed, axis=-1, keepdims=True)
        total = passed + inverse * (scaled - normed * mean)
        low = total.astype(BF)
        branch_ref[0] = low
        att_ref[0] = matmul_cols(low, w_ref[...]).astype(BF)

        @pl.when(block == 2 * at_ref[1])
        def own():
            own_ref[...] = total

    pair = pl.BlockSpec((1, seg_len, width), lambda i, at: (i // 2, 0, 0))
    full = pl.BlockSpec((1, seg_len, width), lambda i, at: (i, 0, 0))
    return pl.pallas_call(
        body,
        grid_spec=pltpu.PrefetchScalarGridSpec(
            num_scalar_prefetch=1,
            grid=(blocks,),
            in_specs=[
                pair,
                pair,
                full,
                pl.BlockSpec((1, width), lambda i, at: (0, 0)),
                pair,
                pair,
                pl.BlockSpec((quarter, width), lambda i, at: (2 * at[1] + at[2], 0)),
            ],
            out_specs=[
                full,
                pl.BlockSpec((1, seg_len, quarter), lambda i, at: (i, 0, 0)),
                pl.BlockSpec((seg_len, width), lambda i, at: (0, 0)),
            ],
        ),
        out_shape=[
            jax.ShapeDtypeStruct((blocks, seg_len, width), BF),
            jax.ShapeDtypeStruct((blocks, seg_len, quarter), BF),
            jax.ShapeDtypeStruct((seg_len, width), F32),
        ],
        compiler_params=pltpu.CompilerParams(vmem_limit_bytes=VMEM_BYTES),
        cost_estimate=SHORT,
        name="branch_back",
    )(group_place(), mine, recv, x_one, gain, g_mine, g_recv, w_out)


def input_back(mine, recv, x_all, gain, passed):
    unused, seg_len, width = x_all.shape

    def body(at_ref, mine_ref, recv_ref, x_ref, gain_ref, passed_ref, out_ref):
        values = x_ref[0].astype(F32)
        inverse = lax.rsqrt(jnp.mean(values * values, axis=-1, keepdims=True) + EPSILON)
        normed = values * inverse
        scaled = (mine_ref[...].astype(F32) + recv_ref[...].astype(F32)) * gain_ref[...]
        mean = jnp.mean(scaled * normed, axis=-1, keepdims=True)
        out_ref[...] = (passed_ref[...] + inverse * (scaled - normed * mean)).astype(BF)

    tokens = pl.BlockSpec((seg_len, width), lambda i, at: (0, 0))
    return pl.pallas_call(
        body,
        grid_spec=pltpu.PrefetchScalarGridSpec(
            num_scalar_prefetch=1,
            grid=(1,),
            in_specs=[
                tokens,
                tokens,
                pl.BlockSpec((1, seg_len, width), lambda i, at: (2 * at[1], 0, 0)),
                pl.BlockSpec((1, width), lambda i, at: (0, 0)),
                tokens,
            ],
            out_specs=tokens,
        ),
        out_shape=jax.ShapeDtypeStruct((seg_len, width), BF),
        compiler_params=pltpu.CompilerParams(vmem_limit_bytes=VMEM_BYTES),
        cost_estimate=SHORT,
        name="input_back",
    )(group_place(), mine, recv, x_all, gain, passed)


def add_kernel(one, two):
    def body(one_ref, two_ref, out_ref):
        out_ref[...] = (one_ref[...].astype(F32) + two_ref[...].astype(F32)).astype(BF)

    return pl.pallas_call(
        body,
        in_specs=[pl.BlockSpec(memory_space=pltpu.VMEM)] * 2,
        out_specs=pl.BlockSpec(memory_space=pltpu.VMEM),
        out_shape=jax.ShapeDtypeStruct(one.shape, BF),
        compiler_params=pltpu.CompilerParams(vmem_limit_bytes=VMEM_BYTES),
        cost_estimate=SHORT,
        name="add_kernel",
    )(one, two)


def add_low(one, two):
    return (one.astype(F32) + two.astype(F32)).astype(BF)


def lane_blocks(value):
    return [value[:, i : i + LANES] for i in range(0, value.shape[1], LANES)]


PIECES = ((0, 0), (0, 1), (1, 0), (1, 1), (2, 0), (3, 0), (2, 1))
N_COMMON = 5
N_GROUPS = 4


def head_of(value, head):
    return value[:, head * HD : (head + 1) * HD]


def forward_kernel(q_ref, k_ref, v_ref, mine_ref, other_ref, *refs):
    key_refs, value_refs = refs[:N_GROUPS], refs[N_GROUPS : 2 * N_GROUPS]
    o_ref, of_ref, p_ref, pl_ref, inv_ref, s_ref, top_ref, total_ref, acc_ref = refs[2 * N_GROUPS :]
    heads = range(q_ref.shape[2] // HD)
    scale = HD ** (-0.5) * LOG2_E
    block = pl.program_id(0)
    upper = block >= 2
    queries = q_ref[0]
    seg_len = queries.shape[0]
    per = key_refs[0].shape[1] // LANES
    first = block % 2 == 0

    def bias(at):
        return jnp.where(first, mine_ref[0, at], other_ref[0, at]).astype(F32)

    local_bias = jnp.concatenate([bias(len(PIECES) * per + i) for i in range(cdiv(seg_len, LANES))], 1)[:, :seg_len]
    s_local = [
        jnp.minimum(matmul_cols(head_of(queries, h), head_of(k_ref[0], h)) * scale, local_bias) for h in heads
    ]

    def score(t, tops):
        group, low = PIECES[t]
        keys = key_refs[group][low]
        parts = [lane_blocks(matmul_cols(head_of(queries, h), head_of(keys, h)) * scale) for h in heads]
        for i in range(per):
            limit = bias(t * per + i)
            for h in heads:
                part = jnp.minimum(parts[h][i], limit)
                s_ref[h, t, :, i * LANES : (i + 1) * LANES] = part
                tops[h] = part if tops[h] is None else jnp.maximum(tops[h], part)
        return tops

    tops = [None for h in heads]
    for t in range(N_COMMON):
        tops = score(t, tops)
    for h in heads:
        top_ref[h] = tops[h]

    @pl.when(upper)
    def more_scores():
        tops = [top_ref[h] for h in heads]
        for t in range(N_COMMON, len(PIECES)):
            tops = score(t, tops)
        for h in heads:
            top_ref[h] = tops[h]

    row_max, e_local = [], []
    for h in heads:
        row_max.append(
            jnp.maximum(
                jnp.max(s_local[h], axis=-1, keepdims=True), jnp.max(top_ref[h], axis=-1, keepdims=True)
            )
        )
        expo = jnp.exp2(s_local[h] - row_max[h])
        e_local.append(jnp.sum(expo, axis=-1, keepdims=True))
        chances = expo.astype(BF)
        pl_ref[0, h] = chances
        acc_ref[h] = matmul(chances, head_of(v_ref[0], h))

    def weigh(t, h, total, acc):
        group, low = PIECES[t]
        expo = jnp.exp2(s_ref[h, t] - row_max[h])
        for part in lane_blocks(expo):
            total = part if total is None else total + part
        chances = expo.astype(BF)
        p_ref[0, h, t] = chances
        return total, acc + matmul(chances, head_of(value_refs[group][low], h))

    for h in heads:
        total, acc = None, acc_ref[h]
        for t in range(N_COMMON):
            total, acc = weigh(t, h, total, acc)
        total_ref[h] = total
        acc_ref[h] = acc

    @pl.when(upper)
    def more_values():
        for h in heads:
            total, acc = total_ref[h], acc_ref[h]
            for t in range(N_COMMON, len(PIECES)):
                total, acc = weigh(t, h, total, acc)
            total_ref[h] = total
            acc_ref[h] = acc

    for h in heads:
        inverse = 1.0 / (e_local[h] + jnp.sum(total_ref[h], axis=-1, keepdims=True))
        out = acc_ref[h] * inverse
        of_ref[0, :, h * HD : (h + 1) * HD] = out
        o_ref[0, :, h * HD : (h + 1) * HD] = out.astype(BF)
        inv_ref[0, h] = inverse


def backward_local_kernel(do_ref, of_ref, q_ref, k_ref, v_ref, inv_ref, pl_ref, cos_ref, sin_ref, dkv_ref, dq_ref):
    scale = HD ** (-0.5)
    for h in range(q_ref.shape[2] // HD):
        span = slice(h * HD, (h + 1) * HD)
        d_out = do_ref[0, :, span]
        delta = jnp.sum(d_out.astype(F32) * of_ref[0, :, span], axis=-1, keepdims=True)
        chances = pl_ref[0, h].astype(F32) * inv_ref[0, h]
        ds = (chances * (matmul_cols(d_out, v_ref[0, :, span]) - delta)).astype(BF)
        dq_ref[0, :, span] = matmul(ds, k_ref[0, :, span])
        dk = matmul_rows(ds, q_ref[0, :, span])
        dkv_ref[0, 0, :, span] = (
            (dk * cos_ref[...] - pltpu.roll(dk, HD // 2, 1) * sin_ref[...]) * scale
        ).astype(BF)
        dkv_ref[1, 0, :, span] = matmul_rows(chances.astype(BF), d_out).astype(BF)


def backward_kernel(do_ref, of_ref, local_ref, inv_ref, p_ref, cos_ref, sin_ref, *refs):
    key_refs, value_refs = refs[:N_GROUPS], refs[N_GROUPS : 2 * N_GROUPS]
    out_ref, dq_ref = refs[2 * N_GROUPS :]
    heads = range(do_ref.shape[2] // HD)
    scale = HD ** (-0.5)
    upper = pl.program_id(0) >= 2
    d_out = [do_ref[0, :, h * HD : (h + 1) * HD] for h in heads]
    inverse = [inv_ref[0, h] for h in heads]
    delta = [
        jnp.sum(d_out[h].astype(F32) * of_ref[0, :, h * HD : (h + 1) * HD], axis=-1, keepdims=True) for h in heads
    ]

    def piece(t, h, dq):
        group, low = PIECES[t]
        dp = matmul_cols(d_out[h], head_of(value_refs[group][low], h))
        ds = (p_ref[0, h, t].astype(F32) * ((dp - delta[h]) * inverse[h])).astype(BF)
        return dq + matmul(ds, head_of(key_refs[group][low], h))

    for h in heads:
        dq = local_ref[0, :, h * HD : (h + 1) * HD]
        for t in range(N_COMMON):
            dq = piece(t, h, dq)
        dq_ref[h] = dq

    @pl.when(upper)
    def more():
        for h in heads:
            dq = dq_ref[h]
            for t in range(N_COMMON, len(PIECES)):
                dq = piece(t, h, dq)
            dq_ref[h] = dq

    for h in heads:
        dq = dq_ref[h]
        out_ref[0, :, h * HD : (h + 1) * HD] = (
            (dq * cos_ref[...] - pltpu.roll(dq, HD // 2, 1) * sin_ref[...]) * scale
        ).astype(BF)


def attention_specs(piece_rows, seg_len, width):
    heads = width // HD
    tokens = pl.BlockSpec((1, seg_len, width), lambda r: (r, 0, 0))
    piece = pl.BlockSpec((2, piece_rows, width), lambda r: (0, 0, 0))
    p_spec = pl.BlockSpec((1, heads, len(PIECES), seg_len, piece_rows), lambda r: (r, 0, 0, 0, 0))
    pl_spec = pl.BlockSpec((1, heads, seg_len, seg_len), lambda r: (r, 0, 0, 0))
    inv_spec = pl.BlockSpec((1, heads, seg_len, 1), lambda r: (r, 0, 0, 0))
    return tokens, piece, p_spec, pl_spec, inv_spec


def attention_forward(queries, keys, values, mask, other_mask, key_pieces, value_pieces):
    blocks, seg_len, width = queries.shape
    heads = width // HD
    piece_rows = key_pieces[0].shape[1]
    tokens, piece, p_spec, pl_spec, inv_spec = attention_specs(piece_rows, seg_len, width)
    mask_spec = pl.BlockSpec((1,) + mask.shape[1:], lambda r: (r // 2, 0, 0, 0))
    return pl.pallas_call(
        forward_kernel,
        grid=(blocks,),
        in_specs=[tokens, tokens, tokens, mask_spec, mask_spec] + [piece] * (2 * N_GROUPS),
        out_specs=[tokens, tokens, p_spec, pl_spec, inv_spec],
        out_shape=[
            jax.ShapeDtypeStruct(queries.shape, BF),
            jax.ShapeDtypeStruct(queries.shape, F32),
            jax.ShapeDtypeStruct((blocks, heads, len(PIECES), seg_len, piece_rows), BF),
            jax.ShapeDtypeStruct((blocks, heads, seg_len, seg_len), BF),
            jax.ShapeDtypeStruct((blocks, heads, seg_len, 1), F32),
        ],
        scratch_shapes=[
            pltpu.VMEM((heads, len(PIECES), seg_len, piece_rows), F32),
            pltpu.VMEM((heads, seg_len, LANES), F32),
            pltpu.VMEM((heads, seg_len, LANES), F32),
            pltpu.VMEM((heads, seg_len, HD), F32),
        ],
        compiler_params=pltpu.CompilerParams(vmem_limit_bytes=VMEM_BYTES),
        cost_estimate=SHORT,
        name="attention_forward",
    )(queries, keys, values, mask, other_mask, *key_pieces, *value_pieces)


def attention_backward_local(d_out, out_f32, queries, keys, values, inverse, p_local, cosine, sine):
    blocks, seg_len, width = queries.shape
    tokens, unused, unused, pl_spec, inv_spec = attention_specs(seg_len, seg_len, width)
    table = pl.BlockSpec((seg_len, HD), lambda r: (0, 0))
    return pl.pallas_call(
        backward_local_kernel,
        grid=(blocks,),
        in_specs=[tokens, tokens, tokens, tokens, tokens, inv_spec, pl_spec, table, table],
        out_specs=[pl.BlockSpec((2, 1, seg_len, width), lambda r: (0, r, 0, 0)), tokens],
        out_shape=[
            jax.ShapeDtypeStruct((2, blocks, seg_len, width), BF),
            jax.ShapeDtypeStruct(queries.shape, F32),
        ],
        compiler_params=pltpu.CompilerParams(vmem_limit_bytes=VMEM_BYTES),
        cost_estimate=SHORT,
        name="attention_backward_local",
    )(d_out, out_f32, queries, keys, values, inverse, p_local, cosine, sine)


def attention_backward(d_out, out_f32, dq_local, inverse, p_memory, cosine, sine, key_pieces, value_pieces):
    blocks, seg_len, width = d_out.shape
    piece_rows = key_pieces[0].shape[1]
    tokens, piece, p_spec, unused, inv_spec = attention_specs(piece_rows, seg_len, width)
    table = pl.BlockSpec((seg_len, HD), lambda r: (0, 0))
    return pl.pallas_call(
        backward_kernel,
        grid=(blocks,),
        in_specs=[tokens, tokens, tokens, inv_spec, p_spec, table, table] + [piece] * (2 * N_GROUPS),
        out_specs=tokens,
        out_shape=jax.ShapeDtypeStruct((blocks, seg_len, width), BF),
        scratch_shapes=[pltpu.VMEM((width // HD, seg_len, HD), F32)],
        compiler_params=pltpu.CompilerParams(vmem_limit_bytes=VMEM_BYTES),
        cost_estimate=SHORT,
        name="attention_backward",
    )(d_out, out_f32, dq_local, inverse, p_memory, cosine, sine, *key_pieces, *value_pieces)


def allow_local_of(live):
    seg_len = live.shape[-1]
    position = jnp.arange(seg_len, dtype=jnp.int32)
    same = position[None, :] == position[:, None]
    return same[None] | ((position[None, :] < position[:, None])[None] & (live == 1))


def split_heads(value):
    rows, seg_len, width = value.shape
    return value.reshape(rows, seg_len, width // HD, HD)


def stream_forward(queries, keys, values, live, allow, memory):
    scale = HD ** (-0.5)
    q4, k4, v4 = split_heads(queries), split_heads(keys), split_heads(values)
    scores = jnp.einsum("rqhd,rkhd->rhqk", q4, k4, preferred_element_type=F32) * scale
    scores = jnp.where(allow_local_of(live)[:, None], scores, NEG_BIG)
    row_max = jnp.max(scores, axis=-1)
    expo = jnp.exp(scores - row_max[..., None])
    state = (
        row_max,
        jnp.sum(expo, axis=-1),
        jnp.einsum("rhqk,rkhd->rhqd", expo.astype(BF), v4, preferred_element_type=F32),
    )

    def step(running, item):
        row_max, row_total, acc = running
        block, allowed = item
        k3 = block[0].reshape(block.shape[1], -1, HD)
        v3 = block[1].reshape(block.shape[1], -1, HD)
        scores = jnp.einsum("rqhd,khd->rhqk", q4, k3, preferred_element_type=F32) * scale
        scores = jnp.where(allowed[:, None] > 0, scores, NEG_BIG)
        new_max = jnp.maximum(row_max, jnp.max(scores, axis=-1))
        shrink = jnp.exp(row_max - new_max)
        expo = jnp.exp(scores - new_max[..., None])
        acc = acc * shrink[..., None] + jnp.einsum(
            "rhqk,khd->rhqd", expo.astype(BF), v3, preferred_element_type=F32
        )
        return (new_max, row_total * shrink + jnp.sum(expo, axis=-1), acc), None

    (row_max, row_total, acc), unused = lax.scan(step, state, (memory, allow))
    out = (acc / row_total[..., None]).transpose(0, 2, 1, 3).reshape(queries.shape)
    return out.astype(BF), out, row_max + jnp.log(row_total)


def stream_backward(d_out, out_f32, queries, keys, values, live, log_total, allow, memory, cosine, sine):
    scale = HD ** (-0.5)
    q4, k4, v4, d4 = split_heads(queries), split_heads(keys), split_heads(values), split_heads(d_out)
    delta = jnp.sum(d4.astype(F32) * split_heads(out_f32), axis=-1).transpose(0, 2, 1)
    scores = jnp.einsum("rqhd,rkhd->rhqk", q4, k4, preferred_element_type=F32) * scale
    scores = jnp.where(allow_local_of(live)[:, None], scores, NEG_BIG)
    chances = jnp.exp(scores - log_total[..., None])
    dp = jnp.einsum("rqhd,rkhd->rhqk", d4, v4, preferred_element_type=F32)
    ds = (chances * (dp - delta[..., None])).astype(BF)
    dq = jnp.einsum("rhqk,rkhd->rqhd", ds, k4, preferred_element_type=F32)
    dk = jnp.einsum("rhqk,rqhd->rkhd", ds, q4, preferred_element_type=F32)
    dv = jnp.einsum("rhqk,rqhd->rkhd", chances.astype(BF), d4, preferred_element_type=F32)

    def step(running, item):
        block, allowed = item
        k3 = block[0].reshape(block.shape[1], -1, HD)
        v3 = block[1].reshape(block.shape[1], -1, HD)
        scores = jnp.einsum("rqhd,khd->rhqk", q4, k3, preferred_element_type=F32) * scale
        scores = jnp.where(allowed[:, None] > 0, scores, NEG_BIG)
        chances = jnp.exp(scores - log_total[..., None])
        dp = jnp.einsum("rqhd,khd->rhqk", d4, v3, preferred_element_type=F32)
        ds = (chances * (dp - delta[..., None])).astype(BF)
        return running + jnp.einsum("rhqk,khd->rqhd", ds, k3, preferred_element_type=F32), None

    dq, unused = lax.scan(step, dq, (memory, allow))

    def back(value):
        turned = rope_heads(value.reshape((-1,) + value.shape[2:]), jnp.tile(cosine, (value.shape[0], 1)), -jnp.tile(sine, (value.shape[0], 1)))
        return (turned * scale).reshape(queries.shape).astype(BF)

    return jnp.stack([back(dq), back(dk), dv.reshape(queries.shape).astype(BF)])


def local(
    layer_input,
    live,
    knn_index,
    mem_keys,
    mem_values,
    gain_attn,
    w_query,
    w_key,
    w_value,
    w_out,
    gain_ffn,
    w_gate,
    w_up,
    w_down,
    cotangent,
):
    seg_len, width = layer_input.shape[1:]
    quarter = width // 4
    n_seg = lax.axis_size("seg")
    n_devices = n_seg * lax.axis_size("rep")
    tokens = seg_len * n_seg
    n_high = n_seg // 4
    x, low, high, y, core = place()
    use_kernel = n_high <= KERNEL_HIGH
    kv_rows = 2 * seg_len
    group_tokens = 4 * seg_len

    def by_quarter(value):
        return [value[:, i * quarter : (i + 1) * quarter] for i in range(4)]

    gains = None if width // n_devices % 16 == 0 else jnp.concatenate(
        [gain_attn[:, None], gain_ffn[:, None], jnp.zeros((gain_attn.shape[0], LANES - 2), BF)], 1
    )
    if gains is None:
        qo = gather_columns((w_query, w_key, w_value, w_out), gain_attn, gain_ffn)
    else:
        stacked = [by_quarter(w) for w in (w_query, w_key, w_value, w_out)]
        qo = jnp.stack([jnp.concatenate([s[i] for s in stacked] + [gains], 1) for i in range(4)])

    def core_quarters(value, side):
        return jnp.stack([cut(value, side * quarter, quarter), cut(value, (2 + side) * quarter, quarter)])

    def core_memory(side):
        return jnp.stack([core_quarters(mem_keys[0], side), core_quarters(mem_values[0], side)])

    coded = knn_index[0] * 2 + live[0][:, None]
    qo = qo.reshape(2, 2, -1, qo.shape[-1])
    qo_keep, qo_give = halves(qo, 1, core)
    kv_keep, kv_give = core_memory(core), core_memory(1 - core)
    qo_recv, kv_recv, coded_recv = flip_core(qo_give), flip_core(kv_give), flip_z(coded)
    qo_keep, kv_keep, coded, qo_recv, kv_recv, coded_recv, w_gate_, w_up_ = fence(
        qo_keep, kv_keep, coded, qo_recv, kv_recv, coded_recv, w_gate, w_up
    )

    qo_keep, qo_give = halves(ordered(qo_keep, qo_recv, core, 1), 0, low)
    kv_keep, kv_give = halves(ordered(kv_keep, kv_recv, core, 2), 1, low)
    coded = ordered(coded[None], coded_recv[None], low, 0)
    kv_recv = flip_z(kv_give)
    qo_near = flip_z(qo_give)
    down_w = w_down[None, None, None, None]
    x_own = layer_input[0]
    gate_up = split_units(w_gate_, w_up_, n_devices).reshape(2, 2, 2, -1, w_gate.shape[1] // 4)

    def places_of(codes, row_core):
        picks = lax.shift_right_arithmetic(codes, 1)
        pair = picks >= tokens
        slot = jnp.where(pair, picks - tokens, picks)
        slot_seg = slot // seg_len
        kv_row = jnp.bitwise_xor(pair.astype(jnp.int32), row_core)
        return picks, slot_seg, kv_row * seg_len + (slot - slot_seg * seg_len)

    split = 3 * quarter
    g_own = cotangent[0]
    cosine, sine = rope_tables(seg_len)
    if use_kernel:
        qo_far, qo_side = flip(qo_keep, "seg", 4), flip(qo_give, "seg", 6)
        picks, slot_seg, within = places_of(coded, core)
        slot_x, slot_low = slot_seg % 2, (slot_seg // 2) % 2
        same_x = slot_x == x
        in_group = jnp.where(same_x, 5, 4 + 2 * slot_low)
        before = jnp.where(same_x, 0, 2) + slot_low
        piece_no = jnp.where(slot_seg // 4 == high, in_group, before)
        columns = jnp.where(picks >= 0, piece_no * kv_rows + within, -1)
        live_two = jnp.bitwise_and(coded[:, :, 0], 1)[:, None, :]
        live_two = jnp.pad(live_two, ((0, 0), (0, 0), (0, cdiv(seg_len, LANES) * LANES - seg_len)))
        down_recv = flip(down_w, "seg", 4)
        (
            qo_keep, qo_near, qo_far, qo_side, kv_keep, kv_recv, x_own, gate_up, columns, live_two, down_w, down_recv
        ) = fence(
            qo_keep, qo_near, qo_far, qo_side, kv_keep, kv_recv, x_own, gate_up, columns, live_two, down_w, down_recv
        )

        pieces = ordered(kv_keep[:, None], kv_recv[:, None], low, 1)
        own_k, own_v = pieces[0], pieces[1]
        near = ordered(qo_keep[None, None], qo_near[None, None], low, 1)
        far = ordered(qo_far[None, None], qo_side[None, None], low, 1)
        qo = ordered(near, far, high, 0)[:, :, None, None]
        qo_a, qo_b = qo[..., :split], qo[..., split:]
        up_high = [(i, i + 4) for i in range(n_seg - 4)]

        def cross(value):
            return lax.ppermute(value, "seg", up_high)

        cross_k, side_k = cross(own_k), flip_x(own_k)
        a_recv, b_recv = flip_x(qo_a), flip_y(qo_b)
        x_recv = flip_z(x_own)
        gu_keep, gu_give = halves(gate_up, 1, core)
        gu_recv = flip_core(gu_give)
        mask = build_mask(columns, live_two, len(PIECES) * kv_rows // LANES)
        qo_a, qo_b, a_recv, b_recv, cross_k, side_k, own_v, x_own, x_recv, gu_keep, gu_recv, mask, down_w, down_recv = fence(
            qo_a, qo_b, a_recv, b_recv, cross_k, side_k, own_v, x_own, x_recv, gu_keep, gu_recv, mask, down_w, down_recv
        )

        cross_v, cross_side_k = cross(own_v), flip_x(cross_k)
        qo_a, qo_b = ordered(qo_a, a_recv, x, 2), ordered(qo_b, b_recv, y, 3)
        a_recv, b_recv = flip_y(qo_a), flip_x(qo_b)
        gu_keep, gu_give = halves(ordered(gu_keep, gu_recv, core, 2), 0, low)
        gu_recv = flip_z(gu_give)
        x_two = ordered(x_own[None], x_recv[None], low, 0)
        x_recv = flip_core(x_two)
        qo_a, qo_b, a_recv, b_recv, cross_v, cross_side_k, own_v, gu_keep, gu_recv, x_two, x_recv, mask, down_w, down_recv = fence(
            qo_a, qo_b, a_recv, b_recv, cross_v, cross_side_k, own_v, gu_keep, gu_recv, x_two, x_recv, mask, down_w, down_recv
        )

        cross_side_v, side_v = flip_x(cross_v), flip_x(own_v)
        other_mask = flip_core(mask)
        g_far = flip_z(g_own)
        w_a, w_b = flat(ordered(qo_a, a_recv, y, 3)), flat(ordered(qo_b, b_recv, x, 2))
        gate_up = ordered(gu_keep[:, None], gu_recv[:, None], low, 1)[:, None]
        gu_recv = flip(gate_up, "seg", 4)
        down_w = ordered(down_w, down_recv, high, 0)
        down_recv = flip_y(down_w)
        x_all = jnp.stack([x_two, x_recv], 1).reshape(4, seg_len, width)
        queries, keys, values, h_one, inv_one = project(x_all, w_a, w_b, cosine, sine)
        wo_near = w_b[:, :quarter]
        (
            queries, keys, values, cross_side_v, side_v, gate_up, gu_recv, down_w, down_recv, wo_near, g_own, g_far, other_mask
        ) = fence(
            queries, keys, values, cross_side_v, side_v, gate_up, gu_recv, down_w, down_recv, wo_near, g_own, g_far, other_mask
        )

        key_pieces = (cross_k, cross_side_k, side_k, own_k)
        value_pieces = (cross_v, cross_side_v, side_v, own_v)
        gate, upw = [ordered(gate_up[i], gu_recv[i], high, 0)[:, :, None, None] for i in range(2)]
        down_w = ordered(down_w, down_recv, y, 3)
        down_a, down_b = down_w[..., : 3 * width // 8], down_w[..., 3 * width // 8 :]
        g_recv, u_recv, a_recv, wo_far = flip_x(gate), flip_y(upw), flip_x(down_a), flip_z(wo_near)
        out_low, out_f32, p_memory, p_local, inverse = attention_forward(
            queries, keys, values, mask, other_mask, key_pieces, value_pieces
        )
        wo_recv = flip_core(wo_near)
        out_low, gate, upw, g_recv, u_recv, down_a, a_recv, down_b, wo_near, wo_far, wo_recv, g_own, g_far = fence(
            out_low, gate, upw, g_recv, u_recv, down_a, a_recv, down_b, wo_near, wo_far, wo_recv, g_own, g_far
        )
    else:
        qo = gather_high(ordered(qo_keep[None], qo_near[None], low, 0)[None, :, None, None])
        kv = ordered(kv_keep[:, None], kv_recv[:, None], low, 1)
        w_a, w_b = flat(gather_y(gather_x(qo[..., :split]))), flat(gather_x(gather_y(qo[..., split:])))
        x_all = all_blocks(two_rows(x_own))
        gu_keep, gu_give = halves(gate_up, 1, core)
        gu_keep, gu_give = halves(ordered(gu_keep, flip_core(gu_give), core, 2), 0, low)
        gate, upw = gather_high_pair(ordered(gu_keep[:, None], flip_z(gu_give)[:, None], low, 1))
        down_w = gather_y(gather_high(down_w))
        down_a, down_b = down_w[..., : 3 * width // 8], down_w[..., 3 * width // 8 :]
        coded = all_blocks(coded)
        row_core = jnp.bitwise_xor(core, jnp.arange(4, dtype=jnp.int32) % 2)[:, None, None]
        picks, slot_seg, within = places_of(coded, row_core)
        live_all = jnp.bitwise_and(coded[:, :, 0], 1)[:, None, :]
        columns = jnp.where(picks >= 0, slot_seg * kv_rows + within, n_seg * kv_rows)
        blocks_at = jnp.arange(4)[:, None, None]
        queries_at = jnp.arange(seg_len)[None, :, None]
        allow = jnp.zeros((4, seg_len, n_seg * kv_rows), BF).at[blocks_at, queries_at, columns].set(1.0, mode="drop")
        allow = allow.reshape(4, seg_len, n_seg, kv_rows).transpose(2, 0, 1, 3)
        memory = jnp.swapaxes(kv, 0, 1)[None, :, None]
        memory = gather_x(gather_high(memory)).reshape(n_seg, 2, kv_rows, quarter)
        queries, keys, values, h_one, inv_one = project(x_all, w_a, w_b, cosine, sine)
        wo_near = w_b[:, :quarter]
        out_low, out_f32, log_total = stream_forward(queries, keys, values, live_all, allow, memory)
        g_recv, u_recv, a_recv, wo_far = flip_x(gate), flip_y(upw), flip_x(down_a), flip_z(wo_near)
        g_far = flip_z(g_own)
        wo_recv = flip_core(wo_near)

    h_one = h_one.reshape(group_tokens, width)
    inv_one = inv_one.reshape(group_tokens, 1)
    x_float = x_all.reshape(group_tokens, width).astype(F32)
    g_attn = w_b[:, quarter].astype(F32)
    g_ffn = w_b[:, quarter + 1].astype(F32)
    att_near = out_low.reshape(group_tokens, quarter)
    att_far = flip_z(att_near)
    gate, upw = ordered(gate, g_recv, x, 2), ordered(upw, u_recv, y, 3)
    g_recv, u_recv = flip_y(gate), flip_x(upw)
    wo = join_four(wo_near, wo_far, wo_recv, flip_core(wo_far), False)
    att_recv = flip_core(att_near)
    att_near, att_far, att_recv, gate, upw, g_recv, u_recv, down_b, wo, g_own, g_far = fence(
        att_near, att_far, att_recv, gate, upw, g_recv, u_recv, down_b, wo, g_own, g_far
    )

    att_far_recv = flip_core(att_far)
    down_recv = flip_x(down_b)
    g_two = ordered(g_own[None], g_far[None], low, 0)
    g_recv_core = flip_core(g_two)
    wg, wu = flat(ordered(gate, g_recv, y, 3)), flat(ordered(upw, u_recv, x, 2))
    attended = join_four(att_near, att_far, att_recv, att_far_recv, True)
    x_one = x_float + matmul(attended, wo)
    h_two_f, inv_two = norm_forward(x_one, g_ffn)
    h_two = h_two_f.astype(BF)
    gate_out = matmul(h_two, wg)
    up_out = matmul(h_two, wu)
    sigma = jax.nn.sigmoid(gate_out)
    swish = gate_out * sigma
    hidden = (swish * up_out).astype(BF)
    grad_out = jnp.stack([g_two, g_recv_core], 1).reshape(group_tokens, width)

    down_b, hidden = fence(down_b, hidden)
    wd = jnp.concatenate([flat(ordered(down_a, a_recv, x, 2)), flat(ordered(down_b, down_recv, x, 2))], 1)
    d_hidden = matmul_cols(grad_out, wd)
    d_gate = (d_hidden * up_out * sigma * (1.0 + gate_out * (1.0 - sigma))).astype(BF)
    d_up = (d_hidden * swish).astype(BF)
    sums_keep, sums_give = back_project([d_gate, d_up], [wg, wu])
    sums_recv = flip_core(sums_give)
    (keep_g, give_g), (keep_u, give_u) = gradient((h_two, [d_gate], "x", None), (h_two, [d_up], "y", None))
    sums_keep, sums_recv, keep_g, give_g, keep_u, give_u, hidden, wd = fence(
        sums_keep, sums_recv, keep_g, give_g, keep_u, give_u, hidden, wd
    )

    sums = add_kernel(sums_keep, sums_recv)
    far_sums = flip_z(sums)
    recv_g, recv_u = flip_x(give_g), flip_y(give_u)
    down_keep, down_give = back_project([hidden], [wd], False)
    down_recv = flip_core(down_give)
    keep_wd, give_wd = gradient_units(hidden, grad_out)
    sums, far_sums, keep_g, keep_u, recv_g, recv_u, down_keep, down_recv, keep_wd, give_wd = fence(
        sums, far_sums, keep_g, keep_u, recv_g, recv_u, down_keep, down_recv, keep_wd, give_wd
    )

    own = 2 * low * seg_len
    summed = add_kernel(sums, far_sums)
    summed_recv = flip_core(summed)
    d_branch, d_att, d_x_own = branch_back(
        summed,
        summed_recv,
        x_one.reshape(4, seg_len, width),
        g_ffn[None],
        g_two,
        g_recv_core,
        wo,
    )
    d_branch = d_branch.reshape(group_tokens, width)
    keep_g, keep_u, recv_g, recv_u, d_att, d_branch, down_keep, down_recv = fence(
        keep_g, keep_u, recv_g, recv_u, d_att, d_branch, down_keep, down_recv
    )

    keep_g, give_g = split_sums(keep_g, recv_g, "y")
    keep_u, give_u = split_sums(keep_u, recv_u, "x")
    down_own, down_give = pair_add(down_keep, down_recv)
    w_thirds = [w_a[:, i * quarter : (i + 1) * quarter] for i in range(3)]
    if use_kernel:
        recv_g, recv_u = flip_y(give_g), flip_x(give_u)
        down_recv = flip_z(down_give)
        d_kv, dq_local = attention_backward_local(
            d_att, out_f32, queries, keys, values, inverse, p_local, cosine, sine
        )
        d_kv = d_kv.reshape(2, group_tokens, quarter)
        (keep_kv, give_kv), (keep_wo, give_wo) = gradient(
            (h_one, [d_kv[0], d_kv[1]], "y", None), (attended, [d_branch], "y", quarter)
        )
        give_kvo = jnp.concatenate([give_kv, give_wo], -1)
        keep_kvo = jnp.concatenate([keep_kv, keep_wo], -1)
        keep_kvo, give_kvo, keep_g, recv_g, keep_u, recv_u, dq_local, keep_wd, give_wd, down_own, down_recv = fence(
            keep_kvo, give_kvo, keep_g, recv_g, keep_u, recv_u, dq_local, keep_wd, give_wd, down_own, down_recv
        )
        gu_parts = plane_sort((keep_g, recv_g), (keep_u, recv_u))
        recv_kvo = flip_y(give_kvo)
        gu_flips = z_flips(gu_parts)
        recv_wd = flip_x(give_wd)
        d_q = attention_backward(
            d_att, out_f32, dq_local, inverse, p_memory, cosine, sine, key_pieces, value_pieces
        )
        d_q, keep_kvo = fence(d_q, keep_kvo)

        d_q = d_q.reshape(group_tokens, quarter)
        ((keep_q, *give_q),) = gradient((h_one, [d_q], "xy", None))
        keep_q, give_q, d_q, keep_kvo, recv_kvo, keep_wd, recv_wd, gu_kept, gu_flips = fence(
            keep_q, give_q, d_q, keep_kvo, recv_kvo, keep_wd, recv_wd, gu_parts[0], gu_flips
        )
        recv_q = plane_flips(give_q)
        keep_kvo, give_kvo = split_sums(keep_kvo, recv_kvo, "x")
        keep_wd, give_wd = split_sums(
            keep_wd.reshape((-1,) + keep_wd.shape[2:]), recv_wd.reshape((-1,) + keep_wd.shape[2:]), "y"
        )
        recv_wd = flip_y(give_wd)
        recv_kvo = flip_x(give_kvo)
        d_h_keep, d_h_give = back_project([d_q, d_kv[0], d_kv[1]], w_thirds)
        gu_keep, gu_give = z_merge(gu_kept, *gu_flips)
        keep_q, recv_q, keep_kvo, recv_kvo, keep_wd, recv_wd, d_h_keep, d_h_give, gu_keep, gu_give = fence(
            keep_q, recv_q, keep_kvo, recv_kvo, keep_wd, recv_wd, d_h_keep, d_h_give, gu_keep, gu_give
        )
        *parts, wd_own = plane_sort((keep_q,) + tuple(recv_q), (keep_kvo, recv_kvo), units=(keep_wd, recv_wd))
        parts, d_h_give, wd_own = fence(parts, d_h_give, wd_own)
        d_h_recv = flip_core(d_h_give)
        flips = z_flips(parts)
        d_h_own, d_h_give = pair_add(d_h_keep, d_h_recv)
        d_h_recv = flip_z(d_h_give)
        gu_recv = flip_core(gu_give)
        sum_wg, sum_wu, grad_g_ffn = join_units(gu_keep, gu_recv, (w_gate, w_up), gain_ffn, n_devices)
        grad_x = input_back(d_h_own, d_h_recv, x_all, g_attn[None], d_x_own)
        kept, flips, grad_x, wd_own, sum_wg, sum_wu = fence(parts[0], flips, grad_x, wd_own, sum_wg, sum_wu)
        qkvo_keep, qkvo_give = z_merge(kept, *flips)
        qkvo_recv = flip_core(qkvo_give)
        wd_recv = flips[1][kept.shape[0] : kept.shape[0] + wd_own.shape[0]]
        sum_wd = wd_own.astype(F32) + wd_recv.astype(F32)
    else:
        down_recv = flip_z(down_give)
        recv_wd = flip_x(give_wd)
        d_q, *d_kv = stream_backward(
            d_att, out_f32, queries, keys, values, live_all, log_total, allow, memory, cosine, sine
        ).reshape(3, group_tokens, quarter)

        def by_chip(value):
            return value.reshape(n_high, 2, -1, value.shape[-1])

        (keep_qkv, *give_qkv), (keep_wo, *give_wo) = gradient(
            (h_one, [d_q, d_kv[0], d_kv[1]], "xy", None), (attended, [d_branch], "xy", quarter)
        )
        plane_gu = [add_low(keep_g, flip_y(give_g)), add_low(keep_u, flip_x(give_u))]
        z_gu = z_plain(by_chip(jnp.concatenate(plane_gu, -1)))
        plane_qkvo = [add_all(keep_qkv, *plane_flips(give_qkv)), add_all(keep_wo, *plane_flips(give_wo))]
        z_qkvo = z_plain(by_chip(jnp.concatenate(plane_qkvo, -1)))
        (gu_keep, gu_give), (qkvo_keep, qkvo_give) = core_halves(z_gu), core_halves(z_qkvo)
        qkvo_recv, gu_recv = flip_core(qkvo_give), flip_core(gu_give)
        keep_wd, give_wd = halves(add_low(keep_wd, recv_wd), 1, y)
        recv_wd = flip_y(give_wd)
        d_h_keep, d_h_give = back_project([d_q, d_kv[0], d_kv[1]], w_thirds)
        d_h_own, d_h_give = pair_add(d_h_keep, flip_core(d_h_give))
        d_h_recv = flip_z(d_h_give)
        grad_x = input_back(d_h_own, d_h_recv, x_all, g_attn[None], d_x_own)
        sum_wd = reduce_high(add_low(keep_wd, recv_wd)[:, None])[0].astype(F32)
        sum_wg, sum_wu, grad_g_ffn = join_units(gu_keep, gu_recv, (w_gate, w_up), gain_ffn, n_devices)
    layer_output = (cut(x_one, own, seg_len, 0) + down_own.astype(F32) + down_recv.astype(F32)).astype(BF)
    sum_q, sum_k, sum_v, sum_o, grad_g_attn = join_columns(
        qkvo_keep, qkvo_recv, (w_query, w_key, w_value), gain_attn, 4
    )
    return (
        layer_output[None],
        grad_x[None],
        grad_g_attn,
        sum_q,
        sum_k,
        sum_v,
        sum_o,
        grad_g_ffn,
        sum_wg,
        sum_wu,
        sum_wd,
    )


def solution(mesh):
    tokens = P("rep", "seg", None)
    vector = P(("seg", "rep"))
    matrix = P(("seg", "rep"), None)
    return jax.shard_map(
        local,
        mesh=mesh,
        in_specs=(
            tokens,
            P("rep", "seg"),
            tokens,
            tokens,
            tokens,
            vector,
            matrix,
            matrix,
            matrix,
            matrix,
            vector,
            matrix,
            matrix,
            matrix,
            tokens,
        ),
        out_specs=(tokens, tokens, vector, matrix, matrix, matrix, matrix, vector, matrix, matrix, matrix),
        check_vma=False,
    )
```
